32 devices in a mesh: seq: 8 (over z, x), seg: 4 (over y, core).
Axes of the slice: x: 2, y: 2, z: 4, core: 2. Of those that a mesh axis runs over, the one named last changes fastest.
Arguments:
- tokens: bfloat16 [4, 2048, 1024], P('seg', 'seq'), may hold values from -6 to 6
- article_lengths: int32 [4, 8], P('seg'), may hold values from 1 to 2041, as said below
- gain_one: float32 [1024], replicated, may hold values from 0.1 to 1.9
- bias_one: float32 [1024], replicated, may hold values from -3 to 3
- w_qkv: bfloat16 [1024, 3072], P('seg'), may hold values from -0.25 to 0.25
- w_out: bfloat16 [1024, 1024], P('seg'), may hold values from -0.5 to 0.5
- gain_two: float32 [1024], replicated, may hold values from 0.1 to 1.9
- bias_two: float32 [1024], replicated, may hold values from -3 to 3
- w_up: bfloat16 [1024, 4096], P('seg'), may hold values from -0.1875 to 0.1875
- w_down: bfloat16 [4096, 1024], P('seg'), may hold values from -0.125 to 0.125
- cotangent: bfloat16 [4, 2048, 1024], P('seg', 'seq'), may hold values from -6 to 6
Outputs:
- result: bfloat16 [4, 2048, 1024], P('seg', 'seq')
- input_grad: float32 [4, 2048, 1024], P('seg', 'seq')
- grad_gain_one: float32 [1024], replicated
- grad_bias_one: float32 [1024], replicated
- grad_qkv: float32 [1024, 3072], P('seg', 'seq')
- grad_out: float32 [1024, 1024], P('seg', 'seq')
- grad_gain_two: float32 [1024], replicated
- grad_bias_two: float32 [1024], replicated
- grad_up: float32 [1024, 4096], P('seg', 'seq')
- grad_down: float32 [4096, 1024], P('seg', 'seq')
The draws below stay inside these ranges and needn't reach their ends.
Inputs may be any that keep to these rules, and one draw needn't show every extreme that they name: `article_lengths`: each row holds 8 article lengths that sum to 2048; one of them, at a place drawn from the seed, exceeds 2048 - 256, the others are at most 32.
All inputs are finite; a program needn't handle non-finite values.
Results may differ from the reference program's by a relative error of at most 0.02.
Values may be sent and summed in bfloat16 or wider, within the bound.
A program may use at most 192 MiB of HBM per device.

```python
import math
import jax
import jax.numpy as jnp
from jax import lax

D = 1024
HEADS = 8
HEAD_DIM = 128
FF = 4096
TOK_DEV = 256
ARTS = 8
SEG_LEN = 2048
SEGMENTS = 4


def draw_article_lengths(key, part):
    key = jax.random.fold_in(key, 5)
    short_key, place_key, row_key = jax.random.split(key, 3)
    shorts = jax.random.randint(short_key, (SEGMENTS, ARTS - 1), 1, TOK_DEV // ARTS + 1).astype(jnp.int32)
    picked_row = jax.random.randint(row_key, (), 0, SEGMENTS).astype(jnp.int32)
    row_index = jnp.arange(SEGMENTS, dtype=jnp.int32)[:, None]
    shorts = jnp.where(row_index == picked_row, jnp.ones_like(shorts), shorts).astype(jnp.int32)
    longest = SEG_LEN - jnp.sum(shorts, axis=1)
    where_long = jax.random.randint(place_key, (SEGMENTS, 1), 0, ARTS).astype(jnp.int32)
    column = jnp.arange(ARTS, dtype=jnp.int32)[None, :]
    before = jnp.concatenate([shorts, shorts[:, :1]], axis=1)
    after = jnp.concatenate([shorts[:, :1], shorts], axis=1)
    chosen = jnp.where(column == where_long, longest[:, None], after)
    return jnp.where(column < where_long, before, chosen).astype(jnp.int32)


def level_of(stream_key, extent, pieces, smallest, top_value):
    level = 1.0
    for axis_at, shards_of in pieces:
        steps = jax.random.uniform(jax.random.fold_in(jax.random.fold_in(stream_key, 6), axis_at), (shards_of,), jnp.float32, smallest / len(pieces), top_value / len(pieces))
        level = level * jnp.repeat(jnp.exp(steps), extent[axis_at] // shards_of).reshape((-1,) + (1,) * (len(extent) - 1 - axis_at))
    return level


def bell_draw(rng, extent, deviation, bound, pieces=(), kind=jnp.bfloat16):
    values = jax.random.normal(rng, extent, jnp.float32) * deviation
    if len(pieces) > 0:
        values = level_of(rng, extent, pieces, -0.22, 0.18) * values
    return jnp.clip(values, min=-bound, max=bound).astype(kind)


def setup_inputs(seed: int = 0) -> dict:
    streams_of = jax.random.split(jax.random.key(seed), 12)
    tokens = bell_draw(streams_of[0], (SEGMENTS, SEG_LEN, D), 1.0, 6.0, ((0, 4), (1, 8)))
    article_lengths = draw_article_lengths(jax.random.fold_in(streams_of[11], 71), 0)
    gain_one = jnp.clip(1.0 + 0.18 * jax.random.normal(streams_of[2], (D,), jnp.float32), 0.1, 1.9)
    bias_one = bell_draw(streams_of[3], (D,), 0.5, 3.0, (), jnp.float32)
    w_qkv = bell_draw(streams_of[4], (D, 3 * D), (D // 2) ** -0.5, 0.25, ((0, 4),))
    w_out = bell_draw(streams_of[5], (D, D), (D // 8) ** -0.5, 0.5, ((0, 4),))
    gain_two = jnp.clip(1.0 + 0.18 * jax.random.normal(streams_of[6], (D,), jnp.float32), 0.1, 1.9)
    bias_two = bell_draw(streams_of[7], (D,), 0.5, 3.0, (), jnp.float32)
    w_up = bell_draw(streams_of[8], (D, FF), D ** -0.5, 0.1875, ((0, 4),))
    w_down = bell_draw(streams_of[9], (FF, D), (FF // 2) ** -0.5, 0.125, ((0, 4),))
    cotangent = bell_draw(streams_of[10], (SEGMENTS, SEG_LEN, D), 1.0, 6.0, ((0, 4), (1, 8)))
    return dict(tokens=tokens, article_lengths=article_lengths, gain_one=gain_one, bias_one=bias_one, w_qkv=w_qkv, w_out=w_out, gain_two=gain_two, bias_two=bias_two, w_up=w_up, w_down=w_down, cotangent=cotangent)


@jax.custom_vjp
def low(v):
    return lax.optimization_barrier(v.astype(jnp.bfloat16)).astype(jnp.float32)

@jax.custom_vjp
def low_back(v):
    return v

def low_keep(v):
    return (low(v), None)

def low_pass(kept, grad):
    return (grad,)

def back_keep(v):
    return (v, None)

def back_low(kept, grad):
    return (low(grad),)
low.defvjp(low_keep, low_pass)
low_back.defvjp(back_keep, back_low)
highest = lax.Precision.HIGHEST

def layer_norm(values, gain, bias):
    center = values - lax.optimization_barrier(jnp.mean(values, axis=-1, keepdims=True))
    spread = lax.optimization_barrier(jnp.mean(center * center, axis=-1, keepdims=True))
    return center * lax.rsqrt(spread + 1e-05) * gain + bias

def article_numbers(lengths_row, positions):
    bounds = jnp.cumsum(lengths_row)
    return lax.optimization_barrier(jnp.sum((positions[:, None] >= bounds[None, :]).astype(jnp.int32), axis=1))

def attend_segment(queries, keys, values, lengths_row):
    seg_rows = queries.shape[0]
    block_rows = math.gcd(seg_rows, 512)
    key_pos = jnp.arange(seg_rows, dtype=jnp.int32)
    key_art = article_numbers(lengths_row, key_pos)
    scale = 1.0 / math.sqrt(HEAD_DIM)

    def one_block(packed):
        query_block, start = packed
        query_pos = start + jnp.arange(block_rows, dtype=jnp.int32)
        query_art = article_numbers(lengths_row, query_pos)
        scores = low_back(jnp.einsum('qhd,khd->hqk', query_block, keys, precision=highest) * scale)
        allowed = (key_pos[None, :] <= query_pos[:, None]) & (key_art[None, :] == query_art[:, None])
        scores = jnp.where(allowed[None], scores, -1e+30)
        top = lax.optimization_barrier(jnp.max(scores, axis=2, keepdims=True))
        weights = jnp.exp(scores - top)
        weights = weights / lax.optimization_barrier(jnp.sum(weights, axis=2, keepdims=True))
        return jnp.einsum('hqk,khd->qhd', low(weights), values, precision=highest)
    query_blocks = queries.reshape(seg_rows // block_rows, block_rows, HEADS, HEAD_DIM)
    starts = (jnp.arange(seg_rows // block_rows) * block_rows).astype(jnp.int32)
    mixed = lax.map(jax.checkpoint(one_block), (query_blocks, starts))
    return mixed.reshape(seg_rows, HEADS * HEAD_DIM)

def segment_layer(inputs, lengths_row, params):
    gain_one, bias_one, w_qkv, w_out, gain_two, bias_two, w_up, w_down = params
    seg_rows = inputs.shape[0]
    normed = low(layer_norm(inputs, gain_one, bias_one))
    projected = low(low_back(jnp.dot(normed, w_qkv, precision=highest)))
    queries = projected[:, :D].reshape(seg_rows, HEADS, HEAD_DIM)
    keys = projected[:, D:2 * D].reshape(seg_rows, HEADS, HEAD_DIM)
    values = projected[:, 2 * D:].reshape(seg_rows, HEADS, HEAD_DIM)
    attended = low(low_back(attend_segment(queries, keys, values, lengths_row)))
    middle = inputs + low_back(jnp.dot(attended, w_out, precision=highest))
    normed_two = low(layer_norm(middle, gain_two, bias_two))
    hidden = low_back(jnp.dot(normed_two, w_up, precision=highest))
    activated = low(jax.nn.gelu(hidden, approximate=True))
    return middle + low_back(jnp.dot(activated, w_down, precision=highest))

def reference(tokens, article_lengths, gain_one, bias_one, w_qkv, w_out, gain_two, bias_two, w_up, w_down, cotangent):

    def whole(inputs, gain_a, bias_a, weight_a, weight_b, gain_b, bias_b, weight_c, weight_d):
        params = (gain_a, bias_a, weight_a, weight_b, gain_b, bias_b, weight_c, weight_d)

        def per_segment(packed):
            return jax.checkpoint(segment_layer)(packed[0], packed[1], params)
        return lax.map(per_segment, (inputs, article_lengths))
    outputs, pullback = jax.vjp(whole, tokens.astype(jnp.float32), gain_one, bias_one, w_qkv.astype(jnp.float32), w_out.astype(jnp.float32), gain_two, bias_two, w_up.astype(jnp.float32), w_down.astype(jnp.float32))
    grads = pullback(cotangent.astype(jnp.float32))
    return (outputs.astype(jnp.bfloat16), grads[0], grads[1], grads[2], grads[3], grads[4], grads[5], grads[6], grads[7], grads[8])
```

```python
import math

import jax
import jax.numpy as jnp
from jax import lax
from jax.experimental import pallas as pl
from jax.experimental.pallas import tpu as pltpu
from jax.sharding import PartitionSpec as P

HEADS = 8
HEAD_DIM = 128


def passed_along(block, axis, distance):
    devices = range(lax.axis_size(axis))
    route = [(i - distance, i) for i in devices if i - distance in devices]
    return lax.ppermute(block, axis, route)


def shifted(value, axis, by):
    size = lax.axis_size(axis)
    return lax.ppermute(value, axis, [(i, (i + by) % size) for i in range(size)])


def layer_norm(values, gain, bias):
    center = values - jnp.mean(values, axis=-1, keepdims=True)
    spread = jnp.mean(center * center, axis=-1, keepdims=True)
    return center * lax.rsqrt(spread + 1e-05) * gain + bias


def smooth_act(values):
    return jax.nn.gelu(values, approximate=True)


def article_numbers(lengths_row, positions):
    bounds = jnp.cumsum(lengths_row)
    return jnp.sum((positions[:, None] >= bounds[None, :]).astype(jnp.int32), axis=1)


def per_device(
    tokens,
    article_lengths,
    gain_one,
    bias_one,
    w_qkv,
    w_out,
    gain_two,
    bias_two,
    w_up,
    w_down,
    cotangent,
):
    tok_rows = tokens.shape[1]
    model_width = tokens.shape[2]
    head_count = HEADS
    head_size = HEAD_DIM
    scale = 1.0 / math.sqrt(head_size)
    blocks_seq = lax.axis_size("seq")
    my_place = lax.axis_index("seq")
    full_qkv, full_out, full_up, full_down = (
        lax.all_gather(w_qkv, "seg", axis=0, tiled=True),
        lax.all_gather(w_out, "seg", axis=0, tiled=True),
        lax.all_gather(w_up, "seg", axis=0, tiled=True),
        lax.all_gather(w_down, "seg", axis=0, tiled=True),
    )
    inputs = tokens[0].astype(jnp.float32)
    normed, norm_one_back = jax.vjp(layer_norm, inputs, gain_one, bias_one)
    normed_low = normed.astype(jnp.bfloat16)
    projected = jnp.dot(normed_low, full_qkv, preferred_element_type=jnp.float32).astype(
        jnp.bfloat16
    )
    query_low = projected[:, :model_width]
    key_low = projected[:, model_width : 2 * model_width]
    value_low = projected[:, 2 * model_width :]
    query_heads = query_low.reshape(tok_rows, head_count, head_size)
    lengths_row = article_lengths[0]
    positions = my_place * tok_rows + jnp.arange(tok_rows, dtype=jnp.int32)
    query_art = article_numbers(lengths_row, positions)

    def scores_of(key_block, source):
        key_pos = source * tok_rows + jnp.arange(tok_rows, dtype=jnp.int32)
        key_art = article_numbers(lengths_row, key_pos)
        allowed = (key_pos[None, :] <= positions[:, None]) & (
            key_art[None, :] == query_art[:, None]
        )
        raw = (
            jnp.einsum(
                "qhd,khd->hqk",
                query_heads,
                key_block.reshape(tok_rows, head_count, head_size),
                preferred_element_type=jnp.float32,
            )
            * scale
        )
        return jnp.where(allowed[None], raw, -1e30)

    def forward_block(state, key_block, value_block, source):

        def forward_work(operands):
            (top, total, accum), key_now, value_now = operands
            scores = scores_of(key_now, source)
            new_top = jnp.maximum(top, jnp.max(scores, axis=2))
            factor = jnp.exp(top - new_top)
            weights = jnp.exp(scores - new_top[:, :, None])
            total = total * factor + jnp.sum(weights, axis=2)
            gathered = jnp.einsum(
                "hqk,khd->qhd",
                weights.astype(jnp.bfloat16),
                value_now.reshape(tok_rows, head_count, head_size),
                preferred_element_type=jnp.float32,
            ).reshape(tok_rows, model_width)
            accum = accum * jnp.repeat(factor.T, head_size, axis=1) + gathered
            return (new_top, total, accum)

        def forward_keep(operands):
            return operands[0]

        return lax.cond(
            source <= my_place, forward_work, forward_keep, (state, key_block, value_block)
        )

    start_state = (
        jnp.full((head_count, tok_rows), -1e30, jnp.float32),
        jnp.zeros((head_count, tok_rows), jnp.float32),
        jnp.zeros((tok_rows, model_width), jnp.float32),
    )
    state = forward_block(start_state, key_low, value_low, my_place)

    def forward_step(step, carry):
        key_block, value_block, state_now = carry
        key_block, value_block = passed_along((key_block, value_block), "seq", 1)
        source = (my_place - step) % blocks_seq
        return (key_block, value_block, forward_block(state_now, key_block, value_block, source))

    _, _, state = lax.fori_loop(1, blocks_seq, forward_step, (key_low, value_low, state))
    top, total, accum = state
    log_total = top + jnp.log(total)
    attended = accum / jnp.repeat(total.T, head_size, axis=1)
    attended_low = attended.astype(jnp.bfloat16)
    middle = inputs + jnp.dot(attended_low, full_out, preferred_element_type=jnp.float32)
    normed_two, norm_two_back = jax.vjp(layer_norm, middle, gain_two, bias_two)
    normed_two_low = normed_two.astype(jnp.bfloat16)
    hidden = jnp.dot(normed_two_low, full_up, preferred_element_type=jnp.float32)
    activated, act_back = jax.vjp(smooth_act, hidden)
    activated_low = activated.astype(jnp.bfloat16)
    outputs = middle + jnp.dot(activated_low, full_down, preferred_element_type=jnp.float32)
    result = outputs.astype(jnp.bfloat16)[None]
    grad_top = cotangent[0].astype(jnp.float32)
    grad_top_low = cotangent[0]
    grad_down = jnp.einsum(
        "tf,td->fd", activated_low, grad_top_low, preferred_element_type=jnp.float32
    )
    grad_act = jnp.einsum("td,fd->tf", grad_top_low, full_down, preferred_element_type=jnp.float32)
    (grad_hidden,) = act_back(grad_act)
    grad_hidden_low = grad_hidden.astype(jnp.bfloat16)
    grad_up = jnp.einsum(
        "td,tf->df", normed_two_low, grad_hidden_low, preferred_element_type=jnp.float32
    )
    grad_normed_two = jnp.einsum(
        "tf,df->td", grad_hidden_low, full_up, preferred_element_type=jnp.float32
    )
    grad_mid_norm, grad_gain_two, grad_bias_two = norm_two_back(grad_normed_two)
    grad_middle = grad_top + grad_mid_norm
    grad_middle_low = grad_middle.astype(jnp.bfloat16)
    grad_out = jnp.einsum(
        "tc,td->cd", attended_low, grad_middle_low, preferred_element_type=jnp.float32
    )
    grad_att = jnp.einsum(
        "td,cd->tc", grad_middle_low, full_out, preferred_element_type=jnp.float32
    )
    grad_att_low = grad_att.astype(jnp.bfloat16)
    grad_att_heads = grad_att_low.reshape(tok_rows, head_count, head_size)
    offsets = jnp.sum(
        (grad_att_low.astype(jnp.float32) * attended).reshape(tok_rows, head_count, head_size),
        axis=2,
    ).T

    def backward_block(operands, source):

        def backward_work(inner):
            grad_query, grad_key, grad_value, key_now, value_now = inner
            key_heads = key_now.reshape(tok_rows, head_count, head_size)
            value_heads = value_now.reshape(tok_rows, head_count, head_size)
            probs = jnp.exp(scores_of(key_now, source) - log_total[:, :, None])
            probs_low = probs.astype(jnp.bfloat16)
            grad_value = grad_value + jnp.einsum(
                "hqk,qhd->khd", probs_low, grad_att_heads, preferred_element_type=jnp.float32
            ).reshape(tok_rows, model_width)
            grad_probs = jnp.einsum(
                "qhd,khd->hqk", grad_att_heads, value_heads, preferred_element_type=jnp.float32
            )
            grad_scores = (probs * (grad_probs - offsets[:, :, None])).astype(jnp.bfloat16)
            grad_query = (
                grad_query
                + jnp.einsum(
                    "hqk,khd->qhd", grad_scores, key_heads, preferred_element_type=jnp.float32
                ).reshape(tok_rows, model_width)
                * scale
            )
            grad_key = (
                grad_key
                + jnp.einsum(
                    "hqk,qhd->khd", grad_scores, query_heads, preferred_element_type=jnp.float32
                ).reshape(tok_rows, model_width)
                * scale
            )
            return (grad_query, grad_key, grad_value, key_now, value_now)

        def backward_keep(inner):
            return inner

        return lax.cond(source <= my_place, backward_work, backward_keep, operands)

    def backward_step(step, carry):
        source = (my_place - step) % blocks_seq
        grad_query, grad_key, grad_value, key_block, value_block = backward_block(carry, source)
        key_block, value_block = passed_along((key_block, value_block), "seq", 1)
        grad_key, grad_value = (
            shifted(grad_key.astype(jnp.bfloat16), "seq", 1).astype(grad_key.dtype),
            shifted(grad_value.astype(jnp.bfloat16), "seq", 1).astype(grad_value.dtype),
        )
        return (grad_query, grad_key, grad_value, key_block, value_block)

    zero_rows = jnp.zeros((tok_rows, model_width), jnp.float32)
    grad_query, grad_key, grad_value, _, _ = lax.fori_loop(
        0, blocks_seq, backward_step, (zero_rows, zero_rows, zero_rows, key_low, value_low)
    )
    grad_proj_low = jnp.concatenate([grad_query, grad_key, grad_value], axis=1).astype(jnp.bfloat16)
    grad_qkv = jnp.einsum(
        "tc,tk->ck", normed_low, grad_proj_low, preferred_element_type=jnp.float32
    )
    grad_normed = jnp.einsum(
        "tk,ck->tc", grad_proj_low, full_qkv, preferred_element_type=jnp.float32
    )
    grad_in_norm, grad_gain_one, grad_bias_one = norm_one_back(grad_normed)
    input_grad = (grad_middle + grad_in_norm)[None]
    part_qkv, part_out, part_up, part_down = (
        lax.psum_scatter(
            grad_qkv.astype(jnp.bfloat16), "seg", scatter_dimension=0, tiled=True
        ).astype(jnp.float32),
        lax.psum_scatter(
            grad_out.astype(jnp.bfloat16), "seg", scatter_dimension=0, tiled=True
        ).astype(jnp.float32),
        lax.psum_scatter(
            grad_up.astype(jnp.bfloat16), "seg", scatter_dimension=0, tiled=True
        ).astype(jnp.float32),
        lax.psum_scatter(
            grad_down.astype(jnp.bfloat16), "seg", scatter_dimension=0, tiled=True
        ).astype(jnp.float32),
    )
    sum_qkv, sum_out, sum_up, sum_down = (
        lax.psum_scatter(
            part_qkv.astype(jnp.bfloat16), "seq", scatter_dimension=1, tiled=True
        ).astype(jnp.float32),
        lax.psum_scatter(
            part_out.astype(jnp.bfloat16), "seq", scatter_dimension=1, tiled=True
        ).astype(jnp.float32),
        lax.psum_scatter(
            part_up.astype(jnp.bfloat16), "seq", scatter_dimension=1, tiled=True
        ).astype(jnp.float32),
        lax.psum_scatter(
            part_down.astype(jnp.bfloat16), "seq", scatter_dimension=1, tiled=True
        ).astype(jnp.float32),
    )
    sum_gain_one, sum_bias_one, sum_gain_two, sum_bias_two = lax.psum(
        (grad_gain_one, grad_bias_one, grad_gain_two, grad_bias_two), ("seq", "seg")
    )
    return (
        result,
        input_grad,
        sum_gain_one,
        sum_bias_one,
        sum_qkv,
        sum_out,
        sum_gain_two,
        sum_bias_two,
        sum_up,
        sum_down,
    )


MESH = pl.DeviceIdType.MESH
BF = jnp.bfloat16
F32 = jnp.float32
NEAR_FIRST = ((0, 1, 2, 3), (1, 0, 2, 3), (2, 1, 3, 0), (3, 2, 1, 0))
FAR_FIRST = ((3, 2, 1, 0), (3, 0, 2, 1), (0, 3, 1, 2), (0, 1, 2, 3))


def pick(table, row, column):
    out = jnp.int32(0)
    for r, line in enumerate(table):
        for c, entry in enumerate(line):
            if entry:
                out = jnp.where((row == r) & (column == c), entry, out)
    return out


def dot_nn(a, b):
    return lax.dot_general(a, b, (((1,), (0,)), ((), ())), preferred_element_type=F32)


def dot_nt(a, b):
    return lax.dot_general(a, b, (((1,), (1,)), ((), ())), preferred_element_type=F32)


def dot_tn(a, b):
    return lax.dot_general(a, b, (((0,), (0,)), ((), ())), preferred_element_type=F32)


def remote(src, dst, send, recv, **place):
    return pltpu.make_async_remote_copy(
        src_ref=src, dst_ref=dst, send_sem=send, recv_sem=recv, device_id=place, device_id_type=MESH
    )


def norm_parts(values):
    center = values - jnp.mean(values, axis=-1, keepdims=True)
    spread = jnp.mean(center * center, axis=-1, keepdims=True)
    inverse = lax.rsqrt(spread + 1e-05)
    return center * inverse, inverse


def greet(q, s):
    barrier = pltpu.get_barrier_semaphore()
    for d in range(1, 8):
        pl.semaphore_signal(barrier, 1, device_id={"seq": lax.rem(q + d, 8)}, device_id_type=MESH)
    for d in range(1, 4):
        pl.semaphore_signal(barrier, 1, device_id={"seg": lax.rem(s + d, 4)}, device_id_type=MESH)
    pl.semaphore_wait(barrier, 10)


def first_columns(lengths_ref, base, rows):
    place = base + lax.broadcasted_iota(jnp.int32, (rows, 1), 0)
    start = jnp.zeros((rows, 1), jnp.int32)
    bound = jnp.int32(0)
    for i in range(lengths_ref.shape[1]):
        bound = bound + lengths_ref[0, i]
        start = jnp.where(place >= bound, bound, start)
    return start


def seen_mask(start, base_q, base_k, rows, columns):
    place = base_q + lax.broadcasted_iota(jnp.int32, (rows, columns), 0)
    key = base_k + lax.broadcasted_iota(jnp.int32, (rows, columns), 1)
    return (key <= place) & (key >= start)


def attend_kernel(
    x_ref, len_ref, gain_ref, bias_ref, wq_ref, wo_ref, wu_ref, wd_ref,
    o_ref, wof, wuf, wdf, xs, h1, wh, qkv, of, lse,
    ob, wd_v, wu_v, wo_v, local_sem, qs, qr, ws, wr, xs_send, xs_recv, os_send, os_recv,
):
    q, s = lax.axis_index("seq"), lax.axis_index("seg")
    z, x = q // 2, q % 2
    y, c = s // 2, s % 2
    sib = s + 1 - 2 * c
    across = (1 - y) * 2 + c
    corner = (1 - y) * 2 + 1 - c
    xq = z * 2 + 1 - x
    T = 256
    scale = 1.0 / math.sqrt(HEAD_DIM)

    def rows(k, n):
        return pl.ds(pl.multiple_of(k * n, n), n)

    for j in range(3):
        wh[rows(s, T), j * 128 : (j + 1) * 128] = wq_ref[:, pl.ds(pl.multiple_of(j * 1024 + q * 128, 128), 128)]
    greet(q, s)

    def wq_copy(k, quarter, place):
        return remote(wh.at[rows(quarter, T)], wh.at[rows(quarter, T)], qs.at[k], qr.at[k], seg=place)

    q_across, q_sib = wq_copy(0, s, across), wq_copy(1, s, sib)
    q_across.start()
    q_sib.start()

    def x_copy(b, k, to):
        src = xs.at[rows(b, T)]
        return remote(src, src, xs_send.at[k], xs_recv.at[b], seq=to)

    xs[rows(q, T)] = x_ref[...]

    half = wd_ref.shape[0] // 2

    def part(full, quarter, size, start=0, n=None):
        n = size if n is None else n
        return full.at[pl.ds(pl.multiple_of(quarter * size + start, 16), n)]

    down_half = x * half
    y_down = remote(wd_ref.at[pl.ds(pl.multiple_of(down_half, half), half)],
                    part(wdf, s, 2 * half, down_half, half), ws.at[0], wr.at[0], seg=across)
    y_up = remote(wu_ref, part(wuf, s, T), ws.at[1], wr.at[1], seg=across)
    y_out = remote(wo_ref, part(wof, s, T), ws.at[2], wr.at[2], seg=across)
    s_down = remote(wd_ref, part(wdf, s, 2 * half), ws.at[3], wr.at[3], seg=sib)
    s_up = remote(wu_ref, part(wuf, s, T), ws.at[4], wr.at[4], seg=sib)
    s_out = remote(wo_ref, part(wof, s, T), ws.at[5], wr.at[5], seg=sib)
    got = part(wdf, across, 2 * half, down_half, half)
    x_down = remote(got, got, ws.at[6], wr.at[6], seq=xq)
    f_down_a = remote(got, got, ws.at[7], wr.at[7], seg=sib)
    other = part(wdf, across, 2 * half, half - down_half, half)
    f_down_b = remote(other, other, ws.at[8], wr.at[8], seg=sib)
    up = part(wuf, across, T)
    f_up = remote(up, up, ws.at[9], wr.at[9], seg=sib)
    out = part(wof, across, T)
    f_out = remote(out, out, ws.at[10], wr.at[10], seg=sib)
    own_in = (
        pltpu.make_async_copy(wd_ref, wd_v, local_sem.at[0]),
        pltpu.make_async_copy(wu_ref, wu_v, local_sem.at[1]),
        pltpu.make_async_copy(wo_ref, wo_v, local_sem.at[2]),
    )
    own = (
        pltpu.make_async_copy(wd_v, part(wdf, s, 2 * half), local_sem.at[4]),
        pltpu.make_async_copy(wu_v, part(wuf, s, T), local_sem.at[5]),
        pltpu.make_async_copy(wo_v, part(wof, s, T), local_sem.at[6]),
    )
    for copy in (y_down, y_up, y_out):
        copy.start()

    q_across.wait_recv()
    q_pass = wq_copy(2, across, sib)
    q_pass.start()
    for copy in (s_down, s_up, s_out) + own_in:
        copy.start()
    q_sib.wait_recv()
    q_pass.wait_recv()

    gain, bias = gain_ref[...], bias_ref[...]

    def project(b):
        unit, _ = norm_parts(xs[rows(b, T)].astype(F32))
        low = (unit * gain + bias).astype(BF)
        h1[rows(b, T)] = low
        qkv[rows(b, T)] = dot_nn(low, wh[...]).astype(BF)

    def z_step(i, _):
        zz = pick(NEAR_FIRST, z, i)
        b = zz * 2 + x

        @pl.when(i > 0)
        def _():
            x_copy(b, 0, q).wait_recv()

        @pl.when((zz <= z) & (z < 3))
        def _():
            x_copy(b, zz, q + 2).start()

        @pl.when((zz >= z) & (z > 0))
        def _():
            x_copy(b, 4 + zz, q - 2).start()

        x_copy(b, 8 + zz, xq).start()
        project(b)
        return 0

    lax.fori_loop(0, 4, z_step, 0)
    for arrived, copy in zip(own_in, own):
        arrived.wait()
        copy.start()
    y_down.wait_recv()
    x_down.start()
    f_down_a.start()

    def x_step(i, _):
        b = pick(NEAR_FIRST, z, i) * 2 + 1 - x
        x_copy(b, 0, q).wait_recv()
        project(b)
        return 0

    lax.fori_loop(0, 4, x_step, 0)

    def z_end(zz, _):
        @pl.when((zz <= z) & (z < 3))
        def _():
            x_copy(zz * 2 + x, zz, q + 2).wait_send()

        @pl.when((zz >= z) & (z > 0))
        def _():
            x_copy(zz * 2 + x, 4 + zz, q - 2).wait_send()

        x_copy(zz * 2 + x, 8 + zz, xq).wait_send()
        return 0

    def o_copy(i, sender):
        columns = pl.ds(pl.multiple_of(sender * 128, 128), 128)
        return remote(ob.at[i], o_ref.at[:, columns], os_send.at[i], os_recv.at[sender], seq=i)

    mine = pltpu.make_async_copy(
        ob.at[q], o_ref.at[:, pl.ds(pl.multiple_of(q * 128, 128), 128)], local_sem.at[3]
    )
    for i in range(8):
        n = (i + 1) * T
        start = first_columns(len_ref, i * T, T)
        scores = dot_nt(qkv[i * T : n, :128], qkv[:n, 128:256]) * scale
        scores = jnp.where(seen_mask(start, i * T, 0, T, n), scores, -1e30)
        top = jnp.max(scores, axis=1, keepdims=True)
        weights = jnp.exp(scores - top)
        total = jnp.sum(weights, axis=1, keepdims=True)
        mixed = dot_nn(weights.astype(BF), qkv[:n, 256:384]) / total
        of[i * T : n] = mixed
        lse[i * T : n] = top + jnp.log(total)
        ob[i] = mixed.astype(BF)

        @pl.when(q != i)
        def _():
            o_copy(i, q).start()

        @pl.when(q == i)
        def _():
            mine.start()

    y_up.wait_recv()
    f_up.start()
    y_out.wait_recv()
    f_out.start()
    x_down.wait_recv()
    f_down_b.start()

    lax.fori_loop(0, 4, z_end, 0)
    for i in range(8):
        @pl.when(q != i)
        def _():
            o_copy(i, q).wait_send()
            o_copy(i, i).wait_recv()

    mine.wait()
    for copy in own:
        copy.wait()
    for copy in (q_across, q_sib, q_pass):
        copy.wait_send()
    for copy in (y_down, y_up, y_out, s_down, s_up, s_out, x_down, f_down_a, f_down_b, f_up, f_out):
        copy.wait_send()
    for copy in (s_down, s_up, s_out, f_down_a, f_down_b, f_up, f_out):
        copy.wait_recv()


VM = pl.BlockSpec(memory_space=pltpu.VMEM)
HB = pl.BlockSpec(memory_space=pl.ANY)
SM = pl.BlockSpec(memory_space=pltpu.SMEM)


def attend(x, lengths, gain, bias, wq, wo, wu, wd):
    S = jax.ShapeDtypeStruct
    dma = pltpu.SemaphoreType.DMA
    return pl.pallas_call(
        attend_kernel,
        out_shape=(
            S((256, 1024), BF), S((1024, 1024), BF), S((1024, 4096), BF), S((4096, 1024), BF),
            S((2048, 1024), BF), S((2048, 1024), BF), S((1024, 384), BF), S((2048, 384), BF),
            S((2048, 128), F32), S((2048, 1), F32),
        ),
        in_specs=[VM, SM, VM, VM, VM, HB, HB, HB],
        out_specs=(VM, HB, HB, HB, VM, VM, VM, VM, VM, VM),
        scratch_shapes=[
            pltpu.VMEM((8, 256, 128), BF), pltpu.VMEM((1024, 1024), BF), pltpu.VMEM((256, 4096), BF),
            pltpu.VMEM((256, 1024), BF), dma((7,)), dma((3,)), dma((3,)), dma((11,)), dma((11,)),
            dma((12,)), dma((8,)), dma((8,)), dma((8,)),
        ],
        compiler_params=pltpu.CompilerParams(
            collective_id=0, has_side_effects=True, vmem_limit_bytes=58 * 2**20
        ),
        cost_estimate=pl.CostEstimate(flops=5 * 10**9, bytes_accessed=40 * 2**20, transcendentals=2 * 2**20),
        name="attend",
    )(x, lengths, gain, bias, wq, wo, wu, wd)


def gelu_parts(u):
    root = math.sqrt(2.0 / math.pi)
    square = u * u
    t = jnp.tanh(root * (u + 0.044715 * (square * u)))
    value = 0.5 * u * (1.0 + t)
    slope = 0.5 * (1.0 + t) + 0.5 * u * (1.0 - t * t) * (root * (1.0 + 0.134145 * square))
    return value, slope


def norm_back(grad, gain, unit, inverse):
    through = grad * gain
    a = jnp.mean(through, axis=-1, keepdims=True)
    b = jnp.mean(through * unit, axis=-1, keepdims=True)
    return inverse * (through - a - unit * b)


def ffn_kernel(
    x_ref, o_ref, g_ref, gain_ref, bias_ref, wo_ref, wu_ref, wd_ref,
    result_ref, dx_ref, do_ref, sums_ref, pack_ref,
    pack, middle, unit_v, inv_v, h2, acc, dh2, up_sem, down_sem, out_sem,
):
    f = pl.program_id(0)
    T = 256

    @pl.when(f == 0)
    def _():
        value = x_ref[...].astype(F32) + dot_nn(o_ref[...], wo_ref[...])
        middle[...] = value
        unit, inverse = norm_parts(value)
        unit_v[...] = unit
        inv_v[...] = inverse
        h2[...] = (unit * gain_ref[...] + bias_ref[...]).astype(BF)
        acc[...] = jnp.zeros_like(acc)
        dh2[...] = jnp.zeros_like(dh2)

    g = g_ref[...]
    value, slope = gelu_parts(dot_nn(h2[...], wu_ref[...]))
    low = value.astype(BF)
    acc[...] += dot_nn(low, wd_ref[...])
    du = (slope * dot_nt(g, wd_ref[...])).astype(BF)
    dh2[...] += dot_nt(du, wu_ref[...])
    pack[:, f, :, 0:512] = dot_tn(h2[...], du).astype(BF).reshape(4, T, 512)
    down = dot_tn(low, g).astype(BF)
    base = 512 + (f % 2) * 256
    for jj in range(2):
        for k in range(8):
            pack[f // 2, k, :, pl.ds(pl.multiple_of(base + jj * 128, 128), 128)] = down[
                jj * T : (jj + 1) * T, k * 128 : (k + 1) * 128
            ]

    def up_copy(n):
        return pltpu.make_async_copy(
            pack.at[:, n, :, 0:512], pack_ref.at[:, n, :, 0:512], up_sem.at[n]
        )

    def down_copy(n):
        columns = pl.ds(pl.multiple_of(512 + (n % 2) * 256, 256), 256)
        return pltpu.make_async_copy(
            pack.at[n // 2, :, :, columns], pack_ref.at[n // 2, :, :, columns], down_sem.at[n]
        )

    up_copy(f).start()
    down_copy(f).start()

    @pl.when(f == 7)
    def _():
        result_ref[...] = (middle[...] + acc[...]).astype(BF)
        unit, grad = unit_v[...], dh2[...]
        sums_ref[0:1] = jnp.sum(grad * unit, axis=0, keepdims=True)
        sums_ref[1:2] = jnp.sum(grad, axis=0, keepdims=True)
        dx = g.astype(F32) + norm_back(grad, gain_ref[...], unit, inv_v[...])
        dx_ref[...] = dx
        dy = dx.astype(BF)
        do_ref[...] = dot_nt(dy, wo_ref[...]).astype(BF)
        out = dot_tn(o_ref[...], dy).astype(BF)
        for quarter in range(4):
            for k in range(8):
                pack[quarter, k, :, 1024:1152] = out[
                    quarter * T : (quarter + 1) * T, k * 128 : (k + 1) * 128
                ]
        copy = pltpu.make_async_copy(pack.at[:, :, :, 1024:1152], pack_ref.at[:, :, :, 1024:1152], out_sem)
        copy.start()
        for n in range(8):
            up_copy(n).wait()
            down_copy(n).wait()
        copy.wait()


def ffn(x, o, g, gain, bias, wo, wu, wd):
    S = jax.ShapeDtypeStruct
    dma = pltpu.SemaphoreType.DMA
    whole = lambda r, n: pl.BlockSpec((r, n), lambda f: (0, 0))
    return pl.pallas_call(
        ffn_kernel,
        grid=(8,),
        out_shape=(
            S((256, 1024), BF), S((256, 1024), F32), S((256, 1024), BF), S((2, 1024), F32),
            S((4, 8, 256, 1152), BF),
        ),
        in_specs=[
            whole(256, 1024), whole(256, 1024), whole(256, 1024), whole(1, 1024), whole(1, 1024),
            whole(1024, 1024), pl.BlockSpec((1024, 512), lambda f: (0, f)),
            pl.BlockSpec((512, 1024), lambda f: (f, 0)),
        ],
        out_specs=(
            whole(256, 1024), whole(256, 1024), whole(256, 1024), whole(2, 1024), HB,
        ),
        scratch_shapes=[
            pltpu.VMEM((4, 8, 256, 1152), BF), pltpu.VMEM((256, 1024), F32), pltpu.VMEM((256, 1024), F32),
            pltpu.VMEM((256, 1), F32), pltpu.VMEM((256, 1024), BF), pltpu.VMEM((256, 1024), F32),
            pltpu.VMEM((256, 1024), F32), dma((8,)), dma((8,)), dma,
        ],
        compiler_params=pltpu.CompilerParams(
            dimension_semantics=("arbitrary",), vmem_limit_bytes=58 * 2**20
        ),
        cost_estimate=pl.CostEstimate(flops=15 * 10**9, bytes_accessed=40 * 2**20, transcendentals=2**20),
        name="ffn",
    )(x, o, g, gain, bias, wo, wu, wd)


def grads_kernel(
    pack_ref, do_ref, dx_ref, sums2_ref, xs_ref, h1_ref, wh_ref, qkv_ref, of_ref, lse_ref, len_ref, gain_ref,
    dx_out, gqkv_out, gout_out, gup_out, gdown_out, sums_out,
    load, core_r, y_r, x_r, z_r, doh, dq, dk, dv, dh_s, dhx_r, dhz_r, gq, gq_b, gq_c, gq_y, gq_s, gq_r,
    vec, vec_r, xbuf, hbuf,
    load_sem, cs, cr, ys, yr, gxs, gxr, gzs, gzr, dos, dor, dxs, dxr, dzs, dzr, qs, qr, vs, vr, blk_sem,
):
    q, s = lax.axis_index("seq"), lax.axis_index("seg")
    z, x = q // 2, q % 2
    y, c = s // 2, s % 2
    sib = s + 1 - 2 * c
    across = (1 - y) * 2 + c
    xq = z * 2 + 1 - x
    T = 256
    scale = 1.0 / math.sqrt(HEAD_DIM)

    def rows(k, n):
        return pl.ds(pl.multiple_of(k * n, n), n)

    def lanes(k):
        return pl.ds(pl.multiple_of(k * 128, 128), 128)

    def dest(k):
        return pick(FAR_FIRST, z, k // 2) * 2 + jnp.where(k % 2 == 0, 1 - x, x)

    greet(q, s)

    def do_copy(b, sender):
        return remote(do_ref.at[:, lanes(b)], doh.at[rows(sender, T)], dos.at[b], dor.at[sender], seq=b)

    do_mine = pltpu.make_async_copy(do_ref.at[:, lanes(q)], doh.at[rows(q, T)], blk_sem.at[4])
    do_mine.start()
    for b in range(8):
        @pl.when(q != b)
        def _():
            do_copy(b, q).start()

    def core_copy(t):
        return remote(pack_ref.at[:, 1 - c, t], core_r.at[t], cs.at[t], cr.at[t], seg=sib)

    def load_copy(k):
        return pltpu.make_async_copy(pack_ref.at[:, c, dest(k)], load.at[k % 2], load_sem.at[k % 2])

    def y_copy(t):
        return remote(core_r.at[t, 1 - y], y_r.at[t], ys.at[t], yr.at[t], seg=across)

    def start_core(k, _):
        core_copy(dest(k)).start()
        return 0

    lax.fori_loop(0, 8, start_core, 0)
    load_copy(0).start()

    def core_step(k, _):
        t = dest(k)

        @pl.when(k < 7)
        def _():
            load_copy(k + 1).start()

        load_copy(k).wait()
        core_copy(t).wait_recv()
        for part in range(2):
            core_r[t, part] = (core_r[t, part].astype(F32) + load[k % 2, part].astype(F32)).astype(BF)

        @pl.when(k < 5)
        def _():
            y_copy(t).start()

        return 0

    lax.fori_loop(0, 8, core_step, 0)
    for b in range(8):
        @pl.when(q != b)
        def _():
            do_copy(b, b).wait_recv()

    do_mine.wait()

    dk[...] = jnp.zeros_like(dk)
    dv[...] = jnp.zeros_like(dv)
    for i in range(8):
        top = i * T
        start = first_columns(len_ref, top, T)
        query = qkv_ref[top : top + T, :128]
        grad = doh[top : top + T]
        delta = jnp.sum(grad.astype(F32) * of_ref[top : top + T], axis=1, keepdims=True)
        log_total = lse_ref[top : top + T]
        total = jnp.zeros((T, 128), F32)
        for base in range(0, top + T, 1024):
            n = min(1024, top + T - base)
            keys = qkv_ref[base : base + n, 128:256]
            probs = jnp.exp(dot_nt(query, keys) * scale - log_total)
            probs = jnp.where(seen_mask(start, top, base, T, n), probs, 0.0)
            dp = dot_nt(grad, qkv_ref[base : base + n, 256:384])
            ds = (probs * (dp - delta)).astype(BF)
            dv[base : base + n] += dot_tn(probs.astype(BF), grad)
            dk[base : base + n] += dot_tn(ds, query)
            total += dot_nn(ds, keys)
        dq[top : top + T] = total

    gq[...] = jnp.zeros_like(gq)
    vec[...] = jnp.zeros_like(vec)
    vec[2:4] = sums2_ref[...]

    def block_of(i):
        return pick(FAR_FIRST, z, i % 4) * 2 + jnp.where(i < 4, 1 - x, x)

    def x_load(i):
        return pltpu.make_async_copy(xs_ref.at[rows(block_of(i), T)], xbuf.at[i % 2], blk_sem.at[i % 2])

    def h_load(i):
        return pltpu.make_async_copy(h1_ref.at[rows(block_of(i), T)], hbuf.at[i % 2], blk_sem.at[2 + i % 2])

    def dhx_copy(zz):
        return remote(dh_s.at[zz * 2 + 1 - x], dhx_r.at[zz], dxs.at[zz], dxr.at[zz], seq=xq)

    x_load(0).start()
    h_load(0).start()

    def block_step(i, _):
        b = block_of(i)

        @pl.when(i < 7)
        def _():
            x_load(i + 1).start()
            h_load(i + 1).start()

        at = rows(b, T)
        low = jnp.concatenate([dq[at] * scale, dk[at] * scale, dv[at]], axis=1).astype(BF)
        dh = dot_nt(low, wh_ref[...])
        dh_s[b] = dh.astype(BF)

        @pl.when(i < 4)
        def _():
            dhx_copy(pick(FAR_FIRST, z, i % 4)).start()

        x_load(i).wait()
        h_load(i).wait()
        gq[...] += dot_tn(hbuf[i % 2], low)
        unit, _ = norm_parts(xbuf[i % 2].astype(F32))
        vec[0:1] += jnp.sum(dh * unit, axis=0, keepdims=True)
        vec[1:2] += jnp.sum(dh, axis=0, keepdims=True)
        return 0

    lax.fori_loop(0, 8, block_step, 0)

    gq_b[...] = gq[...].astype(BF).reshape(2, 2, T, 384)
    q_core = remote(gq_b.at[:, 1 - c], gq_c, qs.at[0], qr.at[0], seg=sib)
    q_core.start()
    v_core = remote(vec, vec_r.at[0], vs.at[0], vr.at[0], seg=sib)
    v_core.start()
    q_core.wait_recv()
    for part in range(2):
        gq_c[part] = (gq_c[part].astype(F32) + gq_b[part, c].astype(F32)).astype(BF)
    q_y = remote(gq_c.at[1 - y], gq_y, qs.at[1], qr.at[1], seg=across)
    q_y.start()
    v_core.wait()
    vec[...] += vec_r[0]
    v_y = remote(vec, vec_r.at[1], vs.at[1], vr.at[1], seg=across)
    v_y.start()

    def start_y(k, _):
        y_copy(dest(k)).start()
        return 0

    lax.fori_loop(5, 8, start_y, 0)

    def gx_copy(zz):
        return remote(core_r.at[zz * 2 + 1 - x, y], x_r.at[zz], gxs.at[zz], gxr.at[zz], seq=xq)

    def line_slot(d, place):
        return jnp.where(d == place, 4, d)

    def line(src, into, send, recv, d):
        up = remote(src, into.at[d], send.at[d], recv.at[d], seq=q + 2)
        low = line_slot(d, z - 1)
        down = remote(src, into.at[low], send.at[d], recv.at[low], seq=q - 2)
        return up, down

    def come(into, recv, slot):
        return remote(into.at[slot], into.at[slot], recv.at[slot], recv.at[slot], seq=xq)

    def pass_on(value, keep, into, send, recv, d):
        has_in = jnp.where(d > z, z > 0, z < 3)

        @pl.when(d != z)
        def _():
            @pl.when(has_in)
            def _():
                come(into, recv, d).wait_recv()
                keep[...] = (value() + into[d].astype(F32)).astype(BF)

            @pl.when(jnp.logical_not(has_in))
            def _():
                keep[...] = value().astype(BF)

            up, down = line(keep, into, send, recv, d)

            @pl.when(d > z)
            def _():
                up.start()

            @pl.when(d < z)
            def _():
                down.start()

    def line_step(j, _):
        d = pick(FAR_FIRST, z, j)
        own, other = d * 2 + x, d * 2 + 1 - x
        y_copy(other).wait_recv()
        core_r[other, y] = (core_r[other, y].astype(F32) + y_r[other].astype(F32)).astype(BF)
        gx_copy(d).start()
        dhx_copy(d).wait_recv()
        pass_on(
            lambda: dh_s[own].astype(F32) + dhx_r[d].astype(F32), dh_s.at[own], dhz_r, dzs, dzr, d
        )
        y_copy(own).wait_recv()
        gx_copy(d).wait_recv()
        pass_on(
            lambda: core_r[own, y].astype(F32) + y_r[own].astype(F32) + x_r[d].astype(F32),
            core_r.at[own, y], z_r, gzs, gzr, d,
        )
        return 0

    lax.fori_loop(0, 2, line_step, 0)
    v_y.wait()
    vec[...] += vec_r[1]
    v_x = remote(vec, vec_r.at[2], vs.at[2], vr.at[2], seq=xq)
    v_x.start()
    q_y.wait_recv()
    gq_s[...] = (gq_c[y].astype(F32) + gq_y[...].astype(F32)).astype(BF)

    def column_copy(j):
        column = j * 1024 + q * 128
        owner, slot = column // 384, (column % 384) // 128
        copy = remote(gq_s.at[:, j * 128 : (j + 1) * 128], gq_r.at[slot], qs.at[2 + j], qr.at[2 + slot], seq=owner)
        local = pltpu.make_async_copy(gq_s.at[:, j * 128 : (j + 1) * 128], gq_r.at[slot], qr.at[2 + slot])
        return owner, copy, local

    for j in range(3):
        owner, copy, local = column_copy(j)

        @pl.when(owner != q)
        def _():
            copy.start()

        @pl.when(owner == q)
        def _():
            local.start()

    lax.fori_loop(2, 3, line_step, 0)
    v_x.wait()
    vec[...] += vec_r[2]

    def v_copy(zz, sender):
        return remote(vec, vec_r.at[3 + sender], vs.at[3 + zz], vr.at[3 + sender], seq=zz * 2 + x)

    for zz in range(4):
        @pl.when(zz != z)
        def _():
            v_copy(zz, z).start()

    lax.fori_loop(3, 4, line_step, 0)

    def arrived(into, recv):
        @pl.when(z > 0)
        def _():
            come(into, recv, z).wait_recv()

        @pl.when(z == 0)
        def _():
            into[0] = jnp.zeros_like(into[0])

        @pl.when(z < 3)
        def _():
            come(into, recv, 4).wait_recv()

        @pl.when(z == 3)
        def _():
            into[4] = jnp.zeros_like(into[4])

        return into[z].astype(F32) + into[4].astype(F32)

    dh = dh_s[q].astype(F32) + dhx_r[z].astype(F32) + arrived(dhz_r, dzr)
    mine = pltpu.make_async_copy(xs_ref.at[rows(q, T)], xbuf.at[0], blk_sem.at[0])
    mine.start()
    mine.wait()
    unit, inverse = norm_parts(xbuf[0].astype(F32))
    dx_out[...] = dx_ref[...] + norm_back(dh, gain_ref[...], unit, inverse)
    total = core_r[q, y].astype(F32) + y_r[q].astype(F32) + x_r[z].astype(F32) + arrived(z_r, gzr)
    gup_out[...] = total[:, :512]
    for j in range(4):
        gdown_out[j * T : (j + 1) * T] = total[:, 512 + j * 128 : 640 + j * 128]
    gout_out[...] = total[:, 1024:]
    for slot in range(3):
        come(gq_r, qr.at[pl.ds(2, 3)], slot).wait_recv()
        gqkv_out[:, slot * 128 : (slot + 1) * 128] = gq_r[slot].astype(F32)
    vec_r[3 + z] = vec[...]
    for zz in range(4):
        @pl.when(zz != z)
        def _():
            v_copy(zz, zz).wait_recv()

    sums_out[...] = (vec_r[3] + vec_r[4] + vec_r[5] + vec_r[6])[:4]

    for b in range(8):
        @pl.when(q != b)
        def _():
            do_copy(b, q).wait_send()

    def sent(t, _):
        core_copy(t).wait_send()
        y_copy(t).wait_send()
        return 0

    lax.fori_loop(0, 8, sent, 0)

    def sent_lines(d, _):
        gx_copy(d).wait_send()
        dhx_copy(d).wait_send()

        @pl.when(d != z)
        def _():
            line(dh_s.at[d * 2 + x], dhz_r, dzs, dzr, d)[0].wait_send()
            line(core_r.at[d * 2 + x, y], z_r, gzs, gzr, d)[0].wait_send()

        return 0

    lax.fori_loop(0, 4, sent_lines, 0)
    q_core.wait_send()
    q_y.wait_send()
    for j in range(3):
        owner, copy, _ = column_copy(j)

        @pl.when(owner != q)
        def _():
            copy.wait_send()

    for zz in range(4):
        @pl.when(zz != z)
        def _():
            v_copy(zz, z).wait_send()


def grads(pack, do, dx, sums2, xs, h1, wh, qkv, of, lse, lengths, gain):
    S = jax.ShapeDtypeStruct
    V = pltpu.VMEM
    dma = pltpu.SemaphoreType.DMA
    return pl.pallas_call(
        grads_kernel,
        out_shape=(
            S((256, 1024), F32), S((256, 384), F32), S((256, 128), F32), S((256, 512), F32),
            S((1024, 128), F32), S((4, 1024), F32),
        ),
        in_specs=[HB, VM, VM, VM, HB, HB, VM, VM, VM, VM, SM, VM],
        out_specs=(VM,) * 6,
        scratch_shapes=[
            V((2, 2, 256, 1152), BF), V((8, 2, 256, 1152), BF), V((8, 256, 1152), BF), V((4, 256, 1152), BF),
            V((5, 256, 1152), BF), V((2048, 128), BF), V((2048, 128), F32), V((2048, 128), F32),
            V((2048, 128), F32), V((8, 256, 1024), BF), V((4, 256, 1024), BF), V((5, 256, 1024), BF),
            V((1024, 384), F32), V((2, 2, 256, 384), BF), V((2, 256, 384), BF), V((256, 384), BF),
            V((256, 384), BF), V((3, 256, 128), BF), V((8, 1024), F32), V((7, 8, 1024), F32),
            V((2, 256, 1024), BF), V((2, 256, 1024), BF),
            dma((2,)), dma((8,)), dma((8,)), dma((8,)), dma((8,)), dma((4,)), dma((4,)), dma((4,)), dma((5,)),
            dma((8,)), dma((8,)), dma((4,)), dma((4,)), dma((4,)), dma((5,)), dma((5,)), dma((5,)),
            dma((7,)), dma((7,)), dma((5,)),
        ],
        compiler_params=pltpu.CompilerParams(
            collective_id=1, has_side_effects=True, vmem_limit_bytes=60 * 2**20
        ),
        cost_estimate=pl.CostEstimate(flops=8 * 10**9, bytes_accessed=40 * 2**20, transcendentals=2 * 2**20),
        name="grads",
    )(pack.reshape(2, 2, 8, 256, 1152), do, dx, sums2, xs, h1, wh, qkv, of, lse, lengths, gain)


def per_device_fast(
    tokens, article_lengths, gain_one, bias_one, w_qkv, w_out, gain_two, bias_two, w_up, w_down, cotangent
):
    x = tokens[0]
    o, wo, wu, wd, xs, h1, wh, qkv, of, lse = attend(
        x, article_lengths, gain_one[None], bias_one[None], w_qkv, w_out, w_up, w_down
    )
    result, dx, do, sums2, pack = ffn(
        x, o, cotangent[0], gain_two[None], bias_two[None], wo, wu, wd
    )
    dx, gqkv, gout, gup, gdown, sums = grads(
        pack, do, dx, sums2, xs, h1, wh, qkv, of, lse, article_lengths, gain_one[None]
    )
    return (result[None], dx[None], sums[0], sums[1], gqkv, gout, sums[2], sums[3], gup, gdown)


def solution(mesh):
    one_pair = mesh.shape["seq"] == HEADS and mesh.shape["seg"] == 4
    return jax.shard_map(
        per_device_fast if one_pair else per_device,
        mesh=mesh,
        in_specs=(
            P("seg", "seq", None),
            P("seg", None),
            P(),
            P(),
            P("seg", None),
            P("seg", None),
            P(),
            P(),
            P("seg", None),
            P("seg", None),
            P("seg", "seq", None),
        ),
        out_specs=(
            P("seg", "seq", None),
            P("seg", "seq", None),
            P(),
            P(),
            P("seg", "seq"),
            P("seg", "seq"),
            P(),
            P(),
            P("seg", "seq"),
            P("seg", "seq"),
        ),
        check_vma=False,
    )
```

```python
import math

import jax
import jax.numpy as jnp
from jax import lax
from jax.experimental import pallas as pl
from jax.experimental.pallas import tpu as pltpu
from jax.sharding import PartitionSpec as P

HEADS = 8
HEAD_DIM = 128


def passed_along(block, axis, distance):
    devices = range(lax.axis_size(axis))
    route = [(i - distance, i) for i in devices if i - distance in devices]
    return lax.ppermute(block, axis, route)


def shifted(value, axis, by):
    size = lax.axis_size(axis)
    return lax.ppermute(value, axis, [(i, (i + by) % size) for i in range(size)])


def layer_norm(values, gain, bias):
    center = values - jnp.mean(values, axis=-1, keepdims=True)
    spread = jnp.mean(center * center, axis=-1, keepdims=True)
    return center * lax.rsqrt(spread + 1e-05) * gain + bias


def smooth_act(values):
    return jax.nn.gelu(values, approximate=True)


def article_numbers(lengths_row, positions):
    bounds = jnp.cumsum(lengths_row)
    return jnp.sum((positions[:, None] >= bounds[None, :]).astype(jnp.int32), axis=1)


def per_device(
    tokens,
    article_lengths,
    gain_one,
    bias_one,
    w_qkv,
    w_out,
    gain_two,
    bias_two,
    w_up,
    w_down,
    cotangent,
):
    tok_rows = tokens.shape[1]
    model_width = tokens.shape[2]
    head_count = HEADS
    head_size = HEAD_DIM
    scale = 1.0 / math.sqrt(head_size)
    blocks_seq = lax.axis_size("seq")
    my_place = lax.axis_index("seq")
    full_qkv, full_out, full_up, full_down = (
        lax.all_gather(w_qkv, "seg", axis=0, tiled=True),
        lax.all_gather(w_out, "seg", axis=0, tiled=True),
        lax.all_gather(w_up, "seg", axis=0, tiled=True),
        lax.all_gather(w_down, "seg", axis=0, tiled=True),
    )
    inputs = tokens[0].astype(jnp.float32)
    normed, norm_one_back = jax.vjp(layer_norm, inputs, gain_one, bias_one)
    normed_low = normed.astype(jnp.bfloat16)
    projected = jnp.dot(normed_low, full_qkv, preferred_element_type=jnp.float32).astype(
        jnp.bfloat16
    )
    query_low = projected[:, :model_width]
    key_low = projected[:, model_width : 2 * model_width]
    value_low = projected[:, 2 * model_width :]
    query_heads = query_low.reshape(tok_rows, head_count, head_size)
    lengths_row = article_lengths[0]
    positions = my_place * tok_rows + jnp.arange(tok_rows, dtype=jnp.int32)
    query_art = article_numbers(lengths_row, positions)

    def scores_of(key_block, source):
        key_pos = source * tok_rows + jnp.arange(tok_rows, dtype=jnp.int32)
        key_art = article_numbers(lengths_row, key_pos)
        allowed = (key_pos[None, :] <= positions[:, None]) & (
            key_art[None, :] == query_art[:, None]
        )
        raw = (
            jnp.einsum(
                "qhd,khd->hqk",
                query_heads,
                key_block.reshape(tok_rows, head_count, head_size),
                preferred_element_type=jnp.float32,
            )
            * scale
        )
        return jnp.where(allowed[None], raw, -1e30)

    def forward_block(state, key_block, value_block, source):

        def forward_work(operands):
            (top, total, accum), key_now, value_now = operands
            scores = scores_of(key_now, source)
            new_top = jnp.maximum(top, jnp.max(scores, axis=2))
            factor = jnp.exp(top - new_top)
            weights = jnp.exp(scores - new_top[:, :, None])
            total = total * factor + jnp.sum(weights, axis=2)
            gathered = jnp.einsum(
                "hqk,khd->qhd",
                weights.astype(jnp.bfloat16),
                value_now.reshape(tok_rows, head_count, head_size),
                preferred_element_type=jnp.float32,
            ).reshape(tok_rows, model_width)
            accum = accum * jnp.repeat(factor.T, head_size, axis=1) + gathered
            return (new_top, total, accum)

        def forward_keep(operands):
            return operands[0]

        return lax.cond(
            source <= my_place, forward_work, forward_keep, (state, key_block, value_block)
        )

    start_state = (
        jnp.full((head_count, tok_rows), -1e30, jnp.float32),
        jnp.zeros((head_count, tok_rows), jnp.float32),
        jnp.zeros((tok_rows, model_width), jnp.float32),
    )
    state = forward_block(start_state, key_low, value_low, my_place)

    def forward_step(step, carry):
        key_block, value_block, state_now = carry
        key_block, value_block = passed_along((key_block, value_block), "seq", 1)
        source = (my_place - step) % blocks_seq
        return (key_block, value_block, forward_block(state_now, key_block, value_block, source))

    _, _, state = lax.fori_loop(1, blocks_seq, forward_step, (key_low, value_low, state))
    top, total, accum = state
    log_total = top + jnp.log(total)
    attended = accum / jnp.repeat(total.T, head_size, axis=1)
    attended_low = attended.astype(jnp.bfloat16)
    middle = inputs + jnp.dot(attended_low, full_out, preferred_element_type=jnp.float32)
    normed_two, norm_two_back = jax.vjp(layer_norm, middle, gain_two, bias_two)
    normed_two_low = normed_two.astype(jnp.bfloat16)
    hidden = jnp.dot(normed_two_low, full_up, preferred_element_type=jnp.float32)
    activated, act_back = jax.vjp(smooth_act, hidden)
    activated_low = activated.astype(jnp.bfloat16)
    outputs = middle + jnp.dot(activated_low, full_down, preferred_element_type=jnp.float32)
    result = outputs.astype(jnp.bfloat16)[None]
    grad_top = cotangent[0].astype(jnp.float32)
    grad_top_low = cotangent[0]
    grad_down = jnp.einsum(
        "tf,td->fd", activated_low, grad_top_low, preferred_element_type=jnp.float32
    )
    grad_act = jnp.einsum("td,fd->tf", grad_top_low, full_down, preferred_element_type=jnp.float32)
    (grad_hidden,) = act_back(grad_act)
    grad_hidden_low = grad_hidden.astype(jnp.bfloat16)
    grad_up = jnp.einsum(
        "td,tf->df", normed_two_low, grad_hidden_low, preferred_element_type=jnp.float32
    )
    grad_normed_two = jnp.einsum(
        "tf,df->td", grad_hidden_low, full_up, preferred_element_type=jnp.float32
    )
    grad_mid_norm, grad_gain_two, grad_bias_two = norm_two_back(grad_normed_two)
    grad_middle = grad_top + grad_mid_norm
    grad_middle_low = grad_middle.astype(jnp.bfloat16)
    grad_out = jnp.einsum(
        "tc,td->cd", attended_low, grad_middle_low, preferred_element_type=jnp.float32
    )
    grad_att = jnp.einsum(
        "td,cd->tc", grad_middle_low, full_out, preferred_element_type=jnp.float32
    )
    grad_att_low = grad_att.astype(jnp.bfloat16)
    grad_att_heads = grad_att_low.reshape(tok_rows, head_count, head_size)
    offsets = jnp.sum(
        (grad_att_low.astype(jnp.float32) * attended).reshape(tok_rows, head_count, head_size),
        axis=2,
    ).T

    def backward_block(operands, source):

        def backward_work(inner):
            grad_query, grad_key, grad_value, key_now, value_now = inner
            key_heads = key_now.reshape(tok_rows, head_count, head_size)
            value_heads = value_now.reshape(tok_rows, head_count, head_size)
            probs = jnp.exp(scores_of(key_now, source) - log_total[:, :, None])
            probs_low = probs.astype(jnp.bfloat16)
            grad_value = grad_value + jnp.einsum(
                "hqk,qhd->khd", probs_low, grad_att_heads, preferred_element_type=jnp.float32
            ).reshape(tok_rows, model_width)
            grad_probs = jnp.einsum(
                "qhd,khd->hqk", grad_att_heads, value_heads, preferred_element_type=jnp.float32
            )
            grad_scores = (probs * (grad_probs - offsets[:, :, None])).astype(jnp.bfloat16)
            grad_query = (
                grad_query
                + jnp.einsum(
                    "hqk,khd->qhd", grad_scores, key_heads, preferred_element_type=jnp.float32
                ).reshape(tok_rows, model_width)
                * scale
            )
            grad_key = (
                grad_key
                + jnp.einsum(
                    "hqk,qhd->khd", grad_scores, query_heads, preferred_element_type=jnp.float32
                ).reshape(tok_rows, model_width)
                * scale
            )
            return (grad_query, grad_key, grad_value, key_now, value_now)

        def backward_keep(inner):
            return inner

        return lax.cond(source <= my_place, backward_work, backward_keep, operands)

    def backward_step(step, carry):
        source = (my_place - step) % blocks_seq
        grad_query, grad_key, grad_value, key_block, value_block = backward_block(carry, source)
        key_block, value_block = passed_along((key_block, value_block), "seq", 1)
        grad_key, grad_value = (
            shifted(grad_key.astype(jnp.bfloat16), "seq", 1).astype(grad_key.dtype),
            shifted(grad_value.astype(jnp.bfloat16), "seq", 1).astype(grad_value.dtype),
        )
        return (grad_query, grad_key, grad_value, key_block, value_block)

    zero_rows = jnp.zeros((tok_rows, model_width), jnp.float32)
    grad_query, grad_key, grad_value, _, _ = lax.fori_loop(
        0, blocks_seq, backward_step, (zero_rows, zero_rows, zero_rows, key_low, value_low)
    )
    grad_proj_low = jnp.concatenate([grad_query, grad_key, grad_value], axis=1).astype(jnp.bfloat16)
    grad_qkv = jnp.einsum(
        "tc,tk->ck", normed_low, grad_proj_low, preferred_element_type=jnp.float32
    )
    grad_normed = jnp.einsum(
        "tk,ck->tc", grad_proj_low, full_qkv, preferred_element_type=jnp.float32
    )
    grad_in_norm, grad_gain_one, grad_bias_one = norm_one_back(grad_normed)
    input_grad = (grad_middle + grad_in_norm)[None]
    part_qkv, part_out, part_up, part_down = (
        lax.psum_scatter(
            grad_qkv.astype(jnp.bfloat16), "seg", scatter_dimension=0, tiled=True
        ).astype(jnp.float32),
        lax.psum_scatter(
            grad_out.astype(jnp.bfloat16), "seg", scatter_dimension=0, tiled=True
        ).astype(jnp.float32),
        lax.psum_scatter(
            grad_up.astype(jnp.bfloat16), "seg", scatter_dimension=0, tiled=True
        ).astype(jnp.float32),
        lax.psum_scatter(
            grad_down.astype(jnp.bfloat16), "seg", scatter_dimension=0, tiled=True
        ).astype(jnp.float32),
    )
    sum_qkv, sum_out, sum_up, sum_down = (
        lax.psum_scatter(
            part_qkv.astype(jnp.bfloat16), "seq", scatter_dimension=1, tiled=True
        ).astype(jnp.float32),
        lax.psum_scatter(
            part_out.astype(jnp.bfloat16), "seq", scatter_dimension=1, tiled=True
        ).astype(jnp.float32),
        lax.psum_scatter(
            part_up.astype(jnp.bfloat16), "seq", scatter_dimension=1, tiled=True
        ).astype(jnp.float32),
        lax.psum_scatter(
            part_down.astype(jnp.bfloat16), "seq", scatter_dimension=1, tiled=True
        ).astype(jnp.float32),
    )
    sum_gain_one, sum_bias_one, sum_gain_two, sum_bias_two = lax.psum(
        (grad_gain_one, grad_bias_one, grad_gain_two, grad_bias_two), ("seq", "seg")
    )
    return (
        result,
        input_grad,
        sum_gain_one,
        sum_bias_one,
        sum_qkv,
        sum_out,
        sum_gain_two,
        sum_bias_two,
        sum_up,
        sum_down,
    )


MESH = pl.DeviceIdType.MESH
BF = jnp.bfloat16
F32 = jnp.float32
NEAR_FIRST = ((0, 1, 2, 3), (1, 0, 2, 3), (2, 1, 3, 0), (3, 2, 1, 0))
FAR_FIRST = ((3, 2, 1, 0), (3, 0, 2, 1), (0, 3, 1, 2), (0, 1, 2, 3))


def pick(table, row, column):
    out = jnp.int32(0)
    for r, line in enumerate(table):
        for c, entry in enumerate(line):
            if entry:
                out = jnp.where((row == r) & (column == c), entry, out)
    return out


def dot_nn(a, b):
    return lax.dot_general(a, b, (((1,), (0,)), ((), ())), preferred_element_type=F32)


def dot_nt(a, b):
    return lax.dot_general(a, b, (((1,), (1,)), ((), ())), preferred_element_type=F32)


def dot_tn(a, b):
    return lax.dot_general(a, b, (((0,), (0,)), ((), ())), preferred_element_type=F32)


def remote(src, dst, send, recv, **place):
    return pltpu.make_async_remote_copy(
        src_ref=src, dst_ref=dst, send_sem=send, recv_sem=recv, device_id=place, device_id_type=MESH
    )


def norm_parts(values):
    center = values - jnp.mean(values, axis=-1, keepdims=True)
    spread = jnp.mean(center * center, axis=-1, keepdims=True)
    inverse = lax.rsqrt(spread + 1e-05)
    return center * inverse, inverse


def greet(q, s, transposed=False):
    y, c = s // 2, s % 2
    barrier = pltpu.get_barrier_semaphore()

    def signal(seq, seg):
        pl.semaphore_signal(barrier, 1, device_id={"seq": seq, "seg": seg}, device_id_type=MESH)

    for d in range(1, 8):
        for core in range(2):
            signal(lax.rem(q + d, 8), 2 * y + core)
    for d in range(1, 4):
        signal(q, lax.rem(s + d, 4))
    if transposed:
        turned = s != q // 2

        @pl.when(turned)
        def _():
            signal(2 * s + q % 2, q // 2)

        pl.semaphore_wait(barrier, jnp.where(turned, 18, 17))
    else:
        pl.semaphore_wait(barrier, 17)


def first_columns(lens, base, rows):
    place = base + lax.broadcasted_iota(jnp.int32, (rows, 1), 0)
    start = jnp.zeros((rows, 1), jnp.int32)
    bound = jnp.zeros((1, 1), jnp.int32)
    for i in range(lens.shape[0]):
        bound = bound + lens[i : i + 1, 0:1]
        start = jnp.where(place >= bound, bound, start)
    return start


def seen_mask(start, base_q, base_k, rows, columns):
    place = base_q + lax.broadcasted_iota(jnp.int32, (rows, columns), 0)
    key = base_k + lax.broadcasted_iota(jnp.int32, (rows, columns), 1)
    return (key <= place) & (key >= start)


def rows(k, n):
    return pl.ds(pl.multiple_of(k * n, n), n)


def lanes(k, n=128):
    return pl.ds(pl.multiple_of(k * n, n), n)


T = 256


def attend_kernel(
    x_ref, lens_ref, gain_ref, bias_ref, wq_ref, wo_ref, wu_ref, g_ref,
    o_ref, wof, wuc, gall, xs, h1, wh, qkv, of, lse, lens,
    ob, wq_s, wu_v, lens_r, local_sem, qs, qr, ws, wr, xs_send, xs_recv, os_send, os_recv,
):
    q, s = lax.axis_index("seq"), lax.axis_index("seg")
    z, x = q // 2, q % 2
    y, c = s // 2, s % 2
    sib = s + 1 - 2 * c
    across = (1 - y) * 2 + c
    corner = (1 - y) * 2 + 1 - c
    head = 2 * z + c
    home = c == x
    column = 2 * y + x
    scale = 1.0 / math.sqrt(HEAD_DIM)

    for j in range(3):
        at = slice(j * 128, (j + 1) * 128)
        wh[rows(s, T), at] = wq_ref[:, lanes(8 * j + head)]
        wq_s[0, :, at] = wq_ref[:, lanes(8 * j + head)]
        wq_s[1, :, at] = wq_ref[:, lanes(8 * j + 2 * z + 1 - c)]

    @pl.when(home)
    def _():
        xs[rows(q, T)] = x_ref[...]

    greet(q, s)

    swap = remote(
        x_ref, xs.at[rows(q, T)], xs_send.at[12], xs_recv.at[q], seq=2 * z + 1 - x, seg=2 * y + 1 - c
    )

    @pl.when(jnp.logical_not(home))
    def _():
        swap.start()

    mine_wh = wh.at[rows(s, T)]
    q_across = remote(wq_s.at[0], mine_wh, qs.at[0], qr.at[0], seg=across)
    q_sib = remote(wq_s.at[1], mine_wh, qs.at[1], qr.at[1], seg=sib)
    q_corner = remote(wq_s.at[1], mine_wh, qs.at[2], qr.at[2], seg=corner)
    l_sib = remote(lens_ref, lens_r, qs.at[3], qr.at[3], seg=sib)
    first = (q_across, q_corner, q_sib, l_sib)
    for copy in first:
        copy.start()

    def x_copy(b, k, **to):
        src = xs.at[rows(b, T)]
        return remote(src, src, xs_send.at[k], xs_recv.at[b], **to)

    u_across = remote(wu_ref.at[:, lanes(across, 1024)], wuc.at[rows(s, T)], ws.at[0], wr.at[0], seg=across)
    u_corner = remote(wu_ref.at[:, lanes(corner, 1024)], wuc.at[rows(s, T)], ws.at[1], wr.at[1], seg=corner)
    u_sib = remote(wu_ref.at[:, lanes(sib, 1024)], wuc.at[rows(s, T)], ws.at[2], wr.at[2], seg=sib)
    o_across = remote(wo_ref, wof.at[rows(s, T)], ws.at[3], wr.at[3], seg=across)
    o_sib = remote(wo_ref, wof.at[rows(s, T)], ws.at[4], wr.at[4], seg=sib)
    o_pass = remote(wof.at[rows(across, T)], wof.at[rows(across, T)], ws.at[5], wr.at[5], seg=sib)
    g_across = remote(g_ref, gall.at[rows(s, T)], ws.at[6], wr.at[6], seg=across)
    g_sib = remote(g_ref, gall.at[rows(s, T)], ws.at[7], wr.at[7], seg=sib)
    g_pass = remote(gall.at[rows(across, T)], gall.at[rows(across, T)], ws.at[8], wr.at[8], seg=sib)
    own_in = pltpu.make_async_copy(wu_ref.at[:, lanes(s, 1024)], wu_v, local_sem.at[0])
    own = (
        pltpu.make_async_copy(wo_ref, wof.at[rows(s, T)], local_sem.at[1]),
        pltpu.make_async_copy(g_ref, gall.at[rows(s, T)], local_sem.at[2]),
        pltpu.make_async_copy(wu_v, wuc.at[rows(s, T)], local_sem.at[3]),
    )
    for copy in (own_in, u_across, u_corner, o_across, g_across):
        copy.start()
    for copy in first:
        copy.wait_recv()
    lens[...] = jnp.where(home, lens_ref[...], lens_r[...])
    own_in.wait()
    for copy in own:
        copy.start()

    gain, bias = gain_ref[...], bias_ref[...]

    def project(b):
        unit, _ = norm_parts(xs[rows(b, T)].astype(F32))
        low = (unit * gain + bias).astype(BF)
        h1[rows(b, T)] = low
        qkv[rows(b, T)] = dot_nn(low, wh[...]).astype(BF)

    def track_step(i, _):
        zz = pick(NEAR_FIRST, z, i % 4)
        b = 2 * zz + c

        @pl.when(i < 4)
        def _():
            @pl.when((i > 0) | jnp.logical_not(home))
            def _():
                x_copy(b, 0, seq=q).wait_recv()

            @pl.when((zz <= z) & (z < 3))
            def _():
                x_copy(b, zz, seq=q + 2).start()

            @pl.when((zz >= z) & (z > 0))
            def _():
                x_copy(b, 4 + zz, seq=q - 2).start()

            x_copy(b, 8 + zz, seg=sib).start()
            project(b)

        @pl.when(i > 0)
        def _():
            late = 2 * pick(NEAR_FIRST, z, i - 1) + 1 - c
            x_copy(late, 0, seg=sib).wait_recv()
            project(late)

        return 0

    lax.fori_loop(0, 5, track_step, 0)
    for copy in (u_sib, o_sib, g_sib):
        copy.start()

    def o_copy(i, sender):
        return remote(
            ob.at[i], o_ref.at[:, lanes(sender)], os_send.at[i], os_recv.at[sender], seq=i, seg=column
        )

    mine = pltpu.make_async_copy(ob.at[q], o_ref.at[:, lanes(head)], os_recv.at[head])
    for i in range(8):
        n = (i + 1) * T
        start = first_columns(lens, i * T, T)
        scores = dot_nt(qkv[i * T : n, :128], qkv[:n, 128:256]) * scale
        scores = jnp.where(seen_mask(start, i * T, 0, T, n), scores, -1e30)
        top = jnp.max(scores, axis=1, keepdims=True)
        weights = jnp.exp(scores - top)
        total = jnp.sum(weights, axis=1, keepdims=True)
        mixed = dot_nn(weights.astype(BF), qkv[:n, 256:384]) / total
        of[i * T : n] = mixed
        lse[i * T : n] = top + jnp.log(total)
        ob[i] = mixed.astype(BF)
        here = (q == i) & home

        @pl.when(jnp.logical_not(here))
        def _():
            o_copy(i, head).start()

        @pl.when(here)
        def _():
            mine.start()

    o_across.wait_recv()
    o_pass.start()
    g_across.wait_recv()
    g_pass.start()

    def track_end(zz, _):
        b = 2 * zz + c

        @pl.when((zz <= z) & (z < 3))
        def _():
            x_copy(b, zz, seq=q + 2).wait_send()

        @pl.when((zz >= z) & (z > 0))
        def _():
            x_copy(b, 4 + zz, seq=q - 2).wait_send()

        x_copy(b, 8 + zz, seg=sib).wait_send()
        return 0

    lax.fori_loop(0, 4, track_end, 0)

    @pl.when(jnp.logical_not(home))
    def _():
        swap.wait_send()

    for i in range(8):
        @pl.when(jnp.logical_not((q == i) & home))
        def _():
            o_copy(i, head).wait_send()

        o_copy(i, i).wait_recv()

    for copy in own:
        copy.wait()
    for copy in first + (u_across, u_corner, u_sib, o_across, o_sib, o_pass, g_across, g_sib, g_pass):
        copy.wait_send()
    for copy in (u_across, u_corner, u_sib, o_sib, o_pass, g_sib, g_pass):
        copy.wait_recv()


VM = pl.BlockSpec(memory_space=pltpu.VMEM)
HB = pl.BlockSpec(memory_space=pl.ANY)
S = jax.ShapeDtypeStruct


def attend(x, lens, gain, bias, wq, wo, wu, g):
    dma = pltpu.SemaphoreType.DMA
    return pl.pallas_call(
        attend_kernel,
        out_shape=(
            S((256, 1024), BF), S((1024, 1024), BF), S((1024, 1024), BF), S((1024, 1024), BF),
            S((2048, 1024), BF), S((2048, 1024), BF), S((1024, 384), BF), S((2048, 384), BF),
            S((2048, 128), F32), S((2048, 1), F32), S((8, 128), jnp.int32),
        ),
        in_specs=[VM, VM, VM, VM, VM, VM, HB, VM],
        out_specs=(VM, HB, HB, HB, VM, VM, VM, VM, VM, VM, VM),
        scratch_shapes=[
            pltpu.VMEM((8, 256, 128), BF), pltpu.VMEM((2, 256, 384), BF), pltpu.VMEM((256, 1024), BF),
            pltpu.VMEM((8, 128), jnp.int32), dma((4,)), dma((4,)), dma((4,)), dma((9,)), dma((9,)),
            dma((13,)), dma((8,)), dma((8,)), dma((8,)),
        ],
        compiler_params=pltpu.CompilerParams(
            collective_id=0, has_side_effects=True, vmem_limit_bytes=58 * 2**20
        ),
        cost_estimate=pl.CostEstimate(flops=5 * 10**9, bytes_accessed=40 * 2**20, transcendentals=2 * 2**20),
        name="attend",
    )(x, lens, gain, bias, wq, wo, wu, g)


def gelu_parts(u):
    root = math.sqrt(2.0 / math.pi)
    square = u * u
    t = jnp.tanh(root * (u + 0.044715 * (square * u)))
    value = 0.5 * u * (1.0 + t)
    slope = 0.5 * (1.0 + t) + 0.5 * u * (1.0 - t * t) * (root * (1.0 + 0.134145 * square))
    return value, slope


def norm_back(grad, gain, unit, inverse):
    through = grad * gain
    a = jnp.mean(through, axis=-1, keepdims=True)
    b = jnp.mean(through * unit, axis=-1, keepdims=True)
    return inverse * (through - a - unit * b)


def ffn_kernel(
    x_ref, o_ref, g_ref, gain_ref, bias_ref, wo_ref, wu_ref, wd_ref,
    result_ref, dx_ref, do_ref, sums_ref, pack_ref, outp_ref,
    h2, za, dua, rp, dp, d_s, d_c, d_p, d_y, r_s, r_c, r_p, r_y, hs, hr, ss, sr,
):
    q, s = lax.axis_index("seq"), lax.axis_index("seg")
    y, c = s // 2, s % 2
    sib = s + 1 - 2 * c
    across = (1 - y) * 2 + c
    corner = (1 - y) * 2 + 1 - c

    barrier = pltpu.get_barrier_semaphore()
    for d in range(1, 4):
        pl.semaphore_signal(barrier, 1, device_id={"seg": lax.rem(s + d, 4)}, device_id_type=MESH)
    pl.semaphore_wait(barrier, 3)

    middle = x_ref[...].astype(F32) + dot_nn(o_ref[...], wo_ref[...])
    result_f = middle
    unit, inverse = norm_parts(middle)
    h2[rows(s, T)] = (unit * gain_ref[...] + bias_ref[...]).astype(BF)

    def h_copy(k, block, to):
        src = h2.at[rows(block, T)]
        return remote(src, src, hs.at[k], hr.at[k], seg=to)

    h_across, h_sib, h_pass = h_copy(0, s, across), h_copy(1, s, sib), h_copy(2, across, sib)
    h_across.start()
    h_sib.start()

    def work(block):
        at = rows(block, T)
        value, slope = gelu_parts(dot_nn(h2[at], wu_ref[...]))
        za[at] = value.astype(BF)
        du = (slope * dot_nt(g_ref[at], wd_ref[...])).astype(BF)
        dua[at] = du
        dp[block] = dot_nt(du, wu_ref[...])
        rp[block] = dot_nn(za[at], wd_ref[...])

    work(s)
    h_sib.wait_recv()
    work(sib)
    h_across.wait_recv()
    h_pass.start()
    work(across)
    h_pass.wait_recv()
    work(corner)

    d_s[0], d_s[1] = dp[corner].astype(BF), dp[sib].astype(BF)
    r_s[0], r_s[1] = rp[corner].astype(BF), rp[sib].astype(BF)
    d_core = remote(d_s, d_c, ss.at[0], sr.at[0], seg=sib)
    r_core = remote(r_s, r_c, ss.at[1], sr.at[1], seg=sib)
    d_core.start()
    r_core.start()
    d_core.wait_recv()
    d_p[...] = (dp[across] + d_c[0].astype(F32)).astype(BF)
    d_far = remote(d_p, d_y, ss.at[2], sr.at[2], seg=across)
    d_far.start()
    r_core.wait_recv()
    r_p[...] = (rp[across] + r_c[0].astype(F32)).astype(BF)
    r_far = remote(r_p, r_y, ss.at[3], sr.at[3], seg=across)
    r_far.start()

    up = dot_tn(h2[...], dua[...]).astype(BF)
    for k in range(8):
        pack_ref[k, :, :512] = up[(k // 2) * T : (k // 2 + 1) * T, (k % 2) * 512 : (k % 2 + 1) * 512]
    down = dot_tn(za[...], g_ref[...]).astype(BF)
    for k in range(8):
        for j in range(4):
            pack_ref[k, :, 512 + j * 128 : 640 + j * 128] = down[j * T : (j + 1) * T, k * 128 : (k + 1) * 128]

    d_far.wait_recv()
    grad = dp[s] + d_c[1].astype(F32) + d_y[...].astype(F32)
    sums_ref[0:1] = jnp.sum(grad * unit, axis=0, keepdims=True)
    sums_ref[1:2] = jnp.sum(grad, axis=0, keepdims=True)
    dx = g_ref[rows(s, T)].astype(F32) + norm_back(grad, gain_ref[...], unit, inverse)
    dx_ref[...] = dx
    dy = dx.astype(BF)
    do_ref[...] = dot_nt(dy, wo_ref[...]).astype(BF)
    out = dot_tn(o_ref[...], dy).astype(BF)
    for quarter in range(4):
        for k in range(8):
            outp_ref[quarter // 2, quarter % 2, k] = out[quarter * T : (quarter + 1) * T, k * 128 : (k + 1) * 128]
    r_far.wait_recv()
    result_ref[...] = (result_f + rp[s] + r_c[1].astype(F32) + r_y[...].astype(F32)).astype(BF)
    for copy in (h_across, h_sib, h_pass, d_core, r_core, d_far, r_far):
        copy.wait_send()


def ffn(x, o, g, gain, bias, wo, wu, wd):
    dma = pltpu.SemaphoreType.DMA
    V = pltpu.VMEM
    block = lambda *lead: V(lead + (256, 1024), BF)
    return pl.pallas_call(
        ffn_kernel,
        out_shape=(
            S((256, 1024), BF), S((256, 1024), F32), S((256, 1024), BF), S((2, 1024), F32),
            S((8, 256, 1024), BF), S((2, 2, 8, 256, 128), BF),
        ),
        in_specs=[VM] * 8,
        out_specs=(VM,) * 6,
        scratch_shapes=[
            V((1024, 1024), BF), V((1024, 1024), BF), V((1024, 1024), BF), V((4, 256, 1024), F32),
            V((4, 256, 1024), F32), block(2), block(2), block(), block(), block(2), block(2), block(), block(),
            dma((3,)), dma((3,)), dma((4,)), dma((4,)),
        ],
        compiler_params=pltpu.CompilerParams(
            collective_id=2, has_side_effects=True, vmem_limit_bytes=60 * 2**20
        ),
        cost_estimate=pl.CostEstimate(flops=15 * 10**9, bytes_accessed=40 * 2**20, transcendentals=2**20),
        name="ffn",
    )(x, o, g, gain, bias, wo, wu, wd)


def grads_kernel(
    pack_ref, outp_ref, do_ref, dx_ref, sums2_ref, x_ref, xs_ref, h1_ref, wh_ref, qkv_ref, of_ref, lse_ref, lens_ref,
    gain_ref,
    dx_out, gqkv_out, gout_out, gup_out, gdown_out, sums_out,
    x_r, pk, z_r, up_s, up_r, oc_r, oy_r, ox_r, oz_r, doh, dq, dk, dv, dh_s, dhc_r, dhz_r, dht_s, dht_r,
    gq, gq_b, gq_x, gq_y, gq_s, gq_r, vec, vec_r, xbuf, hbuf,
    gxs, gxr, gzs, gzr, ups, upr, cs, cr, oxs, oxr, ozs, ozr, dos, dor, dcs, dcr, dzs, dzr, dts, dtr,
    qs, qr, vs, vr, blk_sem,
):
    q, s = lax.axis_index("seq"), lax.axis_index("seg")
    z, x = q // 2, q % 2
    y, c = s // 2, s % 2
    sib = s + 1 - 2 * c
    across = (1 - y) * 2 + c
    xq = 2 * z + 1 - x
    head = 2 * z + c
    home = c == x
    column = 2 * y + x
    away = jnp.logical_not(home)
    scale = 1.0 / math.sqrt(HEAD_DIM)
    greet(q, s, True)

    def do_copy(h, block):
        return remote(
            do_ref.at[:, h * 128 : (h + 1) * 128], doh.at[rows(block, T)], dos.at[h], dor.at[block],
            seq=2 * (h // 2) + c, seg=2 * y + h % 2,
        )

    do_mine = pltpu.make_async_copy(do_ref.at[:, lanes(head)], doh.at[rows(q, T)], dor.at[q])
    for h in range(8):
        here = (head == h) & home

        @pl.when(jnp.logical_not(here))
        def _():
            do_copy(h, q).start()

        @pl.when(here)
        def _():
            do_mine.start()

    def gx_copy(d):
        return remote(pack_ref.at[2 * d + 1 - x], x_r.at[d], gxs.at[d], gxr.at[d], seq=xq)

    def start_x(j, _):
        gx_copy(pick(FAR_FIRST, z, j)).start()
        return 0

    out_core = remote(outp_ref.at[:, 1 - c], oc_r, cs.at[0], cr.at[0], seg=sib)
    out_core.start()
    lax.fori_loop(0, 4, start_x, 0)
    out_core.wait_recv()
    for part in range(2):
        oc_r[part] = (oc_r[part].astype(F32) + outp_ref[part, c].astype(F32)).astype(BF)
    out_y = remote(oc_r.at[1 - y], oy_r, cs.at[1], cr.at[1], seg=across)
    out_y.start()

    def line_slot(d, place):
        return jnp.where(d == place, 4, d)

    def line(src, into, send, recv, d):
        up = remote(src, into.at[d], send.at[d], recv.at[d], seq=q + 2)
        low = line_slot(d, z - 1)
        down = remote(src, into.at[low], send.at[d], recv.at[low], seq=q - 2)
        return up, down

    def come(into, recv, slot):
        return remote(into.at[slot], into.at[slot], recv.at[slot], recv.at[slot], seq=xq)

    def pass_on(value, keep, into, send, recv, d):
        has_in = jnp.where(d > z, z > 0, z < 3)

        @pl.when(d != z)
        def _():
            @pl.when(has_in)
            def _():
                come(into, recv, d).wait_recv()
                keep[...] = (value() + into[d].astype(F32)).astype(BF)

            @pl.when(jnp.logical_not(has_in))
            def _():
                keep[...] = value().astype(BF)

            up, down = line(keep, into, send, recv, d)

            @pl.when(d > z)
            def _():
                up.start()

            @pl.when(d < z)
            def _():
                down.start()

    def pack_step(j, _):
        d = pick(FAR_FIRST, z, j)
        own = 2 * d + x
        gx_copy(d).wait_recv()
        pass_on(
            lambda: pack_ref[own].astype(F32) + x_r[d].astype(F32), pk.at[d], z_r, gzs, gzr, d
        )
        return 0

    for b in range(8):
        do_copy(0, b).wait_recv()

    lax.fori_loop(0, 1, pack_step, 0)

    dk[...] = jnp.zeros_like(dk)
    dv[...] = jnp.zeros_like(dv)
    lens = lens_ref[...]
    for i in range(8):
        top = i * T
        start = first_columns(lens, top, T)
        query = qkv_ref[top : top + T, :128]
        grad = doh[top : top + T]
        delta = jnp.sum(grad.astype(F32) * of_ref[top : top + T], axis=1, keepdims=True)
        log_total = lse_ref[top : top + T]
        total = jnp.zeros((T, 128), F32)
        for base in range(0, top + T, 1024):
            n = min(1024, top + T - base)
            keys = qkv_ref[base : base + n, 128:256]
            probs = jnp.exp(dot_nt(query, keys) * scale - log_total)
            probs = jnp.where(seen_mask(start, top, base, T, n), probs, 0.0)
            dp = dot_nt(grad, qkv_ref[base : base + n, 256:384])
            ds = (probs * (dp - delta)).astype(BF)
            dv[base : base + n] += dot_tn(probs.astype(BF), grad)
            dk[base : base + n] += dot_tn(ds, query)
            total += dot_nn(ds, keys)
        dq[top : top + T] = total

    lax.fori_loop(1, 2, pack_step, 0)

    gq[...] = jnp.zeros_like(gq)
    vec[...] = jnp.zeros_like(vec)
    vec[2:4] = sums2_ref[...]

    def block_of(i):
        return pick(FAR_FIRST, z, i % 4) * 2 + jnp.where(i < 4, 1 - c, c)

    def x_load(i):
        return pltpu.make_async_copy(xs_ref.at[rows(block_of(i), T)], xbuf.at[i % 2], blk_sem.at[i % 2])

    def h_load(i):
        return pltpu.make_async_copy(h1_ref.at[rows(block_of(i), T)], hbuf.at[i % 2], blk_sem.at[2 + i % 2])

    def dhc_copy(d):
        return remote(dh_s.at[2 * d + 1 - c], dhc_r.at[d], dcs.at[d], dcr.at[d], seg=sib)

    x_load(0).start()
    h_load(0).start()

    def block_step(i, _):
        b = block_of(i)
        d = pick(FAR_FIRST, z, i % 4)

        @pl.when(i < 7)
        def _():
            x_load(i + 1).start()
            h_load(i + 1).start()

        at = rows(b, T)
        low = jnp.concatenate([dq[at] * scale, dk[at] * scale, dv[at]], axis=1).astype(BF)
        dh = dot_nt(low, wh_ref[...])
        dh_s[b] = dh.astype(BF)

        @pl.when(i < 4)
        def _():
            dhc_copy(d).start()

        @pl.when(i >= 4)
        def _():
            dhc_copy(d).wait_recv()
            pass_on(
                lambda: dh_s[b].astype(F32) + dhc_r[d].astype(F32), dh_s.at[b], dhz_r, dzs, dzr, d
            )

        x_load(i).wait()
        h_load(i).wait()
        gq[...] += dot_tn(hbuf[i % 2], low)
        unit, _ = norm_parts(xbuf[i % 2].astype(F32))
        vec[0:1] += jnp.sum(dh * unit, axis=0, keepdims=True)
        vec[1:2] += jnp.sum(dh, axis=0, keepdims=True)
        return 0

    lax.fori_loop(0, 8, block_step, 0)

    gq_b[...] = gq[...].astype(BF).reshape(2, 2, T, 384)
    q_x = remote(gq_b.at[:, 1 - x], gq_x, qs.at[0], qr.at[0], seq=xq)
    q_x.start()
    v_core = remote(vec, vec_r.at[0], vs.at[0], vr.at[0], seg=sib)
    v_core.start()
    v_core.wait()
    vec[...] += vec_r[0]
    v_y = remote(vec, vec_r.at[1], vs.at[1], vr.at[1], seg=across)
    v_y.start()

    out_y.wait_recv()
    oc_r[y] = (oc_r[y].astype(F32) + oy_r[...].astype(F32)).astype(BF)

    def ox_copy(d):
        return remote(oc_r.at[y, 2 * d + 1 - x], ox_r.at[d], oxs.at[d], oxr.at[d], seq=xq)

    def start_ox(j, _):
        ox_copy(pick(FAR_FIRST, z, j)).start()
        return 0

    lax.fori_loop(0, 4, start_ox, 0)
    v_y.wait()
    vec[...] += vec_r[1]
    v_x = remote(vec, vec_r.at[2], vs.at[2], vr.at[2], seq=xq)
    v_x.start()
    q_x.wait_recv()
    for part in range(2):
        gq_x[part] = (gq_x[part].astype(F32) + gq_b[part, x].astype(F32)).astype(BF)
    q_y = remote(gq_x.at[1 - y], gq_y, qs.at[1], qr.at[1], seg=across)
    q_y.start()
    lax.fori_loop(2, 3, pack_step, 0)

    def out_step(j, _):
        d = pick(FAR_FIRST, z, j)
        own = 2 * d + x
        ox_copy(d).wait_recv()
        pass_on(
            lambda: oc_r[y, own].astype(F32) + ox_r[d].astype(F32), oc_r.at[y, own], oz_r, ozs, ozr, d
        )
        return 0

    lax.fori_loop(0, 4, out_step, 0)
    v_x.wait()
    vec[...] += vec_r[2]

    def v_copy(zz, sender):
        return remote(vec, vec_r.at[3 + sender], vs.at[3 + zz], vr.at[3 + sender], seq=zz * 2 + x)

    for zz in range(4):
        @pl.when(zz != z)
        def _():
            v_copy(zz, z).start()

    q_y.wait_recv()
    gq_s[...] = (gq_x[y].astype(F32) + gq_y[...].astype(F32)).astype(BF)

    def column_copy(j):
        place = 8 * j + head
        owner, slot = place // 3, place % 3
        src = gq_s.at[:, j * 128 : (j + 1) * 128]
        copy = remote(src, gq_r.at[slot], qs.at[2 + j], qr.at[2 + slot], seq=owner, seg=column)
        local = pltpu.make_async_copy(src, gq_r.at[slot], qr.at[2 + slot])
        return (owner == q) & home, copy, local

    for j in range(3):
        here, copy, local = column_copy(j)

        @pl.when(jnp.logical_not(here))
        def _():
            copy.start()

        @pl.when(here)
        def _():
            local.start()

    lax.fori_loop(3, 4, pack_step, 0)

    def arrived(into, recv):
        @pl.when(z > 0)
        def _():
            come(into, recv, z).wait_recv()

        @pl.when(z == 0)
        def _():
            into[0] = jnp.zeros_like(into[0])

        @pl.when(z < 3)
        def _():
            come(into, recv, 4).wait_recv()

        @pl.when(z == 3)
        def _():
            into[4] = jnp.zeros_like(into[4])

        return into[z].astype(F32) + into[4].astype(F32)

    dht_s[...] = (dh_s[2 * z + c].astype(F32) + dhc_r[z].astype(F32) + arrived(dhz_r, dzr)).astype(BF)
    turn = remote(dht_s, dht_r, dts, dtr, seq=xq, seg=sib)

    @pl.when(away)
    def _():
        turn.start()

    total = pack_ref[q].astype(F32) + x_r[z].astype(F32) + arrived(z_r, gzr)
    up_s[...] = total[:, :512].astype(BF)
    turned = s != z
    up_turn = remote(up_s, up_r, ups, upr, seq=2 * s + x, seg=z)
    up_own = pltpu.make_async_copy(up_s, up_r, upr)

    @pl.when(turned)
    def _():
        up_turn.start()

    @pl.when(jnp.logical_not(turned))
    def _():
        up_own.start()

    for j in range(4):
        gdown_out[j * T : (j + 1) * T] = total[:, 512 + j * 128 : 640 + j * 128]
    gout_out[...] = oc_r[y, q].astype(F32) + ox_r[z].astype(F32) + arrived(oz_r, ozr)
    for slot in range(3):
        come(gq_r, qr.at[pl.ds(2, 3)], slot).wait_recv()
        gqkv_out[:, slot * 128 : (slot + 1) * 128] = gq_r[slot].astype(F32)
    vec_r[3 + z] = vec[...]
    for zz in range(4):
        @pl.when(zz != z)
        def _():
            v_copy(zz, zz).wait_recv()

    sums_out[...] = (vec_r[3] + vec_r[4] + vec_r[5] + vec_r[6])[:4]
    unit, inverse = norm_parts(x_ref[...].astype(F32))

    @pl.when(away)
    def _():
        turn.wait()

    @pl.when(home)
    def _():
        dht_r[...] = dht_s[...]

    dx_out[...] = dx_ref[...] + norm_back(dht_r[...].astype(F32), gain_ref[...], unit, inverse)
    up_own.wait()
    gup_out[...] = up_r[...].astype(F32)

    for h in range(8):
        @pl.when(jnp.logical_not((head == h) & home))
        def _():
            do_copy(h, q).wait_send()

    def sent(d, _):
        gx_copy(d).wait_send()
        ox_copy(d).wait_send()
        dhc_copy(d).wait_send()

        @pl.when(d != z)
        def _():
            line(dh_s.at[d * 2 + c], dhz_r, dzs, dzr, d)[0].wait_send()
            line(pk.at[d], z_r, gzs, gzr, d)[0].wait_send()
            line(oc_r.at[y, d * 2 + x], oz_r, ozs, ozr, d)[0].wait_send()

        return 0

    lax.fori_loop(0, 4, sent, 0)
    for copy in (out_core, out_y, q_x, q_y):
        copy.wait_send()

    @pl.when(turned)
    def _():
        up_turn.wait_send()

    for j in range(3):
        here, copy, _ = column_copy(j)

        @pl.when(jnp.logical_not(here))
        def _():
            copy.wait_send()

    for zz in range(4):
        @pl.when(zz != z)
        def _():
            v_copy(zz, z).wait_send()


def grads(pack, outp, do, dx, sums2, x, xs, h1, wh, qkv, of, lse, lens, gain):
    V = pltpu.VMEM
    dma = pltpu.SemaphoreType.DMA
    return pl.pallas_call(
        grads_kernel,
        out_shape=(
            S((256, 1024), F32), S((256, 384), F32), S((256, 128), F32), S((256, 512), F32),
            S((1024, 128), F32), S((4, 1024), F32),
        ),
        in_specs=[VM, VM, VM, VM, VM, VM, HB, HB, VM, VM, VM, VM, VM, VM],
        out_specs=(VM,) * 6,
        scratch_shapes=[
            V((4, 256, 1024), BF), V((4, 256, 1024), BF), V((5, 256, 1024), BF), V((256, 512), BF), V((256, 512), BF),
            V((2, 8, 256, 128), BF), V((8, 256, 128), BF), V((4, 256, 128), BF), V((5, 256, 128), BF),
            V((2048, 128), BF), V((2048, 128), F32), V((2048, 128), F32), V((2048, 128), F32),
            V((8, 256, 1024), BF), V((4, 256, 1024), BF), V((5, 256, 1024), BF), V((256, 1024), BF),
            V((256, 1024), BF), V((1024, 384), F32), V((2, 2, 256, 384), BF), V((2, 256, 384), BF),
            V((256, 384), BF), V((256, 384), BF), V((3, 256, 128), BF), V((8, 1024), F32), V((7, 8, 1024), F32),
            V((2, 256, 1024), BF), V((2, 256, 1024), BF),
            dma((4,)), dma((4,)), dma((4,)), dma((5,)), dma, dma, dma((2,)), dma((2,)), dma((4,)), dma((4,)),
            dma((4,)), dma((5,)), dma((8,)), dma((8,)), dma((4,)), dma((4,)), dma((4,)), dma((5,)), dma, dma,
            dma((5,)), dma((5,)), dma((7,)), dma((7,)), dma((4,)),
        ],
        compiler_params=pltpu.CompilerParams(
            collective_id=1, has_side_effects=True, vmem_limit_bytes=60 * 2**20
        ),
        cost_estimate=pl.CostEstimate(flops=8 * 10**9, bytes_accessed=40 * 2**20, transcendentals=2 * 2**20),
        name="grads",
    )(pack, outp, do, dx, sums2, x, xs, h1, wh, qkv, of, lse, lens, gain)


def per_device_fast(
    tokens, article_lengths, gain_one, bias_one, w_qkv, w_out, gain_two, bias_two, w_up, w_down, cotangent
):
    x = tokens[0]
    lens = jnp.broadcast_to(article_lengths[0][:, None], (article_lengths.shape[1], 128))
    o, wo, wu, g, xs, h1, wh, qkv, of, lse, lens = attend(
        x, lens, gain_one[None], bias_one[None], w_qkv, w_out, w_up, cotangent[0]
    )
    result, dx, do, sums2, pack, outp = ffn(
        x, o, g, gain_two[None], bias_two[None], wo, wu, w_down
    )
    dx, gqkv, gout, gup, gdown, sums = grads(
        pack, outp, do, dx, sums2, x, xs, h1, wh, qkv, of, lse, lens, gain_one[None]
    )
    return (result[None], dx[None], sums[0], sums[1], gqkv, gout, sums[2], sums[3], gup, gdown)


def solution(mesh):
    one_pair = mesh.shape["seq"] == HEADS and mesh.shape["seg"] == 4
    return jax.shard_map(
        per_device_fast if one_pair else per_device,
        mesh=mesh,
        in_specs=(
            P("seg", "seq", None),
            P("seg", None),
            P(),
            P(),
            P("seg", None),
            P("seg", None),
            P(),
            P(),
            P("seg", None),
            P("seg", None),
            P("seg", "seq", None),
        ),
        out_specs=(
            P("seg", "seq", None),
            P("seg", "seq", None),
            P(),
            P(),
            P("seg", "seq"),
            P("seg", "seq"),
            P(),
            P(),
            P("seg", "seq"),
            P("seg", "seq"),
        ),
        check_vma=False,
    )
```

```python
import math

import jax
import jax.numpy as jnp
from jax import lax
from jax.experimental import pallas as pl
from jax.experimental.pallas import tpu as pltpu
from jax.sharding import PartitionSpec as P

HEADS = 8
HEAD_DIM = 128


def passed_along(block, axis, distance):
    devices = range(lax.axis_size(axis))
    route = [(i - distance, i) for i in devices if i - distance in devices]
    return lax.ppermute(block, axis, route)


def shifted(value, axis, by):
    size = lax.axis_size(axis)
    return lax.ppermute(value, axis, [(i, (i + by) % size) for i in range(size)])


def layer_norm(values, gain, bias):
    center = values - jnp.mean(values, axis=-1, keepdims=True)
    spread = jnp.mean(center * center, axis=-1, keepdims=True)
    return center * lax.rsqrt(spread + 1e-05) * gain + bias


def smooth_act(values):
    return jax.nn.gelu(values, approximate=True)


def article_numbers(lengths_row, positions):
    bounds = jnp.cumsum(lengths_row)
    return jnp.sum((positions[:, None] >= bounds[None, :]).astype(jnp.int32), axis=1)


def per_device(
    tokens,
    article_lengths,
    gain_one,
    bias_one,
    w_qkv,
    w_out,
    gain_two,
    bias_two,
    w_up,
    w_down,
    cotangent,
):
    tok_rows = tokens.shape[1]
    model_width = tokens.shape[2]
    head_count = HEADS
    head_size = HEAD_DIM
    scale = 1.0 / math.sqrt(head_size)
    blocks_seq = lax.axis_size("seq")
    my_place = lax.axis_index("seq")
    full_qkv, full_out, full_up, full_down = (
        lax.all_gather(w_qkv, "seg", axis=0, tiled=True),
        lax.all_gather(w_out, "seg", axis=0, tiled=True),
        lax.all_gather(w_up, "seg", axis=0, tiled=True),
        lax.all_gather(w_down, "seg", axis=0, tiled=True),
    )
    inputs = tokens[0].astype(jnp.float32)
    normed, norm_one_back = jax.vjp(layer_norm, inputs, gain_one, bias_one)
    normed_low = normed.astype(jnp.bfloat16)
    projected = jnp.dot(normed_low, full_qkv, preferred_element_type=jnp.float32).astype(
        jnp.bfloat16
    )
    query_low = projected[:, :model_width]
    key_low = projected[:, model_width : 2 * model_width]
    value_low = projected[:, 2 * model_width :]
    query_heads = query_low.reshape(tok_rows, head_count, head_size)
    lengths_row = article_lengths[0]
    positions = my_place * tok_rows + jnp.arange(tok_rows, dtype=jnp.int32)
    query_art = article_numbers(lengths_row, positions)

    def scores_of(key_block, source):
        key_pos = source * tok_rows + jnp.arange(tok_rows, dtype=jnp.int32)
        key_art = article_numbers(lengths_row, key_pos)
        allowed = (key_pos[None, :] <= positions[:, None]) & (
            key_art[None, :] == query_art[:, None]
        )
        raw = (
            jnp.einsum(
                "qhd,khd->hqk",
                query_heads,
                key_block.reshape(tok_rows, head_count, head_size),
                preferred_element_type=jnp.float32,
            )
            * scale
        )
        return jnp.where(allowed[None], raw, -1e30)

    def forward_block(state, key_block, value_block, source):

        def forward_work(operands):
            (top, total, accum), key_now, value_now = operands
            scores = scores_of(key_now, source)
            new_top = jnp.maximum(top, jnp.max(scores, axis=2))
            factor = jnp.exp(top - new_top)
            weights = jnp.exp(scores - new_top[:, :, None])
            total = total * factor + jnp.sum(weights, axis=2)
            gathered = jnp.einsum(
                "hqk,khd->qhd",
                weights.astype(jnp.bfloat16),
                value_now.reshape(tok_rows, head_count, head_size),
                preferred_element_type=jnp.float32,
            ).reshape(tok_rows, model_width)
            accum = accum * jnp.repeat(factor.T, head_size, axis=1) + gathered
            return (new_top, total, accum)

        def forward_keep(operands):
            return operands[0]

        return lax.cond(
            source <= my_place, forward_work, forward_keep, (state, key_block, value_block)
        )

    start_state = (
        jnp.full((head_count, tok_rows), -1e30, jnp.float32),
        jnp.zeros((head_count, tok_rows), jnp.float32),
        jnp.zeros((tok_rows, model_width), jnp.float32),
    )
    state = forward_block(start_state, key_low, value_low, my_place)

    def forward_step(step, carry):
        key_block, value_block, state_now = carry
        key_block, value_block = passed_along((key_block, value_block), "seq", 1)
        source = (my_place - step) % blocks_seq
        return (key_block, value_block, forward_block(state_now, key_block, value_block, source))

    _, _, state = lax.fori_loop(1, blocks_seq, forward_step, (key_low, value_low, state))
    top, total, accum = state
    log_total = top + jnp.log(total)
    attended = accum / jnp.repeat(total.T, head_size, axis=1)
    attended_low = attended.astype(jnp.bfloat16)
    middle = inputs + jnp.dot(attended_low, full_out, preferred_element_type=jnp.float32)
    normed_two, norm_two_back = jax.vjp(layer_norm, middle, gain_two, bias_two)
    normed_two_low = normed_two.astype(jnp.bfloat16)
    hidden = jnp.dot(normed_two_low, full_up, preferred_element_type=jnp.float32)
    activated, act_back = jax.vjp(smooth_act, hidden)
    activated_low = activated.astype(jnp.bfloat16)
    outputs = middle + jnp.dot(activated_low, full_down, preferred_element_type=jnp.float32)
    result = outputs.astype(jnp.bfloat16)[None]
    grad_top = cotangent[0].astype(jnp.float32)
    grad_top_low = cotangent[0]
    grad_down = jnp.einsum(
        "tf,td->fd", activated_low, grad_top_low, preferred_element_type=jnp.float32
    )
    grad_act = jnp.einsum("td,fd->tf", grad_top_low, full_down, preferred_element_type=jnp.float32)
    (grad_hidden,) = act_back(grad_act)
    grad_hidden_low = grad_hidden.astype(jnp.bfloat16)
    grad_up = jnp.einsum(
        "td,tf->df", normed_two_low, grad_hidden_low, preferred_element_type=jnp.float32
    )
    grad_normed_two = jnp.einsum(
        "tf,df->td", grad_hidden_low, full_up, preferred_element_type=jnp.float32
    )
    grad_mid_norm, grad_gain_two, grad_bias_two = norm_two_back(grad_normed_two)
    grad_middle = grad_top + grad_mid_norm
    grad_middle_low = grad_middle.astype(jnp.bfloat16)
    grad_out = jnp.einsum(
        "tc,td->cd", attended_low, grad_middle_low, preferred_element_type=jnp.float32
    )
    grad_att = jnp.einsum(
        "td,cd->tc", grad_middle_low, full_out, preferred_element_type=jnp.float32
    )
    grad_att_low = grad_att.astype(jnp.bfloat16)
    grad_att_heads = grad_att_low.reshape(tok_rows, head_count, head_size)
    offsets = jnp.sum(
        (grad_att_low.astype(jnp.float32) * attended).reshape(tok_rows, head_count, head_size),
        axis=2,
    ).T

    def backward_block(operands, source):

        def backward_work(inner):
            grad_query, grad_key, grad_value, key_now, value_now = inner
            key_heads = key_now.reshape(tok_rows, head_count, head_size)
            value_heads = value_now.reshape(tok_rows, head_count, head_size)
            probs = jnp.exp(scores_of(key_now, source) - log_total[:, :, None])
            probs_low = probs.astype(jnp.bfloat16)
            grad_value = grad_value + jnp.einsum(
                "hqk,qhd->khd", probs_low, grad_att_heads, preferred_element_type=jnp.float32
            ).reshape(tok_rows, model_width)
            grad_probs = jnp.einsum(
                "qhd,khd->hqk", grad_att_heads, value_heads, preferred_element_type=jnp.float32
            )
            grad_scores = (probs * (grad_probs - offsets[:, :, None])).astype(jnp.bfloat16)
            grad_query = (
                grad_query
                + jnp.einsum(
                    "hqk,khd->qhd", grad_scores, key_heads, preferred_element_type=jnp.float32
                ).reshape(tok_rows, model_width)
                * scale
            )
            grad_key = (
                grad_key
                + jnp.einsum(
                    "hqk,qhd->khd", grad_scores, query_heads, preferred_element_type=jnp.float32
                ).reshape(tok_rows, model_width)
                * scale
            )
            return (grad_query, grad_key, grad_value, key_now, value_now)

        def backward_keep(inner):
            return inner

        return lax.cond(source <= my_place, backward_work, backward_keep, operands)

    def backward_step(step, carry):
        source = (my_place - step) % blocks_seq
        grad_query, grad_key, grad_value, key_block, value_block = backward_block(carry, source)
        key_block, value_block = passed_along((key_block, value_block), "seq", 1)
        grad_key, grad_value = (
            shifted(grad_key.astype(jnp.bfloat16), "seq", 1).astype(grad_key.dtype),
            shifted(grad_value.astype(jnp.bfloat16), "seq", 1).astype(grad_value.dtype),
        )
        return (grad_query, grad_key, grad_value, key_block, value_block)

    zero_rows = jnp.zeros((tok_rows, model_width), jnp.float32)
    grad_query, grad_key, grad_value, _, _ = lax.fori_loop(
        0, blocks_seq, backward_step, (zero_rows, zero_rows, zero_rows, key_low, value_low)
    )
    grad_proj_low = jnp.concatenate([grad_query, grad_key, grad_value], axis=1).astype(jnp.bfloat16)
    grad_qkv = jnp.einsum(
        "tc,tk->ck", normed_low, grad_proj_low, preferred_element_type=jnp.float32
    )
    grad_normed = jnp.einsum(
        "tk,ck->tc", grad_proj_low, full_qkv, preferred_element_type=jnp.float32
    )
    grad_in_norm, grad_gain_one, grad_bias_one = norm_one_back(grad_normed)
    input_grad = (grad_middle + grad_in_norm)[None]
    part_qkv, part_out, part_up, part_down = (
        lax.psum_scatter(
            grad_qkv.astype(jnp.bfloat16), "seg", scatter_dimension=0, tiled=True
        ).astype(jnp.float32),
        lax.psum_scatter(
            grad_out.astype(jnp.bfloat16), "seg", scatter_dimension=0, tiled=True
        ).astype(jnp.float32),
        lax.psum_scatter(
            grad_up.astype(jnp.bfloat16), "seg", scatter_dimension=0, tiled=True
        ).astype(jnp.float32),
        lax.psum_scatter(
            grad_down.astype(jnp.bfloat16), "seg", scatter_dimension=0, tiled=True
        ).astype(jnp.float32),
    )
    sum_qkv, sum_out, sum_up, sum_down = (
        lax.psum_scatter(
            part_qkv.astype(jnp.bfloat16), "seq", scatter_dimension=1, tiled=True
        ).astype(jnp.float32),
        lax.psum_scatter(
            part_out.astype(jnp.bfloat16), "seq", scatter_dimension=1, tiled=True
        ).astype(jnp.float32),
        lax.psum_scatter(
            part_up.astype(jnp.bfloat16), "seq", scatter_dimension=1, tiled=True
        ).astype(jnp.float32),
        lax.psum_scatter(
            part_down.astype(jnp.bfloat16), "seq", scatter_dimension=1, tiled=True
        ).astype(jnp.float32),
    )
    sum_gain_one, sum_bias_one, sum_gain_two, sum_bias_two = lax.psum(
        (grad_gain_one, grad_bias_one, grad_gain_two, grad_bias_two), ("seq", "seg")
    )
    return (
        result,
        input_grad,
        sum_gain_one,
        sum_bias_one,
        sum_qkv,
        sum_out,
        sum_gain_two,
        sum_bias_two,
        sum_up,
        sum_down,
    )


MESH = pl.DeviceIdType.MESH
BF = jnp.bfloat16
F32 = jnp.float32
def dot_nn(a, b):
    return lax.dot_general(a, b, (((1,), (0,)), ((), ())), preferred_element_type=F32)


def dot_nt(a, b):
    return lax.dot_general(a, b, (((1,), (1,)), ((), ())), preferred_element_type=F32)


def dot_tn(a, b):
    return lax.dot_general(a, b, (((0,), (0,)), ((), ())), preferred_element_type=F32)


def remote(src, dst, send, recv, **place):
    return pltpu.make_async_remote_copy(
        src_ref=src, dst_ref=dst, send_sem=send, recv_sem=recv, device_id=place, device_id_type=MESH
    )


def norm_parts(values):
    center = values - jnp.mean(values, axis=-1, keepdims=True)
    spread = jnp.mean(center * center, axis=-1, keepdims=True)
    inverse = lax.rsqrt(spread + 1e-05)
    return center * inverse, inverse


def greet(q, s, transposed=False):
    y, c = s // 2, s % 2
    barrier = pltpu.get_barrier_semaphore()

    def signal(seq, seg):
        pl.semaphore_signal(barrier, 1, device_id={"seq": seq, "seg": seg}, device_id_type=MESH)

    for d in range(1, 8):
        for core in range(2):
            signal(lax.rem(q + d, 8), 2 * y + core)
    for d in range(1, 4):
        signal(q, lax.rem(s + d, 4))
    if transposed:
        turned = s != q // 2

        @pl.when(turned)
        def _():
            signal(2 * s + q % 2, q // 2)

        pl.semaphore_wait(barrier, jnp.where(turned, 18, 17))
    else:
        pl.semaphore_wait(barrier, 17)


def first_columns(lens, base, rows):
    place = base + lax.broadcasted_iota(jnp.int32, (rows, 1), 0)
    start = jnp.zeros((rows, 1), jnp.int32)
    bound = jnp.zeros((1, 1), jnp.int32)
    for i in range(lens.shape[0]):
        bound = bound + lens[i : i + 1, 0:1]
        start = jnp.where(place >= bound, bound, start)
    return start


def seen_mask(start, base_q, base_k, rows, columns):
    place = base_q + lax.broadcasted_iota(jnp.int32, (rows, columns), 0)
    key = base_k + lax.broadcasted_iota(jnp.int32, (rows, columns), 1)
    return (key <= place) & (key >= start)


def rows(k, n):
    return pl.ds(pl.multiple_of(k * n, n), n)


def lanes(k, n=128):
    return pl.ds(pl.multiple_of(k * n, n), n)


T = 256
HALF = 128


def places(z, x):
    zn, zc = z + 1 - 2 * (z % 2), (z + 2) % 4
    znc = (zn + 2) % 4
    here, near_z, near_x, cross = 2 * z + x, 2 * zn + x, 2 * z + 1 - x, 2 * zc + x
    blocks = (here, near_x, near_z, cross, 2 * znc + x, 2 * zc + 1 - x, 2 * zn + 1 - x, 2 * znc + 1 - x)
    return here, near_z, near_x, cross, blocks


def nth(values, k):
    out = values[0]
    for i, value in enumerate(values[1:], 1):
        out = jnp.where(k == i, value, out)
    return out


def attend_kernel(
    x_ref, lens_ref, gain_ref, bias_ref, wq_ref, wo_ref, wu_ref, g_ref,
    o_ref, wof, wuc, gall, xs, h1, wh, qkv, of, lse, lens,
    ob, wq_s, wu_v, lens_r, local_sem, qs, qr, ws, wr, xs_send, xs_recv, xu_recv, os_send, os_recv,
):
    q, s = lax.axis_index("seq"), lax.axis_index("seg")
    z, x = q // 2, q % 2
    y, c = s // 2, s % 2
    sib = s + 1 - 2 * c
    across = (1 - y) * 2 + c
    corner = (1 - y) * 2 + 1 - c
    group = z // 2
    head = 4 * (z % 2) + 2 * x + c
    twin = head + 1 - 2 * c
    home = c == group
    column = 2 * y + group
    _, near_z, near_x, cross, blocks = places(z, x)
    scale = 1.0 / math.sqrt(HEAD_DIM)

    for j in range(3):
        at = slice(j * 128, (j + 1) * 128)
        wh[rows(s, T), at] = wq_ref[:, lanes(8 * j + head)]
        wq_s[0, :, at] = wq_ref[:, lanes(8 * j + head)]
        wq_s[1, :, at] = wq_ref[:, lanes(8 * j + twin)]

    @pl.when(home)
    def _():
        xs[rows(q, T)] = x_ref[...]

    greet(q, s)

    def half_rows(b, part):
        return xs.at[pl.ds(pl.multiple_of(b * T + part * HALF, HALF), HALF)]

    def over_copy(part):
        src = x_ref.at[part * HALF : (part + 1) * HALF]
        return remote(src, half_rows(q, part), xs_send.at[24 + part], xs_recv.at[q], seq=cross, seg=2 * y + part)

    def twin_copy(part, recv, k):
        return remote(half_rows(q, part), half_rows(q, part), xs_send.at[24 + k], recv.at[q], seg=sib)

    twin_track, twin_rest = twin_copy(1 - c, xs_recv, 0), twin_copy(c, xu_recv, 1)

    @pl.when(home)
    def _():
        twin_track.start()
        twin_rest.start()

    @pl.when(jnp.logical_not(home))
    def _():
        over_copy(0).start()
        over_copy(1).start()

    mine_wh = wh.at[rows(s, T)]
    q_across = remote(wq_s.at[0], mine_wh, qs.at[0], qr.at[0], seg=across)
    q_sib = remote(wq_s.at[1], mine_wh, qs.at[1], qr.at[1], seg=sib)
    q_corner = remote(wq_s.at[1], mine_wh, qs.at[2], qr.at[2], seg=corner)
    l_sib = remote(lens_ref, lens_r, qs.at[3], qr.at[3], seg=sib)
    first = (q_across, q_corner, q_sib, l_sib)
    for copy in first:
        copy.start()

    def x_copy(b, k, recv, **to):
        src = half_rows(b, c)
        return remote(src, src, xs_send.at[k], recv.at[b], **to)

    own_z, own_x = x_copy(q, 0, xs_recv, seq=near_z), x_copy(q, 8, xs_recv, seq=near_x)

    @pl.when(jnp.logical_not(home))
    def _():
        x_copy(q, 0, xs_recv, seq=q).wait_recv()

    own_z.start()
    own_x.start()

    u_across = remote(wu_ref.at[:, lanes(across, 1024)], wuc.at[rows(s, T)], ws.at[0], wr.at[0], seg=across)
    u_corner = remote(wu_ref.at[:, lanes(corner, 1024)], wuc.at[rows(s, T)], ws.at[1], wr.at[1], seg=corner)
    u_sib = remote(wu_ref.at[:, lanes(sib, 1024)], wuc.at[rows(s, T)], ws.at[2], wr.at[2], seg=sib)
    o_across = remote(wo_ref, wof.at[rows(s, T)], ws.at[3], wr.at[3], seg=across)
    o_sib = remote(wo_ref, wof.at[rows(s, T)], ws.at[4], wr.at[4], seg=sib)
    o_pass = remote(wof.at[rows(across, T)], wof.at[rows(across, T)], ws.at[5], wr.at[5], seg=sib)
    far = lambda k, part: gall.at[pl.ds(2 * T + part * T + k * HALF, HALF)]
    g_across = tuple(
        remote(g_ref.at[k * HALF : (k + 1) * HALF], far(0, k), ws.at[6 + k], wr.at[6 + k], seg=across)
        for k in range(2)
    )
    g_sib = remote(g_ref, gall.at[T : 2 * T], ws.at[8], wr.at[8], seg=sib)
    g_pass = tuple(remote(far(0, k), far(1, k), ws.at[9 + k], wr.at[9 + k], seg=sib) for k in range(2))
    own_in = pltpu.make_async_copy(wu_ref.at[:, lanes(s, 1024)], wu_v, local_sem.at[0])
    own = (
        pltpu.make_async_copy(wo_ref, wof.at[rows(s, T)], local_sem.at[1]),
        pltpu.make_async_copy(g_ref, gall.at[0:T], local_sem.at[2]),
        pltpu.make_async_copy(wu_v, wuc.at[rows(s, T)], local_sem.at[3]),
    )
    for copy in (own_in, u_across, u_corner, o_across) + g_across:
        copy.start()
    for copy in first:
        copy.wait_recv()
    lens[...] = jnp.where(home, lens_ref[...], lens_r[...])
    own_in.wait()
    for copy in own:
        copy.start()

    gain, bias = gain_ref[...], bias_ref[...]

    def project(b):
        unit, _ = norm_parts(xs[rows(b, T)].astype(F32))
        low = (unit * gain + bias).astype(BF)
        h1[rows(b, T)] = low
        qkv[rows(b, T)] = dot_nn(low, wh[...]).astype(BF)

    def track_step(k, _):
        b = nth(blocks, k)

        @pl.when(k < 8)
        def _():
            x_copy(b, 0, xs_recv, seq=q).wait_recv()

        @pl.when((k == 1) | (k == 3))
        def _():
            x_copy(b, k, xs_recv, seq=near_z).start()

        @pl.when((k == 3) | (k == 4))
        def _():
            x_copy(b, 8 + k, xs_recv, seq=near_x).start()

        @pl.when(k < 8)
        def _():
            x_copy(b, 16 + k, xu_recv, seg=sib).start()

        last = nth(blocks, k - 1)

        @pl.when((k > 1) | jnp.logical_not(home))
        def _():
            x_copy(last, 0, xu_recv, seg=sib).wait_recv()

        project(last)

        return 0

    lax.fori_loop(1, 9, track_step, 0)
    for copy in (u_sib, o_sib, g_sib):
        copy.start()

    def o_copy(i, sender):
        return remote(
            ob.at[i], o_ref.at[:, lanes(sender)], os_send.at[i], os_recv.at[sender], seq=i, seg=column
        )

    mine = pltpu.make_async_copy(ob.at[q], o_ref.at[:, lanes(head)], os_recv.at[head])
    for i in range(8):
        n = (i + 1) * T
        start = first_columns(lens, i * T, T)
        scores = dot_nt(qkv[i * T : n, :128], qkv[:n, 128:256]) * scale
        scores = jnp.where(seen_mask(start, i * T, 0, T, n), scores, -1e30)
        top = jnp.max(scores, axis=1, keepdims=True)
        weights = jnp.exp(scores - top)
        total = jnp.sum(weights, axis=1, keepdims=True)
        mixed = dot_nn(weights.astype(BF), qkv[:n, 256:384]) / total
        of[i * T : n] = mixed
        lse[i * T : n] = top + jnp.log(total)
        ob[i] = mixed.astype(BF)
        here = (q == i) & home

        @pl.when(jnp.logical_not(here))
        def _():
            o_copy(i, head).start()

        @pl.when(here)
        def _():
            mine.start()

    o_across.wait_recv()
    o_pass.start()
    for arrived, copy in zip(g_across, g_pass):
        arrived.wait_recv()
        copy.start()

    for k in range(8):
        if k in (0, 1, 3):
            x_copy(blocks[k], k, xs_recv, seq=near_z).wait_send()
        if k in (0, 3, 4):
            x_copy(blocks[k], 8 + k, xs_recv, seq=near_x).wait_send()
        if k:
            x_copy(blocks[k], 16 + k, xu_recv, seg=sib).wait_send()

    @pl.when(home)
    def _():
        twin_track.wait_send()
        twin_rest.wait_send()

    @pl.when(jnp.logical_not(home))
    def _():
        over_copy(0).wait_send()
        over_copy(1).wait_send()

    for i in range(8):
        @pl.when(jnp.logical_not((q == i) & home))
        def _():
            o_copy(i, head).wait_send()

        o_copy(i, i).wait_recv()

    for copy in own:
        copy.wait()
    for copy in first + (u_across, u_corner, u_sib, o_across, o_sib, o_pass, g_sib) + g_across + g_pass:
        copy.wait_send()
    for copy in (u_across, u_corner, u_sib, o_sib, o_pass, g_sib) + g_pass:
        copy.wait_recv()


VM = pl.BlockSpec(memory_space=pltpu.VMEM)
HB = pl.BlockSpec(memory_space=pl.ANY)
S = jax.ShapeDtypeStruct


def attend(x, lens, gain, bias, wq, wo, wu, g):
    dma = pltpu.SemaphoreType.DMA
    return pl.pallas_call(
        attend_kernel,
        out_shape=(
            S((256, 1024), BF), S((1024, 1024), BF), S((1024, 1024), BF), S((1024, 1024), BF),
            S((2048, 1024), BF), S((2048, 1024), BF), S((1024, 384), BF), S((2048, 384), BF),
            S((2048, 128), F32), S((2048, 1), F32), S((8, 128), jnp.int32),
        ),
        in_specs=[VM, VM, VM, VM, VM, VM, HB, VM],
        out_specs=(VM, HB, HB, HB, VM, VM, VM, VM, VM, VM, VM),
        scratch_shapes=[
            pltpu.VMEM((8, 256, 128), BF), pltpu.VMEM((2, 256, 384), BF), pltpu.VMEM((256, 1024), BF),
            pltpu.VMEM((8, 128), jnp.int32), dma((4,)), dma((4,)), dma((4,)), dma((11,)), dma((11,)),
            dma((26,)), dma((8,)), dma((8,)), dma((8,)), dma((8,)),
        ],
        compiler_params=pltpu.CompilerParams(
            collective_id=0, has_side_effects=True, vmem_limit_bytes=58 * 2**20
        ),
        cost_estimate=pl.CostEstimate(flops=5 * 10**9, bytes_accessed=40 * 2**20, transcendentals=2 * 2**20),
        name="attend",
    )(x, lens, gain, bias, wq, wo, wu, g)


def gelu_parts(u):
    root = math.sqrt(2.0 / math.pi)
    square = u * u
    t = jnp.tanh(root * (u + 0.044715 * (square * u)))
    value = 0.5 * u * (1.0 + t)
    slope = 0.5 * (1.0 + t) + 0.5 * u * (1.0 - t * t) * (root * (1.0 + 0.134145 * square))
    return value, slope


def norm_back(grad, gain, unit, inverse):
    through = grad * gain
    a = jnp.mean(through, axis=-1, keepdims=True)
    b = jnp.mean(through * unit, axis=-1, keepdims=True)
    return inverse * (through - a - unit * b)


def layer_kernel(
    x_ref, o_ref, wo_ref, gain2_ref, bias2_ref, gain1_ref, lens_ref, lse_ref,
    g_hbm, wu_hbm, wd_hbm, qkv_hbm, of_hbm, wh_hbm, xs_hbm, h1_hbm,
    result_out, dx_out, gqkv_out, gout_out, gup_out, gdown_out, sums_out,
    g_v, wu_v, wd_v, qkv_v, of_v, wh_v, load_sem,
    middle, h2, big, mine, near_s, near_r, twin_s, twin_r, far_keep, far_s, far_r, dx_v, do_v,
    hs, hr, ns, nr, ts, tr, fs, fr,
    pack, x_r, z_r, up_s, up_r, gxs, gxr, gzs, gzr, ups, upr,
    outp, oc_r, oy_r, ox_r, oz_r, oo_r, cs, cr,
    doh, dq, dk, dv, dos, dor,
    dhc_r, step_r, fin_s, fin_r, dcs, dcr, sts, str_, fns, fnr,
    gq, gq_b, gq_y, gq_r, qs, qr,
    vec, vec_r, vs, vr,
):
    q, s = lax.axis_index("seq"), lax.axis_index("seg")
    z, x = q // 2, q % 2
    y, c = s // 2, s % 2
    sib = s + 1 - 2 * c
    across = (1 - y) * 2 + c
    group = z // 2
    head = 4 * (z % 2) + 2 * x + c
    home = c == group
    away = jnp.logical_not(home)
    column = 2 * y + group
    here, near_z, near_x, cross, blocks = places(z, x)
    scale = 1.0 / math.sqrt(HEAD_DIM)

    loads = tuple(
        pltpu.make_async_copy(src, dst, load_sem.at[k])
        for k, (src, dst) in enumerate(
            ((wu_hbm, wu_v), (wd_hbm, wd_v), (g_hbm, g_v), (qkv_hbm, qkv_v), (of_hbm, of_v), (wh_hbm, wh_v))
        )
    )
    for copy in loads:
        copy.start()
    greet(q, s, True)

    value = x_ref[...].astype(F32) + dot_nn(o_ref[...], wo_ref[...])
    middle[...] = value
    unit, _ = norm_parts(value)
    h2[0:T] = (unit * gain2_ref[...] + bias2_ref[...]).astype(BF)

    def far_rows(ref, part, k):
        return ref.at[pl.ds(2 * T + k * T + part * HALF, HALF)]

    h_far = tuple(
        remote(h2.at[k * HALF : (k + 1) * HALF], far_rows(h2, 0, k), hs.at[k], hr.at[k], seg=across)
        for k in range(2)
    )
    h_pass = tuple(
        remote(far_rows(h2, 0, k), far_rows(h2, 1, k), hs.at[2 + k], hr.at[2 + k], seg=sib) for k in range(2)
    )
    h_sib = remote(h2.at[0:T], h2.at[T : 2 * T], hs.at[4], hr.at[4], seg=sib)
    for copy in h_far + (h_sib,):
        copy.start()
    for copy in loads[:3]:
        copy.wait()

    def work(part):
        at = slice(part * T, (part + 1) * T)
        value, slope = gelu_parts(dot_nn(h2[at], wu_v[...]))
        low = value.astype(BF)
        big[at] = low
        du = (slope * dot_nt(g_v[at], wd_v[...])).astype(BF)
        big[4 * T + part * T : 4 * T + (part + 1) * T] = du
        return dot_nt(du, wu_v[...]), dot_nn(low, wd_v[...])

    near = tuple(remote(near_s.at[k], near_r.at[k], ns.at[k], nr.at[k], seg=sib) for k in range(2))
    twin = tuple(
        tuple(remote(twin_s.at[k, n], twin_r.at[k, n], ts.at[2 * k + n], tr.at[2 * k + n], seg=sib) for n in range(2))
        for k in range(2)
    )
    far = tuple(
        tuple(remote(far_s.at[k, n], far_r.at[k, n], fs.at[2 * k + n], fr.at[2 * k + n], seg=across) for n in range(2))
        for k in range(2)
    )

    def send_twin(n, parts):
        for k in range(2):
            far_keep[k] = parts[k][:HALF]
            twin_s[k, n] = parts[k][HALF:].astype(BF)
            twin[k][n].start()

    def send_far(n):
        for k in range(2):
            twin[k][n].wait_recv()
            far_s[k, n] = (far_keep[k] + twin_r[k, n].astype(F32)).astype(BF)
            if k == 0:
                far[k][n].start()

    parts = work(0)
    for k in range(2):
        mine[k] = parts[k]
    h_sib.wait_recv()
    parts = work(1)
    for k in range(2):
        near_s[k] = parts[k].astype(BF)
        near[k].start()
    h_far[0].wait_recv()
    h_pass[0].start()
    h_pass[0].wait_recv()
    send_twin(0, work(2))
    h_far[1].wait_recv()
    h_pass[1].start()
    send_far(0)
    h_pass[1].wait_recv()
    send_twin(1, work(3))
    send_far(1)

    for j in range(4):
        down = dot_tn(big[: 4 * T, j * T : (j + 1) * T], g_v[...]).astype(BF)
        for k in range(8):
            pack[k, :, 512 + j * 128 : 640 + j * 128] = down[:, k * 128 : (k + 1) * 128]
    for j in range(4):
        up = dot_tn(h2[:, j * T : (j + 1) * T], big[4 * T :]).astype(BF)
        for k in range(2):
            pack[2 * j + k, :, :512] = up[:, k * 512 : (k + 1) * 512]

    def gx_copy(d):
        return remote(pack.at[2 * d + 1 - x], x_r.at[d], gxs.at[d], gxr.at[d], seq=near_x)

    zn, zc = z + 1 - 2 * (z % 2), (z + 2) % 4
    znc = (zn + 2) % 4
    gx_copy(znc).start()
    gx_copy(zc).start()

    near[0].wait_recv()
    far[0][0].wait_recv()
    far[0][1].wait_recv()
    grad = mine[0] + near_r[0].astype(F32) + jnp.concatenate([far_r[0, 0], far_r[0, 1]], axis=0).astype(F32)
    unit, inverse = norm_parts(middle[...])
    vec[...] = jnp.zeros_like(vec)
    vec[2:3] = jnp.sum(grad * unit, axis=0, keepdims=True)
    vec[3:4] = jnp.sum(grad, axis=0, keepdims=True)
    dx = g_v[0:T].astype(F32) + norm_back(grad, gain2_ref[...], unit, inverse)
    dx_v[...] = dx
    dy = dx.astype(BF)
    do_v[...] = dot_nt(dy, wo_ref[...]).astype(BF)

    def do_copy(h, block):
        return remote(
            do_v.at[:, h * 128 : (h + 1) * 128], doh.at[rows(block, T)], dos.at[h], dor.at[block],
            seq=2 * (2 * c + h // 4) + (h // 2) % 2, seg=2 * y + h % 2,
        )

    do_mine = pltpu.make_async_copy(do_v.at[:, lanes(head)], doh.at[rows(q, T)], dor.at[q])
    for h in range(8):
        self_too = (head == h) & home

        @pl.when(jnp.logical_not(self_too))
        def _():
            do_copy(h, q).start()

        @pl.when(self_too)
        def _():
            do_mine.start()

    out = dot_tn(o_ref[...], dy).astype(BF)
    for quarter in range(4):
        for k in range(8):
            outp[quarter // 2, quarter % 2, k // 4, (k // 2) % 2, k % 2] = out[quarter * T : (quarter + 1) * T, k * 128 : (k + 1) * 128]
    out_core = remote(outp.at[:, 1 - c], oc_r, cs.at[0], cr.at[0], seg=sib)
    out_core.start()
    out_core.wait_recv()
    for part in range(2):
        oc_r[part] = (oc_r[part].astype(F32) + outp[part, c].astype(F32)).astype(BF)
    out_y = remote(oc_r.at[1 - y], oy_r, cs.at[1], cr.at[1], seg=across)
    out_y.start()
    far[1][0].start()
    far[1][1].start()

    def come(into, recv, slot):
        return remote(into.at[slot], into.at[slot], recv.at[slot], recv.at[slot], seq=near_x)

    def gz_copy(k, d, to):
        return remote(x_r.at[d], z_r.at[k], gzs.at[k], gzr.at[k], seq=to)

    gz = (gz_copy(0, znc, near_z), gz_copy(1, zn, near_z), gz_copy(2, zc, cross))

    def pack_sum(d):
        gx_copy(d).wait_recv()
        return pack[2 * d + x].astype(F32) + x_r[d].astype(F32)

    x_r[znc] = pack_sum(znc).astype(BF)
    gz[0].start()
    for copy in loads[3:]:
        copy.wait()
    for b in range(8):
        do_copy(0, b).wait_recv()


    gx_copy(zn).start()

    dk[...] = jnp.zeros_like(dk)
    dv[...] = jnp.zeros_like(dv)
    lens = lens_ref[...]
    for i in range(8):
        top = i * T
        start = first_columns(lens, top, T)
        query = qkv_v[top : top + T, :128]
        grad = doh[top : top + T]
        delta = jnp.sum(grad.astype(F32) * of_v[top : top + T], axis=1, keepdims=True)
        log_total = lse_ref[top : top + T]
        total = jnp.zeros((T, 128), F32)
        for base in range(0, top + T, 1024):
            n = min(1024, top + T - base)
            keys = qkv_v[base : base + n, 128:256]
            probs = jnp.exp(dot_nt(query, keys) * scale - log_total)
            probs = jnp.where(seen_mask(start, top, base, T, n), probs, 0.0)
            dp = dot_nt(grad, qkv_v[base : base + n, 256:384])
            ds = (probs * (dp - delta)).astype(BF)
            dv[base : base + n] += dot_tn(probs.astype(BF), grad)
            dk[base : base + n] += dot_tn(ds, query)
            total += dot_nn(ds, keys)
        dq[top : top + T] = total

    gz[0].wait_recv()
    x_r[zc] = (pack_sum(zc) + z_r[0].astype(F32)).astype(BF)
    gz[2].start()

    gq[...] = jnp.zeros_like(gq)
    own_a, other_xa, other_za, own_b, other_zb, other_xb, diag_a, diag_b = blocks
    order = (diag_a, diag_b, other_za, other_xb, other_xa, other_zb, own_a, own_b)

    def x_load(i):
        return pltpu.make_async_copy(xs_hbm.at[rows(nth(order, i), T)], wu_v.at[rows(i % 2, T)], load_sem.at[6 + i % 2])

    def h_load(i):
        return pltpu.make_async_copy(h1_hbm.at[rows(nth(order, i), T)], wu_v.at[rows(2 + i % 2, T)], load_sem.at[8 + i % 2])

    def dhc_copy(b):
        return remote(
            big.at[pl.ds(pl.multiple_of(b * T + (1 - c) * HALF, HALF), HALF)], dhc_r.at[b], dcs.at[b], dcr.at[b], seg=sib
        )

    def half(b):
        return big.at[pl.ds(pl.multiple_of(b * T + c * HALF, HALF), HALF)]

    def step_copy(k, b, to):
        return remote(half(b), step_r.at[k], sts.at[k], str_.at[k], seq=to)

    steps = (
        step_copy(0, diag_a, near_z), step_copy(1, diag_b, near_x), step_copy(2, other_za, near_z),
        step_copy(3, other_xb, near_x), step_copy(4, other_xa, near_x), step_copy(5, other_zb, near_z),
    )
    x_load(0).start()
    h_load(0).start()

    def block_step(i, _):
        @pl.when(i < 8)
        def _():
            b = nth(order, i)

            @pl.when(i < 7)
            def _():
                x_load(i + 1).start()
                h_load(i + 1).start()

            at = rows(b, T)
            low = jnp.concatenate([dq[at] * scale, dk[at] * scale, dv[at]], axis=1).astype(BF)
            dh = dot_nt(low, wh_v[...])
            big[at] = dh.astype(BF)
            dhc_copy(b).start()
            x_load(i).wait()
            h_load(i).wait()
            gq[...] += dot_tn(wu_v[rows(2 + i % 2, T)], low)
            unit, _ = norm_parts(wu_v[rows(i % 2, T)].astype(F32))
            vec[0:1] += jnp.sum(dh * unit, axis=0, keepdims=True)
            vec[1:2] += jnp.sum(dh, axis=0, keepdims=True)

        @pl.when(i > 0)
        def _():
            b = nth(order, i - 1)
            dhc_copy(b).wait_recv()
            place = half(b)
            place[...] = (place[...].astype(F32) + dhc_r[b].astype(F32)).astype(BF)
            for k in range(4):
                @pl.when(i == k + 1)
                def _():
                    steps[k].start()

        return 0

    lax.fori_loop(0, 9, block_step, 0)
    for k, b in ((5, other_zb), (4, other_xa)):
        steps[k - 4].wait_recv()
        place = half(b)
        place[...] = (place[...].astype(F32) + step_r[k - 4].astype(F32)).astype(BF)
        steps[k].start()

    x_r[zn] = pack_sum(zn).astype(BF)
    gz[1].start()

    out_y.wait_recv()
    oc_r[y] = (oc_r[y].astype(F32) + oy_r[...].astype(F32)).astype(BF)
    out_x = remote(oc_r.at[y, :, :, 1 - x], ox_r, cs.at[2], cr.at[2], seq=near_x)
    out_x.start()
    gx_copy(z).start()

    gq_b[...] = gq[...].astype(BF).reshape(2, 2, T, 384)
    q_y = remote(gq_b.at[1 - y], gq_y, qs.at[0], qr.at[0], seg=across)
    q_y.start()
    v_core = remote(vec, vec_r.at[0], vs.at[8], vr.at[8], seg=sib)
    v_core.start()
    v_core.wait()
    vec[...] += vec_r[0]
    v_y = remote(vec, vec_r.at[1], vs.at[9], vr.at[9], seg=across)
    v_y.start()
    for k, b, pair in ((0, own_a, (2, 4)), (1, own_b, (3, 5))):
        for n in pair:
            steps[n].wait_recv()
        fin_s[k] = (
            half(b)[...].astype(F32) + step_r[pair[0]].astype(F32) + step_r[pair[1]].astype(F32)
        ).astype(BF)
    fin_over = remote(fin_s.at[1], fin_r.at[c], fns.at[0], fnr.at[c], seq=cross, seg=column)
    fin_twin = remote(fin_s.at[0], fin_r.at[c], fns.at[1], fnr.at[c], seg=sib)
    fin_own = pltpu.make_async_copy(fin_s.at[0], fin_r.at[c], fnr.at[c])
    fin_over.start()

    @pl.when(away)
    def _():
        fin_twin.start()

    @pl.when(home)
    def _():
        fin_own.start()

    v_y.wait()
    vec[...] += vec_r[1]

    def v_copy(b, sender):
        return remote(vec, vec_r.at[2 + sender], vs.at[b], vr.at[sender], seq=b)

    for b in range(8):
        @pl.when(q != b)
        def _():
            v_copy(b, q).start()

    q_y.wait_recv()
    gq_y[...] = (gq_y[...].astype(F32) + gq_b[y].astype(F32)).astype(BF)

    def column_copy(part, j):
        place = 8 * j + head
        owner, slot = place // 3, place % 3
        src = gq_y.at[part, :, j * 128 : (j + 1) * 128]
        copy = remote(
            src, gq_r.at[slot, group], qs.at[1 + 3 * part + j], qr.at[1 + 2 * slot + group],
            seq=owner, seg=2 * y + part,
        )
        local = pltpu.make_async_copy(src, gq_r.at[slot, group], qr.at[1 + 2 * slot + group])
        return (owner == q) & (c == part), copy, local

    columns = tuple(column_copy(part, j) for part in range(2) for j in range(3))
    out_x.wait_recv()
    ox_r[...] = (ox_r[...].astype(F32) + oc_r[y, :, :, x].astype(F32)).astype(BF)
    out_z = remote(ox_r.at[:, 1 - z % 2], oz_r, cs.at[3], cr.at[3], seq=near_z)
    out_z.start()
    for self_too, copy, local in columns:
        @pl.when(jnp.logical_not(self_too))
        def _():
            copy.start()

        @pl.when(self_too)
        def _():
            local.start()

    out_z.wait_recv()
    oz_r[...] = (oz_r[...].astype(F32) + ox_r[:, z % 2].astype(F32)).astype(BF)
    out_o = remote(oz_r.at[1 - group], oo_r, cs.at[4], cr.at[4], seq=cross)
    out_o.start()

    total = pack_sum(z)
    for k in (1, 2):
        gz[k].wait_recv()
        total = total + z_r[k].astype(F32)
    up_s[...] = total[:, :512].astype(BF)
    turned = s != z
    up_turn = remote(up_s, up_r, ups, upr, seq=2 * s + x, seg=z)
    up_own = pltpu.make_async_copy(up_s, up_r, upr)

    @pl.when(turned)
    def _():
        up_turn.start()

    @pl.when(jnp.logical_not(turned))
    def _():
        up_own.start()

    for j in range(4):
        gdown_out[j * T : (j + 1) * T] = total[:, 512 + j * 128 : 640 + j * 128]
    vec_r[2 + q] = vec[...]
    for b in range(8):
        @pl.when(q != b)
        def _():
            v_copy(b, b).wait_recv()

    vec_sum = vec_r[2]
    for b in range(1, 8):
        vec_sum = vec_sum + vec_r[2 + b]
    out_o.wait_recv()
    gout_out[...] = oz_r[group].astype(F32) + oo_r[...].astype(F32)
    sums_out[...] = vec_sum[:4]
    for slot in range(3):
        for part in range(2):
            pltpu.make_async_copy(gq_r.at[slot, part], gq_r.at[slot, part], qr.at[1 + 2 * slot + part]).wait()
        gqkv_out[:, slot * 128 : (slot + 1) * 128] = gq_r[slot, 0].astype(F32) + gq_r[slot, 1].astype(F32)
    near[1].wait_recv()
    far[1][0].wait_recv()
    far[1][1].wait_recv()
    result_out[...] = (
        middle[...] + mine[1] + near_r[1].astype(F32)
        + jnp.concatenate([far_r[1, 0], far_r[1, 1]], axis=0).astype(F32)
    ).astype(BF)
    unit, inverse = norm_parts(x_ref[...].astype(F32))
    for k in range(2):
        come(fin_r, fnr, k).wait_recv()
    dh = jnp.concatenate([fin_r[0], fin_r[1]], axis=0).astype(F32)
    dx_out[...] = dx_v[...] + norm_back(dh, gain1_ref[...], unit, inverse)
    up_own.wait()
    gup_out[...] = up_r[...].astype(F32)

    for h in range(8):
        @pl.when(jnp.logical_not((head == h) & home))
        def _():
            do_copy(h, q).wait_send()

    for b in range(8):
        dhc_copy(b).wait_send()

        @pl.when(q != b)
        def _():
            v_copy(b, q).wait_send()

    for d in range(4):
        gx_copy(d).wait_send()
    for copy in (out_core, out_y, out_x, out_z, out_o, q_y, h_sib, fin_over) + h_far + h_pass + near + steps + gz:
        copy.wait_send()
    for k in range(2):
        for n in range(2):
            twin[k][n].wait_send()
            far[k][n].wait_send()

    @pl.when(away)
    def _():
        fin_twin.wait_send()

    @pl.when(turned)
    def _():
        up_turn.wait_send()

    for self_too, copy, _ in columns:
        @pl.when(jnp.logical_not(self_too))
        def _():
            copy.wait_send()


def layer(x, o, wo, gain2, bias2, gain1, lens, lse, g, wu, wd, qkv, of, wh, xs, h1):
    dma = pltpu.SemaphoreType.DMA
    low = lambda *shape: pltpu.VMEM(shape, BF)
    wide = lambda *shape: pltpu.VMEM(shape, F32)
    return pl.pallas_call(
        layer_kernel,
        out_shape=(
            S((256, 1024), BF), S((256, 1024), F32), S((256, 384), F32), S((256, 128), F32), S((256, 512), F32),
            S((1024, 128), F32), S((4, 1024), F32),
        ),
        in_specs=[VM] * 8 + [HB] * 8,
        out_specs=(VM,) * 7,
        scratch_shapes=[
            low(1024, 1024), low(1024, 1024), low(1024, 1024), low(2048, 384), wide(2048, 128), low(1024, 384),
            dma((10,)),
            wide(256, 1024), low(1024, 1024), low(2048, 1024), wide(2, 256, 1024),
            low(2, 256, 1024), low(2, 256, 1024), low(2, 2, 128, 1024), low(2, 2, 128, 1024), wide(2, 128, 1024),
            low(2, 2, 128, 1024), low(2, 2, 128, 1024), wide(256, 1024), low(256, 1024),
            dma((5,)), dma((5,)), dma((2,)), dma((2,)), dma((4,)), dma((4,)), dma((4,)), dma((4,)),
            low(8, 256, 1024), low(4, 256, 1024), low(3, 256, 1024), low(256, 512), low(256, 512),
            dma((4,)), dma((4,)), dma((3,)), dma((3,)), dma, dma,
            low(2, 2, 2, 2, 2, 256, 128), low(2, 2, 2, 2, 256, 128), low(2, 2, 2, 256, 128), low(2, 2, 256, 128),
            low(2, 256, 128), low(256, 128), dma((5,)), dma((5,)),
            low(2048, 128), wide(2048, 128), wide(2048, 128), wide(2048, 128), dma((8,)), dma((8,)),
            low(8, 128, 1024), low(6, 128, 1024), low(2, 128, 1024), low(2, 128, 1024),
            dma((8,)), dma((8,)), dma((6,)), dma((6,)), dma((2,)), dma((2,)),
            wide(1024, 384), low(2, 2, 256, 384), low(2, 256, 384), low(3, 2, 256, 128),
            dma((7,)), dma((7,)),
            wide(8, 1024), wide(10, 8, 1024), dma((10,)), dma((10,)),
        ],
        compiler_params=pltpu.CompilerParams(
            collective_id=1, has_side_effects=True, vmem_limit_bytes=63 * 2**20
        ),
        cost_estimate=pl.CostEstimate(flops=2 * 10**10, bytes_accessed=40 * 2**20, transcendentals=2 * 2**20),
        name="layer",
    )(x, o, wo, gain2, bias2, gain1, lens, lse, g, wu, wd, qkv, of, wh, xs, h1)


def per_device_fast(
    tokens, article_lengths, gain_one, bias_one, w_qkv, w_out, gain_two, bias_two, w_up, w_down, cotangent
):
    x = tokens[0]
    lens = jnp.broadcast_to(article_lengths[0][:, None], (article_lengths.shape[1], 128))
    o, wo, wu, g, xs, h1, wh, qkv, of, lse, lens = attend(
        x, lens, gain_one[None], bias_one[None], w_qkv, w_out, w_up, cotangent[0]
    )
    result, dx, gqkv, gout, gup, gdown, sums = layer(
        x, o, wo, gain_two[None], bias_two[None], gain_one[None], lens, lse, g, wu, w_down, qkv, of, wh, xs, h1
    )
    return (result[None], dx[None], sums[0], sums[1], gqkv, gout, sums[2], sums[3], gup, gdown)


def solution(mesh):
    one_pair = mesh.shape["seq"] == HEADS and mesh.shape["seg"] == 4
    return jax.shard_map(
        per_device_fast if one_pair else per_device,
        mesh=mesh,
        in_specs=(
            P("seg", "seq", None),
            P("seg", None),
            P(),
            P(),
            P("seg", None),
            P("seg", None),
            P(),
            P(),
            P("seg", None),
            P("seg", None),
            P("seg", "seq", None),
        ),
        out_specs=(
            P("seg", "seq", None),
            P("seg", "seq", None),
            P(),
            P(),
            P("seg", "seq"),
            P("seg", "seq"),
            P(),
            P(),
            P("seg", "seq"),
            P("seg", "seq"),
        ),
        check_vma=False,
    )
```

```python
import math

import jax
import jax.numpy as jnp
from jax import lax
from jax.experimental import pallas as pl
from jax.experimental.pallas import tpu as pltpu
from jax.sharding import PartitionSpec as P

HEADS = 8
HEAD_DIM = 128


def passed_along(block, axis, distance):
    devices = range(lax.axis_size(axis))
    route = [(i - distance, i) for i in devices if i - distance in devices]
    return lax.ppermute(block, axis, route)


def shifted(value, axis, by):
    size = lax.axis_size(axis)
    return lax.ppermute(value, axis, [(i, (i + by) % size) for i in range(size)])


def layer_norm(values, gain, bias):
    center = values - jnp.mean(values, axis=-1, keepdims=True)
    spread = jnp.mean(center * center, axis=-1, keepdims=True)
    return center * lax.rsqrt(spread + 1e-05) * gain + bias


def smooth_act(values):
    return jax.nn.gelu(values, approximate=True)


def article_numbers(lengths_row, positions):
    bounds = jnp.cumsum(lengths_row)
    return jnp.sum((positions[:, None] >= bounds[None, :]).astype(jnp.int32), axis=1)


def per_device(
    tokens,
    article_lengths,
    gain_one,
    bias_one,
    w_qkv,
    w_out,
    gain_two,
    bias_two,
    w_up,
    w_down,
    cotangent,
):
    tok_rows = tokens.shape[1]
    model_width = tokens.shape[2]
    head_count = HEADS
    head_size = HEAD_DIM
    scale = 1.0 / math.sqrt(head_size)
    blocks_seq = lax.axis_size("seq")
    my_place = lax.axis_index("seq")
    full_qkv, full_out, full_up, full_down = (
        lax.all_gather(w_qkv, "seg", axis=0, tiled=True),
        lax.all_gather(w_out, "seg", axis=0, tiled=True),
        lax.all_gather(w_up, "seg", axis=0, tiled=True),
        lax.all_gather(w_down, "seg", axis=0, tiled=True),
    )
    inputs = tokens[0].astype(jnp.float32)
    normed, norm_one_back = jax.vjp(layer_norm, inputs, gain_one, bias_one)
    normed_low = normed.astype(jnp.bfloat16)
    projected = jnp.dot(normed_low, full_qkv, preferred_element_type=jnp.float32).astype(
        jnp.bfloat16
    )
    query_low = projected[:, :model_width]
    key_low = projected[:, model_width : 2 * model_width]
    value_low = projected[:, 2 * model_width :]
    query_heads = query_low.reshape(tok_rows, head_count, head_size)
    lengths_row = article_lengths[0]
    positions = my_place * tok_rows + jnp.arange(tok_rows, dtype=jnp.int32)
    query_art = article_numbers(lengths_row, positions)

    def scores_of(key_block, source):
        key_pos = source * tok_rows + jnp.arange(tok_rows, dtype=jnp.int32)
        key_art = article_numbers(lengths_row, key_pos)
        allowed = (key_pos[None, :] <= positions[:, None]) & (
            key_art[None, :] == query_art[:, None]
        )
        raw = (
            jnp.einsum(
                "qhd,khd->hqk",
                query_heads,
                key_block.reshape(tok_rows, head_count, head_size),
                preferred_element_type=jnp.float32,
            )
            * scale
        )
        return jnp.where(allowed[None], raw, -1e30)

    def forward_block(state, key_block, value_block, source):

        def forward_work(operands):
            (top, total, accum), key_now, value_now = operands
            scores = scores_of(key_now, source)
            new_top = jnp.maximum(top, jnp.max(scores, axis=2))
            factor = jnp.exp(top - new_top)
            weights = jnp.exp(scores - new_top[:, :, None])
            total = total * factor + jnp.sum(weights, axis=2)
            gathered = jnp.einsum(
                "hqk,khd->qhd",
                weights.astype(jnp.bfloat16),
                value_now.reshape(tok_rows, head_count, head_size),
                preferred_element_type=jnp.float32,
            ).reshape(tok_rows, model_width)
            accum = accum * jnp.repeat(factor.T, head_size, axis=1) + gathered
            return (new_top, total, accum)

        def forward_keep(operands):
            return operands[0]

        return lax.cond(
            source <= my_place, forward_work, forward_keep, (state, key_block, value_block)
        )

    start_state = (
        jnp.full((head_count, tok_rows), -1e30, jnp.float32),
        jnp.zeros((head_count, tok_rows), jnp.float32),
        jnp.zeros((tok_rows, model_width), jnp.float32),
    )
    state = forward_block(start_state, key_low, value_low, my_place)

    def forward_step(step, carry):
        key_block, value_block, state_now = carry
        key_block, value_block = passed_along((key_block, value_block), "seq", 1)
        source = (my_place - step) % blocks_seq
        return (key_block, value_block, forward_block(state_now, key_block, value_block, source))

    _, _, state = lax.fori_loop(1, blocks_seq, forward_step, (key_low, value_low, state))
    top, total, accum = state
    log_total = top + jnp.log(total)
    attended = accum / jnp.repeat(total.T, head_size, axis=1)
    attended_low = attended.astype(jnp.bfloat16)
    middle = inputs + jnp.dot(attended_low, full_out, preferred_element_type=jnp.float32)
    normed_two, norm_two_back = jax.vjp(layer_norm, middle, gain_two, bias_two)
    normed_two_low = normed_two.astype(jnp.bfloat16)
    hidden = jnp.dot(normed_two_low, full_up, preferred_element_type=jnp.float32)
    activated, act_back = jax.vjp(smooth_act, hidden)
    activated_low = activated.astype(jnp.bfloat16)
    outputs = middle + jnp.dot(activated_low, full_down, preferred_element_type=jnp.float32)
    result = outputs.astype(jnp.bfloat16)[None]
    grad_top = cotangent[0].astype(jnp.float32)
    grad_top_low = cotangent[0]
    grad_down = jnp.einsum(
        "tf,td->fd", activated_low, grad_top_low, preferred_element_type=jnp.float32
    )
    grad_act = jnp.einsum("td,fd->tf", grad_top_low, full_down, preferred_element_type=jnp.float32)
    (grad_hidden,) = act_back(grad_act)
    grad_hidden_low = grad_hidden.astype(jnp.bfloat16)
    grad_up = jnp.einsum(
        "td,tf->df", normed_two_low, grad_hidden_low, preferred_element_type=jnp.float32
    )
    grad_normed_two = jnp.einsum(
        "tf,df->td", grad_hidden_low, full_up, preferred_element_type=jnp.float32
    )
    grad_mid_norm, grad_gain_two, grad_bias_two = norm_two_back(grad_normed_two)
    grad_middle = grad_top + grad_mid_norm
    grad_middle_low = grad_middle.astype(jnp.bfloat16)
    grad_out = jnp.einsum(
        "tc,td->cd", attended_low, grad_middle_low, preferred_element_type=jnp.float32
    )
    grad_att = jnp.einsum(
        "td,cd->tc", grad_middle_low, full_out, preferred_element_type=jnp.float32
    )
    grad_att_low = grad_att.astype(jnp.bfloat16)
    grad_att_heads = grad_att_low.reshape(tok_rows, head_count, head_size)
    offsets = jnp.sum(
        (grad_att_low.astype(jnp.float32) * attended).reshape(tok_rows, head_count, head_size),
        axis=2,
    ).T

    def backward_block(operands, source):

        def backward_work(inner):
            grad_query, grad_key, grad_value, key_now, value_now = inner
            key_heads = key_now.reshape(tok_rows, head_count, head_size)
            value_heads = value_now.reshape(tok_rows, head_count, head_size)
            probs = jnp.exp(scores_of(key_now, source) - log_total[:, :, None])
            probs_low = probs.astype(jnp.bfloat16)
            grad_value = grad_value + jnp.einsum(
                "hqk,qhd->khd", probs_low, grad_att_heads, preferred_element_type=jnp.float32
            ).reshape(tok_rows, model_width)
            grad_probs = jnp.einsum(
                "qhd,khd->hqk", grad_att_heads, value_heads, preferred_element_type=jnp.float32
            )
            grad_scores = (probs * (grad_probs - offsets[:, :, None])).astype(jnp.bfloat16)
            grad_query = (
                grad_query
                + jnp.einsum(
                    "hqk,khd->qhd", grad_scores, key_heads, preferred_element_type=jnp.float32
                ).reshape(tok_rows, model_width)
                * scale
            )
            grad_key = (
                grad_key
                + jnp.einsum(
                    "hqk,qhd->khd", grad_scores, query_heads, preferred_element_type=jnp.float32
                ).reshape(tok_rows, model_width)
                * scale
            )
            return (grad_query, grad_key, grad_value, key_now, value_now)

        def backward_keep(inner):
            return inner

        return lax.cond(source <= my_place, backward_work, backward_keep, operands)

    def backward_step(step, carry):
        source = (my_place - step) % blocks_seq
        grad_query, grad_key, grad_value, key_block, value_block = backward_block(carry, source)
        key_block, value_block = passed_along((key_block, value_block), "seq", 1)
        grad_key, grad_value = (
            shifted(grad_key.astype(jnp.bfloat16), "seq", 1).astype(grad_key.dtype),
            shifted(grad_value.astype(jnp.bfloat16), "seq", 1).astype(grad_value.dtype),
        )
        return (grad_query, grad_key, grad_value, key_block, value_block)

    zero_rows = jnp.zeros((tok_rows, model_width), jnp.float32)
    grad_query, grad_key, grad_value, _, _ = lax.fori_loop(
        0, blocks_seq, backward_step, (zero_rows, zero_rows, zero_rows, key_low, value_low)
    )
    grad_proj_low = jnp.concatenate([grad_query, grad_key, grad_value], axis=1).astype(jnp.bfloat16)
    grad_qkv = jnp.einsum(
        "tc,tk->ck", normed_low, grad_proj_low, preferred_element_type=jnp.float32
    )
    grad_normed = jnp.einsum(
        "tk,ck->tc", grad_proj_low, full_qkv, preferred_element_type=jnp.float32
    )
    grad_in_norm, grad_gain_one, grad_bias_one = norm_one_back(grad_normed)
    input_grad = (grad_middle + grad_in_norm)[None]
    part_qkv, part_out, part_up, part_down = (
        lax.psum_scatter(
            grad_qkv.astype(jnp.bfloat16), "seg", scatter_dimension=0, tiled=True
        ).astype(jnp.float32),
        lax.psum_scatter(
            grad_out.astype(jnp.bfloat16), "seg", scatter_dimension=0, tiled=True
        ).astype(jnp.float32),
        lax.psum_scatter(
            grad_up.astype(jnp.bfloat16), "seg", scatter_dimension=0, tiled=True
        ).astype(jnp.float32),
        lax.psum_scatter(
            grad_down.astype(jnp.bfloat16), "seg", scatter_dimension=0, tiled=True
        ).astype(jnp.float32),
    )
    sum_qkv, sum_out, sum_up, sum_down = (
        lax.psum_scatter(
            part_qkv.astype(jnp.bfloat16), "seq", scatter_dimension=1, tiled=True
        ).astype(jnp.float32),
        lax.psum_scatter(
            part_out.astype(jnp.bfloat16), "seq", scatter_dimension=1, tiled=True
        ).astype(jnp.float32),
        lax.psum_scatter(
            part_up.astype(jnp.bfloat16), "seq", scatter_dimension=1, tiled=True
        ).astype(jnp.float32),
        lax.psum_scatter(
            part_down.astype(jnp.bfloat16), "seq", scatter_dimension=1, tiled=True
        ).astype(jnp.float32),
    )
    sum_gain_one, sum_bias_one, sum_gain_two, sum_bias_two = lax.psum(
        (grad_gain_one, grad_bias_one, grad_gain_two, grad_bias_two), ("seq", "seg")
    )
    return (
        result,
        input_grad,
        sum_gain_one,
        sum_bias_one,
        sum_qkv,
        sum_out,
        sum_gain_two,
        sum_bias_two,
        sum_up,
        sum_down,
    )


MESH = pl.DeviceIdType.MESH
BF = jnp.bfloat16
F32 = jnp.float32
def dot_nn(a, b):
    return lax.dot_general(a, b, (((1,), (0,)), ((), ())), preferred_element_type=F32)


def dot_nt(a, b):
    return lax.dot_general(a, b, (((1,), (1,)), ((), ())), preferred_element_type=F32)


def dot_tn(a, b):
    return lax.dot_general(a, b, (((0,), (0,)), ((), ())), preferred_element_type=F32)


def remote(src, dst, send, recv, **place):
    return pltpu.make_async_remote_copy(
        src_ref=src, dst_ref=dst, send_sem=send, recv_sem=recv, device_id=place, device_id_type=MESH
    )


def norm_parts(values):
    center = values - jnp.mean(values, axis=-1, keepdims=True)
    spread = jnp.mean(center * center, axis=-1, keepdims=True)
    inverse = lax.rsqrt(spread + 1e-05)
    return center * inverse, inverse


def greet(q, s, transposed=False):
    y, c = s // 2, s % 2
    barrier = pltpu.get_barrier_semaphore()

    def signal(seq, seg):
        pl.semaphore_signal(barrier, 1, device_id={"seq": seq, "seg": seg}, device_id_type=MESH)

    for d in range(1, 8):
        for core in range(2):
            signal(lax.rem(q + d, 8), 2 * y + core)
    for d in range(1, 4):
        signal(q, lax.rem(s + d, 4))
    if transposed:
        turned = s != q // 2

        @pl.when(turned)
        def _():
            signal(2 * s + q % 2, q // 2)

        return lambda: pl.semaphore_wait(barrier, jnp.where(turned, 18, 17))
    return lambda: pl.semaphore_wait(barrier, 17)


def first_columns(lens, base, rows):
    place = base + lax.broadcasted_iota(jnp.int32, (rows, 1), 0)
    start = jnp.zeros((rows, 1), jnp.int32)
    bound = jnp.zeros((1, 1), jnp.int32)
    for i in range(lens.shape[0]):
        bound = bound + lens[i : i + 1, 0:1]
        start = jnp.where(place >= bound, bound, start)
    return start


def seen_mask(start, base_q, base_k, rows, columns):
    place = base_q + lax.broadcasted_iota(jnp.int32, (rows, columns), 0)
    key = base_k + lax.broadcasted_iota(jnp.int32, (rows, columns), 1)
    return (key <= place) & (key >= start)


def rows(k, n):
    return pl.ds(pl.multiple_of(k * n, n), n)


def lanes(k, n=128):
    return pl.ds(pl.multiple_of(k * n, n), n)


T = 256
HALF = 128


def places(z, x):
    zn, zc = z + 1 - 2 * (z % 2), (z + 2) % 4
    znc = (zn + 2) % 4
    here, near_z, near_x, cross = 2 * z + x, 2 * zn + x, 2 * z + 1 - x, 2 * zc + x
    blocks = (here, near_x, near_z, cross, 2 * znc + x, 2 * zc + 1 - x, 2 * zn + 1 - x, 2 * znc + 1 - x)
    return here, near_z, near_x, cross, blocks


def nth(values, k):
    out = values[0]
    for i, value in enumerate(values[1:], 1):
        out = jnp.where(k == i, value, out)
    return out


def attend_kernel(
    x_ref, lens_ref, gain_ref, bias_ref, wq_ref, wo_ref, wu_ref, g_ref,
    o_ref, wof, wuc, gall, xs_o, h1_o, wh, qkv, of, lse, lens,
    xs, h1, keep_sem, ob, wq_s, wu_v, lens_r, local_sem, qs, qr, ws, wr, xs_send, xs_recv, xu_recv, os_send, os_recv,
):
    q, s = lax.axis_index("seq"), lax.axis_index("seg")
    z, x = q // 2, q % 2
    y, c = s // 2, s % 2
    sib = s + 1 - 2 * c
    across = (1 - y) * 2 + c
    corner = (1 - y) * 2 + 1 - c
    group = z // 2
    head = 4 * (z % 2) + 2 * x + c
    twin = head + 1 - 2 * c
    home = c == group
    column = 2 * y + group
    _, near_z, near_x, cross, blocks = places(z, x)
    scale = 1.0 / math.sqrt(HEAD_DIM)

    met = greet(q, s)

    for j in range(3):
        at = slice(j * 128, (j + 1) * 128)
        wh[rows(s, T), at] = wq_ref[:, lanes(8 * j + head)]
        wq_s[0, :, at] = wq_ref[:, lanes(8 * j + head)]
        wq_s[1, :, at] = wq_ref[:, lanes(8 * j + twin)]

    @pl.when(home)
    def _():
        xs[rows(q, T)] = x_ref[...]

    met()

    def half_rows(b, part):
        return xs.at[pl.ds(pl.multiple_of(b * T + part * HALF, HALF), HALF)]

    def over_copy(part):
        src = x_ref.at[part * HALF : (part + 1) * HALF]
        return remote(src, half_rows(q, part), xs_send.at[24 + part], xs_recv.at[q], seq=cross, seg=2 * y + part)

    def twin_copy(part, recv, k):
        return remote(half_rows(q, part), half_rows(q, part), xs_send.at[24 + k], recv.at[q], seg=sib)

    twin_track, twin_rest = twin_copy(1 - c, xs_recv, 0), twin_copy(c, xu_recv, 1)

    @pl.when(home)
    def _():
        twin_track.start()
        twin_rest.start()

    @pl.when(jnp.logical_not(home))
    def _():
        over_copy(0).start()
        over_copy(1).start()

    mine_wh = wh.at[rows(s, T)]
    q_across = remote(wq_s.at[0], mine_wh, qs.at[0], qr.at[0], seg=across)
    q_sib = remote(wq_s.at[1], mine_wh, qs.at[1], qr.at[1], seg=sib)
    q_corner = remote(wq_s.at[1], mine_wh, qs.at[2], qr.at[2], seg=corner)
    l_sib = remote(lens_ref, lens_r, qs.at[3], qr.at[3], seg=sib)
    first = (q_across, q_corner, q_sib, l_sib)
    for copy in first:
        copy.start()

    def x_copy(b, k, recv, **to):
        src = half_rows(b, c)
        return remote(src, src, xs_send.at[k], recv.at[b], **to)

    own_z, own_x = x_copy(q, 0, xs_recv, seq=near_z), x_copy(q, 8, xs_recv, seq=near_x)

    @pl.when(jnp.logical_not(home))
    def _():
        x_copy(q, 0, xs_recv, seq=q).wait_recv()

    own_z.start()
    own_x.start()

    def u_part(seg, part):
        return wuc.at[pl.ds(pl.multiple_of(seg * T + part * HALF, HALF), HALF)]

    def o_part(seg, part):
        return wof.at[pl.ds(pl.multiple_of(seg * T + part * HALF, HALF), HALF)]

    u_far = tuple(
        remote(
            wu_ref.at[pl.ds(pl.multiple_of(x * HALF, HALF), HALF), lanes(to, 1024)], u_part(s, x), ws.at[k], wr.at[k],
            seg=to,
        )
        for k, to in ((0, across), (1, corner))
    )
    u_over = tuple(
        remote(u_part(of_seg, x), u_part(of_seg, x), ws.at[11 + k], wr.at[11 + k], seq=near_x)
        for k, of_seg in ((0, across), (1, corner))
    )
    u_sib = remote(wu_ref.at[:, lanes(sib, 1024)], wuc.at[rows(s, T)], ws.at[2], wr.at[2], seg=sib)
    o_far = remote(
        wo_ref.at[pl.ds(pl.multiple_of(x * HALF, HALF), HALF)], o_part(s, x), ws.at[3], wr.at[3], seg=across
    )
    o_over = remote(o_part(across, x), o_part(across, x), ws.at[13], wr.at[13], seq=near_x)
    o_sib = remote(wo_ref, wof.at[rows(s, T)], ws.at[4], wr.at[4], seg=sib)
    o_pass = tuple(
        remote(o_part(across, part), o_part(across, part), ws.at[k], wr.at[k], seg=sib)
        for k, part in ((5, x), (14, 1 - x))
    )
    far = lambda k, part: gall.at[pl.ds(2 * T + part * T + k * HALF, HALF)]
    g_across = tuple(
        remote(g_ref.at[k * HALF : (k + 1) * HALF], far(0, k), ws.at[6 + k], wr.at[6 + k], seg=across)
        for k in range(2)
    )
    g_sib = remote(g_ref, gall.at[T : 2 * T], ws.at[8], wr.at[8], seg=sib)
    g_pass = tuple(remote(far(0, k), far(1, k), ws.at[9 + k], wr.at[9 + k], seg=sib) for k in range(2))
    own_in = pltpu.make_async_copy(wu_ref.at[:, lanes(s, 1024)], wu_v, local_sem.at[0])
    own = (
        pltpu.make_async_copy(wo_ref, wof.at[rows(s, T)], local_sem.at[1]),
        pltpu.make_async_copy(g_ref, gall.at[0:T], local_sem.at[2]),
        pltpu.make_async_copy(wu_v, wuc.at[rows(s, T)], local_sem.at[3]),
    )
    for copy in (own_in,) + u_far + (o_far,) + g_across:
        copy.start()
    for copy in first:
        copy.wait_recv()
    lens[...] = jnp.where(home, lens_ref[...], lens_r[...])
    own_in.wait()
    for copy in own:
        copy.start()

    gain, bias = gain_ref[...], bias_ref[...]

    def keep(b):
        at = rows(b, T)
        return (
            pltpu.make_async_copy(xs.at[at], xs_o.at[at], keep_sem.at[b]),
            pltpu.make_async_copy(h1.at[at], h1_o.at[at], keep_sem.at[8 + b]),
        )

    def project(b):
        unit, _ = norm_parts(xs[rows(b, T)].astype(F32))
        low = (unit * gain + bias).astype(BF)
        h1[rows(b, T)] = low
        qkv[rows(b, T)] = dot_nn(low, wh[...]).astype(BF)
        for copy in keep(b):
            copy.start()

    def track_step(k, _):
        b = nth(blocks, k)

        @pl.when(k < 8)
        def _():
            x_copy(b, 0, xs_recv, seq=q).wait_recv()

        @pl.when((k == 1) | (k == 3))
        def _():
            x_copy(b, k, xs_recv, seq=near_z).start()

        @pl.when((k == 3) | (k == 4))
        def _():
            x_copy(b, 8 + k, xs_recv, seq=near_x).start()

        @pl.when(k < 8)
        def _():
            x_copy(b, 16 + k, xu_recv, seg=sib).start()

        last = nth(blocks, k - 1)

        @pl.when((k > 1) | jnp.logical_not(home))
        def _():
            x_copy(last, 0, xu_recv, seg=sib).wait_recv()

        project(last)

        return 0

    lax.fori_loop(1, 6, track_step, 0)
    for arrived, copy in zip(u_far, u_over):
        arrived.wait_recv()
        copy.start()
    lax.fori_loop(6, 9, track_step, 0)
    o_far.wait_recv()
    o_over.start()
    o_pass[0].start()
    for copy in (u_sib, o_sib, g_sib):
        copy.start()

    def o_copy(i, sender):
        return remote(
            ob.at[i], o_ref.at[:, lanes(sender)], os_send.at[i], os_recv.at[sender], seq=i, seg=column
        )

    mine = pltpu.make_async_copy(ob.at[q], o_ref.at[:, lanes(head)], os_recv.at[head])
    for i in range(8):
        n = (i + 1) * T
        start = first_columns(lens, i * T, T)
        scores = dot_nt(qkv[i * T : n, :128], qkv[:n, 128:256]) * scale
        scores = jnp.where(seen_mask(start, i * T, 0, T, n), scores, -1e30)
        top = jnp.max(scores, axis=1, keepdims=True)
        weights = jnp.exp(scores - top)
        total = jnp.sum(weights, axis=1, keepdims=True)
        mixed = dot_nn(weights.astype(BF), qkv[:n, 256:384]) / total
        of[i * T : n] = mixed
        lse[i * T : n] = top + jnp.log(total)
        ob[i] = mixed.astype(BF)
        here = (q == i) & home

        @pl.when(jnp.logical_not(here))
        def _():
            o_copy(i, head).start()

        @pl.when(here)
        def _():
            mine.start()

    o_over.wait_recv()
    o_pass[1].start()
    for arrived, copy in zip(g_across, g_pass):
        arrived.wait_recv()
        copy.start()

    for k in range(1, 8):
        if k in (1, 3):
            x_copy(blocks[k], k, xs_recv, seq=near_z).wait_send()
        if k in (3, 4):
            x_copy(blocks[k], 8 + k, xs_recv, seq=near_x).wait_send()
        x_copy(blocks[k], 16 + k, xu_recv, seg=sib).wait_send()

    @pl.when(home)
    def _():
        twin_track.wait_send()
        twin_rest.wait_send()

    @pl.when(jnp.logical_not(home))
    def _():
        over_copy(0).wait_send()
        over_copy(1).wait_send()

    for i in range(8):
        @pl.when(jnp.logical_not((q == i) & home))
        def _():
            o_copy(i, head).wait_send()

        o_copy(i, i).wait_recv()

    for copy in own:
        copy.wait()
    for b in range(8):
        for copy in keep(b):
            copy.wait()
    for copy in first + u_far + u_over + o_pass + g_across + g_pass + (u_sib, o_far, o_over, o_sib, g_sib, own_z, own_x):
        copy.wait_send()
    for copy in u_over + o_pass + g_pass + (u_sib, o_sib, g_sib):
        copy.wait_recv()


VM = pl.BlockSpec(memory_space=pltpu.VMEM)
HB = pl.BlockSpec(memory_space=pl.ANY)
S = jax.ShapeDtypeStruct


def attend(x, lens, gain, bias, wq, wo, wu, g):
    dma = pltpu.SemaphoreType.DMA
    return pl.pallas_call(
        attend_kernel,
        out_shape=(
            S((256, 1024), BF), S((1024, 1024), BF), S((1024, 1024), BF), S((1024, 1024), BF),
            S((2048, 1024), BF), S((2048, 1024), BF), S((1024, 384), BF), S((2048, 384), BF),
            S((2048, 128), F32), S((2048, 1), F32), S((8, 128), jnp.int32),
        ),
        in_specs=[VM, VM, VM, VM, VM, VM, HB, VM],
        out_specs=(VM, HB, HB, HB, HB, HB, VM, VM, VM, VM, VM),
        scratch_shapes=[
            pltpu.VMEM((2048, 1024), BF), pltpu.VMEM((2048, 1024), BF), dma((16,)),
            pltpu.VMEM((8, 256, 128), BF), pltpu.VMEM((2, 256, 384), BF), pltpu.VMEM((256, 1024), BF),
            pltpu.VMEM((8, 128), jnp.int32), dma((4,)), dma((4,)), dma((4,)), dma((15,)), dma((15,)),
            dma((26,)), dma((8,)), dma((8,)), dma((8,)), dma((8,)),
        ],
        compiler_params=pltpu.CompilerParams(
            collective_id=0, has_side_effects=True, vmem_limit_bytes=58 * 2**20
        ),
        cost_estimate=pl.CostEstimate(flops=5 * 10**9, bytes_accessed=40 * 2**20, transcendentals=2 * 2**20),
        name="attend",
    )(x, lens, gain, bias, wq, wo, wu, g)


def gelu_parts(u):
    root = math.sqrt(2.0 / math.pi)
    square = u * u
    t = jnp.tanh(root * (u + 0.044715 * (square * u)))
    value = 0.5 * u * (1.0 + t)
    slope = 0.5 * (1.0 + t) + 0.5 * u * (1.0 - t * t) * (root * (1.0 + 0.134145 * square))
    return value, slope


def norm_back(grad, gain, unit, inverse):
    through = grad * gain
    a = jnp.mean(through, axis=-1, keepdims=True)
    b = jnp.mean(through * unit, axis=-1, keepdims=True)
    return inverse * (through - a - unit * b)


def layer_kernel(
    x_ref, o_ref, wo_ref, gain2_ref, bias2_ref, lens_ref, lse_ref,
    g_hbm, wu_hbm, wd_hbm, qkv_hbm, of_hbm, wh_hbm, xs_hbm, h1_hbm,
    result_out, dx_v, fin_r, gq_r, gout_out, up_r, gdown_out, sums_out,
    g_v, wu_v, wd_v, qkv_v, of_v, wh_v, load_sem,
    middle, h2, big, mine, near_s, near_r, twin_s, twin_r, far_keep, far_s, far_r, do_v,
    hs, hr, ns, nr, ts, tr, fs, fr,
    pack, x_r, z_r, up_s, gxs, gxr, gzs, gzr, ups, upr,
    outp, oc_r, oy_r, ox_r, oz_r, oo_r, cs, cr,
    doh, dq, dk, dv, dos, dor,
    dhc_r, step_r, fin_s, dcs, dcr, sts, str_, fns, fnr,
    gq, gq_b, gq_y, qs, qr,
    vec, vec_r, vs, vr,
):
    q, s = lax.axis_index("seq"), lax.axis_index("seg")
    z, x = q // 2, q % 2
    y, c = s // 2, s % 2
    sib = s + 1 - 2 * c
    across = (1 - y) * 2 + c
    group = z // 2
    head = 4 * (z % 2) + 2 * x + c
    home = c == group
    away = jnp.logical_not(home)
    column = 2 * y + group
    here, near_z, near_x, cross, blocks = places(z, x)
    scale = 1.0 / math.sqrt(HEAD_DIM)

    loads = tuple(
        pltpu.make_async_copy(src, dst, load_sem.at[k])
        for k, (src, dst) in enumerate(
            ((wu_hbm, wu_v), (wd_hbm, wd_v), (g_hbm, g_v), (qkv_hbm, qkv_v), (of_hbm, of_v), (wh_hbm, wh_v))
        )
    )
    for copy in loads:
        copy.start()
    met = greet(q, s, True)

    value = x_ref[...].astype(F32) + dot_nn(o_ref[...], wo_ref[...])
    middle[...] = value
    unit, _ = norm_parts(value)
    h2[0:T] = (unit * gain2_ref[...] + bias2_ref[...]).astype(BF)

    def far_rows(ref, part, k):
        return ref.at[pl.ds(2 * T + k * T + part * HALF, HALF)]

    h_far = tuple(
        remote(h2.at[k * HALF : (k + 1) * HALF], far_rows(h2, 0, k), hs.at[k], hr.at[k], seg=across)
        for k in range(2)
    )
    h_pass = tuple(
        remote(far_rows(h2, 0, k), far_rows(h2, 1, k), hs.at[2 + k], hr.at[2 + k], seg=sib) for k in range(2)
    )
    h_sib = remote(h2.at[0:T], h2.at[T : 2 * T], hs.at[4], hr.at[4], seg=sib)
    met()
    for copy in h_far + (h_sib,):
        copy.start()
    for copy in loads[:3]:
        copy.wait()

    def work(part):
        at = slice(part * T, (part + 1) * T)
        value, slope = gelu_parts(dot_nn(h2[at], wu_v[...]))
        low = value.astype(BF)
        big[at] = low
        du = (slope * dot_nt(g_v[at], wd_v[...])).astype(BF)
        big[4 * T + part * T : 4 * T + (part + 1) * T] = du
        return dot_nt(du, wu_v[...]), dot_nn(low, wd_v[...])

    near = tuple(remote(near_s.at[k], near_r.at[k], ns.at[k], nr.at[k], seg=sib) for k in range(2))
    twin = tuple(
        tuple(remote(twin_s.at[k, n], twin_r.at[k, n], ts.at[2 * k + n], tr.at[2 * k + n], seg=sib) for n in range(2))
        for k in range(2)
    )
    far = tuple(
        tuple(remote(far_s.at[k, n], far_r.at[k, n], fs.at[2 * k + n], fr.at[2 * k + n], seg=across) for n in range(2))
        for k in range(2)
    )

    def send_twin(n, parts):
        for k in range(2):
            far_keep[k] = parts[k][:HALF]
            twin_s[k, n] = parts[k][HALF:].astype(BF)
            twin[k][n].start()

    def send_far(n):
        for k in range(2):
            twin[k][n].wait_recv()
            far_s[k, n] = (far_keep[k] + twin_r[k, n].astype(F32)).astype(BF)
            if k == 0:
                far[k][n].start()

    parts = work(0)
    for k in range(2):
        mine[k] = parts[k]
    h_sib.wait_recv()
    parts = work(1)
    for k in range(2):
        near_s[k] = parts[k].astype(BF)
        near[k].start()
    h_far[0].wait_recv()
    h_pass[0].start()
    h_pass[0].wait_recv()
    send_twin(0, work(2))
    h_far[1].wait_recv()
    h_pass[1].start()
    send_far(0)
    h_pass[1].wait_recv()
    send_twin(1, work(3))
    send_far(1)

    for j in range(4):
        down = dot_tn(big[: 4 * T, j * T : (j + 1) * T], g_v[...]).astype(BF)
        for k in range(8):
            pack[k, :, 512 + j * 128 : 640 + j * 128] = down[:, k * 128 : (k + 1) * 128]
    for j in range(4):
        up = dot_tn(h2[:, j * T : (j + 1) * T], big[4 * T :]).astype(BF)
        for k in range(2):
            pack[2 * j + k, :, :512] = up[:, k * 512 : (k + 1) * 512]

    def gx_copy(d):
        return remote(pack.at[2 * d + 1 - x], x_r.at[d], gxs.at[d], gxr.at[d], seq=near_x)

    zn, zc = z + 1 - 2 * (z % 2), (z + 2) % 4
    znc = (zn + 2) % 4
    gx_copy(znc).start()
    gx_copy(zc).start()

    near[0].wait_recv()
    far[0][0].wait_recv()
    far[0][1].wait_recv()
    grad = mine[0] + near_r[0].astype(F32) + jnp.concatenate([far_r[0, 0], far_r[0, 1]], axis=0).astype(F32)
    unit, inverse = norm_parts(middle[...])
    vec[...] = jnp.zeros_like(vec)
    vec[2:3] = jnp.sum(grad * unit, axis=0, keepdims=True)
    vec[3:4] = jnp.sum(grad, axis=0, keepdims=True)
    dx = g_v[0:T].astype(F32) + norm_back(grad, gain2_ref[...], unit, inverse)
    dx_v[...] = dx
    dy = dx.astype(BF)
    do_v[...] = dot_nt(dy, wo_ref[...]).astype(BF)

    def do_copy(h, block):
        return remote(
            do_v.at[:, h * 128 : (h + 1) * 128], doh.at[rows(block, T)], dos.at[h], dor.at[block],
            seq=2 * (2 * c + h // 4) + (h // 2) % 2, seg=2 * y + h % 2,
        )

    do_mine = pltpu.make_async_copy(do_v.at[:, lanes(head)], doh.at[rows(q, T)], dor.at[q])
    for h in range(8):
        self_too = (head == h) & home

        @pl.when(jnp.logical_not(self_too))
        def _():
            do_copy(h, q).start()

        @pl.when(self_too)
        def _():
            do_mine.start()

    out = dot_tn(o_ref[...], dy).astype(BF)
    for quarter in range(4):
        for k in range(8):
            outp[quarter // 2, quarter % 2, k // 4, (k // 2) % 2, k % 2] = out[quarter * T : (quarter + 1) * T, k * 128 : (k + 1) * 128]
    out_core = remote(outp.at[:, 1 - c], oc_r, cs.at[0], cr.at[0], seg=sib)
    out_core.start()
    out_core.wait_recv()
    for part in range(2):
        oc_r[part] = (oc_r[part].astype(F32) + outp[part, c].astype(F32)).astype(BF)
    out_y = remote(oc_r.at[1 - y], oy_r, cs.at[1], cr.at[1], seg=across)
    out_y.start()
    far[1][0].start()
    far[1][1].start()

    def come(into, recv, slot):
        return remote(into.at[slot], into.at[slot], recv.at[slot], recv.at[slot], seq=near_x)

    def gz_copy(k, d, to):
        return remote(x_r.at[d], z_r.at[k], gzs.at[k], gzr.at[k], seq=to)

    gz = (gz_copy(0, znc, near_z), gz_copy(1, zn, near_z), gz_copy(2, zc, cross))

    def pack_sum(d):
        gx_copy(d).wait_recv()
        return pack[2 * d + x].astype(F32) + x_r[d].astype(F32)

    x_r[znc] = pack_sum(znc).astype(BF)
    gz[0].start()
    for copy in loads[3:]:
        copy.wait()

    gx_copy(zn).start()

    dk[...] = jnp.zeros_like(dk)
    dv[...] = jnp.zeros_like(dv)
    lens = lens_ref[...]
    for i in range(8):
        do_copy(0, i).wait_recv()
        top = i * T
        start = first_columns(lens, top, T)
        query = qkv_v[top : top + T, :128]
        grad = doh[top : top + T]
        delta = jnp.sum(grad.astype(F32) * of_v[top : top + T], axis=1, keepdims=True)
        log_total = lse_ref[top : top + T]
        total = jnp.zeros((T, 128), F32)
        for base in range(0, top + T, 1024):
            n = min(1024, top + T - base)
            keys = qkv_v[base : base + n, 128:256]
            probs = jnp.exp(dot_nt(query, keys) * scale - log_total)
            probs = jnp.where(seen_mask(start, top, base, T, n), probs, 0.0)
            dp = dot_nt(grad, qkv_v[base : base + n, 256:384])
            ds = (probs * (dp - delta)).astype(BF)
            dv[base : base + n] += dot_tn(probs.astype(BF), grad)
            dk[base : base + n] += dot_tn(ds, query)
            total += dot_nn(ds, keys)
        dq[top : top + T] = total

    gz[0].wait_recv()
    x_r[zc] = (pack_sum(zc) + z_r[0].astype(F32)).astype(BF)
    gz[2].start()

    gq[...] = jnp.zeros_like(gq)
    own_a, other_xa, other_za, own_b, other_zb, other_xb, diag_a, diag_b = blocks
    order = (diag_a, diag_b, other_za, other_xb, other_xa, other_zb, own_a, own_b)

    def x_load(i):
        return pltpu.make_async_copy(xs_hbm.at[rows(nth(order, i), T)], wu_v.at[rows(i % 2, T)], load_sem.at[6 + i % 2])

    def h_load(i):
        return pltpu.make_async_copy(h1_hbm.at[rows(nth(order, i), T)], wu_v.at[rows(2 + i % 2, T)], load_sem.at[8 + i % 2])

    def dhc_copy(b):
        return remote(
            big.at[pl.ds(pl.multiple_of(b * T + (1 - c) * HALF, HALF), HALF)], dhc_r.at[b], dcs.at[b], dcr.at[b], seg=sib
        )

    def half(b):
        return big.at[pl.ds(pl.multiple_of(b * T + c * HALF, HALF), HALF)]

    def step_copy(k, b, to):
        return remote(dhc_r.at[b], step_r.at[k], sts.at[k], str_.at[k], seq=to)

    steps = (
        step_copy(0, diag_a, near_z), step_copy(1, diag_b, near_x), step_copy(2, other_za, near_z),
        step_copy(3, other_xb, near_x), step_copy(4, other_xa, near_x), step_copy(5, other_zb, near_z),
    )
    x_load(0).start()
    h_load(0).start()

    def grads_at(at):
        return jnp.concatenate([dq[at] * scale, dk[at] * scale, dv[at]], axis=1).astype(BF)

    def block_step(i, _):
        @pl.when(i < 8)
        def _():
            b = nth(order, i)

            at = rows(b, T)
            big[at] = dot_nt(grads_at(at), wh_v[...]).astype(BF)
            dhc_copy(b).start()

        @pl.when(i > 0)
        def _():
            b = nth(order, i - 1)
            dhc_copy(b).wait_recv()
            dhc_r[b] = (half(b)[...].astype(F32) + dhc_r[b].astype(F32)).astype(BF)
            for k in range(4):
                @pl.when(i == k + 1)
                def _():
                    steps[k].start()

        return 0

    lax.fori_loop(0, 9, block_step, 0)

    def sum_step(i, _):
        @pl.when(i < 7)
        def _():
            x_load(i + 1).start()
            h_load(i + 1).start()

        at = rows(nth(order, i), T)
        dh = big[at].astype(F32)
        x_load(i).wait()
        h_load(i).wait()
        gq[...] += dot_tn(wu_v[rows(2 + i % 2, T)], grads_at(at))
        unit, _ = norm_parts(wu_v[rows(i % 2, T)].astype(F32))
        vec[0:1] += jnp.sum(dh * unit, axis=0, keepdims=True)
        vec[1:2] += jnp.sum(dh, axis=0, keepdims=True)
        return 0

    lax.fori_loop(0, 8, sum_step, 0)
    for k, b in ((5, other_zb), (4, other_xa)):
        steps[k - 4].wait_recv()
        dhc_r[b] = (dhc_r[b].astype(F32) + step_r[k - 4].astype(F32)).astype(BF)
        steps[k].start()

    x_r[zn] = pack_sum(zn).astype(BF)
    gz[1].start()

    out_y.wait_recv()
    oc_r[y] = (oc_r[y].astype(F32) + oy_r[...].astype(F32)).astype(BF)
    out_x = remote(oc_r.at[y, :, :, 1 - x], ox_r, cs.at[2], cr.at[2], seq=near_x)
    out_x.start()
    gx_copy(z).start()

    gq_b[...] = gq[...].astype(BF).reshape(2, 2, T, 384)
    q_y = remote(gq_b.at[1 - y], gq_y, qs.at[0], qr.at[0], seg=across)
    q_y.start()
    v_core = remote(vec, vec_r.at[0], vs.at[8], vr.at[8], seg=sib)
    v_core.start()
    v_core.wait()
    vec[...] += vec_r[0]
    v_y = remote(vec, vec_r.at[1], vs.at[9], vr.at[9], seg=across)
    v_y.start()
    for k, b, pair in ((0, own_a, (2, 4)), (1, own_b, (3, 5))):
        for n in pair:
            steps[n].wait_recv()
        fin_s[k] = (
            dhc_r[b].astype(F32) + step_r[pair[0]].astype(F32) + step_r[pair[1]].astype(F32)
        ).astype(BF)
    fin_over = remote(fin_s.at[1], fin_r.at[c], fns.at[0], fnr.at[c], seq=cross, seg=column)
    fin_twin = remote(fin_s.at[0], fin_r.at[c], fns.at[1], fnr.at[c], seg=sib)
    fin_own = pltpu.make_async_copy(fin_s.at[0], fin_r.at[c], fnr.at[c])
    fin_over.start()

    @pl.when(away)
    def _():
        fin_twin.start()

    @pl.when(home)
    def _():
        fin_own.start()

    v_y.wait()
    vec[...] += vec_r[1]

    def v_copy(b, sender):
        return remote(vec, vec_r.at[2 + sender], vs.at[b], vr.at[sender], seq=b)

    for b in range(8):
        @pl.when(q != b)
        def _():
            v_copy(b, q).start()

    q_y.wait_recv()
    gq_y[...] = (gq_y[...].astype(F32) + gq_b[y].astype(F32)).astype(BF)

    def column_copy(part, j):
        place = 8 * j + head
        owner, slot = place // 3, place % 3
        src = gq_y.at[part, :, j * 128 : (j + 1) * 128]
        copy = remote(
            src, gq_r.at[slot, group], qs.at[1 + 3 * part + j], qr.at[1 + 2 * slot + group],
            seq=owner, seg=2 * y + part,
        )
        local = pltpu.make_async_copy(src, gq_r.at[slot, group], qr.at[1 + 2 * slot + group])
        return (owner == q) & (c == part), copy, local

    columns = tuple(column_copy(part, j) for part in range(2) for j in range(3))
    out_x.wait_recv()
    ox_r[...] = (ox_r[...].astype(F32) + oc_r[y, :, :, x].astype(F32)).astype(BF)
    out_z = remote(ox_r.at[:, 1 - z % 2], oz_r, cs.at[3], cr.at[3], seq=near_z)
    out_z.start()
    for self_too, copy, local in columns:
        @pl.when(jnp.logical_not(self_too))
        def _():
            copy.start()

        @pl.when(self_too)
        def _():
            local.start()

    out_z.wait_recv()
    oz_r[...] = (oz_r[...].astype(F32) + ox_r[:, z % 2].astype(F32)).astype(BF)
    out_o = remote(oz_r.at[1 - group], oo_r, cs.at[4], cr.at[4], seq=cross)
    out_o.start()

    total = pack_sum(z)
    for k in (1, 2):
        gz[k].wait_recv()
        total = total + z_r[k].astype(F32)
    up_s[...] = total[:, :512].astype(BF)
    turned = s != z
    up_turn = remote(up_s, up_r, ups, upr, seq=2 * s + x, seg=z)
    up_own = pltpu.make_async_copy(up_s, up_r, upr)

    @pl.when(turned)
    def _():
        up_turn.start()

    @pl.when(jnp.logical_not(turned))
    def _():
        up_own.start()

    for j in range(4):
        gdown_out[j * T : (j + 1) * T] = total[:, 512 + j * 128 : 640 + j * 128]
    vec_r[2 + q] = vec[...]
    for b in range(8):
        @pl.when(q != b)
        def _():
            v_copy(b, b).wait_recv()

    vec_sum = vec_r[2]
    for b in range(1, 8):
        vec_sum = vec_sum + vec_r[2 + b]
    out_o.wait_recv()
    gout_out[...] = oz_r[group].astype(F32) + oo_r[...].astype(F32)
    sums_out[...] = vec_sum
    for slot in range(3):
        for part in range(2):
            pltpu.make_async_copy(gq_r.at[slot, part], gq_r.at[slot, part], qr.at[1 + 2 * slot + part]).wait()
    near[1].wait_recv()
    far[1][0].wait_recv()
    far[1][1].wait_recv()
    result_out[...] = (
        middle[...] + mine[1] + near_r[1].astype(F32)
        + jnp.concatenate([far_r[1, 0], far_r[1, 1]], axis=0).astype(F32)
    ).astype(BF)
    for k in range(2):
        come(fin_r, fnr, k).wait_recv()
    up_own.wait()

    for h in range(8):
        @pl.when(jnp.logical_not((head == h) & home))
        def _():
            do_copy(h, q).wait_send()

    for b in range(8):
        dhc_copy(b).wait_send()

        @pl.when(q != b)
        def _():
            v_copy(b, q).wait_send()

    for d in range(4):
        gx_copy(d).wait_send()
    for copy in (out_core, out_y, out_x, out_z, out_o, q_y, h_sib, fin_over) + h_far + h_pass + near + steps + gz:
        copy.wait_send()
    for k in range(2):
        for n in range(2):
            twin[k][n].wait_send()
            far[k][n].wait_send()

    @pl.when(away)
    def _():
        fin_twin.wait_send()

    @pl.when(turned)
    def _():
        up_turn.wait_send()

    for self_too, copy, _ in columns:
        @pl.when(jnp.logical_not(self_too))
        def _():
            copy.wait_send()


def layer(x, o, wo, gain2, bias2, lens, lse, g, wu, wd, qkv, of, wh, xs, h1):
    dma = pltpu.SemaphoreType.DMA
    low = lambda *shape: pltpu.VMEM(shape, BF)
    wide = lambda *shape: pltpu.VMEM(shape, F32)
    return pl.pallas_call(
        layer_kernel,
        out_shape=(
            S((256, 1024), BF), S((256, 1024), F32), S((2, 128, 1024), BF), S((3, 2, 256, 128), BF),
            S((256, 128), F32), S((256, 512), BF), S((1024, 128), F32), S((8, 1024), F32),
        ),
        in_specs=[VM] * 7 + [HB] * 8,
        out_specs=(VM,) * 8,
        scratch_shapes=[
            low(1024, 1024), low(1024, 1024), low(1024, 1024), low(2048, 384), wide(2048, 128), low(1024, 384),
            dma((10,)),
            wide(256, 1024), low(1024, 1024), low(2048, 1024), wide(2, 256, 1024),
            low(2, 256, 1024), low(2, 256, 1024), low(2, 2, 128, 1024), low(2, 2, 128, 1024), wide(2, 128, 1024),
            low(2, 2, 128, 1024), low(2, 2, 128, 1024), low(256, 1024),
            dma((5,)), dma((5,)), dma((2,)), dma((2,)), dma((4,)), dma((4,)), dma((4,)), dma((4,)),
            low(8, 256, 1024), low(4, 256, 1024), low(3, 256, 1024), low(256, 512),
            dma((4,)), dma((4,)), dma((3,)), dma((3,)), dma, dma,
            low(2, 2, 2, 2, 2, 256, 128), low(2, 2, 2, 2, 256, 128), low(2, 2, 2, 256, 128), low(2, 2, 256, 128),
            low(2, 256, 128), low(256, 128), dma((5,)), dma((5,)),
            low(2048, 128), wide(2048, 128), wide(2048, 128), wide(2048, 128), dma((8,)), dma((8,)),
            low(8, 128, 1024), low(6, 128, 1024), low(2, 128, 1024),
            dma((8,)), dma((8,)), dma((6,)), dma((6,)), dma((2,)), dma((2,)),
            wide(1024, 384), low(2, 2, 256, 384), low(2, 256, 384),
            dma((7,)), dma((7,)),
            wide(8, 1024), wide(10, 8, 1024), dma((10,)), dma((10,)),
        ],
        compiler_params=pltpu.CompilerParams(
            collective_id=1, has_side_effects=True, vmem_limit_bytes=63 * 2**20
        ),
        cost_estimate=pl.CostEstimate(flops=2 * 10**10, bytes_accessed=40 * 2**20, transcendentals=2 * 2**20),
        name="layer",
    )(x, o, wo, gain2, bias2, lens, lse, g, wu, wd, qkv, of, wh, xs, h1)


def finish_kernel(
    x_ref, gain_ref, result_ref, dx_ref, fin_ref, gq_ref, out_ref, up_ref, down_ref, sums_ref,
    result, dx, gain_one, bias_one, gqkv, gout, gain_two, bias_two, gup, gdown,
):
    result[...] = result_ref[...]
    unit, inverse = norm_parts(x_ref[...].astype(F32))
    dh = jnp.concatenate([fin_ref[0], fin_ref[1]], axis=0).astype(F32)
    dx[...] = dx_ref[...] + norm_back(dh, gain_ref[...], unit, inverse)
    for slot in range(3):
        gqkv[:, slot * 128 : (slot + 1) * 128] = gq_ref[slot, 0].astype(F32) + gq_ref[slot, 1].astype(F32)
    gout[...] = out_ref[...]
    gup[...] = up_ref[...].astype(F32)
    gdown[...] = down_ref[...]
    for k, ref in enumerate((gain_one, bias_one, gain_two, bias_two)):
        ref[...] = sums_ref[k]


def finish(x, gain, *parts):
    line = S((1024,), F32)
    return pl.pallas_call(
        finish_kernel,
        out_shape=(
            S((256, 1024), BF), S((256, 1024), F32), line, line, S((256, 384), F32), S((256, 128), F32), line, line,
            S((256, 512), F32), S((1024, 128), F32),
        ),
        in_specs=[VM] * 10,
        out_specs=(VM,) * 10,
        compiler_params=pltpu.CompilerParams(vmem_limit_bytes=60 * 2**20),
        name="finish",
    )(x, gain, *parts)


def per_device_fast(
    tokens, article_lengths, gain_one, bias_one, w_qkv, w_out, gain_two, bias_two, w_up, w_down, cotangent
):
    x = tokens[0]
    lens = jnp.broadcast_to(article_lengths[0][:, None], (article_lengths.shape[1], 128))
    o, wo, wu, g, xs, h1, wh, qkv, of, lse, lens = attend(
        x, lens, gain_one[None], bias_one[None], w_qkv, w_out, w_up, cotangent[0]
    )
    parts = layer(x, o, wo, gain_two[None], bias_two[None], lens, lse, g, wu, w_down, qkv, of, wh, xs, h1)
    result, dx, *rest = finish(x, gain_one[None], *parts)
    return (result[None], dx[None], *rest)


def solution(mesh):
    one_pair = mesh.shape["seq"] == HEADS and mesh.shape["seg"] == 4
    return jax.shard_map(
        per_device_fast if one_pair else per_device,
        mesh=mesh,
        in_specs=(
            P("seg", "seq", None),
            P("seg", None),
            P(),
            P(),
            P("seg", None),
            P("seg", None),
            P(),
            P(),
            P("seg", None),
            P("seg", None),
            P("seg", "seq", None),
        ),
        out_specs=(
            P("seg", "seq", None),
            P("seg", "seq", None),
            P(),
            P(),
            P("seg", "seq"),
            P("seg", "seq"),
            P(),
            P(),
            P("seg", "seq"),
            P("seg", "seq"),
        ),
        check_vma=False,
    )
```

```python
import math

import jax
import jax.numpy as jnp
from jax import lax
from jax.experimental import pallas as pl
from jax.experimental.pallas import tpu as pltpu
from jax.sharding import PartitionSpec as P

HEADS = 8
HEAD_DIM = 128


def passed_along(block, axis, distance):
    devices = range(lax.axis_size(axis))
    route = [(i - distance, i) for i in devices if i - distance in devices]
    return lax.ppermute(block, axis, route)


def shifted(value, axis, by):
    size = lax.axis_size(axis)
    return lax.ppermute(value, axis, [(i, (i + by) % size) for i in range(size)])


def layer_norm(values, gain, bias):
    center = values - jnp.mean(values, axis=-1, keepdims=True)
    spread = jnp.mean(center * center, axis=-1, keepdims=True)
    return center * lax.rsqrt(spread + 1e-05) * gain + bias


def smooth_act(values):
    return jax.nn.gelu(values, approximate=True)


def article_numbers(lengths_row, positions):
    bounds = jnp.cumsum(lengths_row)
    return jnp.sum((positions[:, None] >= bounds[None, :]).astype(jnp.int32), axis=1)


def per_device(
    tokens,
    article_lengths,
    gain_one,
    bias_one,
    w_qkv,
    w_out,
    gain_two,
    bias_two,
    w_up,
    w_down,
    cotangent,
):
    tok_rows = tokens.shape[1]
    model_width = tokens.shape[2]
    head_count = HEADS
    head_size = HEAD_DIM
    scale = 1.0 / math.sqrt(head_size)
    blocks_seq = lax.axis_size("seq")
    my_place = lax.axis_index("seq")
    full_qkv, full_out, full_up, full_down = (
        lax.all_gather(w_qkv, "seg", axis=0, tiled=True),
        lax.all_gather(w_out, "seg", axis=0, tiled=True),
        lax.all_gather(w_up, "seg", axis=0, tiled=True),
        lax.all_gather(w_down, "seg", axis=0, tiled=True),
    )
    inputs = tokens[0].astype(jnp.float32)
    normed, norm_one_back = jax.vjp(layer_norm, inputs, gain_one, bias_one)
    normed_low = normed.astype(jnp.bfloat16)
    projected = jnp.dot(normed_low, full_qkv, preferred_element_type=jnp.float32).astype(
        jnp.bfloat16
    )
    query_low = projected[:, :model_width]
    key_low = projected[:, model_width : 2 * model_width]
    value_low = projected[:, 2 * model_width :]
    query_heads = query_low.reshape(tok_rows, head_count, head_size)
    lengths_row = article_lengths[0]
    positions = my_place * tok_rows + jnp.arange(tok_rows, dtype=jnp.int32)
    query_art = article_numbers(lengths_row, positions)

    def scores_of(key_block, source):
        key_pos = source * tok_rows + jnp.arange(tok_rows, dtype=jnp.int32)
        key_art = article_numbers(lengths_row, key_pos)
        allowed = (key_pos[None, :] <= positions[:, None]) & (
            key_art[None, :] == query_art[:, None]
        )
        raw = (
            jnp.einsum(
                "qhd,khd->hqk",
                query_heads,
                key_block.reshape(tok_rows, head_count, head_size),
                preferred_element_type=jnp.float32,
            )
            * scale
        )
        return jnp.where(allowed[None], raw, -1e30)

    def forward_block(state, key_block, value_block, source):

        def forward_work(operands):
            (top, total, accum), key_now, value_now = operands
            scores = scores_of(key_now, source)
            new_top = jnp.maximum(top, jnp.max(scores, axis=2))
            factor = jnp.exp(top - new_top)
            weights = jnp.exp(scores - new_top[:, :, None])
            total = total * factor + jnp.sum(weights, axis=2)
            gathered = jnp.einsum(
                "hqk,khd->qhd",
                weights.astype(jnp.bfloat16),
                value_now.reshape(tok_rows, head_count, head_size),
                preferred_element_type=jnp.float32,
            ).reshape(tok_rows, model_width)
            accum = accum * jnp.repeat(factor.T, head_size, axis=1) + gathered
            return (new_top, total, accum)

        def forward_keep(operands):
            return operands[0]

        return lax.cond(
            source <= my_place, forward_work, forward_keep, (state, key_block, value_block)
        )

    start_state = (
        jnp.full((head_count, tok_rows), -1e30, jnp.float32),
        jnp.zeros((head_count, tok_rows), jnp.float32),
        jnp.zeros((tok_rows, model_width), jnp.float32),
    )
    state = forward_block(start_state, key_low, value_low, my_place)

    def forward_step(step, carry):
        key_block, value_block, state_now = carry
        key_block, value_block = passed_along((key_block, value_block), "seq", 1)
        source = (my_place - step) % blocks_seq
        return (key_block, value_block, forward_block(state_now, key_block, value_block, source))

    _, _, state = lax.fori_loop(1, blocks_seq, forward_step, (key_low, value_low, state))
    top, total, accum = state
    log_total = top + jnp.log(total)
    attended = accum / jnp.repeat(total.T, head_size, axis=1)
    attended_low = attended.astype(jnp.bfloat16)
    middle = inputs + jnp.dot(attended_low, full_out, preferred_element_type=jnp.float32)
    normed_two, norm_two_back = jax.vjp(layer_norm, middle, gain_two, bias_two)
    normed_two_low = normed_two.astype(jnp.bfloat16)
    hidden = jnp.dot(normed_two_low, full_up, preferred_element_type=jnp.float32)
    activated, act_back = jax.vjp(smooth_act, hidden)
    activated_low = activated.astype(jnp.bfloat16)
    outputs = middle + jnp.dot(activated_low, full_down, preferred_element_type=jnp.float32)
    result = outputs.astype(jnp.bfloat16)[None]
    grad_top = cotangent[0].astype(jnp.float32)
    grad_top_low = cotangent[0]
    grad_down = jnp.einsum(
        "tf,td->fd", activated_low, grad_top_low, preferred_element_type=jnp.float32
    )
    grad_act = jnp.einsum("td,fd->tf", grad_top_low, full_down, preferred_element_type=jnp.float32)
    (grad_hidden,) = act_back(grad_act)
    grad_hidden_low = grad_hidden.astype(jnp.bfloat16)
    grad_up = jnp.einsum(
        "td,tf->df", normed_two_low, grad_hidden_low, preferred_element_type=jnp.float32
    )
    grad_normed_two = jnp.einsum(
        "tf,df->td", grad_hidden_low, full_up, preferred_element_type=jnp.float32
    )
    grad_mid_norm, grad_gain_two, grad_bias_two = norm_two_back(grad_normed_two)
    grad_middle = grad_top + grad_mid_norm
    grad_middle_low = grad_middle.astype(jnp.bfloat16)
    grad_out = jnp.einsum(
        "tc,td->cd", attended_low, grad_middle_low, preferred_element_type=jnp.float32
    )
    grad_att = jnp.einsum(
        "td,cd->tc", grad_middle_low, full_out, preferred_element_type=jnp.float32
    )
    grad_att_low = grad_att.astype(jnp.bfloat16)
    grad_att_heads = grad_att_low.reshape(tok_rows, head_count, head_size)
    offsets = jnp.sum(
        (grad_att_low.astype(jnp.float32) * attended).reshape(tok_rows, head_count, head_size),
        axis=2,
    ).T

    def backward_block(operands, source):

        def backward_work(inner):
            grad_query, grad_key, grad_value, key_now, value_now = inner
            key_heads = key_now.reshape(tok_rows, head_count, head_size)
            value_heads = value_now.reshape(tok_rows, head_count, head_size)
            probs = jnp.exp(scores_of(key_now, source) - log_total[:, :, None])
            probs_low = probs.astype(jnp.bfloat16)
            grad_value = grad_value + jnp.einsum(
                "hqk,qhd->khd", probs_low, grad_att_heads, preferred_element_type=jnp.float32
            ).reshape(tok_rows, model_width)
            grad_probs = jnp.einsum(
                "qhd,khd->hqk", grad_att_heads, value_heads, preferred_element_type=jnp.float32
            )
            grad_scores = (probs * (grad_probs - offsets[:, :, None])).astype(jnp.bfloat16)
            grad_query = (
                grad_query
                + jnp.einsum(
                    "hqk,khd->qhd", grad_scores, key_heads, preferred_element_type=jnp.float32
                ).reshape(tok_rows, model_width)
                * scale
            )
            grad_key = (
                grad_key
                + jnp.einsum(
                    "hqk,qhd->khd", grad_scores, query_heads, preferred_element_type=jnp.float32
                ).reshape(tok_rows, model_width)
                * scale
            )
            return (grad_query, grad_key, grad_value, key_now, value_now)

        def backward_keep(inner):
            return inner

        return lax.cond(source <= my_place, backward_work, backward_keep, operands)

    def backward_step(step, carry):
        source = (my_place - step) % blocks_seq
        grad_query, grad_key, grad_value, key_block, value_block = backward_block(carry, source)
        key_block, value_block = passed_along((key_block, value_block), "seq", 1)
        grad_key, grad_value = (
            shifted(grad_key.astype(jnp.bfloat16), "seq", 1).astype(grad_key.dtype),
            shifted(grad_value.astype(jnp.bfloat16), "seq", 1).astype(grad_value.dtype),
        )
        return (grad_query, grad_key, grad_value, key_block, value_block)

    zero_rows = jnp.zeros((tok_rows, model_width), jnp.float32)
    grad_query, grad_key, grad_value, _, _ = lax.fori_loop(
        0, blocks_seq, backward_step, (zero_rows, zero_rows, zero_rows, key_low, value_low)
    )
    grad_proj_low = jnp.concatenate([grad_query, grad_key, grad_value], axis=1).astype(jnp.bfloat16)
    grad_qkv = jnp.einsum(
        "tc,tk->ck", normed_low, grad_proj_low, preferred_element_type=jnp.float32
    )
    grad_normed = jnp.einsum(
        "tk,ck->tc", grad_proj_low, full_qkv, preferred_element_type=jnp.float32
    )
    grad_in_norm, grad_gain_one, grad_bias_one = norm_one_back(grad_normed)
    input_grad = (grad_middle + grad_in_norm)[None]
    part_qkv, part_out, part_up, part_down = (
        lax.psum_scatter(
            grad_qkv.astype(jnp.bfloat16), "seg", scatter_dimension=0, tiled=True
        ).astype(jnp.float32),
        lax.psum_scatter(
            grad_out.astype(jnp.bfloat16), "seg", scatter_dimension=0, tiled=True
        ).astype(jnp.float32),
        lax.psum_scatter(
            grad_up.astype(jnp.bfloat16), "seg", scatter_dimension=0, tiled=True
        ).astype(jnp.float32),
        lax.psum_scatter(
            grad_down.astype(jnp.bfloat16), "seg", scatter_dimension=0, tiled=True
        ).astype(jnp.float32),
    )
    sum_qkv, sum_out, sum_up, sum_down = (
        lax.psum_scatter(
            part_qkv.astype(jnp.bfloat16), "seq", scatter_dimension=1, tiled=True
        ).astype(jnp.float32),
        lax.psum_scatter(
            part_out.astype(jnp.bfloat16), "seq", scatter_dimension=1, tiled=True
        ).astype(jnp.float32),
        lax.psum_scatter(
            part_up.astype(jnp.bfloat16), "seq", scatter_dimension=1, tiled=True
        ).astype(jnp.float32),
        lax.psum_scatter(
            part_down.astype(jnp.bfloat16), "seq", scatter_dimension=1, tiled=True
        ).astype(jnp.float32),
    )
    sum_gain_one, sum_bias_one, sum_gain_two, sum_bias_two = lax.psum(
        (grad_gain_one, grad_bias_one, grad_gain_two, grad_bias_two), ("seq", "seg")
    )
    return (
        result,
        input_grad,
        sum_gain_one,
        sum_bias_one,
        sum_qkv,
        sum_out,
        sum_gain_two,
        sum_bias_two,
        sum_up,
        sum_down,
    )


MESH = pl.DeviceIdType.MESH
BF = jnp.bfloat16
F32 = jnp.float32
def dot_nn(a, b):
    return lax.dot_general(a, b, (((1,), (0,)), ((), ())), preferred_element_type=F32)


def dot_nt(a, b):
    return lax.dot_general(a, b, (((1,), (1,)), ((), ())), preferred_element_type=F32)


def dot_tn(a, b):
    return lax.dot_general(a, b, (((0,), (0,)), ((), ())), preferred_element_type=F32)


def remote(src, dst, send, recv, **place):
    return pltpu.make_async_remote_copy(
        src_ref=src, dst_ref=dst, send_sem=send, recv_sem=recv, device_id=place, device_id_type=MESH
    )


def norm_parts(values):
    center = values - jnp.mean(values, axis=-1, keepdims=True)
    spread = jnp.mean(center * center, axis=-1, keepdims=True)
    inverse = lax.rsqrt(spread + 1e-05)
    return center * inverse, inverse


def greet(q, s, transposed=False):
    y, c = s // 2, s % 2
    barrier = pltpu.get_barrier_semaphore()

    def signal(seq, seg):
        pl.semaphore_signal(barrier, 1, device_id={"seq": seq, "seg": seg}, device_id_type=MESH)

    for d in range(1, 8):
        for core in range(2):
            signal(lax.rem(q + d, 8), 2 * y + core)
    for d in range(1, 4):
        signal(q, lax.rem(s + d, 4))
    if transposed:
        turned = s != q // 2

        @pl.when(turned)
        def _():
            signal(2 * s + q % 2, q // 2)

        return lambda: pl.semaphore_wait(barrier, jnp.where(turned, 18, 17))
    return lambda: pl.semaphore_wait(barrier, 17)


def first_columns(lens, base, rows):
    place = base + lax.broadcasted_iota(jnp.int32, (rows, 1), 0)
    start = jnp.zeros((rows, 1), jnp.int32)
    bound = jnp.zeros((1, 1), jnp.int32)
    for i in range(lens.shape[0]):
        bound = bound + lens[i : i + 1, 0:1]
        start = jnp.where(place >= bound, bound, start)
    return start


def seen_mask(start, base_q, base_k, rows, columns):
    place = base_q + lax.broadcasted_iota(jnp.int32, (rows, columns), 0)
    key = base_k + lax.broadcasted_iota(jnp.int32, (rows, columns), 1)
    return (key <= place) & (key >= start)


def rows(k, n):
    return pl.ds(k * n if isinstance(k, int) else pl.multiple_of(k * n, n), n)


def lanes(k, n=128):
    return pl.ds(pl.multiple_of(k * n, n), n)


T = 256
HALF = 128


def places(z, x):
    zn, zc = z + 1 - 2 * (z % 2), (z + 2) % 4
    znc = (zn + 2) % 4
    here, near_z, near_x, cross = 2 * z + x, 2 * zn + x, 2 * z + 1 - x, 2 * zc + x
    blocks = (here, near_x, near_z, cross, 2 * znc + x, 2 * zc + 1 - x, 2 * zn + 1 - x, 2 * znc + 1 - x)
    return here, near_z, near_x, cross, blocks


def nth(values, k):
    out = values[0]
    for i, value in enumerate(values[1:], 1):
        out = jnp.where(k == i, value, out)
    return out


VM = pl.BlockSpec(memory_space=pltpu.VMEM)
HB = pl.BlockSpec(memory_space=pl.ANY)
S = jax.ShapeDtypeStruct
SM = pl.BlockSpec(memory_space=pltpu.SMEM)


def gelu_parts(u):
    root = math.sqrt(2.0 / math.pi)
    square = u * u
    t = jnp.tanh(root * (u + 0.044715 * (square * u)))
    value = 0.5 * u * (1.0 + t)
    slope = 0.5 * (1.0 + t) + 0.5 * u * (1.0 - t * t) * (root * (1.0 + 0.134145 * square))
    return value, slope


def norm_back(grad, gain, unit, inverse):
    through = grad * gain
    a = jnp.mean(through, axis=-1, keepdims=True)
    b = jnp.mean(through * unit, axis=-1, keepdims=True)
    return inverse * (through - a - unit * b)


def layer_kernel(
    x_ref, lens_ref, g_ref, wo_ref, gain_ref, bias_ref, gain2_ref, bias2_ref, wq_hbm, wu_hbm, wd_hbm,
    result_out, dx_v, fin_r, gq_r, gout_out, up_r, gdown_out, sums_out, xs_hbm, h1_hbm,
    g_v, wu_v, wd_v, wo_v, o_v, qkv_v, of_v, lse_v, wh_v, load_sem,
    keep_sem, ob, wq_s, lens_s, lens_r, qs, qr, ws, wr, xs_send, xs_recv, xu_recv, os_send, os_recv,
    middle, h2, big, mine, near_s, near_r, twin_s, twin_r, far_keep, far_s, far_r, do_v,
    hs, hr, ns, nr, ts, tr, fs, fr,
    pack, x_r, z_r, up_s, gxs, gxr, gzs, gzr, ups, upr,
    oc_r, oy_r, ox_r, oz_r, oo_r, cs, cr,
    doh, dq, dk, dv, dos, dor,
    fin_s, dcs, dcr, sts, str_, fns, fnr,
    gq, gq_b, gq_y, gqs, gqr,
    vec, vec_r, vs, vr,
):
    q, s = lax.axis_index("seq"), lax.axis_index("seg")
    z, x = q // 2, q % 2
    y, c = s // 2, s % 2
    sib = s + 1 - 2 * c
    across = (1 - y) * 2 + c
    corner = (1 - y) * 2 + 1 - c
    group = z // 2
    head = 4 * (z % 2) + 2 * x + c
    other_head = head + 1 - 2 * c
    home = c == group
    away = jnp.logical_not(home)
    column = 2 * y + group
    here, near_z, near_x, cross, blocks = places(z, x)
    scale = 1.0 / math.sqrt(HEAD_DIM)

    met = greet(q, s, True)

    picks = tuple(
        pltpu.make_async_copy(
            wq_hbm.at[:, lanes(8 * j + of_head)], wq_s.at[k, :, j * 128 : (j + 1) * 128], load_sem.at[10 + 3 * k + j]
        )
        for k, of_head in enumerate((head, other_head))
        for j in range(3)
    )
    loads = tuple(
        pltpu.make_async_copy(src, dst, load_sem.at[k])
        for k, (src, dst) in enumerate(((wd_hbm, wd_v), (wu_hbm.at[:, lanes(s, 1024)], wu_v.at[rows(s, T)])))
    )
    for copy in picks + loads:
        copy.start()
    for k in range(lens_ref.shape[1]):
        lens_s[k : k + 1] = jnp.full((1, 128), lens_ref[0, k], jnp.int32)

    @pl.when(home)
    def _():
        big[rows(q, T)] = x_ref[...]

    for copy in picks:
        copy.wait()
    wh_v[rows(s, T)] = wq_s[0]
    met()

    def half_rows(b, part):
        return big.at[pl.ds(pl.multiple_of(b * T + part * HALF, HALF), HALF)]

    def over_copy(part):
        src = x_ref.at[part * HALF : (part + 1) * HALF]
        return remote(src, half_rows(q, part), xs_send.at[24 + part], xs_recv.at[q], seq=cross, seg=2 * y + part)

    def twin_copy(part, recv, k):
        return remote(half_rows(q, part), half_rows(q, part), xs_send.at[24 + k], recv.at[q], seg=sib)

    twin_track, twin_rest = twin_copy(1 - c, xs_recv, 0), twin_copy(c, xu_recv, 1)

    @pl.when(home)
    def _():
        twin_track.start()
        twin_rest.start()

    @pl.when(jnp.logical_not(home))
    def _():
        over_copy(0).start()
        over_copy(1).start()

    mine_wh = wh_v.at[rows(s, T)]
    q_across = remote(wq_s.at[0], mine_wh, qs.at[0], qr.at[0], seg=across)
    q_sib = remote(wq_s.at[1], mine_wh, qs.at[1], qr.at[1], seg=sib)
    q_corner = remote(wq_s.at[1], mine_wh, qs.at[2], qr.at[2], seg=corner)
    l_sib = remote(lens_s, lens_r, qs.at[3], qr.at[3], seg=sib)
    first = (q_across, q_corner, q_sib, l_sib)
    for copy in first:
        copy.start()

    def x_copy(b, k, recv, **to):
        src = half_rows(b, c)
        return remote(src, src, xs_send.at[k], recv.at[b], **to)

    own_z, own_x = x_copy(q, 0, xs_recv, seq=near_z), x_copy(q, 8, xs_recv, seq=near_x)

    @pl.when(jnp.logical_not(home))
    def _():
        x_copy(q, 0, xs_recv, seq=q).wait_recv()

    own_z.start()
    own_x.start()

    def u_part(seg, part):
        return wu_v.at[pl.ds(pl.multiple_of(seg * T + part * HALF, HALF), HALF)]

    def o_part(seg, part):
        return wo_v.at[pl.ds(pl.multiple_of(seg * T + part * HALF, HALF), HALF)]

    u_far = tuple(
        remote(
            wu_hbm.at[pl.ds(pl.multiple_of(x * HALF, HALF), HALF), lanes(to, 1024)], u_part(s, x), ws.at[k], wr.at[k],
            seg=to,
        )
        for k, to in ((0, across), (1, corner))
    )
    u_over = tuple(
        remote(u_part(of_seg, x), u_part(of_seg, x), ws.at[11 + k], wr.at[11 + k], seq=near_x)
        for k, of_seg in ((0, across), (1, corner))
    )
    u_sib = remote(wu_hbm.at[:, lanes(sib, 1024)], wu_v.at[rows(s, T)], ws.at[2], wr.at[2], seg=sib)
    o_far = remote(
        wo_ref.at[pl.ds(pl.multiple_of(x * HALF, HALF), HALF)], o_part(s, x), ws.at[3], wr.at[3], seg=across
    )
    o_over = remote(o_part(across, x), o_part(across, x), ws.at[13], wr.at[13], seq=near_x)
    o_sib = remote(wo_ref, wo_v.at[rows(s, T)], ws.at[4], wr.at[4], seg=sib)
    o_pass = tuple(
        remote(o_part(across, part), o_part(across, part), ws.at[k], wr.at[k], seg=sib)
        for k, part in ((5, x), (14, 1 - x))
    )
    g_rows = lambda k, part: g_v.at[pl.ds(2 * T + part * T + k * HALF, HALF)]
    g_across = tuple(
        remote(g_ref.at[k * HALF : (k + 1) * HALF], g_rows(0, k), ws.at[6 + k], wr.at[6 + k], seg=across)
        for k in range(2)
    )
    g_sib = remote(g_ref, g_v.at[T : 2 * T], ws.at[8], wr.at[8], seg=sib)
    g_pass = tuple(remote(g_rows(0, k), g_rows(1, k), ws.at[9 + k], wr.at[9 + k], seg=sib) for k in range(2))
    wo_v[rows(s, T)] = wo_ref[...]
    g_v[0:T] = g_ref[...]
    for copy in u_far + (o_far,) + g_across:
        copy.start()
    for copy in first:
        copy.wait_recv()
    lens = jnp.where(home, lens_s[...], lens_r[...])

    gain, bias = gain_ref[...], bias_ref[...]

    def keep(b):
        at = rows(b, T)
        return (
            pltpu.make_async_copy(big.at[at], xs_hbm.at[at], keep_sem.at[b]),
            pltpu.make_async_copy(pack.at[b], h1_hbm.at[at], keep_sem.at[8 + b]),
        )

    def project(b):
        unit, _ = norm_parts(big[rows(b, T)].astype(F32))
        low = (unit * gain + bias).astype(BF)
        pack[b] = low
        qkv_v[rows(b, T)] = dot_nn(low, wh_v[...]).astype(BF)
        for copy in keep(b):
            copy.start()

    def track_step(k, _):
        b = nth(blocks, k)

        @pl.when(k < 8)
        def _():
            x_copy(b, 0, xs_recv, seq=q).wait_recv()

        @pl.when((k == 1) | (k == 3))
        def _():
            x_copy(b, k, xs_recv, seq=near_z).start()

        @pl.when((k == 3) | (k == 4))
        def _():
            x_copy(b, 8 + k, xs_recv, seq=near_x).start()

        @pl.when(k < 8)
        def _():
            x_copy(b, 16 + k, xu_recv, seg=sib).start()

        last = nth(blocks, k - 1)

        @pl.when((k > 1) | jnp.logical_not(home))
        def _():
            x_copy(last, 0, xu_recv, seg=sib).wait_recv()

        project(last)

        return 0

    lax.fori_loop(1, 6, track_step, 0)
    for arrived, copy in zip(u_far, u_over):
        arrived.wait_recv()
        copy.start()
    lax.fori_loop(6, 9, track_step, 0)
    o_far.wait_recv()
    o_over.start()
    o_pass[0].start()
    for copy in (u_sib, o_sib, g_sib):
        copy.start()

    def o_copy(i, sender):
        return remote(
            ob.at[i // 4, (i // 2) % 2, i % 2], o_v.at[:, lanes(sender)], os_send.at[i], os_recv.at[sender], seq=i, seg=column
        )

    o_mine = pltpu.make_async_copy(ob.at[group, z % 2, x], o_v.at[:, lanes(head)], os_recv.at[head])
    for i in (4, 5, 6, 7, 0, 1, 2, 3):
        n = (i + 1) * T
        start = first_columns(lens, i * T, T)
        scores = dot_nt(qkv_v[i * T : n, :128], qkv_v[:n, 128:256]) * scale
        scores = jnp.where(seen_mask(start, i * T, 0, T, n), scores, -1e30)
        top = jnp.max(scores, axis=1, keepdims=True)
        weights = jnp.exp(scores - top)
        total = jnp.sum(weights, axis=1, keepdims=True)
        mixed = dot_nn(weights.astype(BF), qkv_v[:n, 256:384]) / total
        of_v[i * T : n] = mixed
        lse_v[:, i : i + 1] = top + jnp.log(total)
        ob[i // 4, (i // 2) % 2, i % 2] = mixed.astype(BF)
        here = (q == i) & home

        @pl.when(jnp.logical_not(here))
        def _():
            o_copy(i, head).start()

        @pl.when(here)
        def _():
            o_mine.start()

    o_over.wait_recv()
    o_pass[1].start()
    for arrived, copy in zip(g_across, g_pass):
        arrived.wait_recv()
        copy.start()

    for i in range(8):
        o_copy(i, i).wait_recv()
    for copy in o_pass + (o_sib,):
        copy.wait_recv()

    value = x_ref[...].astype(F32) + dot_nn(o_v[...], wo_v[...])
    middle[...] = value
    unit, _ = norm_parts(value)
    h2[0:T] = (unit * gain2_ref[...] + bias2_ref[...]).astype(BF)

    def far_rows(ref, part, k):
        return ref.at[pl.ds(2 * T + k * T + part * HALF, HALF)]

    h_far = tuple(
        remote(h2.at[k * HALF : (k + 1) * HALF], far_rows(h2, 0, k), hs.at[k], hr.at[k], seg=across)
        for k in range(2)
    )
    h_pass = tuple(
        remote(far_rows(h2, 0, k), far_rows(h2, 1, k), hs.at[2 + k], hr.at[2 + k], seg=sib) for k in range(2)
    )
    h_sib = remote(h2.at[0:T], h2.at[T : 2 * T], hs.at[4], hr.at[4], seg=sib)
    for copy in h_far + (h_sib,):
        copy.start()
    for copy in loads:
        copy.wait()
    for copy in u_over + g_pass + (u_sib, g_sib):
        copy.wait_recv()
    for b in range(8):
        for copy in keep(b):
            copy.wait()
    for k in range(1, 8):
        if k in (1, 3):
            x_copy(blocks[k], k, xs_recv, seq=near_z).wait_send()
        if k in (3, 4):
            x_copy(blocks[k], 8 + k, xs_recv, seq=near_x).wait_send()
        x_copy(blocks[k], 16 + k, xu_recv, seg=sib).wait_send()

    @pl.when(home)
    def _():
        twin_track.wait_send()
        twin_rest.wait_send()

    @pl.when(jnp.logical_not(home))
    def _():
        over_copy(0).wait_send()
        over_copy(1).wait_send()

    for i in range(8):
        @pl.when(jnp.logical_not((q == i) & home))
        def _():
            o_copy(i, head).wait_send()

    for copy in first + u_far + u_over + o_pass + g_across + g_pass + (u_sib, o_far, o_over, o_sib, g_sib, own_z, own_x):
        copy.wait_send()

    def work(part):
        at = slice(part * T, (part + 1) * T)
        value, slope = gelu_parts(dot_nn(h2[at], wu_v[...]))
        low = value.astype(BF)
        big[at] = low
        du = (slope * dot_nt(g_v[at], wd_v[...])).astype(BF)
        big[4 * T + part * T : 4 * T + (part + 1) * T] = du
        return dot_nt(du, wu_v[...]), dot_nn(low, wd_v[...])

    near = tuple(remote(near_s.at[k], near_r.at[k], ns.at[k], nr.at[k], seg=sib) for k in range(2))
    twin = tuple(
        tuple(remote(twin_s.at[k, n], twin_r.at[k, n], ts.at[2 * k + n], tr.at[2 * k + n], seg=sib) for n in range(2))
        for k in range(2)
    )
    far = tuple(
        tuple(remote(far_s.at[k, n], far_r.at[k, n], fs.at[2 * k + n], fr.at[2 * k + n], seg=across) for n in range(2))
        for k in range(2)
    )

    def send_twin(n, parts):
        for k in range(2):
            far_keep[k] = parts[k][:HALF]
            twin_s[k, n] = parts[k][HALF:].astype(BF)
            twin[k][n].start()

    def send_far(n):
        for k in range(2):
            twin[k][n].wait_recv()
            far_s[k, n] = (far_keep[k] + twin_r[k, n].astype(F32)).astype(BF)
            if k == 0:
                far[k][n].start()

    parts = work(0)
    for k in range(2):
        mine[k] = parts[k]
    h_sib.wait_recv()
    parts = work(1)
    for k in range(2):
        near_s[k] = parts[k].astype(BF)
        near[k].start()
    h_far[0].wait_recv()
    h_pass[0].start()
    h_pass[0].wait_recv()
    send_twin(0, work(2))
    h_far[1].wait_recv()
    h_pass[1].start()
    send_far(0)
    h_pass[1].wait_recv()
    send_twin(1, work(3))
    send_far(1)

    for j in range(4):
        down = dot_tn(big[: 4 * T, j * T : (j + 1) * T], g_v[...]).astype(BF)
        for k in range(8):
            pack[k, :, 512 + j * 128 : 640 + j * 128] = down[:, k * 128 : (k + 1) * 128]
    for j in range(4):
        up = dot_tn(h2[:, j * T : (j + 1) * T], big[4 * T :]).astype(BF)
        for k in range(2):
            pack[2 * j + k, :, :512] = up[:, k * 512 : (k + 1) * 512]

    def gx_copy(d):
        return remote(pack.at[2 * d + 1 - x], x_r.at[d], gxs.at[d], gxr.at[d], seq=near_x)

    zn, zc = z + 1 - 2 * (z % 2), (z + 2) % 4
    znc = (zn + 2) % 4
    gx_copy(znc).start()
    gx_copy(zc).start()

    near[0].wait_recv()
    far[0][0].wait_recv()
    far[0][1].wait_recv()
    grad = mine[0] + near_r[0].astype(F32) + jnp.concatenate([far_r[0, 0], far_r[0, 1]], axis=0).astype(F32)
    unit, inverse = norm_parts(middle[...])
    vec[...] = jnp.zeros_like(vec)
    vec[2:3] = jnp.sum(grad * unit, axis=0, keepdims=True)
    vec[3:4] = jnp.sum(grad, axis=0, keepdims=True)
    dx = g_v[0:T].astype(F32) + norm_back(grad, gain2_ref[...], unit, inverse)
    dx_v[...] = dx
    dy = dx.astype(BF)
    do_v[...] = dot_nt(dy, wo_v[...]).astype(BF)

    def do_copy(h, block):
        return remote(
            do_v.at[:, h * 128 : (h + 1) * 128], doh.at[rows(block, T)], dos.at[h], dor.at[block],
            seq=2 * (2 * c + h // 4) + (h // 2) % 2, seg=2 * y + h % 2,
        )

    do_mine = pltpu.make_async_copy(do_v.at[:, lanes(head)], doh.at[rows(q, T)], dor.at[q])
    for h in range(8):
        self_too = (head == h) & home

        @pl.when(jnp.logical_not(self_too))
        def _():
            do_copy(h, q).start()

        @pl.when(self_too)
        def _():
            do_mine.start()

    for copy in h_far + h_pass + (h_sib,):
        copy.wait_send()
    h2[...] = dot_tn(o_v[...], dy).astype(BF)

    def out_rows(part, core):
        return h2.at[rows(2 * part + core, T)]

    out_core = tuple(remote(out_rows(k, 1 - c), oc_r.at[k], cs.at[5 + k], cr.at[5 + k], seg=sib) for k in range(2))
    for copy in out_core:
        copy.start()
    for part in range(2):
        out_core[part].wait_recv()
        oc_r[part] = (oc_r[part].astype(F32) + out_rows(part, c)[...].astype(F32)).astype(BF)
    out_y = remote(oc_r.at[1 - y], oy_r, cs.at[1], cr.at[1], seg=across)
    out_y.start()
    far[1][0].start()
    far[1][1].start()

    def come(into, recv, slot):
        return remote(into.at[slot], into.at[slot], recv.at[slot], recv.at[slot], seq=near_x)

    def gz_copy(k, d, to):
        return remote(x_r.at[d], z_r.at[k], gzs.at[k], gzr.at[k], seq=to)

    gz = (gz_copy(0, znc, near_z), gz_copy(1, zn, near_z), gz_copy(2, zc, cross))

    def pack_sum(d):
        gx_copy(d).wait_recv()
        return pack[2 * d + x].astype(F32) + x_r[d].astype(F32)

    x_r[znc] = pack_sum(znc).astype(BF)
    gz[0].start()

    gx_copy(zn).start()

    dk[...] = jnp.zeros_like(dk)
    dv[...] = jnp.zeros_like(dv)
    for i in range(8):
        do_copy(0, i).wait_recv()
        top = i * T
        start = first_columns(lens, top, T)
        query = qkv_v[top : top + T, :128]
        grad = doh[top : top + T]
        delta = jnp.sum(grad.astype(F32) * of_v[top : top + T], axis=1, keepdims=True)
        log_total = lse_v[:, i : i + 1]
        total = jnp.zeros((T, 128), F32)
        for base in range(0, top + T, 1024):
            n = min(1024, top + T - base)
            keys = qkv_v[base : base + n, 128:256]
            probs = jnp.exp(dot_nt(query, keys) * scale - log_total)
            probs = jnp.where(seen_mask(start, top, base, T, n), probs, 0.0)
            dp = dot_nt(grad, qkv_v[base : base + n, 256:384])
            ds = (probs * (dp - delta)).astype(BF)
            dv[base : base + n] += dot_tn(probs.astype(BF), grad)
            dk[base : base + n] += dot_tn(ds, query)
            total += dot_nn(ds, keys)
        dq[top : top + T] = total

    gz[0].wait_recv()
    x_r[zc] = (pack_sum(zc) + z_r[0].astype(F32)).astype(BF)
    gz[2].start()

    gq[...] = jnp.zeros_like(gq)
    own_a, other_xa, other_za, own_b, other_zb, other_xb, diag_a, diag_b = blocks
    order = (diag_a, diag_b, other_za, other_xb, other_xa, other_zb, own_a, own_b)

    def x_load(i):
        return pltpu.make_async_copy(xs_hbm.at[rows(nth(order, i), T)], wu_v.at[rows(i % 2, T)], load_sem.at[2 + i % 2])

    def h_load(i):
        return pltpu.make_async_copy(h1_hbm.at[rows(nth(order, i), T)], wu_v.at[rows(2 + i % 2, T)], load_sem.at[4 + i % 2])

    def dhc_copy(b):
        return remote(
            big.at[pl.ds(pl.multiple_of(b * T + (1 - c) * HALF, HALF), HALF)], wo_v.at[rows(b, HALF)], dcs.at[b], dcr.at[b], seg=sib
        )

    def half(b):
        return big.at[pl.ds(pl.multiple_of(b * T + c * HALF, HALF), HALF)]

    def step_copy(k, b, to):
        return remote(wo_v.at[rows(b, HALF)], wd_v.at[rows(k, HALF)], sts.at[k], str_.at[k], seq=to)

    steps = (
        step_copy(0, diag_a, near_z), step_copy(1, diag_b, near_x), step_copy(2, other_za, near_z),
        step_copy(3, other_xb, near_x), step_copy(4, other_xa, near_x), step_copy(5, other_zb, near_z),
    )
    x_load(0).start()
    h_load(0).start()

    def grads_at(at):
        return jnp.concatenate([dq[at] * scale, dk[at] * scale, dv[at]], axis=1).astype(BF)

    def block_step(i, _):
        @pl.when(i < 8)
        def _():
            b = nth(order, i)

            at = rows(b, T)
            big[at] = dot_nt(grads_at(at), wh_v[...]).astype(BF)
            dhc_copy(b).start()

        @pl.when(i > 0)
        def _():
            b = nth(order, i - 1)
            dhc_copy(b).wait_recv()
            wo_v[rows(b, HALF)] = (half(b)[...].astype(F32) + wo_v[rows(b, HALF)].astype(F32)).astype(BF)
            for k in range(4):
                @pl.when(i == k + 1)
                def _():
                    steps[k].start()

        return 0

    lax.fori_loop(0, 9, block_step, 0)

    def sum_step(i, _):
        @pl.when(i < 7)
        def _():
            x_load(i + 1).start()
            h_load(i + 1).start()

        at = rows(nth(order, i), T)
        dh = big[at].astype(F32)
        x_load(i).wait()
        h_load(i).wait()
        gq[...] += dot_tn(wu_v[rows(2 + i % 2, T)], grads_at(at))
        unit, _ = norm_parts(wu_v[rows(i % 2, T)].astype(F32))
        vec[0:1] += jnp.sum(dh * unit, axis=0, keepdims=True)
        vec[1:2] += jnp.sum(dh, axis=0, keepdims=True)
        return 0

    lax.fori_loop(0, 8, sum_step, 0)
    for k, b in ((5, other_zb), (4, other_xa)):
        steps[k - 4].wait_recv()
        wo_v[rows(b, HALF)] = (wo_v[rows(b, HALF)].astype(F32) + wd_v[(k - 4) * HALF : (k - 3) * HALF].astype(F32)).astype(BF)
        steps[k].start()

    x_r[zn] = pack_sum(zn).astype(BF)
    gz[1].start()

    out_y.wait_recv()
    out = (oc_r[y].astype(F32) + oy_r[...].astype(F32)).astype(BF)
    for k in range(8):
        ob[k // 4, (k // 2) % 2, k % 2] = out[:, k * 128 : (k + 1) * 128]
    out_x = remote(ob.at[:, :, 1 - x], ox_r, cs.at[2], cr.at[2], seq=near_x)
    out_x.start()
    gx_copy(z).start()

    gq_b[...] = gq[...].astype(BF).reshape(2, 2, T, 384)
    q_y = remote(gq_b.at[1 - y], gq_y, gqs.at[0], gqr.at[0], seg=across)
    q_y.start()
    v_core = remote(vec, vec_r.at[0], vs.at[8], vr.at[8], seg=sib)
    v_core.start()
    v_core.wait()
    vec[...] += vec_r[0]
    v_y = remote(vec, vec_r.at[1], vs.at[9], vr.at[9], seg=across)
    v_y.start()
    for k, b, pair in ((0, own_a, (2, 4)), (1, own_b, (3, 5))):
        for n in pair:
            steps[n].wait_recv()
        fin_s[k] = (
            wo_v[rows(b, HALF)].astype(F32) + wd_v[rows(pair[0], HALF)].astype(F32)
            + wd_v[rows(pair[1], HALF)].astype(F32)
        ).astype(BF)
    fin_over = remote(fin_s.at[1], fin_r.at[c], fns.at[0], fnr.at[c], seq=cross, seg=column)
    fin_twin = remote(fin_s.at[0], fin_r.at[c], fns.at[1], fnr.at[c], seg=sib)
    fin_own = pltpu.make_async_copy(fin_s.at[0], fin_r.at[c], fnr.at[c])
    fin_over.start()

    @pl.when(away)
    def _():
        fin_twin.start()

    @pl.when(home)
    def _():
        fin_own.start()

    v_y.wait()
    vec[...] += vec_r[1]

    def v_copy(b, sender):
        return remote(vec, vec_r.at[2 + sender], vs.at[b], vr.at[sender], seq=b)

    for b in range(8):
        @pl.when(q != b)
        def _():
            v_copy(b, q).start()

    q_y.wait_recv()
    gq_y[...] = (gq_y[...].astype(F32) + gq_b[y].astype(F32)).astype(BF)

    def column_copy(part, j):
        place = 8 * j + head
        owner, slot = place // 3, place % 3
        src = gq_y.at[part, :, j * 128 : (j + 1) * 128]
        copy = remote(
            src, gq_r.at[slot, group], gqs.at[1 + 3 * part + j], gqr.at[1 + 2 * slot + group],
            seq=owner, seg=2 * y + part,
        )
        local = pltpu.make_async_copy(src, gq_r.at[slot, group], gqr.at[1 + 2 * slot + group])
        return (owner == q) & (c == part), copy, local

    columns = tuple(column_copy(part, j) for part in range(2) for j in range(3))
    out_x.wait_recv()
    ox_r[...] = (ox_r[...].astype(F32) + ob[:, :, x].astype(F32)).astype(BF)
    out_z = remote(ox_r.at[:, 1 - z % 2], oz_r, cs.at[3], cr.at[3], seq=near_z)
    out_z.start()
    for self_too, copy, local in columns:
        @pl.when(jnp.logical_not(self_too))
        def _():
            copy.start()

        @pl.when(self_too)
        def _():
            local.start()

    out_z.wait_recv()
    oz_r[...] = (oz_r[...].astype(F32) + ox_r[:, z % 2].astype(F32)).astype(BF)
    out_o = remote(oz_r.at[1 - group], oo_r, cs.at[4], cr.at[4], seq=cross)
    out_o.start()

    total = pack_sum(z)
    for k in (1, 2):
        gz[k].wait_recv()
        total = total + z_r[k].astype(F32)
    up_s[...] = total[:, :512].astype(BF)
    turned = s != z
    up_turn = remote(up_s, up_r, ups, upr, seq=2 * s + x, seg=z)
    up_own = pltpu.make_async_copy(up_s, up_r, upr)

    @pl.when(turned)
    def _():
        up_turn.start()

    @pl.when(jnp.logical_not(turned))
    def _():
        up_own.start()

    for j in range(4):
        gdown_out[j * T : (j + 1) * T] = total[:, 512 + j * 128 : 640 + j * 128]
    vec_r[2 + q] = vec[...]
    for b in range(8):
        @pl.when(q != b)
        def _():
            v_copy(b, b).wait_recv()

    vec_sum = vec_r[2]
    for b in range(1, 8):
        vec_sum = vec_sum + vec_r[2 + b]
    out_o.wait_recv()
    gout_out[...] = oz_r[group].astype(F32) + oo_r[...].astype(F32)
    sums_out[...] = vec_sum
    for slot in range(3):
        for part in range(2):
            pltpu.make_async_copy(gq_r.at[slot, part], gq_r.at[slot, part], gqr.at[1 + 2 * slot + part]).wait()
    near[1].wait_recv()
    far[1][0].wait_recv()
    far[1][1].wait_recv()
    result_out[...] = (
        middle[...] + mine[1] + near_r[1].astype(F32)
        + jnp.concatenate([far_r[1, 0], far_r[1, 1]], axis=0).astype(F32)
    ).astype(BF)
    for k in range(2):
        come(fin_r, fnr, k).wait_recv()
    up_own.wait()

    for h in range(8):
        @pl.when(jnp.logical_not((head == h) & home))
        def _():
            do_copy(h, q).wait_send()

    for b in range(8):
        dhc_copy(b).wait_send()

        @pl.when(q != b)
        def _():
            v_copy(b, q).wait_send()

    for d in range(4):
        gx_copy(d).wait_send()
    for copy in out_core + (out_y, out_x, out_z, out_o, q_y, fin_over) + near + steps + gz:
        copy.wait_send()
    for k in range(2):
        for n in range(2):
            twin[k][n].wait_send()
            far[k][n].wait_send()

    @pl.when(away)
    def _():
        fin_twin.wait_send()

    @pl.when(turned)
    def _():
        up_turn.wait_send()

    for self_too, copy, _ in columns:
        @pl.when(jnp.logical_not(self_too))
        def _():
            copy.wait_send()


def layer(x, lens, g, wo, gain, bias, gain2, bias2, wq, wu, wd):
    dma = pltpu.SemaphoreType.DMA
    low = lambda *shape: pltpu.VMEM(shape, BF)
    wide = lambda *shape: pltpu.VMEM(shape, F32)
    return pl.pallas_call(
        layer_kernel,
        out_shape=(
            S((256, 1024), BF), S((256, 1024), F32), S((2, 128, 1024), BF), S((3, 2, 256, 128), BF),
            S((256, 128), F32), S((256, 512), BF), S((1024, 128), F32), S((8, 1024), F32),
            S((2048, 1024), BF), S((2048, 1024), BF),
        ),
        in_specs=[VM, SM] + [VM] * 6 + [HB] * 3,
        out_specs=(VM,) * 8 + (HB,) * 2,
        scratch_shapes=[
            low(1024, 1024), low(1024, 1024), low(1024, 1024), low(1024, 1024), low(256, 1024), low(2048, 384),
            wide(2048, 128), wide(256, 8), low(1024, 384), dma((16,)),
            dma((16,)), low(2, 2, 2, 256, 128), low(2, 256, 384), pltpu.VMEM((8, 128), jnp.int32),
            pltpu.VMEM((8, 128), jnp.int32), dma((4,)), dma((4,)), dma((15,)), dma((15,)),
            dma((26,)), dma((8,)), dma((8,)), dma((8,)), dma((8,)),
            wide(256, 1024), low(1024, 1024), low(2048, 1024), wide(2, 256, 1024),
            low(2, 256, 1024), low(2, 256, 1024), low(2, 2, 128, 1024), low(2, 2, 128, 1024), wide(2, 128, 1024),
            low(2, 2, 128, 1024), low(2, 2, 128, 1024), low(256, 1024),
            dma((5,)), dma((5,)), dma((2,)), dma((2,)), dma((4,)), dma((4,)), dma((4,)), dma((4,)),
            low(8, 256, 1024), low(4, 256, 1024), low(3, 256, 1024), low(256, 512),
            dma((4,)), dma((4,)), dma((3,)), dma((3,)), dma, dma,
            low(2, 256, 1024), low(256, 1024), low(2, 2, 256, 128),
            low(2, 256, 128), low(256, 128), dma((7,)), dma((7,)),
            low(2048, 128), wide(2048, 128), wide(2048, 128), wide(2048, 128), dma((8,)), dma((8,)),
            low(2, 128, 1024),
            dma((8,)), dma((8,)), dma((6,)), dma((6,)), dma((2,)), dma((2,)),
            wide(1024, 384), low(2, 2, 256, 384), low(2, 256, 384),
            dma((7,)), dma((7,)),
            wide(8, 1024), wide(10, 8, 1024), dma((10,)), dma((10,)),
        ],
        compiler_params=pltpu.CompilerParams(
            collective_id=1, has_side_effects=True, vmem_limit_bytes=63 * 2**20
        ),
        cost_estimate=pl.CostEstimate(flops=2 * 10**10, bytes_accessed=40 * 2**20, transcendentals=2 * 2**20),
        name="layer",
    )(x, lens, g, wo, gain, bias, gain2, bias2, wq, wu, wd)


def finish_kernel(
    x_ref, gain_ref, result_ref, dx_ref, fin_ref, gq_ref, out_ref, up_ref, down_ref, sums_ref,
    result, dx, gain_one, bias_one, gqkv, gout, gain_two, bias_two, gup, gdown,
):
    result[...] = result_ref[...]
    unit, inverse = norm_parts(x_ref[...].astype(F32))
    dh = jnp.concatenate([fin_ref[0], fin_ref[1]], axis=0).astype(F32)
    dx[...] = dx_ref[...] + norm_back(dh, gain_ref[...], unit, inverse)
    for slot in range(3):
        gqkv[:, slot * 128 : (slot + 1) * 128] = gq_ref[slot, 0].astype(F32) + gq_ref[slot, 1].astype(F32)
    gout[...] = out_ref[...]
    gup[...] = up_ref[...].astype(F32)
    gdown[...] = down_ref[...]
    for k, ref in enumerate((gain_one, bias_one, gain_two, bias_two)):
        ref[...] = sums_ref[k]


def finish(x, gain, *parts):
    line = S((1024,), F32)
    return pl.pallas_call(
        finish_kernel,
        out_shape=(
            S((256, 1024), BF), S((256, 1024), F32), line, line, S((256, 384), F32), S((256, 128), F32), line, line,
            S((256, 512), F32), S((1024, 128), F32),
        ),
        in_specs=[VM] * 10,
        out_specs=(VM,) * 10,
        compiler_params=pltpu.CompilerParams(vmem_limit_bytes=60 * 2**20),
        name="finish",
    )(x, gain, *parts)


def per_device_fast(
    tokens, article_lengths, gain_one, bias_one, w_qkv, w_out, gain_two, bias_two, w_up, w_down, cotangent
):
    x = tokens[0]
    *parts, _, _ = layer(
        x, article_lengths, cotangent[0], w_out, gain_one[None], bias_one[None], gain_two[None], bias_two[None],
        w_qkv, w_up, w_down,
    )
    result, dx, *rest = finish(x, gain_one[None], *parts)
    return (result[None], dx[None], *rest)


def solution(mesh):
    one_pair = mesh.shape["seq"] == HEADS and mesh.shape["seg"] == 4
    return jax.shard_map(
        per_device_fast if one_pair else per_device,
        mesh=mesh,
        in_specs=(
            P("seg", "seq", None),
            P("seg", None),
            P(),
            P(),
            P("seg", None),
            P("seg", None),
            P(),
            P(),
            P("seg", None),
            P("seg", None),
            P("seg", "seq", None),
        ),
        out_specs=(
            P("seg", "seq", None),
            P("seg", "seq", None),
            P(),
            P(),
            P("seg", "seq"),
            P("seg", "seq"),
            P(),
            P(),
            P("seg", "seq"),
            P("seg", "seq"),
        ),
        check_vma=False,
    )
```

```python
import math

import jax
import jax.numpy as jnp
from jax import lax
from jax.experimental import pallas as pl
from jax.experimental.pallas import tpu as pltpu
from jax.sharding import PartitionSpec as P

HEADS = 8
HEAD_DIM = 128


def passed_along(block, axis, distance):
    devices = range(lax.axis_size(axis))
    route = [(i - distance, i) for i in devices if i - distance in devices]
    return lax.ppermute(block, axis, route)


def shifted(value, axis, by):
    size = lax.axis_size(axis)
    return lax.ppermute(value, axis, [(i, (i + by) % size) for i in range(size)])


def layer_norm(values, gain, bias):
    center = values - jnp.mean(values, axis=-1, keepdims=True)
    spread = jnp.mean(center * center, axis=-1, keepdims=True)
    return center * lax.rsqrt(spread + 1e-05) * gain + bias


def smooth_act(values):
    return jax.nn.gelu(values, approximate=True)


def article_numbers(lengths_row, positions):
    bounds = jnp.cumsum(lengths_row)
    return jnp.sum((positions[:, None] >= bounds[None, :]).astype(jnp.int32), axis=1)


def per_device(
    tokens,
    article_lengths,
    gain_one,
    bias_one,
    w_qkv,
    w_out,
    gain_two,
    bias_two,
    w_up,
    w_down,
    cotangent,
):
    tok_rows = tokens.shape[1]
    model_width = tokens.shape[2]
    head_count = HEADS
    head_size = HEAD_DIM
    scale = 1.0 / math.sqrt(head_size)
    blocks_seq = lax.axis_size("seq")
    my_place = lax.axis_index("seq")
    full_qkv, full_out, full_up, full_down = (
        lax.all_gather(w_qkv, "seg", axis=0, tiled=True),
        lax.all_gather(w_out, "seg", axis=0, tiled=True),
        lax.all_gather(w_up, "seg", axis=0, tiled=True),
        lax.all_gather(w_down, "seg", axis=0, tiled=True),
    )
    inputs = tokens[0].astype(jnp.float32)
    normed, norm_one_back = jax.vjp(layer_norm, inputs, gain_one, bias_one)
    normed_low = normed.astype(jnp.bfloat16)
    projected = jnp.dot(normed_low, full_qkv, preferred_element_type=jnp.float32).astype(
        jnp.bfloat16
    )
    query_low = projected[:, :model_width]
    key_low = projected[:, model_width : 2 * model_width]
    value_low = projected[:, 2 * model_width :]
    query_heads = query_low.reshape(tok_rows, head_count, head_size)
    lengths_row = article_lengths[0]
    positions = my_place * tok_rows + jnp.arange(tok_rows, dtype=jnp.int32)
    query_art = article_numbers(lengths_row, positions)

    def scores_of(key_block, source):
        key_pos = source * tok_rows + jnp.arange(tok_rows, dtype=jnp.int32)
        key_art = article_numbers(lengths_row, key_pos)
        allowed = (key_pos[None, :] <= positions[:, None]) & (
            key_art[None, :] == query_art[:, None]
        )
        raw = (
            jnp.einsum(
                "qhd,khd->hqk",
                query_heads,
                key_block.reshape(tok_rows, head_count, head_size),
                preferred_element_type=jnp.float32,
            )
            * scale
        )
        return jnp.where(allowed[None], raw, -1e30)

    def forward_block(state, key_block, value_block, source):

        def forward_work(operands):
            (top, total, accum), key_now, value_now = operands
            scores = scores_of(key_now, source)
            new_top = jnp.maximum(top, jnp.max(scores, axis=2))
            factor = jnp.exp(top - new_top)
            weights = jnp.exp(scores - new_top[:, :, None])
            total = total * factor + jnp.sum(weights, axis=2)
            gathered = jnp.einsum(
                "hqk,khd->qhd",
                weights.astype(jnp.bfloat16),
                value_now.reshape(tok_rows, head_count, head_size),
                preferred_element_type=jnp.float32,
            ).reshape(tok_rows, model_width)
            accum = accum * jnp.repeat(factor.T, head_size, axis=1) + gathered
            return (new_top, total, accum)

        def forward_keep(operands):
            return operands[0]

        return lax.cond(
            source <= my_place, forward_work, forward_keep, (state, key_block, value_block)
        )

    start_state = (
        jnp.full((head_count, tok_rows), -1e30, jnp.float32),
        jnp.zeros((head_count, tok_rows), jnp.float32),
        jnp.zeros((tok_rows, model_width), jnp.float32),
    )
    state = forward_block(start_state, key_low, value_low, my_place)

    def forward_step(step, carry):
        key_block, value_block, state_now = carry
        key_block, value_block = passed_along((key_block, value_block), "seq", 1)
        source = (my_place - step) % blocks_seq
        return (key_block, value_block, forward_block(state_now, key_block, value_block, source))

    _, _, state = lax.fori_loop(1, blocks_seq, forward_step, (key_low, value_low, state))
    top, total, accum = state
    log_total = top + jnp.log(total)
    attended = accum / jnp.repeat(total.T, head_size, axis=1)
    attended_low = attended.astype(jnp.bfloat16)
    middle = inputs + jnp.dot(attended_low, full_out, preferred_element_type=jnp.float32)
    normed_two, norm_two_back = jax.vjp(layer_norm, middle, gain_two, bias_two)
    normed_two_low = normed_two.astype(jnp.bfloat16)
    hidden = jnp.dot(normed_two_low, full_up, preferred_element_type=jnp.float32)
    activated, act_back = jax.vjp(smooth_act, hidden)
    activated_low = activated.astype(jnp.bfloat16)
    outputs = middle + jnp.dot(activated_low, full_down, preferred_element_type=jnp.float32)
    result = outputs.astype(jnp.bfloat16)[None]
    grad_top = cotangent[0].astype(jnp.float32)
    grad_top_low = cotangent[0]
    grad_down = jnp.einsum(
        "tf,td->fd", activated_low, grad_top_low, preferred_element_type=jnp.float32
    )
    grad_act = jnp.einsum("td,fd->tf", grad_top_low, full_down, preferred_element_type=jnp.float32)
    (grad_hidden,) = act_back(grad_act)
    grad_hidden_low = grad_hidden.astype(jnp.bfloat16)
    grad_up = jnp.einsum(
        "td,tf->df", normed_two_low, grad_hidden_low, preferred_element_type=jnp.float32
    )
    grad_normed_two = jnp.einsum(
        "tf,df->td", grad_hidden_low, full_up, preferred_element_type=jnp.float32
    )
    grad_mid_norm, grad_gain_two, grad_bias_two = norm_two_back(grad_normed_two)
    grad_middle = grad_top + grad_mid_norm
    grad_middle_low = grad_middle.astype(jnp.bfloat16)
    grad_out = jnp.einsum(
        "tc,td->cd", attended_low, grad_middle_low, preferred_element_type=jnp.float32
    )
    grad_att = jnp.einsum(
        "td,cd->tc", grad_middle_low, full_out, preferred_element_type=jnp.float32
    )
    grad_att_low = grad_att.astype(jnp.bfloat16)
    grad_att_heads = grad_att_low.reshape(tok_rows, head_count, head_size)
    offsets = jnp.sum(
        (grad_att_low.astype(jnp.float32) * attended).reshape(tok_rows, head_count, head_size),
        axis=2,
    ).T

    def backward_block(operands, source):

        def backward_work(inner):
            grad_query, grad_key, grad_value, key_now, value_now = inner
            key_heads = key_now.reshape(tok_rows, head_count, head_size)
            value_heads = value_now.reshape(tok_rows, head_count, head_size)
            probs = jnp.exp(scores_of(key_now, source) - log_total[:, :, None])
            probs_low = probs.astype(jnp.bfloat16)
            grad_value = grad_value + jnp.einsum(
                "hqk,qhd->khd", probs_low, grad_att_heads, preferred_element_type=jnp.float32
            ).reshape(tok_rows, model_width)
            grad_probs = jnp.einsum(
                "qhd,khd->hqk", grad_att_heads, value_heads, preferred_element_type=jnp.float32
            )
            grad_scores = (probs * (grad_probs - offsets[:, :, None])).astype(jnp.bfloat16)
            grad_query = (
                grad_query
                + jnp.einsum(
                    "hqk,khd->qhd", grad_scores, key_heads, preferred_element_type=jnp.float32
                ).reshape(tok_rows, model_width)
                * scale
            )
            grad_key = (
                grad_key
                + jnp.einsum(
                    "hqk,qhd->khd", grad_scores, query_heads, preferred_element_type=jnp.float32
                ).reshape(tok_rows, model_width)
                * scale
            )
            return (grad_query, grad_key, grad_value, key_now, value_now)

        def backward_keep(inner):
            return inner

        return lax.cond(source <= my_place, backward_work, backward_keep, operands)

    def backward_step(step, carry):
        source = (my_place - step) % blocks_seq
        grad_query, grad_key, grad_value, key_block, value_block = backward_block(carry, source)
        key_block, value_block = passed_along((key_block, value_block), "seq", 1)
        grad_key, grad_value = (
            shifted(grad_key.astype(jnp.bfloat16), "seq", 1).astype(grad_key.dtype),
            shifted(grad_value.astype(jnp.bfloat16), "seq", 1).astype(grad_value.dtype),
        )
        return (grad_query, grad_key, grad_value, key_block, value_block)

    zero_rows = jnp.zeros((tok_rows, model_width), jnp.float32)
    grad_query, grad_key, grad_value, _, _ = lax.fori_loop(
        0, blocks_seq, backward_step, (zero_rows, zero_rows, zero_rows, key_low, value_low)
    )
    grad_proj_low = jnp.concatenate([grad_query, grad_key, grad_value], axis=1).astype(jnp.bfloat16)
    grad_qkv = jnp.einsum(
        "tc,tk->ck", normed_low, grad_proj_low, preferred_element_type=jnp.float32
    )
    grad_normed = jnp.einsum(
        "tk,ck->tc", grad_proj_low, full_qkv, preferred_element_type=jnp.float32
    )
    grad_in_norm, grad_gain_one, grad_bias_one = norm_one_back(grad_normed)
    input_grad = (grad_middle + grad_in_norm)[None]
    part_qkv, part_out, part_up, part_down = (
        lax.psum_scatter(
            grad_qkv.astype(jnp.bfloat16), "seg", scatter_dimension=0, tiled=True
        ).astype(jnp.float32),
        lax.psum_scatter(
            grad_out.astype(jnp.bfloat16), "seg", scatter_dimension=0, tiled=True
        ).astype(jnp.float32),
        lax.psum_scatter(
            grad_up.astype(jnp.bfloat16), "seg", scatter_dimension=0, tiled=True
        ).astype(jnp.float32),
        lax.psum_scatter(
            grad_down.astype(jnp.bfloat16), "seg", scatter_dimension=0, tiled=True
        ).astype(jnp.float32),
    )
    sum_qkv, sum_out, sum_up, sum_down = (
        lax.psum_scatter(
            part_qkv.astype(jnp.bfloat16), "seq", scatter_dimension=1, tiled=True
        ).astype(jnp.float32),
        lax.psum_scatter(
            part_out.astype(jnp.bfloat16), "seq", scatter_dimension=1, tiled=True
        ).astype(jnp.float32),
        lax.psum_scatter(
            part_up.astype(jnp.bfloat16), "seq", scatter_dimension=1, tiled=True
        ).astype(jnp.float32),
        lax.psum_scatter(
            part_down.astype(jnp.bfloat16), "seq", scatter_dimension=1, tiled=True
        ).astype(jnp.float32),
    )
    sum_gain_one, sum_bias_one, sum_gain_two, sum_bias_two = lax.psum(
        (grad_gain_one, grad_bias_one, grad_gain_two, grad_bias_two), ("seq", "seg")
    )
    return (
        result,
        input_grad,
        sum_gain_one,
        sum_bias_one,
        sum_qkv,
        sum_out,
        sum_gain_two,
        sum_bias_two,
        sum_up,
        sum_down,
    )


MESH = pl.DeviceIdType.MESH
BF = jnp.bfloat16
F32 = jnp.float32
def dot_nn(a, b):
    return lax.dot_general(a, b, (((1,), (0,)), ((), ())), preferred_element_type=F32)


def dot_nt(a, b):
    return lax.dot_general(a, b, (((1,), (1,)), ((), ())), preferred_element_type=F32)


def dot_tn(a, b):
    return lax.dot_general(a, b, (((0,), (0,)), ((), ())), preferred_element_type=F32)


def remote(src, dst, send, recv, **place):
    return pltpu.make_async_remote_copy(
        src_ref=src, dst_ref=dst, send_sem=send, recv_sem=recv, device_id=place, device_id_type=MESH
    )


def norm_parts(values):
    center = values - jnp.mean(values, axis=-1, keepdims=True)
    spread = jnp.mean(center * center, axis=-1, keepdims=True)
    inverse = lax.rsqrt(spread + 1e-05)
    return center * inverse, inverse


def greet(q, s, transposed=False):
    y, c = s // 2, s % 2
    barrier = pltpu.get_barrier_semaphore()

    def signal(seq, seg):
        pl.semaphore_signal(barrier, 1, device_id={"seq": seq, "seg": seg}, device_id_type=MESH)

    for d in range(1, 8):
        for core in range(2):
            signal(lax.rem(q + d, 8), 2 * y + core)
    for d in range(1, 4):
        signal(q, lax.rem(s + d, 4))
    if transposed:
        turned = s != q // 2

        @pl.when(turned)
        def _():
            signal(2 * s + q % 2, q // 2)

        return lambda: pl.semaphore_wait(barrier, jnp.where(turned, 18, 17))
    return lambda: pl.semaphore_wait(barrier, 17)


def first_columns(lens, base, rows):
    place = base + lax.broadcasted_iota(jnp.int32, (rows, 1), 0)
    start = jnp.zeros((rows, 1), jnp.int32)
    bound = jnp.zeros((1, 1), jnp.int32)
    for i in range(lens.shape[0]):
        bound = bound + lens[i : i + 1, 0:1]
        start = jnp.where(place >= bound, bound, start)
    return start


def seen_mask(start, base_q, base_k, rows, columns):
    place = base_q + lax.broadcasted_iota(jnp.int32, (rows, columns), 0)
    key = base_k + lax.broadcasted_iota(jnp.int32, (rows, columns), 1)
    return (key <= place) & (key >= start)


def rows(k, n):
    return pl.ds(k * n if isinstance(k, int) else pl.multiple_of(k * n, n), n)


def lanes(k, n=128):
    return pl.ds(pl.multiple_of(k * n, n), n)


T = 256
HALF = 128


def places(z, x):
    zn, zc = z + 1 - 2 * (z % 2), (z + 2) % 4
    znc = (zn + 2) % 4
    here, near_z, near_x, cross = 2 * z + x, 2 * zn + x, 2 * z + 1 - x, 2 * zc + x
    blocks = (here, near_x, near_z, cross, 2 * znc + x, 2 * zc + 1 - x, 2 * zn + 1 - x, 2 * znc + 1 - x)
    return here, near_z, near_x, cross, blocks


def nth(values, k):
    out = values[0]
    for i, value in enumerate(values[1:], 1):
        out = jnp.where(k == i, value, out)
    return out


VM = pl.BlockSpec(memory_space=pltpu.VMEM)
HB = pl.BlockSpec(memory_space=pl.ANY)
S = jax.ShapeDtypeStruct
SM = pl.BlockSpec(memory_space=pltpu.SMEM)


def gelu_parts(u):
    root = math.sqrt(2.0 / math.pi)
    square = u * u
    t = jnp.tanh(root * (u + 0.044715 * (square * u)))
    value = 0.5 * u * (1.0 + t)
    slope = 0.5 * (1.0 + t) + 0.5 * u * (1.0 - t * t) * (root * (1.0 + 0.134145 * square))
    return value, slope


def norm_back(grad, gain, unit, inverse):
    through = grad * gain
    a = jnp.mean(through, axis=-1, keepdims=True)
    b = jnp.mean(through * unit, axis=-1, keepdims=True)
    return inverse * (through - a - unit * b)


def layer_kernel(
    x_ref, lens_ref, g_ref, wo_ref, gain_ref, bias_ref, gain2_ref, bias2_ref, wq_hbm, wu_hbm, wd_hbm,
    result_out, dx_v, fin_r, gq_r, gout_out, up_r, gdown_out, sums_out, xs_hbm, h1_hbm,
    g_v, wu_v, wd_v, wo_v, o_v, qkv_v, of_v, lse_v, wh_v, load_sem,
    keep_sem, ob, wq_s, lens_s, lens_r, qs, qr, ws, wr, xs_send, xs_recv, xu_recv, os_send, os_recv,
    middle, h2, big, mine, near_s, near_r, twin_s, twin_r, far_keep, far_s, far_r, do_v,
    hs, hr, ns, nr, ts, tr, fs, fr,
    pack, x_r, z_r, up_s, gxs, gxr, gzs, gzr, ups, upr,
    oc_r, oy_r, ox_r, oz_r, oo_r, cs, cr,
    doh, dq, dk, dv, dos, dor,
    fin_s, dcs, dcr, sts, str_, fns, fnr,
    gq, gq_b, gq_y, gqs, gqr,
    vec, vec_r, vs, vr,
):
    q, s = lax.axis_index("seq"), lax.axis_index("seg")
    z, x = q // 2, q % 2
    y, c = s // 2, s % 2
    sib = s + 1 - 2 * c
    across = (1 - y) * 2 + c
    corner = (1 - y) * 2 + 1 - c
    group = z // 2
    head = 4 * (z % 2) + 2 * x + c
    other_head = head + 1 - 2 * c
    home = c == group
    away = jnp.logical_not(home)
    column = 2 * y + group
    here, near_z, near_x, cross, blocks = places(z, x)
    scale = 1.0 / math.sqrt(HEAD_DIM)

    met = greet(q, s, True)

    picks = tuple(
        pltpu.make_async_copy(
            wq_hbm.at[:, lanes(8 * j + of_head)], wq_s.at[k, :, j * 128 : (j + 1) * 128], load_sem.at[10 + 3 * k + j]
        )
        for k, of_head in enumerate((head, other_head))
        for j in range(3)
    )
    loads = tuple(
        pltpu.make_async_copy(src, dst, load_sem.at[k])
        for k, (src, dst) in enumerate(((wd_hbm, wd_v), (wu_hbm.at[:, lanes(s, 1024)], wu_v.at[rows(s, T)])))
    )
    for copy in picks + loads:
        copy.start()
    for k in range(lens_ref.shape[1]):
        lens_s[k : k + 1] = jnp.full((1, 128), lens_ref[0, k], jnp.int32)

    @pl.when(home)
    def _():
        big[rows(q, T)] = x_ref[...]

    for copy in picks:
        copy.wait()
    wh_v[rows(s, T)] = wq_s[0]
    met()

    def half_rows(b, part):
        return big.at[pl.ds(pl.multiple_of(b * T + part * HALF, HALF), HALF)]

    def over_copy(part):
        src = x_ref.at[part * HALF : (part + 1) * HALF]
        return remote(src, half_rows(q, part), xs_send.at[24 + part], xs_recv.at[q], seq=cross, seg=2 * y + part)

    def twin_copy(part, recv, k):
        return remote(half_rows(q, part), half_rows(q, part), xs_send.at[24 + k], recv.at[q], seg=sib)

    twin_track, twin_rest = twin_copy(1 - c, xs_recv, 0), twin_copy(c, xu_recv, 1)

    @pl.when(home)
    def _():
        twin_track.start()
        twin_rest.start()

    @pl.when(jnp.logical_not(home))
    def _():
        over_copy(0).start()
        over_copy(1).start()

    mine_wh = wh_v.at[rows(s, T)]
    q_across = remote(wq_s.at[0], mine_wh, qs.at[0], qr.at[0], seg=across)
    q_sib = remote(wq_s.at[1], mine_wh, qs.at[1], qr.at[1], seg=sib)
    q_corner = remote(wq_s.at[1], mine_wh, qs.at[2], qr.at[2], seg=corner)
    l_sib = remote(lens_s, lens_r, qs.at[3], qr.at[3], seg=sib)
    first = (q_across, q_corner, q_sib, l_sib)
    for copy in first:
        copy.start()

    def x_copy(b, k, recv, **to):
        src = half_rows(b, c)
        return remote(src, src, xs_send.at[k], recv.at[b], **to)

    own_z, own_x = x_copy(q, 0, xs_recv, seq=near_z), x_copy(q, 8, xs_recv, seq=near_x)

    @pl.when(jnp.logical_not(home))
    def _():
        x_copy(q, 0, xs_recv, seq=q).wait_recv()

    own_z.start()
    own_x.start()

    def u_part(seg, part):
        return wu_v.at[pl.ds(pl.multiple_of(seg * T + part * HALF, HALF), HALF)]

    def o_part(seg, part):
        return wo_v.at[pl.ds(pl.multiple_of(seg * T + part * HALF, HALF), HALF)]

    u_far = tuple(
        remote(
            wu_hbm.at[pl.ds(pl.multiple_of(x * HALF, HALF), HALF), lanes(to, 1024)], u_part(s, x), ws.at[k], wr.at[k],
            seg=to,
        )
        for k, to in ((0, across), (1, corner))
    )
    u_over = tuple(
        remote(u_part(of_seg, x), u_part(of_seg, x), ws.at[11 + k], wr.at[11 + k], seq=near_x)
        for k, of_seg in ((0, across), (1, corner))
    )
    u_sib = remote(wu_hbm.at[:, lanes(sib, 1024)], wu_v.at[rows(s, T)], ws.at[2], wr.at[2], seg=sib)
    o_far = remote(
        wo_ref.at[pl.ds(pl.multiple_of(x * HALF, HALF), HALF)], o_part(s, x), ws.at[3], wr.at[3], seg=across
    )
    o_over = remote(o_part(across, x), o_part(across, x), ws.at[13], wr.at[13], seq=near_x)
    o_sib = remote(wo_ref, wo_v.at[rows(s, T)], ws.at[4], wr.at[4], seg=sib)
    o_pass = tuple(
        remote(o_part(across, part), o_part(across, part), ws.at[k], wr.at[k], seg=sib)
        for k, part in ((5, x), (14, 1 - x))
    )
    g_rows = lambda k, part: g_v.at[pl.ds(2 * T + part * T + k * HALF, HALF)]
    g_across = tuple(
        remote(g_ref.at[k * HALF : (k + 1) * HALF], g_rows(0, k), ws.at[6 + k], wr.at[6 + k], seg=across)
        for k in range(2)
    )
    g_sib = remote(g_ref, g_v.at[T : 2 * T], ws.at[8], wr.at[8], seg=sib)
    g_pass = tuple(remote(g_rows(0, k), g_rows(1, k), ws.at[9 + k], wr.at[9 + k], seg=sib) for k in range(2))
    wo_v[rows(s, T)] = wo_ref[...]
    g_v[0:T] = g_ref[...]
    for copy in u_far + (o_far,) + g_across:
        copy.start()
    for copy in first:
        copy.wait_recv()
    lens = jnp.where(home, lens_s[...], lens_r[...])

    gain, bias = gain_ref[...], bias_ref[...]

    def keep(b):
        at = rows(b, T)
        return (
            pltpu.make_async_copy(big.at[at], xs_hbm.at[at], keep_sem.at[b]),
            pltpu.make_async_copy(pack.at[b], h1_hbm.at[at], keep_sem.at[8 + b]),
        )

    def project(b):
        unit, _ = norm_parts(big[rows(b, T)].astype(F32))
        low = (unit * gain + bias).astype(BF)
        pack[b] = low
        qkv_v[rows(b, T)] = dot_nn(low, wh_v[...]).astype(BF)
        for copy in keep(b):
            copy.start()

    def track_step(k, _):
        b = nth(blocks, k)

        @pl.when(k < 8)
        def _():
            x_copy(b, 0, xs_recv, seq=q).wait_recv()

        @pl.when((k == 1) | (k == 3))
        def _():
            x_copy(b, k, xs_recv, seq=near_z).start()

        @pl.when((k == 3) | (k == 4))
        def _():
            x_copy(b, 8 + k, xs_recv, seq=near_x).start()

        @pl.when(k < 8)
        def _():
            x_copy(b, 16 + k, xu_recv, seg=sib).start()

        last = nth(blocks, k - 1)

        @pl.when((k > 1) | jnp.logical_not(home))
        def _():
            x_copy(last, 0, xu_recv, seg=sib).wait_recv()

        project(last)

        return 0

    lax.fori_loop(1, 6, track_step, 0)
    for arrived, copy in zip(u_far, u_over):
        arrived.wait_recv()
        copy.start()
    lax.fori_loop(6, 9, track_step, 0)
    o_far.wait_recv()
    o_over.start()
    o_pass[0].start()
    for copy in (u_sib, o_sib, g_sib):
        copy.start()

    def o_copy(i, sender):
        return remote(
            ob.at[i // 4, (i // 2) % 2, i % 2], o_v.at[:, lanes(sender)], os_send.at[i], os_recv.at[sender], seq=i, seg=column
        )

    o_mine = pltpu.make_async_copy(ob.at[group, z % 2, x], o_v.at[:, lanes(head)], os_recv.at[head])
    for i in (4, 5, 6, 7, 0, 1, 2, 3):
        n = (i + 1) * T
        start = first_columns(lens, i * T, T)
        scores = dot_nt(qkv_v[i * T : n, :128], qkv_v[:n, 128:256]) * scale
        scores = jnp.where(seen_mask(start, i * T, 0, T, n), scores, -1e30)
        top = jnp.max(scores, axis=1, keepdims=True)
        weights = jnp.exp(scores - top)
        total = jnp.sum(weights, axis=1, keepdims=True)
        mixed = dot_nn(weights.astype(BF), qkv_v[:n, 256:384]) / total
        of_v[i * T : n] = mixed
        lse_v[:, i : i + 1] = top + jnp.log(total)
        ob[i // 4, (i // 2) % 2, i % 2] = mixed.astype(BF)
        here = (q == i) & home

        @pl.when(jnp.logical_not(here))
        def _():
            o_copy(i, head).start()

        @pl.when(here)
        def _():
            o_mine.start()

    o_over.wait_recv()
    o_pass[1].start()
    for arrived, copy in zip(g_across, g_pass):
        arrived.wait_recv()
        copy.start()

    for i in range(8):
        o_copy(i, i).wait_recv()
    for copy in o_pass + (o_sib,):
        copy.wait_recv()

    value = x_ref[...].astype(F32) + dot_nn(o_v[...], wo_v[...])
    middle[...] = value
    unit, _ = norm_parts(value)
    h2[0:T] = (unit * gain2_ref[...] + bias2_ref[...]).astype(BF)

    def far_rows(ref, part, k):
        return ref.at[pl.ds(2 * T + k * T + part * HALF, HALF)]

    h_far = tuple(
        remote(h2.at[k * HALF : (k + 1) * HALF], far_rows(h2, 0, k), hs.at[k], hr.at[k], seg=across)
        for k in range(2)
    )
    h_pass = tuple(
        remote(far_rows(h2, 0, k), far_rows(h2, 1, k), hs.at[2 + k], hr.at[2 + k], seg=sib) for k in range(2)
    )
    h_sib = remote(h2.at[0:T], h2.at[T : 2 * T], hs.at[4], hr.at[4], seg=sib)
    for copy in h_far + (h_sib,):
        copy.start()
    for copy in loads:
        copy.wait()
    for copy in u_over + g_pass + (u_sib, g_sib):
        copy.wait_recv()
    for b in range(8):
        for copy in keep(b):
            copy.wait()
    for k in range(1, 8):
        if k in (1, 3):
            x_copy(blocks[k], k, xs_recv, seq=near_z).wait_send()
        if k in (3, 4):
            x_copy(blocks[k], 8 + k, xs_recv, seq=near_x).wait_send()
        x_copy(blocks[k], 16 + k, xu_recv, seg=sib).wait_send()

    @pl.when(home)
    def _():
        twin_track.wait_send()
        twin_rest.wait_send()

    @pl.when(jnp.logical_not(home))
    def _():
        over_copy(0).wait_send()
        over_copy(1).wait_send()

    for i in range(8):
        @pl.when(jnp.logical_not((q == i) & home))
        def _():
            o_copy(i, head).wait_send()

    for copy in first + u_far + u_over + o_pass + g_across + g_pass + (u_sib, o_far, o_over, o_sib, g_sib, own_z, own_x):
        copy.wait_send()

    def work(part):
        at = slice(part * T, (part + 1) * T)
        value, slope = gelu_parts(dot_nn(h2[at], wu_v[...]))
        low = value.astype(BF)
        big[at] = low
        du = (slope * dot_nt(g_v[at], wd_v[...])).astype(BF)
        big[4 * T + part * T : 4 * T + (part + 1) * T] = du
        return dot_nt(du, wu_v[...]), dot_nn(low, wd_v[...])

    near = tuple(remote(near_s.at[k], near_r.at[k], ns.at[k], nr.at[k], seg=sib) for k in range(2))
    twin = tuple(
        tuple(remote(twin_s.at[k, n], twin_r.at[k, n], ts.at[2 * k + n], tr.at[2 * k + n], seg=sib) for n in range(2))
        for k in range(2)
    )
    far = tuple(
        tuple(remote(far_s.at[k, n], far_r.at[k, n], fs.at[2 * k + n], fr.at[2 * k + n], seg=across) for n in range(2))
        for k in range(2)
    )

    def send_twin(n, parts):
        for k in range(2):
            far_keep[k] = parts[k][:HALF]
            twin_s[k, n] = parts[k][HALF:].astype(BF)
            twin[k][n].start()

    def send_far(n):
        for k in range(2):
            twin[k][n].wait_recv()
            far_s[k, n] = (far_keep[k] + twin_r[k, n].astype(F32)).astype(BF)
            if k == 0:
                far[k][n].start()

    parts = work(0)
    for k in range(2):
        mine[k] = parts[k]
    h_sib.wait_recv()
    parts = work(1)
    for k in range(2):
        near_s[k] = parts[k].astype(BF)
        near[k].start()
    h_far[0].wait_recv()
    h_pass[0].start()
    h_pass[0].wait_recv()
    send_twin(0, work(2))
    h_far[1].wait_recv()
    h_pass[1].start()
    send_far(0)
    h_pass[1].wait_recv()
    send_twin(1, work(3))
    send_far(1)

    def gx_copy(d):
        return remote(pack.at[2 * d + 1 - x], x_r.at[d], gxs.at[d], gxr.at[d], seq=near_x)

    zn, zc = z + 1 - 2 * (z % 2), (z + 2) % 4
    znc = (zn + 2) % 4

    def pack_rows(k, _):
        d = nth((znc, zc, zn, z), k)
        up = dot_tn(h2[:, lanes(d, T)], big[4 * T :]).astype(BF)
        down = dot_tn(big[: 4 * T], g_v[:, lanes(d, T)]).astype(BF)
        for e in range(2):
            pack[2 * d + e, :, :512] = up[:, e * 512 : (e + 1) * 512]
            for j in range(4):
                pack[2 * d + e, :, 512 + j * 128 : 640 + j * 128] = down[
                    j * T : (j + 1) * T, e * 128 : (e + 1) * 128
                ]

        @pl.when(k < 1)
        def _():
            gx_copy(d).start()

        return 0

    lax.fori_loop(0, 4, pack_rows, 0)

    near[0].wait_recv()
    far[0][0].wait_recv()
    far[0][1].wait_recv()
    grad = mine[0] + near_r[0].astype(F32) + jnp.concatenate([far_r[0, 0], far_r[0, 1]], axis=0).astype(F32)
    unit, inverse = norm_parts(middle[...])
    vec[...] = jnp.zeros_like(vec)
    vec[2:3] = jnp.sum(grad * unit, axis=0, keepdims=True)
    vec[3:4] = jnp.sum(grad, axis=0, keepdims=True)
    dx = g_v[0:T].astype(F32) + norm_back(grad, gain2_ref[...], unit, inverse)
    dx_v[...] = dx
    dy = dx.astype(BF)
    do_v[...] = dot_nt(dy, wo_v[...]).astype(BF)

    def do_copy(h, block):
        return remote(
            do_v.at[:, h * 128 : (h + 1) * 128], doh.at[rows(block, T)], dos.at[h], dor.at[block],
            seq=2 * (2 * c + h // 4) + (h // 2) % 2, seg=2 * y + h % 2,
        )

    do_mine = pltpu.make_async_copy(do_v.at[:, lanes(head)], doh.at[rows(q, T)], dor.at[q])
    for h in range(8):
        self_too = (head == h) & home

        @pl.when(jnp.logical_not(self_too))
        def _():
            do_copy(h, q).start()

        @pl.when(self_too)
        def _():
            do_mine.start()

    for copy in h_far + h_pass + (h_sib,):
        copy.wait_send()
    h2[...] = dot_tn(o_v[...], dy).astype(BF)

    def out_rows(part, core):
        return h2.at[rows(2 * part + core, T)]

    out_core = tuple(remote(out_rows(k, 1 - c), oc_r.at[k], cs.at[5 + k], cr.at[5 + k], seg=sib) for k in range(2))
    for copy in out_core:
        copy.start()
    for part in range(2):
        out_core[part].wait_recv()
        oc_r[part] = (oc_r[part].astype(F32) + out_rows(part, c)[...].astype(F32)).astype(BF)
    out_y = remote(oc_r.at[1 - y], oy_r, cs.at[1], cr.at[1], seg=across)
    out_y.start()
    far[1][0].start()
    far[1][1].start()

    def come(into, recv, slot):
        return remote(into.at[slot], into.at[slot], recv.at[slot], recv.at[slot], seq=near_x)

    def gz_copy(k, d, to):
        return remote(x_r.at[d], z_r.at[k], gzs.at[k], gzr.at[k], seq=to)

    gz = (gz_copy(0, znc, near_z), gz_copy(1, zn, near_z), gz_copy(2, zc, cross))

    def pack_sum(d):
        gx_copy(d).wait_recv()
        return pack[2 * d + x].astype(F32) + x_r[d].astype(F32)

    x_r[znc] = pack_sum(znc).astype(BF)
    gz[0].start()
    gx_copy(zc).start()

    dk[...] = jnp.zeros_like(dk)
    dv[...] = jnp.zeros_like(dv)
    for i in range(8):
        do_copy(0, i).wait_recv()
        top = i * T
        start = first_columns(lens, top, T)
        query = qkv_v[top : top + T, :128]
        grad = doh[top : top + T]
        delta = jnp.sum(grad.astype(F32) * of_v[top : top + T], axis=1, keepdims=True)
        log_total = lse_v[:, i : i + 1]
        total = jnp.zeros((T, 128), F32)
        for base in range(0, top + T, 1024):
            n = min(1024, top + T - base)
            keys = qkv_v[base : base + n, 128:256]
            probs = jnp.exp(dot_nt(query, keys) * scale - log_total)
            probs = jnp.where(seen_mask(start, top, base, T, n), probs, 0.0)
            dp = dot_nt(grad, qkv_v[base : base + n, 256:384])
            ds = (probs * (dp - delta)).astype(BF)
            dv[base : base + n] += dot_tn(probs.astype(BF), grad)
            dk[base : base + n] += dot_tn(ds, query)
            total += dot_nn(ds, keys)
        dq[top : top + T] = total

    gz[0].wait_recv()
    x_r[zc] = (pack_sum(zc) + z_r[0].astype(F32)).astype(BF)
    gz[2].start()

    gq[...] = jnp.zeros_like(gq)
    own_a, other_xa, other_za, own_b, other_zb, other_xb, diag_a, diag_b = blocks
    order = (diag_a, diag_b, other_za, other_xb, other_xa, other_zb, own_a, own_b)

    def x_load(i):
        return pltpu.make_async_copy(xs_hbm.at[rows(nth(order, i), T)], wu_v.at[rows(i % 2, T)], load_sem.at[2 + i % 2])

    def h_load(i):
        return pltpu.make_async_copy(h1_hbm.at[rows(nth(order, i), T)], wu_v.at[rows(2 + i % 2, T)], load_sem.at[4 + i % 2])

    def dhc_copy(b):
        return remote(
            big.at[pl.ds(pl.multiple_of(b * T + (1 - c) * HALF, HALF), HALF)], wo_v.at[rows(b, HALF)], dcs.at[b], dcr.at[b], seg=sib
        )

    def half(b):
        return big.at[pl.ds(pl.multiple_of(b * T + c * HALF, HALF), HALF)]

    def step_copy(k, b, to):
        return remote(wo_v.at[rows(b, HALF)], wd_v.at[rows(k, HALF)], sts.at[k], str_.at[k], seq=to)

    steps = (
        step_copy(0, diag_a, near_z), step_copy(1, diag_b, near_x), step_copy(2, other_za, near_z),
        step_copy(3, other_xb, near_x), step_copy(4, other_xa, near_x), step_copy(5, other_zb, near_z),
    )
    x_load(0).start()
    h_load(0).start()

    def grads_at(at):
        return jnp.concatenate([dq[at] * scale, dk[at] * scale, dv[at]], axis=1).astype(BF)

    def block_step(i, _):
        @pl.when(i < 8)
        def _():
            b = nth(order, i)

            at = rows(b, T)
            big[at] = dot_nt(grads_at(at), wh_v[...]).astype(BF)
            dhc_copy(b).start()

        @pl.when(i > 0)
        def _():
            b = nth(order, i - 1)
            dhc_copy(b).wait_recv()
            wo_v[rows(b, HALF)] = (half(b)[...].astype(F32) + wo_v[rows(b, HALF)].astype(F32)).astype(BF)
            for k in range(4):
                @pl.when(i == k + 1)
                def _():
                    steps[k].start()

        return 0

    lax.fori_loop(0, 9, block_step, 0)
    gx_copy(zn).start()

    def sum_step(i, _):
        @pl.when(i < 7)
        def _():
            x_load(i + 1).start()
            h_load(i + 1).start()

        at = rows(nth(order, i), T)
        dh = big[at].astype(F32)
        x_load(i).wait()
        h_load(i).wait()
        gq[...] += dot_tn(wu_v[rows(2 + i % 2, T)], grads_at(at))
        unit, _ = norm_parts(wu_v[rows(i % 2, T)].astype(F32))
        vec[0:1] += jnp.sum(dh * unit, axis=0, keepdims=True)
        vec[1:2] += jnp.sum(dh, axis=0, keepdims=True)
        return 0

    lax.fori_loop(0, 8, sum_step, 0)
    for k, b in ((5, other_zb), (4, other_xa)):
        steps[k - 4].wait_recv()
        wo_v[rows(b, HALF)] = (wo_v[rows(b, HALF)].astype(F32) + wd_v[(k - 4) * HALF : (k - 3) * HALF].astype(F32)).astype(BF)
        steps[k].start()

    x_r[zn] = pack_sum(zn).astype(BF)
    gz[1].start()

    out_y.wait_recv()
    out = (oc_r[y].astype(F32) + oy_r[...].astype(F32)).astype(BF)
    for k in range(8):
        ob[k // 4, (k // 2) % 2, k % 2] = out[:, k * 128 : (k + 1) * 128]
    out_x = remote(ob.at[:, :, 1 - x], ox_r, cs.at[2], cr.at[2], seq=near_x)
    out_x.start()
    gx_copy(z).start()

    gq_b[...] = gq[...].astype(BF).reshape(2, 2, T, 384)
    q_y = remote(gq_b.at[1 - y], gq_y, gqs.at[0], gqr.at[0], seg=across)
    q_y.start()
    v_core = remote(vec, vec_r.at[0], vs.at[8], vr.at[8], seg=sib)
    v_core.start()
    v_core.wait()
    vec[...] += vec_r[0]
    v_y = remote(vec, vec_r.at[1], vs.at[9], vr.at[9], seg=across)
    v_y.start()
    def fin_sum(k, b, pair):
        for n in pair:
            steps[n].wait_recv()
        fin_s[k] = (
            wo_v[rows(b, HALF)].astype(F32) + wd_v[rows(pair[0], HALF)].astype(F32)
            + wd_v[rows(pair[1], HALF)].astype(F32)
        ).astype(BF)

    fin_over = remote(fin_s.at[1], fin_r.at[c], fns.at[0], fnr.at[c], seq=cross, seg=column)
    fin_twin = remote(fin_s.at[0], fin_r.at[c], fns.at[1], fnr.at[c], seg=sib)
    fin_own = pltpu.make_async_copy(fin_s.at[0], fin_r.at[c], fnr.at[c])
    fin_sum(1, own_b, (3, 5))
    fin_over.start()
    fin_sum(0, own_a, (2, 4))

    @pl.when(away)
    def _():
        fin_twin.start()

    @pl.when(home)
    def _():
        fin_own.start()

    v_y.wait()
    vec[...] += vec_r[1]

    def v_copy(b, sender):
        return remote(vec, vec_r.at[2 + sender], vs.at[b], vr.at[sender], seq=b)

    for b in range(8):
        @pl.when(q != b)
        def _():
            v_copy(b, q).start()

    q_y.wait_recv()
    gq_y[...] = (gq_y[...].astype(F32) + gq_b[y].astype(F32)).astype(BF)

    def column_copy(part, j):
        place = 8 * j + head
        owner, slot = place // 3, place % 3
        src = gq_y.at[part, :, j * 128 : (j + 1) * 128]
        copy = remote(
            src, gq_r.at[slot, group], gqs.at[1 + 3 * part + j], gqr.at[1 + 2 * slot + group],
            seq=owner, seg=2 * y + part,
        )
        local = pltpu.make_async_copy(src, gq_r.at[slot, group], gqr.at[1 + 2 * slot + group])
        return (owner == q) & (c == part), copy, local

    columns = tuple(column_copy(part, j) for part in range(2) for j in range(3))
    out_x.wait_recv()
    ox_r[...] = (ox_r[...].astype(F32) + ob[:, :, x].astype(F32)).astype(BF)
    out_z = remote(ox_r.at[:, 1 - z % 2], oz_r, cs.at[3], cr.at[3], seq=near_z)
    out_z.start()
    for self_too, copy, local in columns:
        @pl.when(jnp.logical_not(self_too))
        def _():
            copy.start()

        @pl.when(self_too)
        def _():
            local.start()

    out_z.wait_recv()
    oz_r[...] = (oz_r[...].astype(F32) + ox_r[:, z % 2].astype(F32)).astype(BF)
    out_o = remote(oz_r.at[1 - group], oo_r, cs.at[4], cr.at[4], seq=cross)
    out_o.start()

    total = pack_sum(z)
    for k in (1, 2):
        gz[k].wait_recv()
        total = total + z_r[k].astype(F32)
    up_s[...] = total[:, :512].astype(BF)
    turned = s != z
    up_turn = remote(up_s, up_r, ups, upr, seq=2 * s + x, seg=z)
    up_own = pltpu.make_async_copy(up_s, up_r, upr)

    @pl.when(turned)
    def _():
        up_turn.start()

    @pl.when(jnp.logical_not(turned))
    def _():
        up_own.start()

    for j in range(4):
        gdown_out[j * T : (j + 1) * T] = total[:, 512 + j * 128 : 640 + j * 128]
    vec_r[2 + q] = vec[...]
    for b in range(8):
        @pl.when(q != b)
        def _():
            v_copy(b, b).wait_recv()

    vec_sum = vec_r[2]
    for b in range(1, 8):
        vec_sum = vec_sum + vec_r[2 + b]
    out_o.wait_recv()
    gout_out[...] = oz_r[group].astype(F32) + oo_r[...].astype(F32)
    sums_out[...] = vec_sum
    for slot in range(3):
        for part in range(2):
            pltpu.make_async_copy(gq_r.at[slot, part], gq_r.at[slot, part], gqr.at[1 + 2 * slot + part]).wait()
    near[1].wait_recv()
    far[1][0].wait_recv()
    far[1][1].wait_recv()
    result_out[...] = (
        middle[...] + mine[1] + near_r[1].astype(F32)
        + jnp.concatenate([far_r[1, 0], far_r[1, 1]], axis=0).astype(F32)
    ).astype(BF)
    for k in range(2):
        come(fin_r, fnr, k).wait_recv()
    up_own.wait()

    for h in range(8):
        @pl.when(jnp.logical_not((head == h) & home))
        def _():
            do_copy(h, q).wait_send()

    for b in range(8):
        dhc_copy(b).wait_send()

        @pl.when(q != b)
        def _():
            v_copy(b, q).wait_send()

    for d in range(4):
        gx_copy(d).wait_send()
    for copy in out_core + (out_y, out_x, out_z, out_o, q_y, fin_over) + near + steps + gz:
        copy.wait_send()
    for k in range(2):
        for n in range(2):
            twin[k][n].wait_send()
            far[k][n].wait_send()

    @pl.when(away)
    def _():
        fin_twin.wait_send()

    @pl.when(turned)
    def _():
        up_turn.wait_send()

    for self_too, copy, _ in columns:
        @pl.when(jnp.logical_not(self_too))
        def _():
            copy.wait_send()


def layer(x, lens, g, wo, gain, bias, gain2, bias2, wq, wu, wd):
    dma = pltpu.SemaphoreType.DMA
    low = lambda *shape: pltpu.VMEM(shape, BF)
    wide = lambda *shape: pltpu.VMEM(shape, F32)
    return pl.pallas_call(
        layer_kernel,
        out_shape=(
            S((256, 1024), BF), S((256, 1024), F32), S((2, 128, 1024), BF), S((3, 2, 256, 128), BF),
            S((256, 128), F32), S((256, 512), BF), S((1024, 128), F32), S((8, 1024), F32),
            S((2048, 1024), BF), S((2048, 1024), BF),
        ),
        in_specs=[VM, SM] + [VM] * 6 + [HB] * 3,
        out_specs=(VM,) * 8 + (HB,) * 2,
        scratch_shapes=[
            low(1024, 1024), low(1024, 1024), low(1024, 1024), low(1024, 1024), low(256, 1024), low(2048, 384),
            wide(2048, 128), wide(256, 8), low(1024, 384), dma((16,)),
            dma((16,)), low(2, 2, 2, 256, 128), low(2, 256, 384), pltpu.VMEM((8, 128), jnp.int32),
            pltpu.VMEM((8, 128), jnp.int32), dma((4,)), dma((4,)), dma((15,)), dma((15,)),
            dma((26,)), dma((8,)), dma((8,)), dma((8,)), dma((8,)),
            wide(256, 1024), low(1024, 1024), low(2048, 1024), wide(2, 256, 1024),
            low(2, 256, 1024), low(2, 256, 1024), low(2, 2, 128, 1024), low(2, 2, 128, 1024), wide(2, 128, 1024),
            low(2, 2, 128, 1024), low(2, 2, 128, 1024), low(256, 1024),
            dma((5,)), dma((5,)), dma((2,)), dma((2,)), dma((4,)), dma((4,)), dma((4,)), dma((4,)),
            low(8, 256, 1024), low(4, 256, 1024), low(3, 256, 1024), low(256, 512),
            dma((4,)), dma((4,)), dma((3,)), dma((3,)), dma, dma,
            low(2, 256, 1024), low(256, 1024), low(2, 2, 256, 128),
            low(2, 256, 128), low(256, 128), dma((7,)), dma((7,)),
            low(2048, 128), wide(2048, 128), wide(2048, 128), wide(2048, 128), dma((8,)), dma((8,)),
            low(2, 128, 1024),
            dma((8,)), dma((8,)), dma((6,)), dma((6,)), dma((2,)), dma((2,)),
            wide(1024, 384), low(2, 2, 256, 384), low(2, 256, 384),
            dma((7,)), dma((7,)),
            wide(8, 1024), wide(10, 8, 1024), dma((10,)), dma((10,)),
        ],
        compiler_params=pltpu.CompilerParams(
            collective_id=1, has_side_effects=True, vmem_limit_bytes=63 * 2**20
        ),
        cost_estimate=pl.CostEstimate(flops=2 * 10**10, bytes_accessed=40 * 2**20, transcendentals=2 * 2**20),
        name="layer",
    )(x, lens, g, wo, gain, bias, gain2, bias2, wq, wu, wd)


def finish_kernel(
    x_ref, gain_ref, result_ref, dx_ref, fin_ref, gq_ref, out_ref, up_ref, down_ref, sums_ref,
    result, dx, gain_one, bias_one, gqkv, gout, gain_two, bias_two, gup, gdown,
):
    result[...] = result_ref[...]
    unit, inverse = norm_parts(x_ref[...].astype(F32))
    dx[...] = dx_ref[...] + norm_back(fin_ref[0].astype(F32), gain_ref[...], unit, inverse)
    for slot in range(3):
        gqkv[:, slot * 128 : (slot + 1) * 128] = gq_ref[slot, 0].astype(F32) + gq_ref[slot, 1].astype(F32)
    gout[...] = out_ref[...]
    gup[...] = up_ref[...].astype(F32)
    gdown[...] = down_ref[...]
    for k, ref in enumerate((gain_one, bias_one, gain_two, bias_two)):
        ref[...] = sums_ref[k]


def finish(x, gain, *parts):
    line = S((1024,), F32)
    part = lambda r, n: pl.BlockSpec((r // 2, n), lambda i: (i, 0))
    whole = lambda r, n: pl.BlockSpec((r, n), lambda i: (0, 0))
    row = pl.BlockSpec((1024,), lambda i: (0,))
    return pl.pallas_call(
        finish_kernel,
        grid=(2,),
        out_shape=(
            S((256, 1024), BF), S((256, 1024), F32), line, line, S((256, 384), F32), S((256, 128), F32), line, line,
            S((256, 512), F32), S((1024, 128), F32),
        ),
        in_specs=[
            part(256, 1024), whole(1, 1024), part(256, 1024), part(256, 1024),
            pl.BlockSpec((1, 128, 1024), lambda i: (i, 0, 0)),
            pl.BlockSpec((3, 2, 128, 128), lambda i: (0, 0, i, 0)), part(256, 128), part(256, 512), part(1024, 128),
            whole(8, 1024),
        ],
        out_specs=(
            part(256, 1024), part(256, 1024), row, row, part(256, 384), part(256, 128), row, row, part(256, 512),
            part(1024, 128),
        ),
        compiler_params=pltpu.CompilerParams(vmem_limit_bytes=60 * 2**20),
        name="finish",
    )(x, gain, *parts)


def per_device_fast(
    tokens, article_lengths, gain_one, bias_one, w_qkv, w_out, gain_two, bias_two, w_up, w_down, cotangent
):
    x = tokens[0]
    *parts, _, _ = layer(
        x, article_lengths, cotangent[0], w_out, gain_one[None], bias_one[None], gain_two[None], bias_two[None],
        w_qkv, w_up, w_down,
    )
    result, dx, *rest = finish(x, gain_one[None], *parts)
    return (result[None], dx[None], *rest)


def solution(mesh):
    one_pair = mesh.shape["seq"] == HEADS and mesh.shape["seg"] == 4
    return jax.shard_map(
        per_device_fast if one_pair else per_device,
        mesh=mesh,
        in_specs=(
            P("seg", "seq", None),
            P("seg", None),
            P(),
            P(),
            P("seg", None),
            P("seg", None),
            P(),
            P(),
            P("seg", None),
            P("seg", None),
            P("seg", "seq", None),
        ),
        out_specs=(
            P("seg", "seq", None),
            P("seg", "seq", None),
            P(),
            P(),
            P("seg", "seq"),
            P("seg", "seq"),
            P(),
            P(),
            P("seg", "seq"),
            P("seg", "seq"),
        ),
        check_vma=False,
    )
```

```python
import math

import jax
import jax.numpy as jnp
from jax import lax
from jax.experimental import pallas as pl
from jax.experimental.pallas import tpu as pltpu
from jax.sharding import PartitionSpec as P

HEADS = 8
HEAD_DIM = 128


def passed_along(block, axis, distance):
    devices = range(lax.axis_size(axis))
    route = [(i - distance, i) for i in devices if i - distance in devices]
    return lax.ppermute(block, axis, route)


def shifted(value, axis, by):
    size = lax.axis_size(axis)
    return lax.ppermute(value, axis, [(i, (i + by) % size) for i in range(size)])


def layer_norm(values, gain, bias):
    center = values - jnp.mean(values, axis=-1, keepdims=True)
    spread = jnp.mean(center * center, axis=-1, keepdims=True)
    return center * lax.rsqrt(spread + 1e-05) * gain + bias


def smooth_act(values):
    return jax.nn.gelu(values, approximate=True)


def article_numbers(lengths_row, positions):
    bounds = jnp.cumsum(lengths_row)
    return jnp.sum((positions[:, None] >= bounds[None, :]).astype(jnp.int32), axis=1)


def per_device(
    tokens,
    article_lengths,
    gain_one,
    bias_one,
    w_qkv,
    w_out,
    gain_two,
    bias_two,
    w_up,
    w_down,
    cotangent,
):
    tok_rows = tokens.shape[1]
    model_width = tokens.shape[2]
    head_count = HEADS
    head_size = HEAD_DIM
    scale = 1.0 / math.sqrt(head_size)
    blocks_seq = lax.axis_size("seq")
    my_place = lax.axis_index("seq")
    full_qkv, full_out, full_up, full_down = (
        lax.all_gather(w_qkv, "seg", axis=0, tiled=True),
        lax.all_gather(w_out, "seg", axis=0, tiled=True),
        lax.all_gather(w_up, "seg", axis=0, tiled=True),
        lax.all_gather(w_down, "seg", axis=0, tiled=True),
    )
    inputs = tokens[0].astype(jnp.float32)
    normed, norm_one_back = jax.vjp(layer_norm, inputs, gain_one, bias_one)
    normed_low = normed.astype(jnp.bfloat16)
    projected = jnp.dot(normed_low, full_qkv, preferred_element_type=jnp.float32).astype(
        jnp.bfloat16
    )
    query_low = projected[:, :model_width]
    key_low = projected[:, model_width : 2 * model_width]
    value_low = projected[:, 2 * model_width :]
    query_heads = query_low.reshape(tok_rows, head_count, head_size)
    lengths_row = article_lengths[0]
    positions = my_place * tok_rows + jnp.arange(tok_rows, dtype=jnp.int32)
    query_art = article_numbers(lengths_row, positions)

    def scores_of(key_block, source):
        key_pos = source * tok_rows + jnp.arange(tok_rows, dtype=jnp.int32)
        key_art = article_numbers(lengths_row, key_pos)
        allowed = (key_pos[None, :] <= positions[:, None]) & (
            key_art[None, :] == query_art[:, None]
        )
        raw = (
            jnp.einsum(
                "qhd,khd->hqk",
                query_heads,
                key_block.reshape(tok_rows, head_count, head_size),
                preferred_element_type=jnp.float32,
            )
            * scale
        )
        return jnp.where(allowed[None], raw, -1e30)

    def forward_block(state, key_block, value_block, source):

        def forward_work(operands):
            (top, total, accum), key_now, value_now = operands
            scores = scores_of(key_now, source)
            new_top = jnp.maximum(top, jnp.max(scores, axis=2))
            factor = jnp.exp(top - new_top)
            weights = jnp.exp(scores - new_top[:, :, None])
            total = total * factor + jnp.sum(weights, axis=2)
            gathered = jnp.einsum(
                "hqk,khd->qhd",
                weights.astype(jnp.bfloat16),
                value_now.reshape(tok_rows, head_count, head_size),
                preferred_element_type=jnp.float32,
            ).reshape(tok_rows, model_width)
            accum = accum * jnp.repeat(factor.T, head_size, axis=1) + gathered
            return (new_top, total, accum)

        def forward_keep(operands):
            return operands[0]

        return lax.cond(
            source <= my_place, forward_work, forward_keep, (state, key_block, value_block)
        )

    start_state = (
        jnp.full((head_count, tok_rows), -1e30, jnp.float32),
        jnp.zeros((head_count, tok_rows), jnp.float32),
        jnp.zeros((tok_rows, model_width), jnp.float32),
    )
    state = forward_block(start_state, key_low, value_low, my_place)

    def forward_step(step, carry):
        key_block, value_block, state_now = carry
        key_block, value_block = passed_along((key_block, value_block), "seq", 1)
        source = (my_place - step) % blocks_seq
        return (key_block, value_block, forward_block(state_now, key_block, value_block, source))

    _, _, state = lax.fori_loop(1, blocks_seq, forward_step, (key_low, value_low, state))
    top, total, accum = state
    log_total = top + jnp.log(total)
    attended = accum / jnp.repeat(total.T, head_size, axis=1)
    attended_low = attended.astype(jnp.bfloat16)
    middle = inputs + jnp.dot(attended_low, full_out, preferred_element_type=jnp.float32)
    normed_two, norm_two_back = jax.vjp(layer_norm, middle, gain_two, bias_two)
    normed_two_low = normed_two.astype(jnp.bfloat16)
    hidden = jnp.dot(normed_two_low, full_up, preferred_element_type=jnp.float32)
    activated, act_back = jax.vjp(smooth_act, hidden)
    activated_low = activated.astype(jnp.bfloat16)
    outputs = middle + jnp.dot(activated_low, full_down, preferred_element_type=jnp.float32)
    result = outputs.astype(jnp.bfloat16)[None]
    grad_top = cotangent[0].astype(jnp.float32)
    grad_top_low = cotangent[0]
    grad_down = jnp.einsum(
        "tf,td->fd", activated_low, grad_top_low, preferred_element_type=jnp.float32
    )
    grad_act = jnp.einsum("td,fd->tf", grad_top_low, full_down, preferred_element_type=jnp.float32)
    (grad_hidden,) = act_back(grad_act)
    grad_hidden_low = grad_hidden.astype(jnp.bfloat16)
    grad_up = jnp.einsum(
        "td,tf->df", normed_two_low, grad_hidden_low, preferred_element_type=jnp.float32
    )
    grad_normed_two = jnp.einsum(
        "tf,df->td", grad_hidden_low, full_up, preferred_element_type=jnp.float32
    )
    grad_mid_norm, grad_gain_two, grad_bias_two = norm_two_back(grad_normed_two)
    grad_middle = grad_top + grad_mid_norm
    grad_middle_low = grad_middle.astype(jnp.bfloat16)
    grad_out = jnp.einsum(
        "tc,td->cd", attended_low, grad_middle_low, preferred_element_type=jnp.float32
    )
    grad_att = jnp.einsum(
        "td,cd->tc", grad_middle_low, full_out, preferred_element_type=jnp.float32
    )
    grad_att_low = grad_att.astype(jnp.bfloat16)
    grad_att_heads = grad_att_low.reshape(tok_rows, head_count, head_size)
    offsets = jnp.sum(
        (grad_att_low.astype(jnp.float32) * attended).reshape(tok_rows, head_count, head_size),
        axis=2,
    ).T

    def backward_block(operands, source):

        def backward_work(inner):
            grad_query, grad_key, grad_value, key_now, value_now = inner
            key_heads = key_now.reshape(tok_rows, head_count, head_size)
            value_heads = value_now.reshape(tok_rows, head_count, head_size)
            probs = jnp.exp(scores_of(key_now, source) - log_total[:, :, None])
            probs_low = probs.astype(jnp.bfloat16)
            grad_value = grad_value + jnp.einsum(
                "hqk,qhd->khd", probs_low, grad_att_heads, preferred_element_type=jnp.float32
            ).reshape(tok_rows, model_width)
            grad_probs = jnp.einsum(
                "qhd,khd->hqk", grad_att_heads, value_heads, preferred_element_type=jnp.float32
            )
            grad_scores = (probs * (grad_probs - offsets[:, :, None])).astype(jnp.bfloat16)
            grad_query = (
                grad_query
                + jnp.einsum(
                    "hqk,khd->qhd", grad_scores, key_heads, preferred_element_type=jnp.float32
                ).reshape(tok_rows, model_width)
                * scale
            )
            grad_key = (
                grad_key
                + jnp.einsum(
                    "hqk,qhd->khd", grad_scores, query_heads, preferred_element_type=jnp.float32
                ).reshape(tok_rows, model_width)
                * scale
            )
            return (grad_query, grad_key, grad_value, key_now, value_now)

        def backward_keep(inner):
            return inner

        return lax.cond(source <= my_place, backward_work, backward_keep, operands)

    def backward_step(step, carry):
        source = (my_place - step) % blocks_seq
        grad_query, grad_key, grad_value, key_block, value_block = backward_block(carry, source)
        key_block, value_block = passed_along((key_block, value_block), "seq", 1)
        grad_key, grad_value = (
            shifted(grad_key.astype(jnp.bfloat16), "seq", 1).astype(grad_key.dtype),
            shifted(grad_value.astype(jnp.bfloat16), "seq", 1).astype(grad_value.dtype),
        )
        return (grad_query, grad_key, grad_value, key_block, value_block)

    zero_rows = jnp.zeros((tok_rows, model_width), jnp.float32)
    grad_query, grad_key, grad_value, _, _ = lax.fori_loop(
        0, blocks_seq, backward_step, (zero_rows, zero_rows, zero_rows, key_low, value_low)
    )
    grad_proj_low = jnp.concatenate([grad_query, grad_key, grad_value], axis=1).astype(jnp.bfloat16)
    grad_qkv = jnp.einsum(
        "tc,tk->ck", normed_low, grad_proj_low, preferred_element_type=jnp.float32
    )
    grad_normed = jnp.einsum(
        "tk,ck->tc", grad_proj_low, full_qkv, preferred_element_type=jnp.float32
    )
    grad_in_norm, grad_gain_one, grad_bias_one = norm_one_back(grad_normed)
    input_grad = (grad_middle + grad_in_norm)[None]
    part_qkv, part_out, part_up, part_down = (
        lax.psum_scatter(
            grad_qkv.astype(jnp.bfloat16), "seg", scatter_dimension=0, tiled=True
        ).astype(jnp.float32),
        lax.psum_scatter(
            grad_out.astype(jnp.bfloat16), "seg", scatter_dimension=0, tiled=True
        ).astype(jnp.float32),
        lax.psum_scatter(
            grad_up.astype(jnp.bfloat16), "seg", scatter_dimension=0, tiled=True
        ).astype(jnp.float32),
        lax.psum_scatter(
            grad_down.astype(jnp.bfloat16), "seg", scatter_dimension=0, tiled=True
        ).astype(jnp.float32),
    )
    sum_qkv, sum_out, sum_up, sum_down = (
        lax.psum_scatter(
            part_qkv.astype(jnp.bfloat16), "seq", scatter_dimension=1, tiled=True
        ).astype(jnp.float32),
        lax.psum_scatter(
            part_out.astype(jnp.bfloat16), "seq", scatter_dimension=1, tiled=True
        ).astype(jnp.float32),
        lax.psum_scatter(
            part_up.astype(jnp.bfloat16), "seq", scatter_dimension=1, tiled=True
        ).astype(jnp.float32),
        lax.psum_scatter(
            part_down.astype(jnp.bfloat16), "seq", scatter_dimension=1, tiled=True
        ).astype(jnp.float32),
    )
    sum_gain_one, sum_bias_one, sum_gain_two, sum_bias_two = lax.psum(
        (grad_gain_one, grad_bias_one, grad_gain_two, grad_bias_two), ("seq", "seg")
    )
    return (
        result,
        input_grad,
        sum_gain_one,
        sum_bias_one,
        sum_qkv,
        sum_out,
        sum_gain_two,
        sum_bias_two,
        sum_up,
        sum_down,
    )


MESH = pl.DeviceIdType.MESH
BF = jnp.bfloat16
F32 = jnp.float32
def dot_nn(a, b):
    return lax.dot_general(a, b, (((1,), (0,)), ((), ())), preferred_element_type=F32)


def dot_nt(a, b):
    return lax.dot_general(a, b, (((1,), (1,)), ((), ())), preferred_element_type=F32)


def dot_tn(a, b):
    return lax.dot_general(a, b, (((0,), (0,)), ((), ())), preferred_element_type=F32)


def remote(src, dst, send, recv, **place):
    return pltpu.make_async_remote_copy(
        src_ref=src, dst_ref=dst, send_sem=send, recv_sem=recv, device_id=place, device_id_type=MESH
    )


def norm_parts(values):
    center = values - jnp.mean(values, axis=-1, keepdims=True)
    spread = jnp.mean(center * center, axis=-1, keepdims=True)
    inverse = lax.rsqrt(spread + 1e-05)
    return center * inverse, inverse


def greet(q, s, transposed=False):
    y, c = s // 2, s % 2
    barrier = pltpu.get_barrier_semaphore()

    def signal(seq, seg):
        pl.semaphore_signal(barrier, 1, device_id={"seq": seq, "seg": seg}, device_id_type=MESH)

    for d in range(1, 8):
        for core in range(2):
            signal(lax.rem(q + d, 8), 2 * y + core)
    for d in range(1, 4):
        signal(q, lax.rem(s + d, 4))
    if transposed:
        turned = s != q // 2

        @pl.when(turned)
        def _():
            signal(2 * s + q % 2, q // 2)

        return lambda: pl.semaphore_wait(barrier, jnp.where(turned, 18, 17))
    return lambda: pl.semaphore_wait(barrier, 17)


def first_columns(lens, base, rows):
    place = base + lax.broadcasted_iota(jnp.int32, (rows, 1), 0)
    start = jnp.zeros((rows, 1), jnp.int32)
    bound = jnp.zeros((1, 1), jnp.int32)
    for i in range(lens.shape[0]):
        bound = bound + lens[i : i + 1, 0:1]
        start = jnp.where(place >= bound, bound, start)
    return start


def seen_mask(start, base_q, base_k, rows, columns):
    place = base_q + lax.broadcasted_iota(jnp.int32, (rows, columns), 0)
    key = base_k + lax.broadcasted_iota(jnp.int32, (rows, columns), 1)
    return (key <= place) & (key >= start)


def rows(k, n):
    return pl.ds(k * n if isinstance(k, int) else pl.multiple_of(k * n, n), n)


def lanes(k, n=128):
    return pl.ds(pl.multiple_of(k * n, n), n)


T = 256
HALF = 128


def places(z, x):
    zn, zc = z + 1 - 2 * (z % 2), (z + 2) % 4
    znc = (zn + 2) % 4
    here, near_z, near_x, cross = 2 * z + x, 2 * zn + x, 2 * z + 1 - x, 2 * zc + x
    blocks = (here, near_x, near_z, cross, 2 * znc + x, 2 * zc + 1 - x, 2 * zn + 1 - x, 2 * znc + 1 - x)
    return here, near_z, near_x, cross, blocks


def nth(values, k):
    out = values[0]
    for i, value in enumerate(values[1:], 1):
        out = jnp.where(k == i, value, out)
    return out


VM = pl.BlockSpec(memory_space=pltpu.VMEM)
HB = pl.BlockSpec(memory_space=pl.ANY)
S = jax.ShapeDtypeStruct
SM = pl.BlockSpec(memory_space=pltpu.SMEM)


def gelu_parts(u):
    root = math.sqrt(2.0 / math.pi)
    square = u * u
    t = jnp.tanh(root * (u + 0.044715 * (square * u)))
    value = 0.5 * u * (1.0 + t)
    slope = 0.5 * (1.0 + t) + 0.5 * u * (1.0 - t * t) * (root * (1.0 + 0.134145 * square))
    return value, slope


def norm_back(grad, gain, unit, inverse):
    through = grad * gain
    a = jnp.mean(through, axis=-1, keepdims=True)
    b = jnp.mean(through * unit, axis=-1, keepdims=True)
    return inverse * (through - a - unit * b)


def layer_kernel(
    x_ref, lens_ref, g_ref, wo_ref, gain_ref, bias_ref, gain2_ref, bias2_ref, wq_hbm, wu_hbm, wd_hbm,
    result_out, dx_v, fin_r, gq_r, gout_out, up_r, gdown_out, sums_out, xs_hbm, h1_hbm,
    g_v, wu_v, wd_v, wo_v, o_v, qkv_v, of_v, lse_v, wh_v, load_sem,
    keep_sem, ob, wq_s, lens_s, lens_r, qs, qr, ws, wr, xs_send, xs_recv, xu_recv, os_send, os_recv,
    middle, h2, big, mine, near_s, near_r, twin_s, twin_r, far_keep, far_s, far_r, do_v,
    hs, hr, ns, nr, ts, tr, fs, fr,
    pack, x_r, z_r, up_s, gxs, gxr, gzs, gzr, ups, upr,
    oc_r, oy_r, ox_r, oz_r, oo_r, cs, cr,
    doh, dq, dk, dv, dos, dor,
    fin_s, dcs, dcr, sts, str_, fns, fnr,
    gq, gq_b, gq_y, gqs, gqr,
    vec, vec_r, vs, vr,
):
    q, s = lax.axis_index("seq"), lax.axis_index("seg")
    z, x = q // 2, q % 2
    y, c = s // 2, s % 2
    sib = s + 1 - 2 * c
    across = (1 - y) * 2 + c
    corner = (1 - y) * 2 + 1 - c
    group = z // 2
    head = 4 * (z % 2) + 2 * x + c
    other_head = head + 1 - 2 * c
    home = c == group
    away = jnp.logical_not(home)
    column = 2 * y + group
    here, near_z, near_x, cross, blocks = places(z, x)
    scale = 1.0 / math.sqrt(HEAD_DIM)

    met = greet(q, s, True)

    picks = tuple(
        pltpu.make_async_copy(
            wq_hbm.at[:, lanes(8 * j + of_head)], wq_s.at[k, :, j * 128 : (j + 1) * 128], load_sem.at[10 + 3 * k + j]
        )
        for k, of_head in enumerate((head, other_head))
        for j in range(3)
    )
    loads = tuple(
        pltpu.make_async_copy(src, dst, load_sem.at[k])
        for k, (src, dst) in enumerate(((wd_hbm, wd_v), (wu_hbm.at[:, lanes(s, 1024)], wu_v.at[rows(s, T)])))
    )
    for copy in picks + loads:
        copy.start()
    for k in range(lens_ref.shape[1]):
        lens_s[k : k + 1] = jnp.full((1, 128), lens_ref[0, k], jnp.int32)

    @pl.when(home)
    def _():
        big[rows(q, T)] = x_ref[...]

    for copy in picks:
        copy.wait()
    wh_v[rows(s, T)] = wq_s[0]
    met()

    def half_rows(b, part):
        return big.at[pl.ds(pl.multiple_of(b * T + part * HALF, HALF), HALF)]

    def over_copy(part):
        src = x_ref.at[part * HALF : (part + 1) * HALF]
        return remote(src, half_rows(q, part), xs_send.at[24 + part], xs_recv.at[q], seq=cross, seg=2 * y + part)

    def twin_copy(part, recv, k):
        return remote(half_rows(q, part), half_rows(q, part), xs_send.at[24 + k], recv.at[q], seg=sib)

    twin_track, twin_rest = twin_copy(1 - c, xs_recv, 0), twin_copy(c, xu_recv, 1)

    @pl.when(home)
    def _():
        twin_track.start()
        twin_rest.start()

    @pl.when(jnp.logical_not(home))
    def _():
        over_copy(0).start()
        over_copy(1).start()

    mine_wh = wh_v.at[rows(s, T)]
    q_across = remote(wq_s.at[0], mine_wh, qs.at[0], qr.at[0], seg=across)
    q_sib = remote(wq_s.at[1], mine_wh, qs.at[1], qr.at[1], seg=sib)
    q_corner = remote(wq_s.at[1], mine_wh, qs.at[2], qr.at[2], seg=corner)
    l_sib = remote(lens_s, lens_r, qs.at[3], qr.at[3], seg=sib)
    first = (q_across, q_corner, q_sib, l_sib)
    for copy in first:
        copy.start()

    def x_copy(b, k, recv, **to):
        src = half_rows(b, c)
        return remote(src, src, xs_send.at[k], recv.at[b], **to)

    own_z, own_x = x_copy(q, 0, xs_recv, seq=near_z), x_copy(q, 8, xs_recv, seq=near_x)

    @pl.when(jnp.logical_not(home))
    def _():
        x_copy(q, 0, xs_recv, seq=q).wait_recv()

    own_z.start()
    own_x.start()

    def u_part(seg, part):
        return wu_v.at[pl.ds(pl.multiple_of(seg * T + part * HALF, HALF), HALF)]

    def o_part(seg, part):
        return wo_v.at[pl.ds(pl.multiple_of(seg * T + part * HALF, HALF), HALF)]

    u_far = tuple(
        remote(
            wu_hbm.at[pl.ds(pl.multiple_of(x * HALF, HALF), HALF), lanes(to, 1024)], u_part(s, x), ws.at[k], wr.at[k],
            seg=to,
        )
        for k, to in ((0, across), (1, corner))
    )
    u_over = tuple(
        remote(u_part(of_seg, x), u_part(of_seg, x), ws.at[11 + k], wr.at[11 + k], seq=near_x)
        for k, of_seg in ((0, across), (1, corner))
    )
    u_sib = remote(wu_hbm.at[:, lanes(sib, 1024)], wu_v.at[rows(s, T)], ws.at[2], wr.at[2], seg=sib)
    o_far = remote(
        wo_ref.at[pl.ds(pl.multiple_of(x * HALF, HALF), HALF)], o_part(s, x), ws.at[3], wr.at[3], seg=across
    )
    o_over = remote(o_part(across, x), o_part(across, x), ws.at[13], wr.at[13], seq=near_x)
    o_sib = remote(wo_ref, wo_v.at[rows(s, T)], ws.at[4], wr.at[4], seg=sib)
    o_pass = tuple(
        remote(o_part(across, part), o_part(across, part), ws.at[k], wr.at[k], seg=sib)
        for k, part in ((5, x), (14, 1 - x))
    )
    g_rows = lambda k, part: g_v.at[pl.ds(2 * T + part * T + k * HALF, HALF)]
    g_across = tuple(
        remote(g_ref.at[k * HALF : (k + 1) * HALF], g_rows(0, k), ws.at[6 + k], wr.at[6 + k], seg=across)
        for k in range(2)
    )
    g_sib = remote(g_ref, g_v.at[T : 2 * T], ws.at[8], wr.at[8], seg=sib)
    g_pass = tuple(remote(g_rows(0, k), g_rows(1, k), ws.at[9 + k], wr.at[9 + k], seg=sib) for k in range(2))
    wo_v[rows(s, T)] = wo_ref[...]
    g_v[0:T] = g_ref[...]
    for copy in u_far + (o_far,) + g_across:
        copy.start()
    for copy in first:
        copy.wait_recv()
    lens = jnp.where(home, lens_s[...], lens_r[...])

    gain, bias = gain_ref[...], bias_ref[...]

    def keep(b):
        at = rows(b, T)
        return (
            pltpu.make_async_copy(big.at[at], xs_hbm.at[at], keep_sem.at[b]),
            pltpu.make_async_copy(pack.at[b], h1_hbm.at[at], keep_sem.at[8 + b]),
        )

    def project(b):
        unit, _ = norm_parts(big[rows(b, T)].astype(F32))
        low = (unit * gain + bias).astype(BF)
        pack[b] = low
        qkv_v[rows(b, T)] = dot_nn(low, wh_v[...]).astype(BF)
        for copy in keep(b):
            copy.start()

    def track_step(k, _):
        b = nth(blocks, k)

        @pl.when(k < 8)
        def _():
            x_copy(b, 0, xs_recv, seq=q).wait_recv()

        @pl.when((k == 1) | (k == 3))
        def _():
            x_copy(b, k, xs_recv, seq=near_z).start()

        @pl.when((k == 3) | (k == 4))
        def _():
            x_copy(b, 8 + k, xs_recv, seq=near_x).start()

        @pl.when(k < 8)
        def _():
            x_copy(b, 16 + k, xu_recv, seg=sib).start()

        last = nth(blocks, k - 1)

        @pl.when((k > 1) | jnp.logical_not(home))
        def _():
            x_copy(last, 0, xu_recv, seg=sib).wait_recv()

        project(last)

        return 0

    lax.fori_loop(1, 6, track_step, 0)
    for arrived, copy in zip(u_far, u_over):
        arrived.wait_recv()
        copy.start()
    lax.fori_loop(6, 9, track_step, 0)
    o_far.wait_recv()
    o_over.start()
    o_pass[0].start()
    for copy in (u_sib, o_sib, g_sib):
        copy.start()

    def o_copy(i, sender):
        return remote(
            ob.at[i // 4, (i // 2) % 2, i % 2], o_v.at[:, lanes(sender)], os_send.at[i], os_recv.at[sender], seq=i, seg=column
        )

    o_mine = pltpu.make_async_copy(ob.at[group, z % 2, x], o_v.at[:, lanes(head)], os_recv.at[head])
    for i in (4, 5, 6, 7, 0, 1, 2, 3):
        n = (i + 1) * T
        start = first_columns(lens, i * T, T)
        scores = dot_nt(qkv_v[i * T : n, :128], qkv_v[:n, 128:256]) * scale
        scores = jnp.where(seen_mask(start, i * T, 0, T, n), scores, -1e30)
        top = jnp.max(scores, axis=1, keepdims=True)
        weights = jnp.exp(scores - top)
        total = jnp.sum(weights, axis=1, keepdims=True)
        mixed = dot_nn(weights.astype(BF), qkv_v[:n, 256:384]) / total
        of_v[i * T : n] = mixed
        lse_v[:, i : i + 1] = top + jnp.log(total)
        ob[i // 4, (i // 2) % 2, i % 2] = mixed.astype(BF)
        here = (q == i) & home

        @pl.when(jnp.logical_not(here))
        def _():
            o_copy(i, head).start()

        @pl.when(here)
        def _():
            o_mine.start()

    o_over.wait_recv()
    o_pass[1].start()
    for arrived, copy in zip(g_across, g_pass):
        arrived.wait_recv()
        copy.start()

    for i in range(8):
        o_copy(i, i).wait_recv()
    for copy in o_pass + (o_sib,):
        copy.wait_recv()

    value = x_ref[...].astype(F32) + dot_nn(o_v[...], wo_v[...])
    middle[...] = value
    unit, _ = norm_parts(value)
    h2[0:T] = (unit * gain2_ref[...] + bias2_ref[...]).astype(BF)

    def far_rows(ref, part, k):
        return ref.at[pl.ds(2 * T + k * T + part * HALF, HALF)]

    h_far = tuple(
        remote(h2.at[k * HALF : (k + 1) * HALF], far_rows(h2, 0, k), hs.at[k], hr.at[k], seg=across)
        for k in range(2)
    )
    h_pass = tuple(
        remote(far_rows(h2, 0, k), far_rows(h2, 1, k), hs.at[2 + k], hr.at[2 + k], seg=sib) for k in range(2)
    )
    h_sib = remote(h2.at[0:T], h2.at[T : 2 * T], hs.at[4], hr.at[4], seg=sib)
    for copy in h_far + (h_sib,):
        copy.start()
    for copy in loads:
        copy.wait()
    for copy in u_over + g_pass + (u_sib, g_sib):
        copy.wait_recv()
    for b in range(8):
        for copy in keep(b):
            copy.wait()
    for k in range(1, 8):
        if k in (1, 3):
            x_copy(blocks[k], k, xs_recv, seq=near_z).wait_send()
        if k in (3, 4):
            x_copy(blocks[k], 8 + k, xs_recv, seq=near_x).wait_send()
        x_copy(blocks[k], 16 + k, xu_recv, seg=sib).wait_send()

    @pl.when(home)
    def _():
        twin_track.wait_send()
        twin_rest.wait_send()

    @pl.when(jnp.logical_not(home))
    def _():
        over_copy(0).wait_send()
        over_copy(1).wait_send()

    for i in range(8):
        @pl.when(jnp.logical_not((q == i) & home))
        def _():
            o_copy(i, head).wait_send()

    for copy in first + u_far + u_over + o_pass + g_across + g_pass + (u_sib, o_far, o_over, o_sib, g_sib, own_z, own_x):
        copy.wait_send()

    def work(part):
        at = slice(part * T, (part + 1) * T)
        value, slope = gelu_parts(dot_nn(h2[at], wu_v[...]))
        low = value.astype(BF)
        big[at] = low
        du = (slope * dot_nt(g_v[at], wd_v[...])).astype(BF)
        big[4 * T + part * T : 4 * T + (part + 1) * T] = du
        return dot_nt(du, wu_v[...]), dot_nn(low, wd_v[...])

    near = tuple(remote(near_s.at[k], near_r.at[k], ns.at[k], nr.at[k], seg=sib) for k in range(2))
    twin = tuple(
        tuple(remote(twin_s.at[k, n], twin_r.at[k, n], ts.at[2 * k + n], tr.at[2 * k + n], seg=sib) for n in range(2))
        for k in range(2)
    )
    far = tuple(
        tuple(remote(far_s.at[k, n], far_r.at[k, n], fs.at[2 * k + n], fr.at[2 * k + n], seg=across) for n in range(2))
        for k in range(2)
    )

    def send_twin(n, parts):
        for k in range(2):
            far_keep[k] = parts[k][:HALF]
            twin_s[k, n] = parts[k][HALF:].astype(BF)
            twin[k][n].start()

    def send_far(n):
        for k in range(2):
            twin[k][n].wait_recv()
            far_s[k, n] = (far_keep[k] + twin_r[k, n].astype(F32)).astype(BF)
            if k == 0:
                far[k][n].start()

    parts = work(0)
    for k in range(2):
        mine[k] = parts[k]
    h_sib.wait_recv()
    parts = work(1)
    for k in range(2):
        near_s[k] = parts[k].astype(BF)
        near[k].start()
    h_far[0].wait_recv()
    h_pass[0].start()
    h_pass[0].wait_recv()
    send_twin(0, work(2))
    h_far[1].wait_recv()
    h_pass[1].start()
    send_far(0)
    h_pass[1].wait_recv()
    send_twin(1, work(3))
    send_far(1)

    def gx_copy(d):
        return remote(pack.at[2 * d + 1 - x], x_r.at[d], gxs.at[d], gxr.at[d], seq=near_x)

    zn, zc = z + 1 - 2 * (z % 2), (z + 2) % 4
    znc = (zn + 2) % 4

    def pack_rows(k, _):
        d = nth((znc, zc, zn, z), k)
        up = dot_tn(h2[:, lanes(d, T)], big[4 * T :]).astype(BF)
        down = dot_tn(big[: 4 * T], g_v[:, lanes(d, T)]).astype(BF)
        for e in range(2):
            pack[2 * d + e, :, :512] = up[:, e * 512 : (e + 1) * 512]
            for j in range(4):
                pack[2 * d + e, :, 512 + j * 128 : 640 + j * 128] = down[
                    j * T : (j + 1) * T, e * 128 : (e + 1) * 128
                ]

        @pl.when(k < 1)
        def _():
            gx_copy(d).start()

        return 0

    lax.fori_loop(0, 4, pack_rows, 0)

    near[0].wait_recv()
    far[0][0].wait_recv()
    far[0][1].wait_recv()
    grad = mine[0] + near_r[0].astype(F32) + jnp.concatenate([far_r[0, 0], far_r[0, 1]], axis=0).astype(F32)
    unit, inverse = norm_parts(middle[...])
    vec[...] = jnp.zeros_like(vec)
    vec[2:3] = jnp.sum(grad * unit, axis=0, keepdims=True)
    vec[3:4] = jnp.sum(grad, axis=0, keepdims=True)
    dx = g_v[0:T].astype(F32) + norm_back(grad, gain2_ref[...], unit, inverse)
    dx_v[...] = dx
    dy = dx.astype(BF)
    do_v[...] = dot_nt(dy, wo_v[...]).astype(BF)

    def do_copy(h, block):
        return remote(
            do_v.at[:, h * 128 : (h + 1) * 128], doh.at[rows(block, T)], dos.at[h], dor.at[block],
            seq=2 * (2 * c + h // 4) + (h // 2) % 2, seg=2 * y + h % 2,
        )

    do_mine = pltpu.make_async_copy(do_v.at[:, lanes(head)], doh.at[rows(q, T)], dor.at[q])
    for h in range(8):
        self_too = (head == h) & home

        @pl.when(jnp.logical_not(self_too))
        def _():
            do_copy(h, q).start()

        @pl.when(self_too)
        def _():
            do_mine.start()

    for copy in h_far + h_pass + (h_sib,):
        copy.wait_send()
    h2[...] = dot_tn(o_v[...], dy).astype(BF)

    def out_rows(part, core):
        return h2.at[rows(2 * part + core, T)]

    out_core = tuple(remote(out_rows(k, 1 - c), oc_r.at[k], cs.at[5 + k], cr.at[5 + k], seg=sib) for k in range(2))
    for copy in out_core:
        copy.start()
    for part in range(2):
        out_core[part].wait_recv()
        oc_r[part] = (oc_r[part].astype(F32) + out_rows(part, c)[...].astype(F32)).astype(BF)
    out_y = remote(oc_r.at[1 - y], oy_r, cs.at[1], cr.at[1], seg=across)
    out_y.start()
    far[1][0].start()
    far[1][1].start()

    def come(into, recv, slot):
        return remote(into.at[slot], into.at[slot], recv.at[slot], recv.at[slot], seq=near_x)

    def gz_copy(k, d, to):
        return remote(x_r.at[d], z_r.at[k], gzs.at[k], gzr.at[k], seq=to)

    gz = (gz_copy(0, znc, near_z), gz_copy(1, zn, near_z), gz_copy(2, zc, cross))

    def pack_sum(d):
        gx_copy(d).wait_recv()
        return pack[2 * d + x].astype(F32) + x_r[d].astype(F32)

    x_r[znc] = pack_sum(znc).astype(BF)
    gz[0].start()
    gx_copy(zc).start()

    dk[...] = jnp.zeros_like(dk)
    dv[...] = jnp.zeros_like(dv)
    for i in range(8):
        do_copy(0, i).wait_recv()
        top = i * T
        start = first_columns(lens, top, T)
        query = qkv_v[top : top + T, :128]
        grad = doh[top : top + T]
        delta = jnp.sum(grad.astype(F32) * of_v[top : top + T], axis=1, keepdims=True)
        log_total = lse_v[:, i : i + 1]
        total = jnp.zeros((T, 128), F32)
        for base in range(0, top + T, 1024):
            n = min(1024, top + T - base)
            keys = qkv_v[base : base + n, 128:256]
            probs = jnp.exp(dot_nt(query, keys) * scale - log_total)
            probs = jnp.where(seen_mask(start, top, base, T, n), probs, 0.0)
            dp = dot_nt(grad, qkv_v[base : base + n, 256:384])
            ds = (probs * (dp - delta)).astype(BF)
            dv[base : base + n] += dot_tn(probs.astype(BF), grad)
            dk[base : base + n] += dot_tn(ds, query)
            total += dot_nn(ds, keys)
        dq[top : top + T] = total

    gq[...] = jnp.zeros_like(gq)
    own_a, other_xa, other_za, own_b, other_zb, other_xb, diag_a, diag_b = blocks
    order = (diag_a, diag_b, other_za, other_xb, other_xa, other_zb, own_a, own_b)

    def x_load(i):
        return pltpu.make_async_copy(xs_hbm.at[rows(nth(order, i), T)], wu_v.at[rows(i % 2, T)], load_sem.at[2 + i % 2])

    def h_load(i):
        return pltpu.make_async_copy(h1_hbm.at[rows(nth(order, i), T)], wu_v.at[rows(2 + i % 2, T)], load_sem.at[4 + i % 2])

    def dhc_copy(b):
        return remote(
            big.at[pl.ds(pl.multiple_of(b * T + (1 - c) * HALF, HALF), HALF)], wo_v.at[rows(b, HALF)], dcs.at[b], dcr.at[b], seg=sib
        )

    def half(b):
        return big.at[pl.ds(pl.multiple_of(b * T + c * HALF, HALF), HALF)]

    def step_copy(k, b, to):
        return remote(wo_v.at[rows(b, HALF)], wd_v.at[rows(k, HALF)], sts.at[k], str_.at[k], seq=to)

    steps = (
        step_copy(0, diag_a, near_z), step_copy(1, diag_b, near_x), step_copy(2, other_za, near_z),
        step_copy(3, other_xb, near_x), step_copy(4, other_xa, near_x), step_copy(5, other_zb, near_z),
    )
    x_load(0).start()
    h_load(0).start()

    def grads_at(at):
        return jnp.concatenate([dq[at] * scale, dk[at] * scale, dv[at]], axis=1).astype(BF)

    def block_step(i, _):
        @pl.when(i < 8)
        def _():
            b = nth(order, i)

            at = rows(b, T)
            big[at] = dot_nt(grads_at(at), wh_v[...]).astype(BF)
            dhc_copy(b).start()

        @pl.when(i > 0)
        def _():
            b = nth(order, i - 1)
            dhc_copy(b).wait_recv()
            wo_v[rows(b, HALF)] = (half(b)[...].astype(F32) + wo_v[rows(b, HALF)].astype(F32)).astype(BF)
            for k in range(4):
                @pl.when(i == k + 1)
                def _():
                    steps[k].start()

        return 0

    lax.fori_loop(0, 9, block_step, 0)
    gx_copy(zn).start()
    gz[0].wait_recv()
    x_r[zc] = (pack_sum(zc) + z_r[0].astype(F32)).astype(BF)
    gz[2].start()


    def sum_step(i, _):
        @pl.when(i < 7)
        def _():
            x_load(i + 1).start()
            h_load(i + 1).start()

        at = rows(nth(order, i), T)
        dh = big[at].astype(F32)
        x_load(i).wait()
        h_load(i).wait()
        gq[...] += dot_tn(wu_v[rows(2 + i % 2, T)], grads_at(at))
        unit, _ = norm_parts(wu_v[rows(i % 2, T)].astype(F32))
        vec[0:1] += jnp.sum(dh * unit, axis=0, keepdims=True)
        vec[1:2] += jnp.sum(dh, axis=0, keepdims=True)
        return 0

    lax.fori_loop(0, 8, sum_step, 0)
    for k, b in ((5, other_zb), (4, other_xa)):
        steps[k - 4].wait_recv()
        wo_v[rows(b, HALF)] = (wo_v[rows(b, HALF)].astype(F32) + wd_v[(k - 4) * HALF : (k - 3) * HALF].astype(F32)).astype(BF)
        steps[k].start()

    x_r[zn] = pack_sum(zn).astype(BF)
    gz[1].start()

    out_y.wait_recv()
    out = (oc_r[y].astype(F32) + oy_r[...].astype(F32)).astype(BF)
    for k in range(8):
        ob[k // 4, (k // 2) % 2, k % 2] = out[:, k * 128 : (k + 1) * 128]
    out_x = remote(ob.at[:, :, 1 - x], ox_r, cs.at[2], cr.at[2], seq=near_x)
    out_x.start()
    gx_copy(z).start()

    gq_b[...] = gq[...].astype(BF).reshape(2, 2, T, 384)
    q_y = remote(gq_b.at[1 - y], gq_y, gqs.at[0], gqr.at[0], seg=across)
    q_y.start()
    v_core = remote(vec, vec_r.at[0], vs.at[8], vr.at[8], seg=sib)
    v_core.start()
    v_core.wait()
    vec[...] += vec_r[0]
    v_y = remote(vec, vec_r.at[1], vs.at[9], vr.at[9], seg=across)
    v_y.start()
    def fin_sum(k, b, pair):
        for n in pair:
            steps[n].wait_recv()
        fin_s[k] = (
            wo_v[rows(b, HALF)].astype(F32) + wd_v[rows(pair[0], HALF)].astype(F32)
            + wd_v[rows(pair[1], HALF)].astype(F32)
        ).astype(BF)

    fin_over = remote(fin_s.at[1], fin_r.at[c], fns.at[0], fnr.at[c], seq=cross, seg=column)
    fin_twin = remote(fin_s.at[0], fin_r.at[c], fns.at[1], fnr.at[c], seg=sib)
    fin_own = pltpu.make_async_copy(fin_s.at[0], fin_r.at[c], fnr.at[c])
    fin_sum(1, own_b, (3, 5))
    fin_over.start()
    fin_sum(0, own_a, (2, 4))

    @pl.when(away)
    def _():
        fin_twin.start()

    @pl.when(home)
    def _():
        fin_own.start()

    v_y.wait()
    vec[...] += vec_r[1]

    def v_copy(b, sender):
        return remote(vec, vec_r.at[2 + sender], vs.at[b], vr.at[sender], seq=b)

    for b in range(8):
        @pl.when(q != b)
        def _():
            v_copy(b, q).start()

    q_y.wait_recv()
    gq_y[...] = (gq_y[...].astype(F32) + gq_b[y].astype(F32)).astype(BF)

    def column_copy(part, j):
        place = 8 * j + head
        owner, slot = place // 3, place % 3
        src = gq_y.at[part, :, j * 128 : (j + 1) * 128]
        copy = remote(
            src, gq_r.at[slot, group], gqs.at[1 + 3 * part + j], gqr.at[1 + 2 * slot + group],
            seq=owner, seg=2 * y + part,
        )
        local = pltpu.make_async_copy(src, gq_r.at[slot, group], gqr.at[1 + 2 * slot + group])
        return (owner == q) & (c == part), copy, local

    columns = tuple(column_copy(part, j) for part in range(2) for j in range(3))
    out_x.wait_recv()
    ox_r[...] = (ox_r[...].astype(F32) + ob[:, :, x].astype(F32)).astype(BF)
    out_z = remote(ox_r.at[:, 1 - z % 2], oz_r, cs.at[3], cr.at[3], seq=near_z)
    out_z.start()
    for self_too, copy, local in columns:
        @pl.when(jnp.logical_not(self_too))
        def _():
            copy.start()

        @pl.when(self_too)
        def _():
            local.start()

    out_z.wait_recv()
    oz_r[...] = (oz_r[...].astype(F32) + ox_r[:, z % 2].astype(F32)).astype(BF)
    out_o = remote(oz_r.at[1 - group], oo_r, cs.at[4], cr.at[4], seq=cross)
    out_o.start()

    total = pack_sum(z)
    for k in (1, 2):
        gz[k].wait_recv()
        total = total + z_r[k].astype(F32)
    up_s[...] = total[:, :512].astype(BF)
    turned = s != z
    up_turn = remote(up_s, up_r, ups, upr, seq=2 * s + x, seg=z)
    up_own = pltpu.make_async_copy(up_s, up_r, upr)

    @pl.when(turned)
    def _():
        up_turn.start()

    @pl.when(jnp.logical_not(turned))
    def _():
        up_own.start()

    for j in range(4):
        gdown_out[j * T : (j + 1) * T] = total[:, 512 + j * 128 : 640 + j * 128]
    vec_r[2 + q] = vec[...]
    for b in range(8):
        @pl.when(q != b)
        def _():
            v_copy(b, b).wait_recv()

    vec_sum = vec_r[2]
    for b in range(1, 8):
        vec_sum = vec_sum + vec_r[2 + b]
    out_o.wait_recv()
    gout_out[...] = oz_r[group].astype(F32) + oo_r[...].astype(F32)
    sums_out[...] = vec_sum
    for slot in range(3):
        for part in range(2):
            pltpu.make_async_copy(gq_r.at[slot, part], gq_r.at[slot, part], gqr.at[1 + 2 * slot + part]).wait()
    near[1].wait_recv()
    far[1][0].wait_recv()
    far[1][1].wait_recv()
    result_out[...] = (
        middle[...] + mine[1] + near_r[1].astype(F32)
        + jnp.concatenate([far_r[1, 0], far_r[1, 1]], axis=0).astype(F32)
    ).astype(BF)
    for k in range(2):
        come(fin_r, fnr, k).wait_recv()
    up_own.wait()

    for h in range(8):
        @pl.when(jnp.logical_not((head == h) & home))
        def _():
            do_copy(h, q).wait_send()

    for b in range(8):
        dhc_copy(b).wait_send()

        @pl.when(q != b)
        def _():
            v_copy(b, q).wait_send()

    for d in range(4):
        gx_copy(d).wait_send()
    for copy in out_core + (out_y, out_x, out_z, out_o, q_y, fin_over) + near + steps + gz:
        copy.wait_send()
    for k in range(2):
        for n in range(2):
            twin[k][n].wait_send()
            far[k][n].wait_send()

    @pl.when(away)
    def _():
        fin_twin.wait_send()

    @pl.when(turned)
    def _():
        up_turn.wait_send()

    for self_too, copy, _ in columns:
        @pl.when(jnp.logical_not(self_too))
        def _():
            copy.wait_send()


def layer(x, lens, g, wo, gain, bias, gain2, bias2, wq, wu, wd):
    dma = pltpu.SemaphoreType.DMA
    low = lambda *shape: pltpu.VMEM(shape, BF)
    wide = lambda *shape: pltpu.VMEM(shape, F32)
    return pl.pallas_call(
        layer_kernel,
        out_shape=(
            S((256, 1024), BF), S((256, 1024), F32), S((2, 128, 1024), BF), S((3, 2, 256, 128), BF),
            S((256, 128), F32), S((256, 512), BF), S((1024, 128), F32), S((8, 1024), F32),
            S((2048, 1024), BF), S((2048, 1024), BF),
        ),
        in_specs=[VM, SM] + [VM] * 6 + [HB] * 3,
        out_specs=(VM,) * 8 + (HB,) * 2,
        scratch_shapes=[
            low(1024, 1024), low(1024, 1024), low(1024, 1024), low(1024, 1024), low(256, 1024), low(2048, 384),
            wide(2048, 128), wide(256, 8), low(1024, 384), dma((16,)),
            dma((16,)), low(2, 2, 2, 256, 128), low(2, 256, 384), pltpu.VMEM((8, 128), jnp.int32),
            pltpu.VMEM((8, 128), jnp.int32), dma((4,)), dma((4,)), dma((15,)), dma((15,)),
            dma((26,)), dma((8,)), dma((8,)), dma((8,)), dma((8,)),
            wide(256, 1024), low(1024, 1024), low(2048, 1024), wide(2, 256, 1024),
            low(2, 256, 1024), low(2, 256, 1024), low(2, 2, 128, 1024), low(2, 2, 128, 1024), wide(2, 128, 1024),
            low(2, 2, 128, 1024), low(2, 2, 128, 1024), low(256, 1024),
            dma((5,)), dma((5,)), dma((2,)), dma((2,)), dma((4,)), dma((4,)), dma((4,)), dma((4,)),
            low(8, 256, 1024), low(4, 256, 1024), low(3, 256, 1024), low(256, 512),
            dma((4,)), dma((4,)), dma((3,)), dma((3,)), dma, dma,
            low(2, 256, 1024), low(256, 1024), low(2, 2, 256, 128),
            low(2, 256, 128), low(256, 128), dma((7,)), dma((7,)),
            low(2048, 128), wide(2048, 128), wide(2048, 128), wide(2048, 128), dma((8,)), dma((8,)),
            low(2, 128, 1024),
            dma((8,)), dma((8,)), dma((6,)), dma((6,)), dma((2,)), dma((2,)),
            wide(1024, 384), low(2, 2, 256, 384), low(2, 256, 384),
            dma((7,)), dma((7,)),
            wide(8, 1024), wide(10, 8, 1024), dma((10,)), dma((10,)),
        ],
        compiler_params=pltpu.CompilerParams(
            collective_id=1, has_side_effects=True, vmem_limit_bytes=63 * 2**20
        ),
        cost_estimate=pl.CostEstimate(flops=2 * 10**10, bytes_accessed=40 * 2**20, transcendentals=2 * 2**20),
        name="layer",
    )(x, lens, g, wo, gain, bias, gain2, bias2, wq, wu, wd)


def finish_kernel(
    x_ref, gain_ref, result_ref, dx_ref, fin_ref, gq_ref, out_ref, up_ref, down_ref, sums_ref,
    result, dx, gain_one, bias_one, gqkv, gout, gain_two, bias_two, gup, gdown,
):
    result[...] = result_ref[...]
    unit, inverse = norm_parts(x_ref[...].astype(F32))
    dx[...] = dx_ref[...] + norm_back(fin_ref[0].astype(F32), gain_ref[...], unit, inverse)
    for slot in range(3):
        gqkv[:, slot * 128 : (slot + 1) * 128] = gq_ref[slot, 0].astype(F32) + gq_ref[slot, 1].astype(F32)
    gout[...] = out_ref[...]
    gup[...] = up_ref[...].astype(F32)
    gdown[...] = down_ref[...]
    for k, ref in enumerate((gain_one, bias_one, gain_two, bias_two)):
        ref[...] = sums_ref[k]


def finish(x, gain, *parts):
    line = S((1024,), F32)
    part = lambda r, n: pl.BlockSpec((r // 2, n), lambda i: (i, 0))
    whole = lambda r, n: pl.BlockSpec((r, n), lambda i: (0, 0))
    row = pl.BlockSpec((1024,), lambda i: (0,))
    return pl.pallas_call(
        finish_kernel,
        grid=(2,),
        out_shape=(
            S((256, 1024), BF), S((256, 1024), F32), line, line, S((256, 384), F32), S((256, 128), F32), line, line,
            S((256, 512), F32), S((1024, 128), F32),
        ),
        in_specs=[
            part(256, 1024), whole(1, 1024), part(256, 1024), part(256, 1024),
            pl.BlockSpec((1, 128, 1024), lambda i: (i, 0, 0)),
            pl.BlockSpec((3, 2, 128, 128), lambda i: (0, 0, i, 0)), part(256, 128), part(256, 512), part(1024, 128),
            whole(8, 1024),
        ],
        out_specs=(
            part(256, 1024), part(256, 1024), row, row, part(256, 384), part(256, 128), row, row, part(256, 512),
            part(1024, 128),
        ),
        compiler_params=pltpu.CompilerParams(vmem_limit_bytes=60 * 2**20),
        name="finish",
    )(x, gain, *parts)


def per_device_fast(
    tokens, article_lengths, gain_one, bias_one, w_qkv, w_out, gain_two, bias_two, w_up, w_down, cotangent
):
    x = tokens[0]
    *parts, _, _ = layer(
        x, article_lengths, cotangent[0], w_out, gain_one[None], bias_one[None], gain_two[None], bias_two[None],
        w_qkv, w_up, w_down,
    )
    result, dx, *rest = finish(x, gain_one[None], *parts)
    return (result[None], dx[None], *rest)


def solution(mesh):
    one_pair = mesh.shape["seq"] == HEADS and mesh.shape["seg"] == 4
    return jax.shard_map(
        per_device_fast if one_pair else per_device,
        mesh=mesh,
        in_specs=(
            P("seg", "seq", None),
            P("seg", None),
            P(),
            P(),
            P("seg", None),
            P("seg", None),
            P(),
            P(),
            P("seg", None),
            P("seg", None),
            P("seg", "seq", None),
        ),
        out_specs=(
            P("seg", "seq", None),
            P("seg", "seq", None),
            P(),
            P(),
            P("seg", "seq"),
            P("seg", "seq"),
            P(),
            P(),
            P("seg", "seq"),
            P("seg", "seq"),
        ),
        check_vma=False,
    )
```

```python
import math

import jax
import jax.numpy as jnp
from jax import lax
from jax.experimental import pallas as pl
from jax.experimental.pallas import tpu as pltpu
from jax.sharding import PartitionSpec as P

HEADS = 8
HEAD_DIM = 128


def passed_along(block, axis, distance):
    devices = range(lax.axis_size(axis))
    route = [(i - distance, i) for i in devices if i - distance in devices]
    return lax.ppermute(block, axis, route)


def shifted(value, axis, by):
    size = lax.axis_size(axis)
    return lax.ppermute(value, axis, [(i, (i + by) % size) for i in range(size)])


def layer_norm(values, gain, bias):
    center = values - jnp.mean(values, axis=-1, keepdims=True)
    spread = jnp.mean(center * center, axis=-1, keepdims=True)
    return center * lax.rsqrt(spread + 1e-05) * gain + bias


def smooth_act(values):
    return jax.nn.gelu(values, approximate=True)


def article_numbers(lengths_row, positions):
    bounds = jnp.cumsum(lengths_row)
    return jnp.sum((positions[:, None] >= bounds[None, :]).astype(jnp.int32), axis=1)


def per_device(
    tokens,
    article_lengths,
    gain_one,
    bias_one,
    w_qkv,
    w_out,
    gain_two,
    bias_two,
    w_up,
    w_down,
    cotangent,
):
    tok_rows = tokens.shape[1]
    model_width = tokens.shape[2]
    head_count = HEADS
    head_size = HEAD_DIM
    scale = 1.0 / math.sqrt(head_size)
    blocks_seq = lax.axis_size("seq")
    my_place = lax.axis_index("seq")
    full_qkv, full_out, full_up, full_down = (
        lax.all_gather(w_qkv, "seg", axis=0, tiled=True),
        lax.all_gather(w_out, "seg", axis=0, tiled=True),
        lax.all_gather(w_up, "seg", axis=0, tiled=True),
        lax.all_gather(w_down, "seg", axis=0, tiled=True),
    )
    inputs = tokens[0].astype(jnp.float32)
    normed, norm_one_back = jax.vjp(layer_norm, inputs, gain_one, bias_one)
    normed_low = normed.astype(jnp.bfloat16)
    projected = jnp.dot(normed_low, full_qkv, preferred_element_type=jnp.float32).astype(
        jnp.bfloat16
    )
    query_low = projected[:, :model_width]
    key_low = projected[:, model_width : 2 * model_width]
    value_low = projected[:, 2 * model_width :]
    query_heads = query_low.reshape(tok_rows, head_count, head_size)
    lengths_row = article_lengths[0]
    positions = my_place * tok_rows + jnp.arange(tok_rows, dtype=jnp.int32)
    query_art = article_numbers(lengths_row, positions)

    def scores_of(key_block, source):
        key_pos = source * tok_rows + jnp.arange(tok_rows, dtype=jnp.int32)
        key_art = article_numbers(lengths_row, key_pos)
        allowed = (key_pos[None, :] <= positions[:, None]) & (
            key_art[None, :] == query_art[:, None]
        )
        raw = (
            jnp.einsum(
                "qhd,khd->hqk",
                query_heads,
                key_block.reshape(tok_rows, head_count, head_size),
                preferred_element_type=jnp.float32,
            )
            * scale
        )
        return jnp.where(allowed[None], raw, -1e30)

    def forward_block(state, key_block, value_block, source):

        def forward_work(operands):
            (top, total, accum), key_now, value_now = operands
            scores = scores_of(key_now, source)
            new_top = jnp.maximum(top, jnp.max(scores, axis=2))
            factor = jnp.exp(top - new_top)
            weights = jnp.exp(scores - new_top[:, :, None])
            total = total * factor + jnp.sum(weights, axis=2)
            gathered = jnp.einsum(
                "hqk,khd->qhd",
                weights.astype(jnp.bfloat16),
                value_now.reshape(tok_rows, head_count, head_size),
                preferred_element_type=jnp.float32,
            ).reshape(tok_rows, model_width)
            accum = accum * jnp.repeat(factor.T, head_size, axis=1) + gathered
            return (new_top, total, accum)

        def forward_keep(operands):
            return operands[0]

        return lax.cond(
            source <= my_place, forward_work, forward_keep, (state, key_block, value_block)
        )

    start_state = (
        jnp.full((head_count, tok_rows), -1e30, jnp.float32),
        jnp.zeros((head_count, tok_rows), jnp.float32),
        jnp.zeros((tok_rows, model_width), jnp.float32),
    )
    state = forward_block(start_state, key_low, value_low, my_place)

    def forward_step(step, carry):
        key_block, value_block, state_now = carry
        key_block, value_block = passed_along((key_block, value_block), "seq", 1)
        source = (my_place - step) % blocks_seq
        return (key_block, value_block, forward_block(state_now, key_block, value_block, source))

    _, _, state = lax.fori_loop(1, blocks_seq, forward_step, (key_low, value_low, state))
    top, total, accum = state
    log_total = top + jnp.log(total)
    attended = accum / jnp.repeat(total.T, head_size, axis=1)
    attended_low = attended.astype(jnp.bfloat16)
    middle = inputs + jnp.dot(attended_low, full_out, preferred_element_type=jnp.float32)
    normed_two, norm_two_back = jax.vjp(layer_norm, middle, gain_two, bias_two)
    normed_two_low = normed_two.astype(jnp.bfloat16)
    hidden = jnp.dot(normed_two_low, full_up, preferred_element_type=jnp.float32)
    activated, act_back = jax.vjp(smooth_act, hidden)
    activated_low = activated.astype(jnp.bfloat16)
    outputs = middle + jnp.dot(activated_low, full_down, preferred_element_type=jnp.float32)
    result = outputs.astype(jnp.bfloat16)[None]
    grad_top = cotangent[0].astype(jnp.float32)
    grad_top_low = cotangent[0]
    grad_down = jnp.einsum(
        "tf,td->fd", activated_low, grad_top_low, preferred_element_type=jnp.float32
    )
    grad_act = jnp.einsum("td,fd->tf", grad_top_low, full_down, preferred_element_type=jnp.float32)
    (grad_hidden,) = act_back(grad_act)
    grad_hidden_low = grad_hidden.astype(jnp.bfloat16)
    grad_up = jnp.einsum(
        "td,tf->df", normed_two_low, grad_hidden_low, preferred_element_type=jnp.float32
    )
    grad_normed_two = jnp.einsum(
        "tf,df->td", grad_hidden_low, full_up, preferred_element_type=jnp.float32
    )
    grad_mid_norm, grad_gain_two, grad_bias_two = norm_two_back(grad_normed_two)
    grad_middle = grad_top + grad_mid_norm
    grad_middle_low = grad_middle.astype(jnp.bfloat16)
    grad_out = jnp.einsum(
        "tc,td->cd", attended_low, grad_middle_low, preferred_element_type=jnp.float32
    )
    grad_att = jnp.einsum(
        "td,cd->tc", grad_middle_low, full_out, preferred_element_type=jnp.float32
    )
    grad_att_low = grad_att.astype(jnp.bfloat16)
    grad_att_heads = grad_att_low.reshape(tok_rows, head_count, head_size)
    offsets = jnp.sum(
        (grad_att_low.astype(jnp.float32) * attended).reshape(tok_rows, head_count, head_size),
        axis=2,
    ).T

    def backward_block(operands, source):

        def backward_work(inner):
            grad_query, grad_key, grad_value, key_now, value_now = inner
            key_heads = key_now.reshape(tok_rows, head_count, head_size)
            value_heads = value_now.reshape(tok_rows, head_count, head_size)
            probs = jnp.exp(scores_of(key_now, source) - log_total[:, :, None])
            probs_low = probs.astype(jnp.bfloat16)
            grad_value = grad_value + jnp.einsum(
                "hqk,qhd->khd", probs_low, grad_att_heads, preferred_element_type=jnp.float32
            ).reshape(tok_rows, model_width)
            grad_probs = jnp.einsum(
                "qhd,khd->hqk", grad_att_heads, value_heads, preferred_element_type=jnp.float32
            )
            grad_scores = (probs * (grad_probs - offsets[:, :, None])).astype(jnp.bfloat16)
            grad_query = (
                grad_query
                + jnp.einsum(
                    "hqk,khd->qhd", grad_scores, key_heads, preferred_element_type=jnp.float32
                ).reshape(tok_rows, model_width)
                * scale
            )
            grad_key = (
                grad_key
                + jnp.einsum(
                    "hqk,qhd->khd", grad_scores, query_heads, preferred_element_type=jnp.float32
                ).reshape(tok_rows, model_width)
                * scale
            )
            return (grad_query, grad_key, grad_value, key_now, value_now)

        def backward_keep(inner):
            return inner

        return lax.cond(source <= my_place, backward_work, backward_keep, operands)

    def backward_step(step, carry):
        source = (my_place - step) % blocks_seq
        grad_query, grad_key, grad_value, key_block, value_block = backward_block(carry, source)
        key_block, value_block = passed_along((key_block, value_block), "seq", 1)
        grad_key, grad_value = (
            shifted(grad_key.astype(jnp.bfloat16), "seq", 1).astype(grad_key.dtype),
            shifted(grad_value.astype(jnp.bfloat16), "seq", 1).astype(grad_value.dtype),
        )
        return (grad_query, grad_key, grad_value, key_block, value_block)

    zero_rows = jnp.zeros((tok_rows, model_width), jnp.float32)
    grad_query, grad_key, grad_value, _, _ = lax.fori_loop(
        0, blocks_seq, backward_step, (zero_rows, zero_rows, zero_rows, key_low, value_low)
    )
    grad_proj_low = jnp.concatenate([grad_query, grad_key, grad_value], axis=1).astype(jnp.bfloat16)
    grad_qkv = jnp.einsum(
        "tc,tk->ck", normed_low, grad_proj_low, preferred_element_type=jnp.float32
    )
    grad_normed = jnp.einsum(
        "tk,ck->tc", grad_proj_low, full_qkv, preferred_element_type=jnp.float32
    )
    grad_in_norm, grad_gain_one, grad_bias_one = norm_one_back(grad_normed)
    input_grad = (grad_middle + grad_in_norm)[None]
    part_qkv, part_out, part_up, part_down = (
        lax.psum_scatter(
            grad_qkv.astype(jnp.bfloat16), "seg", scatter_dimension=0, tiled=True
        ).astype(jnp.float32),
        lax.psum_scatter(
            grad_out.astype(jnp.bfloat16), "seg", scatter_dimension=0, tiled=True
        ).astype(jnp.float32),
        lax.psum_scatter(
            grad_up.astype(jnp.bfloat16), "seg", scatter_dimension=0, tiled=True
        ).astype(jnp.float32),
        lax.psum_scatter(
            grad_down.astype(jnp.bfloat16), "seg", scatter_dimension=0, tiled=True
        ).astype(jnp.float32),
    )
    sum_qkv, sum_out, sum_up, sum_down = (
        lax.psum_scatter(
            part_qkv.astype(jnp.bfloat16), "seq", scatter_dimension=1, tiled=True
        ).astype(jnp.float32),
        lax.psum_scatter(
            part_out.astype(jnp.bfloat16), "seq", scatter_dimension=1, tiled=True
        ).astype(jnp.float32),
        lax.psum_scatter(
            part_up.astype(jnp.bfloat16), "seq", scatter_dimension=1, tiled=True
        ).astype(jnp.float32),
        lax.psum_scatter(
            part_down.astype(jnp.bfloat16), "seq", scatter_dimension=1, tiled=True
        ).astype(jnp.float32),
    )
    sum_gain_one, sum_bias_one, sum_gain_two, sum_bias_two = lax.psum(
        (grad_gain_one, grad_bias_one, grad_gain_two, grad_bias_two), ("seq", "seg")
    )
    return (
        result,
        input_grad,
        sum_gain_one,
        sum_bias_one,
        sum_qkv,
        sum_out,
        sum_gain_two,
        sum_bias_two,
        sum_up,
        sum_down,
    )


MESH = pl.DeviceIdType.MESH
BF = jnp.bfloat16
F32 = jnp.float32
def dot_nn(a, b):
    return lax.dot_general(a, b, (((1,), (0,)), ((), ())), preferred_element_type=F32)


def dot_nt(a, b):
    return lax.dot_general(a, b, (((1,), (1,)), ((), ())), preferred_element_type=F32)


def dot_tn(a, b):
    return lax.dot_general(a, b, (((0,), (0,)), ((), ())), preferred_element_type=F32)


def remote(src, dst, send, recv, **place):
    return pltpu.make_async_remote_copy(
        src_ref=src, dst_ref=dst, send_sem=send, recv_sem=recv, device_id=place, device_id_type=MESH
    )


def norm_parts(values):
    center = values - jnp.mean(values, axis=-1, keepdims=True)
    spread = jnp.mean(center * center, axis=-1, keepdims=True)
    inverse = lax.rsqrt(spread + 1e-05)
    return center * inverse, inverse


def greet(q, s, transposed=False):
    y, c = s // 2, s % 2
    barrier = pltpu.get_barrier_semaphore()

    def signal(seq, seg):
        pl.semaphore_signal(barrier, 1, device_id={"seq": seq, "seg": seg}, device_id_type=MESH)

    for d in range(1, 8):
        for core in range(2):
            signal(lax.rem(q + d, 8), 2 * y + core)
    for d in range(1, 4):
        signal(q, lax.rem(s + d, 4))
    if transposed:
        turned = s != q // 2

        @pl.when(turned)
        def _():
            signal(2 * s + q % 2, q // 2)

        return lambda: pl.semaphore_wait(barrier, jnp.where(turned, 18, 17))
    return lambda: pl.semaphore_wait(barrier, 17)


def first_columns(lens, base, rows):
    place = base + lax.broadcasted_iota(jnp.int32, (rows, 1), 0)
    start = jnp.zeros((rows, 1), jnp.int32)
    bound = jnp.zeros((1, 1), jnp.int32)
    for i in range(lens.shape[0]):
        bound = bound + lens[i : i + 1, 0:1]
        start = jnp.where(place >= bound, bound, start)
    return start


def seen_mask(start, base_q, base_k, rows, columns):
    place = base_q + lax.broadcasted_iota(jnp.int32, (rows, columns), 0)
    key = base_k + lax.broadcasted_iota(jnp.int32, (rows, columns), 1)
    return (key <= place) & (key >= start)


def rows(k, n):
    return pl.ds(k * n if isinstance(k, int) else pl.multiple_of(k * n, n), n)


def lanes(k, n=128):
    return pl.ds(pl.multiple_of(k * n, n), n)


T = 256
HALF = 128


def places(z, x):
    zn, zc = z + 1 - 2 * (z % 2), (z + 2) % 4
    znc = (zn + 2) % 4
    here, near_z, near_x, cross = 2 * z + x, 2 * zn + x, 2 * z + 1 - x, 2 * zc + x
    blocks = (here, near_x, near_z, cross, 2 * znc + x, 2 * zc + 1 - x, 2 * zn + 1 - x, 2 * znc + 1 - x)
    return here, near_z, near_x, cross, blocks


def nth(values, k):
    out = values[0]
    for i, value in enumerate(values[1:], 1):
        out = jnp.where(k == i, value, out)
    return out


VM = pl.BlockSpec(memory_space=pltpu.VMEM)
HB = pl.BlockSpec(memory_space=pl.ANY)
S = jax.ShapeDtypeStruct
SM = pl.BlockSpec(memory_space=pltpu.SMEM)


def gelu_parts(u):
    root = math.sqrt(2.0 / math.pi)
    square = u * u
    t = jnp.tanh(root * (u + 0.044715 * (square * u)))
    value = 0.5 * u * (1.0 + t)
    slope = 0.5 * (1.0 + t) + 0.5 * u * (1.0 - t * t) * (root * (1.0 + 0.134145 * square))
    return value, slope


def norm_back(grad, gain, unit, inverse):
    through = grad * gain
    a = jnp.mean(through, axis=-1, keepdims=True)
    b = jnp.mean(through * unit, axis=-1, keepdims=True)
    return inverse * (through - a - unit * b)


def layer_kernel(
    x_ref, lens_ref, g_ref, wo_ref, gain_ref, bias_ref, gain2_ref, bias2_ref, wq_hbm, wu_hbm, wd_hbm,
    result_out, dx_v, fin_r, gq_r, gout_out, up_r, gdown_out, sums_out, xs_hbm, h1_hbm,
    g_v, wu_v, wd_v, wo_v, o_v, qkv_v, of_v, lse_v, wh_v, load_sem,
    keep_sem, ob, wq_s, lens_s, lens_r, qs, qr, ws, wr, xs_send, xs_recv, xu_recv, os_send, os_recv,
    middle, h2, big, mine, near_s, near_r, twin_s, twin_r, far_keep, far_s, far_r, do_v,
    hs, hr, ns, nr, ts, tr, fs, fr,
    pack, x_r, z_r, up_s, gxs, gxr, gzs, gzr, ups, upr,
    oc_r, oy_r, ox_r, oz_r, oo_r, cs, cr,
    doh, dq, dk, dv, dos, dor,
    fin_s, dcs, dcr, sts, str_, fns, fnr,
    gq, gq_b, gq_y, gqs, gqr,
    vec, vec_r, vs, vr,
):
    q, s = lax.axis_index("seq"), lax.axis_index("seg")
    z, x = q // 2, q % 2
    y, c = s // 2, s % 2
    sib = s + 1 - 2 * c
    across = (1 - y) * 2 + c
    corner = (1 - y) * 2 + 1 - c
    group = z // 2
    head = 4 * (z % 2) + 2 * x + c
    other_head = head + 1 - 2 * c
    home = c == group
    away = jnp.logical_not(home)
    column = 2 * y + group
    here, near_z, near_x, cross, blocks = places(z, x)
    scale = 1.0 / math.sqrt(HEAD_DIM)

    met = greet(q, s, True)

    picks = tuple(
        pltpu.make_async_copy(
            wq_hbm.at[:, lanes(8 * j + of_head)], wq_s.at[k, :, j * 128 : (j + 1) * 128], load_sem.at[10 + 3 * k + j]
        )
        for k, of_head in enumerate((head, other_head))
        for j in range(3)
    )
    loads = tuple(
        pltpu.make_async_copy(src, dst, load_sem.at[k])
        for k, (src, dst) in enumerate(((wd_hbm, wd_v), (wu_hbm.at[:, lanes(s, 1024)], wu_v.at[rows(s, T)])))
    )
    for copy in picks + loads:
        copy.start()
    for k in range(lens_ref.shape[1]):
        lens_s[k : k + 1] = jnp.full((1, 128), lens_ref[0, k], jnp.int32)

    @pl.when(home)
    def _():
        big[rows(q, T)] = x_ref[...]

    for copy in picks:
        copy.wait()
    wh_v[rows(s, T)] = wq_s[0]
    met()

    def half_rows(b, part):
        return big.at[pl.ds(pl.multiple_of(b * T + part * HALF, HALF), HALF)]

    def over_copy(part):
        src = x_ref.at[part * HALF : (part + 1) * HALF]
        return remote(src, half_rows(q, part), xs_send.at[24 + part], xs_recv.at[q], seq=cross, seg=2 * y + part)

    def twin_copy(part, recv, k):
        return remote(half_rows(q, part), half_rows(q, part), xs_send.at[24 + k], recv.at[q], seg=sib)

    twin_track, twin_rest = twin_copy(1 - c, xs_recv, 0), twin_copy(c, xu_recv, 1)

    @pl.when(home)
    def _():
        twin_track.start()
        twin_rest.start()

    @pl.when(jnp.logical_not(home))
    def _():
        over_copy(0).start()
        over_copy(1).start()

    mine_wh = wh_v.at[rows(s, T)]
    q_across = remote(wq_s.at[0], mine_wh, qs.at[0], qr.at[0], seg=across)
    q_sib = remote(wq_s.at[1], mine_wh, qs.at[1], qr.at[1], seg=sib)
    q_corner = remote(wq_s.at[1], mine_wh, qs.at[2], qr.at[2], seg=corner)
    l_sib = remote(lens_s, lens_r, qs.at[3], qr.at[3], seg=sib)
    first = (q_across, q_corner, q_sib, l_sib)
    for copy in first:
        copy.start()

    def x_copy(b, k, recv, **to):
        src = half_rows(b, c)
        return remote(src, src, xs_send.at[k], recv.at[b], **to)

    own_z, own_x = x_copy(q, 0, xs_recv, seq=near_z), x_copy(q, 8, xs_recv, seq=near_x)

    @pl.when(jnp.logical_not(home))
    def _():
        x_copy(q, 0, xs_recv, seq=q).wait_recv()

    own_z.start()
    own_x.start()

    def u_part(seg, part):
        return wu_v.at[pl.ds(pl.multiple_of(seg * T + part * HALF, HALF), HALF)]

    def o_part(seg, part):
        return wo_v.at[pl.ds(pl.multiple_of(seg * T + part * HALF, HALF), HALF)]

    u_far = tuple(
        remote(
            wu_hbm.at[pl.ds(pl.multiple_of(x * HALF, HALF), HALF), lanes(to, 1024)], u_part(s, x), ws.at[k], wr.at[k],
            seg=to,
        )
        for k, to in ((0, across), (1, corner))
    )
    u_over = tuple(
        remote(u_part(of_seg, x), u_part(of_seg, x), ws.at[11 + k], wr.at[11 + k], seq=near_x)
        for k, of_seg in ((0, across), (1, corner))
    )
    u_sib = remote(wu_hbm.at[:, lanes(sib, 1024)], wu_v.at[rows(s, T)], ws.at[2], wr.at[2], seg=sib)
    o_far = remote(
        wo_ref.at[pl.ds(pl.multiple_of(x * HALF, HALF), HALF)], o_part(s, x), ws.at[3], wr.at[3], seg=across
    )
    o_over = remote(o_part(across, x), o_part(across, x), ws.at[13], wr.at[13], seq=near_x)
    o_sib = remote(wo_ref, wo_v.at[rows(s, T)], ws.at[4], wr.at[4], seg=sib)
    o_pass = tuple(
        remote(o_part(across, part), o_part(across, part), ws.at[k], wr.at[k], seg=sib)
        for k, part in ((5, x), (14, 1 - x))
    )
    g_rows = lambda k, part: g_v.at[pl.ds(2 * T + part * T + k * HALF, HALF)]
    g_across = tuple(
        remote(g_ref.at[k * HALF : (k + 1) * HALF], g_rows(0, k), ws.at[6 + k], wr.at[6 + k], seg=across)
        for k in range(2)
    )
    g_sib = remote(g_ref, g_v.at[T : 2 * T], ws.at[8], wr.at[8], seg=sib)
    g_pass = tuple(remote(g_rows(0, k), g_rows(1, k), ws.at[9 + k], wr.at[9 + k], seg=sib) for k in range(2))
    wo_v[rows(s, T)] = wo_ref[...]
    g_v[0:T] = g_ref[...]
    for copy in u_far + (o_far,) + g_across:
        copy.start()
    for copy in first:
        copy.wait_recv()
    lens = jnp.where(home, lens_s[...], lens_r[...])

    gain, bias = gain_ref[...], bias_ref[...]

    def keep(b):
        at = rows(b, T)
        return (
            pltpu.make_async_copy(big.at[at], xs_hbm.at[at], keep_sem.at[b]),
            pltpu.make_async_copy(pack.at[b], h1_hbm.at[at], keep_sem.at[8 + b]),
        )

    def project(b):
        unit, _ = norm_parts(big[rows(b, T)].astype(F32))
        low = (unit * gain + bias).astype(BF)
        pack[b] = low
        qkv_v[rows(b, T)] = dot_nn(low, wh_v[...]).astype(BF)
        for copy in keep(b):
            copy.start()

    def track_step(k, _):
        b = nth(blocks, k)

        @pl.when(k < 8)
        def _():
            x_copy(b, 0, xs_recv, seq=q).wait_recv()

        @pl.when((k == 1) | (k == 3))
        def _():
            x_copy(b, k, xs_recv, seq=near_z).start()

        @pl.when((k == 3) | (k == 4))
        def _():
            x_copy(b, 8 + k, xs_recv, seq=near_x).start()

        @pl.when(k < 8)
        def _():
            x_copy(b, 16 + k, xu_recv, seg=sib).start()

        last = nth(blocks, k - 1)

        @pl.when((k > 1) | jnp.logical_not(home))
        def _():
            x_copy(last, 0, xu_recv, seg=sib).wait_recv()

        project(last)

        return 0

    lax.fori_loop(1, 6, track_step, 0)
    for arrived, copy in zip(u_far, u_over):
        arrived.wait_recv()
        copy.start()
    lax.fori_loop(6, 9, track_step, 0)
    o_far.wait_recv()
    o_over.start()
    o_pass[0].start()
    for copy in (u_sib, o_sib, g_sib):
        copy.start()

    def o_copy(i, sender):
        return remote(
            ob.at[i // 4, (i // 2) % 2, i % 2], o_v.at[:, lanes(sender)], os_send.at[i], os_recv.at[sender], seq=i, seg=column
        )

    o_mine = pltpu.make_async_copy(ob.at[group, z % 2, x], o_v.at[:, lanes(head)], os_recv.at[head])
    for i in (4, 5, 6, 7, 0, 1, 2, 3):
        n = (i + 1) * T
        start = first_columns(lens, i * T, T)
        scores = dot_nt(qkv_v[i * T : n, :128], qkv_v[:n, 128:256]) * scale
        scores = jnp.where(seen_mask(start, i * T, 0, T, n), scores, -1e30)
        top = jnp.max(scores, axis=1, keepdims=True)
        weights = jnp.exp(scores - top)
        total = jnp.sum(weights, axis=1, keepdims=True)
        mixed = dot_nn(weights.astype(BF), qkv_v[:n, 256:384]) / total
        of_v[i * T : n] = mixed
        lse_v[:, i : i + 1] = top + jnp.log(total)
        ob[i // 4, (i // 2) % 2, i % 2] = mixed.astype(BF)
        here = (q == i) & home

        @pl.when(jnp.logical_not(here))
        def _():
            o_copy(i, head).start()

        @pl.when(here)
        def _():
            o_mine.start()

    o_over.wait_recv()
    o_pass[1].start()
    for arrived, copy in zip(g_across, g_pass):
        arrived.wait_recv()
        copy.start()

    for i in range(8):
        o_copy(i, i).wait_recv()
    for copy in o_pass + (o_sib,):
        copy.wait_recv()

    value = x_ref[...].astype(F32) + dot_nn(o_v[...], wo_v[...])
    middle[...] = value
    unit, _ = norm_parts(value)
    h2[0:T] = (unit * gain2_ref[...] + bias2_ref[...]).astype(BF)

    def far_rows(ref, part, k):
        return ref.at[pl.ds(2 * T + k * T + part * HALF, HALF)]

    h_far = tuple(
        remote(h2.at[k * HALF : (k + 1) * HALF], far_rows(h2, 0, k), hs.at[k], hr.at[k], seg=across)
        for k in range(2)
    )
    h_pass = tuple(
        remote(far_rows(h2, 0, k), far_rows(h2, 1, k), hs.at[2 + k], hr.at[2 + k], seg=sib) for k in range(2)
    )
    h_sib = remote(h2.at[0:T], h2.at[T : 2 * T], hs.at[4], hr.at[4], seg=sib)
    for copy in h_far + (h_sib,):
        copy.start()
    for copy in loads:
        copy.wait()
    for copy in u_over + g_pass + (u_sib, g_sib):
        copy.wait_recv()
    for b in range(8):
        for copy in keep(b):
            copy.wait()
    for k in range(1, 8):
        if k in (1, 3):
            x_copy(blocks[k], k, xs_recv, seq=near_z).wait_send()
        if k in (3, 4):
            x_copy(blocks[k], 8 + k, xs_recv, seq=near_x).wait_send()
        x_copy(blocks[k], 16 + k, xu_recv, seg=sib).wait_send()

    @pl.when(home)
    def _():
        twin_track.wait_send()
        twin_rest.wait_send()

    @pl.when(jnp.logical_not(home))
    def _():
        over_copy(0).wait_send()
        over_copy(1).wait_send()

    for i in range(8):
        @pl.when(jnp.logical_not((q == i) & home))
        def _():
            o_copy(i, head).wait_send()

    for copy in first + u_far + u_over + o_pass + g_across + g_pass + (u_sib, o_far, o_over, o_sib, g_sib, own_z, own_x):
        copy.wait_send()

    def work(part):
        at = slice(part * T, (part + 1) * T)
        value, slope = gelu_parts(dot_nn(h2[at], wu_v[...]))
        low = value.astype(BF)
        big[at] = low
        du = (slope * dot_nt(g_v[at], wd_v[...])).astype(BF)
        big[4 * T + part * T : 4 * T + (part + 1) * T] = du
        return dot_nt(du, wu_v[...]), dot_nn(low, wd_v[...])

    near = tuple(remote(near_s.at[k], near_r.at[k], ns.at[k], nr.at[k], seg=sib) for k in range(2))
    twin = tuple(
        tuple(remote(twin_s.at[k, n], twin_r.at[k, n], ts.at[2 * k + n], tr.at[2 * k + n], seg=sib) for n in range(2))
        for k in range(2)
    )
    far = tuple(
        tuple(remote(far_s.at[k, n], far_r.at[k, n], fs.at[2 * k + n], fr.at[2 * k + n], seg=across) for n in range(2))
        for k in range(2)
    )

    def send_twin(n, parts):
        for k in range(2):
            far_keep[k] = parts[k][:HALF]
            twin_s[k, n] = parts[k][HALF:].astype(BF)
            twin[k][n].start()

    def send_far(n):
        for k in range(2):
            twin[k][n].wait_recv()
            far_s[k, n] = (far_keep[k] + twin_r[k, n].astype(F32)).astype(BF)
            if k == 0:
                far[k][n].start()

    parts = work(0)
    for k in range(2):
        mine[k] = parts[k]
    h_sib.wait_recv()
    parts = work(1)
    for k in range(2):
        near_s[k] = parts[k].astype(BF)
        near[k].start()
    h_far[0].wait_recv()
    h_pass[0].start()
    h_pass[0].wait_recv()
    send_twin(0, work(2))
    h_far[1].wait_recv()
    h_pass[1].start()
    send_far(0)
    h_pass[1].wait_recv()
    send_twin(1, work(3))
    send_far(1)

    def gx_copy(d):
        return remote(pack.at[2 * d + 1 - x], x_r.at[d], gxs.at[d], gxr.at[d], seq=near_x)

    zn, zc = z + 1 - 2 * (z % 2), (z + 2) % 4
    znc = (zn + 2) % 4

    def pack_rows(k, _):
        d = nth((znc, zc, zn, z), k)
        up = dot_tn(h2[:, lanes(d, T)], big[4 * T :]).astype(BF)
        down = dot_tn(big[: 4 * T], g_v[:, lanes(d, T)]).astype(BF)
        for e in range(2):
            pack[2 * d + e, :, :512] = up[:, e * 512 : (e + 1) * 512]
            for j in range(4):
                pack[2 * d + e, :, 512 + j * 128 : 640 + j * 128] = down[
                    j * T : (j + 1) * T, e * 128 : (e + 1) * 128
                ]

        @pl.when(k < 1)
        def _():
            gx_copy(d).start()

        return 0

    lax.fori_loop(0, 4, pack_rows, 0)

    near[0].wait_recv()
    far[0][0].wait_recv()
    far[0][1].wait_recv()
    grad = mine[0] + near_r[0].astype(F32) + jnp.concatenate([far_r[0, 0], far_r[0, 1]], axis=0).astype(F32)
    unit, inverse = norm_parts(middle[...])
    vec[...] = jnp.zeros_like(vec)
    vec[2:3] = jnp.sum(grad * unit, axis=0, keepdims=True)
    vec[3:4] = jnp.sum(grad, axis=0, keepdims=True)
    dx = g_v[0:T].astype(F32) + norm_back(grad, gain2_ref[...], unit, inverse)
    dx_v[...] = dx
    dy = dx.astype(BF)
    do_v[...] = dot_nt(dy, wo_v[...]).astype(BF)

    def do_copy(h, block):
        return remote(
            do_v.at[:, h * 128 : (h + 1) * 128], doh.at[rows(block, T)], dos.at[h], dor.at[block],
            seq=2 * (2 * c + h // 4) + (h // 2) % 2, seg=2 * y + h % 2,
        )

    do_mine = pltpu.make_async_copy(do_v.at[:, lanes(head)], doh.at[rows(q, T)], dor.at[q])
    for h in range(8):
        self_too = (head == h) & home

        @pl.when(jnp.logical_not(self_too))
        def _():
            do_copy(h, q).start()

        @pl.when(self_too)
        def _():
            do_mine.start()

    for copy in h_far + h_pass + (h_sib,):
        copy.wait_send()
    h2[...] = dot_tn(o_v[...], dy).astype(BF)

    def out_rows(part, core):
        return h2.at[rows(2 * part + core, T)]

    out_core = tuple(remote(out_rows(k, 1 - c), oc_r.at[k], cs.at[5 + k], cr.at[5 + k], seg=sib) for k in range(2))
    for copy in out_core:
        copy.start()
    for part in range(2):
        out_core[part].wait_recv()
        oc_r[part] = (oc_r[part].astype(F32) + out_rows(part, c)[...].astype(F32)).astype(BF)
    out_y = remote(oc_r.at[1 - y], oy_r, cs.at[1], cr.at[1], seg=across)
    out_y.start()
    far[1][0].start()
    far[1][1].start()

    def come(into, recv, slot):
        return remote(into.at[slot], into.at[slot], recv.at[slot], recv.at[slot], seq=near_x)

    def gz_copy(k, d, to):
        return remote(x_r.at[d], z_r.at[k], gzs.at[k], gzr.at[k], seq=to)

    gz = (gz_copy(0, znc, near_z), gz_copy(1, zn, near_z), gz_copy(2, zc, cross))

    def pack_sum(d):
        gx_copy(d).wait_recv()
        return pack[2 * d + x].astype(F32) + x_r[d].astype(F32)

    x_r[znc] = pack_sum(znc).astype(BF)
    gz[0].start()

    dk[...] = jnp.zeros_like(dk)
    dv[...] = jnp.zeros_like(dv)
    for i in range(8):
        do_copy(0, i).wait_recv()
        if i == 7:
            gx_copy(zc).start()
        top = i * T
        start = first_columns(lens, top, T)
        query = qkv_v[top : top + T, :128]
        grad = doh[top : top + T]
        delta = jnp.sum(grad.astype(F32) * of_v[top : top + T], axis=1, keepdims=True)
        log_total = lse_v[:, i : i + 1]
        total = jnp.zeros((T, 128), F32)
        for base in range(0, top + T, 1024):
            n = min(1024, top + T - base)
            keys = qkv_v[base : base + n, 128:256]
            probs = jnp.exp(dot_nt(query, keys) * scale - log_total)
            probs = jnp.where(seen_mask(start, top, base, T, n), probs, 0.0)
            dp = dot_nt(grad, qkv_v[base : base + n, 256:384])
            ds = (probs * (dp - delta)).astype(BF)
            dv[base : base + n] += dot_tn(probs.astype(BF), grad)
            dk[base : base + n] += dot_tn(ds, query)
            total += dot_nn(ds, keys)
        dq[top : top + T] = total

    gq[...] = jnp.zeros_like(gq)
    own_a, other_xa, other_za, own_b, other_zb, other_xb, diag_a, diag_b = blocks
    order = (diag_a, diag_b, other_za, other_xb, other_xa, other_zb, own_a, own_b)

    def x_load(i):
        return pltpu.make_async_copy(xs_hbm.at[rows(nth(order, i), T)], wu_v.at[rows(i % 2, T)], load_sem.at[2 + i % 2])

    def h_load(i):
        return pltpu.make_async_copy(h1_hbm.at[rows(nth(order, i), T)], wu_v.at[rows(2 + i % 2, T)], load_sem.at[4 + i % 2])

    def dhc_copy(b):
        return remote(
            big.at[pl.ds(pl.multiple_of(b * T + (1 - c) * HALF, HALF), HALF)], wo_v.at[rows(b, HALF)], dcs.at[b], dcr.at[b], seg=sib
        )

    def half(b):
        return big.at[pl.ds(pl.multiple_of(b * T + c * HALF, HALF), HALF)]

    def step_copy(k, b, to):
        return remote(wo_v.at[rows(b, HALF)], wd_v.at[rows(k, HALF)], sts.at[k], str_.at[k], seq=to)

    steps = (
        step_copy(0, diag_a, near_z), step_copy(1, diag_b, near_x), step_copy(2, other_za, near_z),
        step_copy(3, other_xb, near_x), step_copy(4, other_xa, near_x), step_copy(5, other_zb, near_z),
    )
    x_load(0).start()
    h_load(0).start()

    def grads_at(at):
        return jnp.concatenate([dq[at] * scale, dk[at] * scale, dv[at]], axis=1).astype(BF)

    def block_step(i, _):
        @pl.when(i < 8)
        def _():
            b = nth(order, i)

            at = rows(b, T)
            big[at] = dot_nt(grads_at(at), wh_v[...]).astype(BF)
            dhc_copy(b).start()

        @pl.when(i > 0)
        def _():
            b = nth(order, i - 1)
            dhc_copy(b).wait_recv()
            wo_v[rows(b, HALF)] = (half(b)[...].astype(F32) + wo_v[rows(b, HALF)].astype(F32)).astype(BF)
            for k in range(4):
                @pl.when(i == k + 1)
                def _():
                    steps[k].start()

        return 0

    lax.fori_loop(0, 9, block_step, 0)
    gx_copy(zn).start()
    gz[0].wait_recv()
    x_r[zc] = (pack_sum(zc) + z_r[0].astype(F32)).astype(BF)
    gz[2].start()


    def sum_step(i, _):
        @pl.when(i < 7)
        def _():
            x_load(i + 1).start()
            h_load(i + 1).start()

        at = rows(nth(order, i), T)
        dh = big[at].astype(F32)
        x_load(i).wait()
        h_load(i).wait()
        gq[...] += dot_tn(wu_v[rows(2 + i % 2, T)], grads_at(at))
        unit, _ = norm_parts(wu_v[rows(i % 2, T)].astype(F32))
        vec[0:1] += jnp.sum(dh * unit, axis=0, keepdims=True)
        vec[1:2] += jnp.sum(dh, axis=0, keepdims=True)
        return 0

    lax.fori_loop(0, 8, sum_step, 0)
    for k, b in ((5, other_zb), (4, other_xa)):
        steps[k - 4].wait_recv()
        wo_v[rows(b, HALF)] = (wo_v[rows(b, HALF)].astype(F32) + wd_v[(k - 4) * HALF : (k - 3) * HALF].astype(F32)).astype(BF)
        steps[k].start()

    x_r[zn] = pack_sum(zn).astype(BF)
    gz[1].start()

    out_y.wait_recv()
    out = (oc_r[y].astype(F32) + oy_r[...].astype(F32)).astype(BF)
    for k in range(8):
        ob[k // 4, (k // 2) % 2, k % 2] = out[:, k * 128 : (k + 1) * 128]
    out_x = remote(ob.at[:, :, 1 - x], ox_r, cs.at[2], cr.at[2], seq=near_x)
    out_x.start()
    gx_copy(z).start()

    gq_b[...] = gq[...].astype(BF).reshape(2, 2, T, 384)
    q_y = remote(gq_b.at[1 - y], gq_y, gqs.at[0], gqr.at[0], seg=across)
    q_y.start()
    v_core = remote(vec, vec_r.at[0], vs.at[8], vr.at[8], seg=sib)
    v_core.start()
    v_core.wait()
    vec[...] += vec_r[0]
    v_y = remote(vec, vec_r.at[1], vs.at[9], vr.at[9], seg=across)
    v_y.start()
    def fin_sum(k, b, pair):
        for n in pair:
            steps[n].wait_recv()
        fin_s[k] = (
            wo_v[rows(b, HALF)].astype(F32) + wd_v[rows(pair[0], HALF)].astype(F32)
            + wd_v[rows(pair[1], HALF)].astype(F32)
        ).astype(BF)

    fin_over = remote(fin_s.at[1], fin_r.at[c], fns.at[0], fnr.at[c], seq=cross, seg=column)
    fin_twin = remote(fin_s.at[0], fin_r.at[c], fns.at[1], fnr.at[c], seg=sib)
    fin_own = pltpu.make_async_copy(fin_s.at[0], fin_r.at[c], fnr.at[c])
    fin_sum(1, own_b, (3, 5))
    fin_over.start()
    fin_sum(0, own_a, (2, 4))

    @pl.when(away)
    def _():
        fin_twin.start()

    @pl.when(home)
    def _():
        fin_own.start()

    v_y.wait()
    vec[...] += vec_r[1]

    def v_copy(b, sender):
        return remote(vec, vec_r.at[2 + sender], vs.at[b], vr.at[sender], seq=b)

    for b in range(8):
        @pl.when(q != b)
        def _():
            v_copy(b, q).start()

    q_y.wait_recv()
    gq_y[...] = (gq_y[...].astype(F32) + gq_b[y].astype(F32)).astype(BF)

    def column_copy(part, j):
        place = 8 * j + head
        owner, slot = place // 3, place % 3
        src = gq_y.at[part, :, j * 128 : (j + 1) * 128]
        copy = remote(
            src, gq_r.at[slot, group], gqs.at[1 + 3 * part + j], gqr.at[1 + 2 * slot + group],
            seq=owner, seg=2 * y + part,
        )
        local = pltpu.make_async_copy(src, gq_r.at[slot, group], gqr.at[1 + 2 * slot + group])
        return (owner == q) & (c == part), copy, local

    columns = tuple(column_copy(part, j) for part in range(2) for j in range(3))
    out_x.wait_recv()
    ox_r[...] = (ox_r[...].astype(F32) + ob[:, :, x].astype(F32)).astype(BF)
    out_z = remote(ox_r.at[:, 1 - z % 2], oz_r, cs.at[3], cr.at[3], seq=near_z)
    out_z.start()
    for self_too, copy, local in columns:
        @pl.when(jnp.logical_not(self_too))
        def _():
            copy.start()

        @pl.when(self_too)
        def _():
            local.start()

    out_z.wait_recv()
    oz_r[...] = (oz_r[...].astype(F32) + ox_r[:, z % 2].astype(F32)).astype(BF)
    out_o = remote(oz_r.at[1 - group], oo_r, cs.at[4], cr.at[4], seq=cross)
    out_o.start()

    total = pack_sum(z)
    for k in (1, 2):
        gz[k].wait_recv()
        total = total + z_r[k].astype(F32)
    up_s[...] = total[:, :512].astype(BF)
    turned = s != z
    up_turn = remote(up_s, up_r, ups, upr, seq=2 * s + x, seg=z)
    up_own = pltpu.make_async_copy(up_s, up_r, upr)

    @pl.when(turned)
    def _():
        up_turn.start()

    @pl.when(jnp.logical_not(turned))
    def _():
        up_own.start()

    for j in range(4):
        gdown_out[j * T : (j + 1) * T] = total[:, 512 + j * 128 : 640 + j * 128]
    vec_r[2 + q] = vec[...]
    for b in range(8):
        @pl.when(q != b)
        def _():
            v_copy(b, b).wait_recv()

    vec_sum = vec_r[2]
    for b in range(1, 8):
        vec_sum = vec_sum + vec_r[2 + b]
    out_o.wait_recv()
    gout_out[...] = oz_r[group].astype(F32) + oo_r[...].astype(F32)
    sums_out[...] = vec_sum
    for slot in range(3):
        for part in range(2):
            pltpu.make_async_copy(gq_r.at[slot, part], gq_r.at[slot, part], gqr.at[1 + 2 * slot + part]).wait()
    near[1].wait_recv()
    far[1][0].wait_recv()
    far[1][1].wait_recv()
    result_out[...] = (
        middle[...] + mine[1] + near_r[1].astype(F32)
        + jnp.concatenate([far_r[1, 0], far_r[1, 1]], axis=0).astype(F32)
    ).astype(BF)
    for k in range(2):
        come(fin_r, fnr, k).wait_recv()
    up_own.wait()

    for h in range(8):
        @pl.when(jnp.logical_not((head == h) & home))
        def _():
            do_copy(h, q).wait_send()

    for b in range(8):
        dhc_copy(b).wait_send()

        @pl.when(q != b)
        def _():
            v_copy(b, q).wait_send()

    for d in range(4):
        gx_copy(d).wait_send()
    for copy in out_core + (out_y, out_x, out_z, out_o, q_y, fin_over) + near + steps + gz:
        copy.wait_send()
    for k in range(2):
        for n in range(2):
            twin[k][n].wait_send()
            far[k][n].wait_send()

    @pl.when(away)
    def _():
        fin_twin.wait_send()

    @pl.when(turned)
    def _():
        up_turn.wait_send()

    for self_too, copy, _ in columns:
        @pl.when(jnp.logical_not(self_too))
        def _():
            copy.wait_send()


def layer(x, lens, g, wo, gain, bias, gain2, bias2, wq, wu, wd):
    dma = pltpu.SemaphoreType.DMA
    low = lambda *shape: pltpu.VMEM(shape, BF)
    wide = lambda *shape: pltpu.VMEM(shape, F32)
    return pl.pallas_call(
        layer_kernel,
        out_shape=(
            S((256, 1024), BF), S((256, 1024), F32), S((2, 128, 1024), BF), S((3, 2, 256, 128), BF),
            S((256, 128), F32), S((256, 512), BF), S((1024, 128), F32), S((8, 1024), F32),
            S((2048, 1024), BF), S((2048, 1024), BF),
        ),
        in_specs=[VM, SM] + [VM] * 6 + [HB] * 3,
        out_specs=(VM,) * 8 + (HB,) * 2,
        scratch_shapes=[
            low(1024, 1024), low(1024, 1024), low(1024, 1024), low(1024, 1024), low(256, 1024), low(2048, 384),
            wide(2048, 128), wide(256, 8), low(1024, 384), dma((16,)),
            dma((16,)), low(2, 2, 2, 256, 128), low(2, 256, 384), pltpu.VMEM((8, 128), jnp.int32),
            pltpu.VMEM((8, 128), jnp.int32), dma((4,)), dma((4,)), dma((15,)), dma((15,)),
            dma((26,)), dma((8,)), dma((8,)), dma((8,)), dma((8,)),
            wide(256, 1024), low(1024, 1024), low(2048, 1024), wide(2, 256, 1024),
            low(2, 256, 1024), low(2, 256, 1024), low(2, 2, 128, 1024), low(2, 2, 128, 1024), wide(2, 128, 1024),
            low(2, 2, 128, 1024), low(2, 2, 128, 1024), low(256, 1024),
            dma((5,)), dma((5,)), dma((2,)), dma((2,)), dma((4,)), dma((4,)), dma((4,)), dma((4,)),
            low(8, 256, 1024), low(4, 256, 1024), low(3, 256, 1024), low(256, 512),
            dma((4,)), dma((4,)), dma((3,)), dma((3,)), dma, dma,
            low(2, 256, 1024), low(256, 1024), low(2, 2, 256, 128),
            low(2, 256, 128), low(256, 128), dma((7,)), dma((7,)),
            low(2048, 128), wide(2048, 128), wide(2048, 128), wide(2048, 128), dma((8,)), dma((8,)),
            low(2, 128, 1024),
            dma((8,)), dma((8,)), dma((6,)), dma((6,)), dma((2,)), dma((2,)),
            wide(1024, 384), low(2, 2, 256, 384), low(2, 256, 384),
            dma((7,)), dma((7,)),
            wide(8, 1024), wide(10, 8, 1024), dma((10,)), dma((10,)),
        ],
        compiler_params=pltpu.CompilerParams(
            collective_id=1, has_side_effects=True, vmem_limit_bytes=63 * 2**20
        ),
        cost_estimate=pl.CostEstimate(flops=2 * 10**10, bytes_accessed=40 * 2**20, transcendentals=2 * 2**20),
        name="layer",
    )(x, lens, g, wo, gain, bias, gain2, bias2, wq, wu, wd)


def finish_kernel(
    x_ref, gain_ref, result_ref, dx_ref, fin_ref, gq_ref, out_ref, up_ref, down_ref, sums_ref,
    result, dx, gain_one, bias_one, gqkv, gout, gain_two, bias_two, gup, gdown,
):
    result[...] = result_ref[...]
    unit, inverse = norm_parts(x_ref[...].astype(F32))
    dx[...] = dx_ref[...] + norm_back(fin_ref[0].astype(F32), gain_ref[...], unit, inverse)
    for slot in range(3):
        gqkv[:, slot * 128 : (slot + 1) * 128] = gq_ref[slot, 0].astype(F32) + gq_ref[slot, 1].astype(F32)
    gout[...] = out_ref[...]
    gup[...] = up_ref[...].astype(F32)
    gdown[...] = down_ref[...]
    for k, ref in enumerate((gain_one, bias_one, gain_two, bias_two)):
        ref[...] = sums_ref[k]


def finish(x, gain, *parts):
    line = S((1024,), F32)
    part = lambda r, n: pl.BlockSpec((r // 2, n), lambda i: (i, 0))
    whole = lambda r, n: pl.BlockSpec((r, n), lambda i: (0, 0))
    row = pl.BlockSpec((1024,), lambda i: (0,))
    return pl.pallas_call(
        finish_kernel,
        grid=(2,),
        out_shape=(
            S((256, 1024), BF), S((256, 1024), F32), line, line, S((256, 384), F32), S((256, 128), F32), line, line,
            S((256, 512), F32), S((1024, 128), F32),
        ),
        in_specs=[
            part(256, 1024), whole(1, 1024), part(256, 1024), part(256, 1024),
            pl.BlockSpec((1, 128, 1024), lambda i: (i, 0, 0)),
            pl.BlockSpec((3, 2, 128, 128), lambda i: (0, 0, i, 0)), part(256, 128), part(256, 512), part(1024, 128),
            whole(8, 1024),
        ],
        out_specs=(
            part(256, 1024), part(256, 1024), row, row, part(256, 384), part(256, 128), row, row, part(256, 512),
            part(1024, 128),
        ),
        compiler_params=pltpu.CompilerParams(vmem_limit_bytes=60 * 2**20),
        name="finish",
    )(x, gain, *parts)


def per_device_fast(
    tokens, article_lengths, gain_one, bias_one, w_qkv, w_out, gain_two, bias_two, w_up, w_down, cotangent
):
    x = tokens[0]
    *parts, _, _ = layer(
        x, article_lengths, cotangent[0], w_out, gain_one[None], bias_one[None], gain_two[None], bias_two[None],
        w_qkv, w_up, w_down,
    )
    result, dx, *rest = finish(x, gain_one[None], *parts)
    return (result[None], dx[None], *rest)


def solution(mesh):
    one_pair = mesh.shape["seq"] == HEADS and mesh.shape["seg"] == 4
    return jax.shard_map(
        per_device_fast if one_pair else per_device,
        mesh=mesh,
        in_specs=(
            P("seg", "seq", None),
            P("seg", None),
            P(),
            P(),
            P("seg", None),
            P("seg", None),
            P(),
            P(),
            P("seg", None),
            P("seg", None),
            P("seg", "seq", None),
        ),
        out_specs=(
            P("seg", "seq", None),
            P("seg", "seq", None),
            P(),
            P(),
            P("seg", "seq"),
            P("seg", "seq"),
            P(),
            P(),
            P("seg", "seq"),
            P("seg", "seq"),
        ),
        check_vma=False,
    )
```
